32 devices in a mesh: expert: 2 (over x), context: 4 (over y, core), dp: 4 (over z).
Axes of the slice: x: 2, y: 2, z: 4, core: 2. Of those that a mesh axis runs over, the one named last changes fastest.
Arguments:
- tokens: bfloat16 [8, 1024, 768], P(('expert', 'dp'), 'context'), may hold values from -6 to 6
- doc_ids: int32 [8, 1024], P(('expert', 'dp')), may hold values from 0 to 1, never falling along the last dimension, each value on 1 to 768 neighbouring positions
- routes: int32 [8, 1024, 2], P(('expert', 'dp'), 'context'), may hold values from 0 to 7, all different within a row; in each aligned block of 256 rows (0 to 255, 256 to 511, ..., all dimensions but the last counted through in order) at most 64 rows name the same one
- prev_logits: float32 [8, 1024, 8], P(('expert', 'dp'), 'context'), may hold values from -3 to 3
- cotangent: float32 [8, 1024, 768], P(('expert', 'dp'), 'context'), may hold values from -6 to 6
- w_query: float32 [768, 768], P(('expert', 'context', 'dp')), may hold values from -0.21875 to 0.21875
- w_key: float32 [768, 768], P(('expert', 'context', 'dp')), may hold values from -0.21875 to 0.21875
- w_value: float32 [768, 768], P(('expert', 'context', 'dp')), may hold values from -0.21875 to 0.21875
- w_out: float32 [768, 768], P(('expert', 'context', 'dp')), may hold values from -0.625 to 0.625
- w_router: float32 [768, 8], P(('expert', 'context', 'dp')), may hold values from -0.15625 to 0.15625
- const_coef: float32 [768, 4], P(('expert', 'context', 'dp')), may hold values from -0.21875 to 0.21875
- const_value: float32 [768, 2], P(('expert', 'context', 'dp')), may hold values from -5 to 5
- norm_gains: float32 [768, 2], P(('expert', 'context', 'dp')), may hold values from 0.5 to 1.5
- expert_gate: float32 [4, 768, 2048], P('expert', None, ('context', 'dp')), may hold values from -0.21875 to 0.21875
- expert_up: float32 [4, 768, 2048], P('expert', None, ('context', 'dp')), may hold values from -0.21875 to 0.21875
- expert_down: float32 [4, 768, 2048], P('expert', None, ('context', 'dp')), may hold values from -0.25 to 0.25
Outputs:
- block_out: float32 [8, 1024, 768], P(('expert', 'dp'), 'context')
- grad_tokens: float32 [8, 1024, 768], P(('expert', 'dp'), 'context')
- grad_prev: float32 [8, 1024, 8], P(('expert', 'dp'), 'context')
- grad_query: float32 [768, 768], P(('expert', 'context', 'dp'))
- grad_key: float32 [768, 768], P(('expert', 'context', 'dp'))
- grad_value: float32 [768, 768], P(('expert', 'context', 'dp'))
- grad_out: float32 [768, 768], P(('expert', 'context', 'dp'))
- grad_router: float32 [768, 8], P(('expert', 'context', 'dp'))
- grad_coef: float32 [768, 4], P(('expert', 'context', 'dp'))
- grad_constant: float32 [768, 2], P(('expert', 'context', 'dp'))
- grad_gains: float32 [768, 2], P(('expert', 'context', 'dp'))
- grad_gate: float32 [4, 768, 2048], P('expert', None, ('context', 'dp'))
- grad_up: float32 [4, 768, 2048], P('expert', None, ('context', 'dp'))
- grad_down: float32 [4, 768, 2048], P('expert', None, ('context', 'dp'))
The draws below stay inside these ranges and needn't reach their ends.
Inputs may be any that keep to these rules, and one draw needn't show every extreme that they name: `routes`: each row names 2 different numbers: below 4 a feed-forward expert, 4 the zero expert, 5 the copy expert, 6 and 7 the constant experts. In the rows of one device no number is named by more than 64 rows. `doc_ids`: within a sequence the document number never falls.
All inputs are finite; a program needn't handle non-finite values.
Results may differ from the reference program's by a relative error of at most 0.015.
Values may be sent and summed in bfloat16 or wider, within the bound.
A program may use at most 192 MiB of HBM per device.

```python
import math
import jax
import jax.numpy as jnp
import numpy as np
from jax import lax

D = 768
HEADS = 12
HEAD_DIM = 64
FF = 2048
EXPERTS = 4
TOP = 2
LENGTH = 1024
ROWS = 256
MOST = 64
SEQS = 8


def shard_levels(key, dims, cuts, least, top_value):
    factor_of, own = 1.0, jax.random.fold_in(key, 6)
    for position, shards_of in cuts:
        steps = jnp.exp(jax.random.uniform(jax.random.fold_in(own, position), (shards_of,), jnp.float32, least / len(cuts), top_value / len(cuts)))
        factor_of = factor_of * jnp.repeat(steps, dims[position] // shards_of).reshape([-1 if axis == position else 1 for axis in range(len(dims))])
    return factor_of


def length_profile(count, total, bound, lean):
    weights = [(1 << 20) // math.isqrt(grade ** lean) + 1 for grade in range(2, count + 1)]
    rest, counts = total - bound - (count - 1), [1] * (count - 1)
    while rest > 0:
        movable = [i for i in range(count - 1) if counts[i] < bound]
        mass, left = sum([weights[i] for i in movable]), rest
        for i in movable:
            extra = min(bound - counts[i], max(1, left * weights[i] // mass), rest)
            counts[i] = counts[i] + extra
            rest = rest - extra
    return np.array([bound] + counts)


def ragged_sizes(stream_key, count, total, limit, slope):
    if count == 2:
        one = jax.random.randint(stream_key, (), max(1, total - limit), min(limit, total - 1) + 1)
        return jnp.stack([one, total - one])
    tallies = jnp.asarray(length_profile(count, total, limit, slope), jnp.int32)
    couples = (count - 1) // 2
    source_of, receiver = tallies[1:1 + 2 * couples:2], tallies[2:2 + 2 * couples:2]
    slack = jnp.minimum(source_of - 1, limit - receiver)
    shifted = jax.random.randint(jax.random.fold_in(stream_key, 1), (couples,), 0, 1 << 20) % (slack + 1)
    tallies = tallies.at[1:1 + 2 * couples:2].set(source_of - shifted).at[2:2 + 2 * couples:2].set(receiver + shifted)
    return tallies[jax.random.permutation(jax.random.fold_in(stream_key, 2), count)]


def deal_out(stream_key, own, number, rows, number_of, top, reach, lean):
    sequence = jax.random.permutation(stream_key, number_of)
    packed, common = shares(number_of, rows * top, reach, lean, True), shares(number_of, rows * top, reach, lean, False)
    places = jnp.arange(number_of)

    def named(lengths, turn):
        used = int((lengths > 0).sum())
        fixed = max(1, used // 4)
        passed = fixed + (places - fixed + turn * (used - fixed)) % max(1, number_of - fixed)
        return jnp.zeros((number_of,), jnp.int32).at[sequence[jnp.where(places < fixed, places, passed)]].set(jnp.asarray(lengths, jnp.int32))

    lengths = jnp.where(number % 4 == 0, named(packed, number // 4), named(common, number - number // 4 - 1))
    mixed = jax.random.permutation(jax.random.fold_in(own, 3), number_of)
    source_of, sink = mixed[0:number_of // 2 * 2:2], mixed[1:number_of // 2 * 2:2]
    room = jnp.minimum(lengths[source_of] - 1, reach - lengths[sink]) // 2
    room = jnp.where((source_of == sequence[0]) | (sink == sequence[0]) | (lengths[sink] == 0), 0, jnp.maximum(room, 0))
    passed = jax.random.randint(jax.random.fold_in(own, 4), (number_of // 2,), 0, 1 << 20) % (room + 1)
    lengths = lengths.at[source_of].add(-passed).at[sink].add(passed)
    members = jnp.searchsorted(jnp.cumsum(lengths), jnp.arange(rows * top), side="right").astype(jnp.int32)
    table = members.reshape(top, rows).T
    table = table[jax.random.permutation(jax.random.fold_in(own, 1), rows)]
    turn = jax.random.randint(jax.random.fold_in(own, 2), (rows, 1), 0, top)
    return jnp.take_along_axis(table, (jnp.arange(top)[None, :] + turn) % top, axis=1)


def shares(count, total, bound, slope, full):
    loads = [(1 << 20) // math.isqrt(rank ** slope) + 1 for rank in range(1, count + 1)]
    largest = bound if full else min(bound, max(-(-total // count), total * loads[0] // sum(loads)))
    least = 1 if total - largest >= count - 1 else 0
    given, rest = [largest] + [least] * (count - 1), total - largest - least * (count - 1)
    while rest > 0:
        candidates = [i for i in range(1, count) if given[i] < largest] or [i for i in range(1, count) if given[i] < bound]
        mass, left = sum([loads[i] for i in candidates]), rest
        for i in candidates:
            more = min(bound - given[i], max(1, left * loads[i] // mass), rest)
            given[i] = given[i] + more
            rest = rest - more
    return np.array(given)


def scatter_about(rng, extent, scale, bound, shards=(), kind=jnp.bfloat16):
    gain = shard_levels(rng, extent, shards, -0.22, 0.18) if shards else 1.0
    values = jax.random.normal(rng, extent, jnp.float32) * scale * gain
    return jnp.minimum(jnp.maximum(values, -bound), bound).astype(kind)


def setup_inputs(seed: int = 0) -> dict:
    streams_of = jax.random.split(jax.random.key(seed), 17)
    tokens = scatter_about(streams_of[0], (SEQS, LENGTH, D), 1.0, 6.0, ((0, 8), (1, 4)))
    doc_ids = jax.vmap(lambda own: jnp.searchsorted(jnp.cumsum(ragged_sizes(own, 2, LENGTH, LENGTH * 3 // 4, 0)), jnp.arange(LENGTH), side="right"))(jax.random.split(streams_of[1], SEQS)).reshape((SEQS, LENGTH)).astype(jnp.int32)
    routes_keys = jax.random.split(jax.random.fold_in(streams_of[2], 1), SEQS * LENGTH // ROWS)
    routes_turns = jax.random.permutation(jax.random.fold_in(streams_of[2], 3), SEQS * LENGTH // ROWS)
    routes = jax.vmap(lambda own, number: deal_out(jax.random.fold_in(streams_of[2], 2), own, number, ROWS, EXPERTS + 4, TOP, MOST, 1))(routes_keys, routes_turns).reshape((SEQS, LENGTH, TOP))
    prev_logits = scatter_about(streams_of[3], (SEQS, LENGTH, EXPERTS + 4), 0.5, 3.0, ((0, 8), (1, 4)), jnp.float32)
    cotangent = scatter_about(streams_of[4], (SEQS, LENGTH, D), 1.0, 6.0, ((0, 8), (1, 4)), jnp.float32)
    w_query = scatter_about(streams_of[5], (D, D), D ** -0.5, 0.21875, ((0, 32),), jnp.float32)
    w_key = scatter_about(streams_of[6], (D, D), D ** -0.5, 0.21875, ((0, 32),), jnp.float32)
    w_value = scatter_about(streams_of[7], (D, D), D ** -0.5, 0.21875, ((0, 32),), jnp.float32)
    w_out = scatter_about(streams_of[8], (D, D), (D // 8) ** -0.5, 0.625, ((0, 32),), jnp.float32)
    w_router = scatter_about(streams_of[9], (D, EXPERTS + 4), (2 * D) ** -0.5, 0.15625, ((0, 32),), jnp.float32)
    const_coef = scatter_about(streams_of[10], (D, 4), D ** -0.5, 0.21875, ((0, 32),), jnp.float32)
    const_value = scatter_about(streams_of[11], (D, 2), 1.0, 5.0, ((0, 32),), jnp.float32)
    norm_gains = jnp.clip(1.0 + 0.1 * jax.random.normal(streams_of[12], (D, 2), jnp.float32), 0.5, 1.5)
    expert_gate = scatter_about(streams_of[13], (EXPERTS, D, FF), D ** -0.5, 0.21875, ((0, 2), (2, 16)), jnp.float32)
    expert_up = scatter_about(streams_of[14], (EXPERTS, D, FF), D ** -0.5, 0.21875, ((0, 2), (2, 16)), jnp.float32)
    expert_down = scatter_about(streams_of[15], (EXPERTS, D, FF), (FF // 4) ** -0.5, 0.25, ((0, 2), (2, 16)), jnp.float32)
    return {"tokens": tokens, "doc_ids": doc_ids, "routes": routes, "prev_logits": prev_logits, "cotangent": cotangent, "w_query": w_query, "w_key": w_key, "w_value": w_value, "w_out": w_out, "w_router": w_router, "const_coef": const_coef, "const_value": const_value, "norm_gains": norm_gains, "expert_gate": expert_gate, "expert_up": expert_up, "expert_down": expert_down}


@jax.custom_vjp
def low(v):
    return lax.optimization_barrier(v.astype(jnp.bfloat16)).astype(jnp.float32)

@jax.custom_vjp
def low_back(v):
    return v

def low_keep(v):
    return (low(v), None)

def low_pass(kept, grad):
    return (grad,)

def back_keep(v):
    return (v, None)

def back_low(kept, grad):
    return (low(grad),)
low.defvjp(low_keep, low_pass)
low_back.defvjp(back_keep, back_low)
EPS = 1e-06
HIGHEST = lax.Precision.HIGHEST

def matmul(left_side, right_side):
    return jnp.dot(left_side, right_side, precision=HIGHEST)

def rms_norm(inputs, gain_row):
    return inputs * lax.rsqrt(lax.optimization_barrier(jnp.mean(inputs * inputs, axis=-1, keepdims=True)) + EPS) * gain_row

def soft_last(scores):
    row_top = lax.optimization_barrier(jnp.max(scores, axis=-1, keepdims=True))
    exponent = jnp.exp(scores - row_top)
    return exponent / lax.optimization_barrier(jnp.sum(exponent, axis=-1, keepdims=True))

def attend_sequence(operands):
    query_rows, key_rows, value_rows, documents = operands
    block_len = math.gcd(512, LENGTH)
    block_count = LENGTH // block_len
    key_heads = key_rows.reshape(LENGTH, HEADS, HEAD_DIM)
    value_heads = value_rows.reshape(LENGTH, HEADS, HEAD_DIM)
    positions = jnp.arange(LENGTH, dtype=jnp.int32)

    def one_block(pieces):
        q_part, q_place, q_docs = pieces
        scores = jnp.einsum('qhd,khd->hqk', q_part, key_heads, precision=HIGHEST) * HEAD_DIM ** (-0.5)
        scores = low_back(scores)
        allowed = (q_docs[:, None] == documents[None, :]) & (q_place[:, None] >= positions[None, :])
        scores = jnp.where(allowed[None, :, :], scores, -1e+30)
        weights_p = low(soft_last(scores))
        return jnp.einsum('hqk,khd->qhd', weights_p, value_heads, precision=HIGHEST)
    attended = lax.map(jax.checkpoint(one_block), (query_rows.reshape(block_count, block_len, HEADS, HEAD_DIM), positions.reshape(block_count, block_len), documents.reshape(block_count, block_len)))
    return attended.reshape(LENGTH, D)

def reference(tokens, doc_ids, routes, prev_logits, cotangent, w_query, w_key, w_value, w_out, w_router, const_coef, const_value, norm_gains, expert_gate, expert_up, expert_down):
    count_all = SEQS * LENGTH
    route_flat = routes.reshape(count_all, TOP).astype(jnp.int32)
    route_ids = route_flat.reshape(-1)
    route_hot = (route_ids[:, None] == jnp.arange(EXPERTS, dtype=jnp.int32)[None, :]).astype(jnp.int32)
    slot_rank = lax.optimization_barrier(jnp.sum((jnp.cumsum(route_hot, axis=0) - route_hot) * route_hot, axis=1))
    capacity = count_all // ROWS * MOST
    slot_index = jnp.where(route_ids < EXPERTS, route_ids * capacity + slot_rank, EXPERTS * capacity).astype(jnp.int32)
    owner_row = (jnp.arange(TOP * count_all, dtype=jnp.int32) // TOP).astype(jnp.int32)
    source = jnp.zeros((EXPERTS * capacity + 1,), jnp.int32).at[slot_index].set(owner_row)[:-1]
    filled = jnp.zeros((EXPERTS * capacity + 1,), jnp.float32).at[slot_index].set(1.0)[:-1]
    slot_pair = slot_index.reshape(count_all, TOP)
    choice_hot = (route_flat[:, :, None] == jnp.arange(EXPERTS + 4, dtype=jnp.int32)[None, None, :]).astype(jnp.float32)
    route_cube = route_flat[:, :, None]

    def forward(token_rows, prev_rows, q_weight, k_weight, v_weight, o_weight, r_weight, c_weight, c_value, gain_pair, gate_weight, up_weight, down_weight):
        row_data = token_rows.reshape(count_all, D)
        gains = low(gain_pair)
        normed_one = low(rms_norm(row_data, gains[:, 0]))
        query_rows = low(low_back(matmul(normed_one, low(q_weight))))
        key_rows = low(low_back(matmul(normed_one, low(k_weight))))
        value_rows = low(low_back(matmul(normed_one, low(v_weight))))
        mixed_rows = lax.map(attend_sequence, (query_rows.reshape(SEQS, LENGTH, D), key_rows.reshape(SEQS, LENGTH, D), value_rows.reshape(SEQS, LENGTH, D), doc_ids.astype(jnp.int32)))
        mixed_rows = low(low_back(mixed_rows.reshape(count_all, D)))
        hidden = row_data + low_back(matmul(mixed_rows, low(o_weight)))
        normed_two = low(rms_norm(hidden, gains[:, 1]))
        logits = low_back(matmul(normed_two, low(r_weight))) + prev_rows.reshape(count_all, EXPERTS + 4)
        chosen = lax.optimization_barrier(jnp.sum(choice_hot * logits[:, None, :], axis=-1))
        gate_w = soft_last(chosen)
        coef_logits = low_back(matmul(normed_two, low(c_weight)))
        first = soft_last(coef_logits[:, 0:2])
        second = soft_last(coef_logits[:, 2:4])
        value_b = low(c_value)
        const_one = first[:, 0:1] * normed_two + first[:, 1:2] * value_b[:, 0][None, :]
        const_two = second[:, 0:1] * normed_two + second[:, 1:2] * value_b[:, 1][None, :]
        buffer = normed_two[source] * filled[:, None]
        buffer = low_back(buffer.reshape(EXPERTS, capacity, D))
        gate_pre = low_back(jnp.einsum('ecd,edf->ecf', buffer, low(gate_weight), precision=HIGHEST))
        up_pre = low_back(jnp.einsum('ecd,edf->ecf', buffer, low(up_weight), precision=HIGHEST))
        hidden_units = low(gate_pre * jax.nn.sigmoid(gate_pre) * up_pre)
        result = low(low_back(jnp.einsum('ecf,edf->ecd', hidden_units, low(down_weight), precision=HIGHEST)))
        padded = jnp.concatenate([result.reshape(EXPERTS * capacity, D), jnp.zeros((1, D), jnp.float32)], axis=0)
        routed = padded[slot_pair]
        picked = jnp.where(route_cube < EXPERTS, routed, jnp.where(route_cube == EXPERTS, jnp.zeros_like(routed), jnp.where(route_cube == EXPERTS + 1, normed_two[:, None, :], jnp.where(route_cube == EXPERTS + 2, const_one[:, None, :], const_two[:, None, :]))))
        block_rows = hidden + lax.optimization_barrier(jnp.sum(gate_w[:, :, None] * picked, axis=1))
        return block_rows.reshape(SEQS, LENGTH, D)
    primals = (tokens.astype(jnp.float32), prev_logits, w_query, w_key, w_value, w_out, w_router, const_coef, const_value, norm_gains, expert_gate, expert_up, expert_down)
    block_out, pullback = jax.vjp(forward, *primals)
    grads = pullback(cotangent.astype(jnp.float32))
    return (block_out, grads[0], grads[1], grads[2], grads[3], grads[4], grads[5], grads[6], grads[7], grads[8], grads[9], grads[10], grads[11], grads[12])
```

```python
import functools

import jax
import jax.numpy as jnp
from jax import lax
from jax.experimental import pallas as pl
from jax.experimental.pallas import tpu as pltpu
from jax.sharding import PartitionSpec as P

D = 768
HEADS = 12
HEAD_DIM = 64
EPS = 1e-06
SMALL = 64
LANES = 128
VMEM_LIMIT = 60 * 2**20
MESH = pl.DeviceIdType.MESH
F32 = jnp.float32
BF16 = jnp.bfloat16
ALL_AXES = ("expert", "context", "dp")


def dot(left, right, left_dim=1, right_dim=0):
    return lax.dot_general(
        left, right, (((left_dim,), (right_dim,)), ((), ())), preferred_element_type=F32
    )


def position():
    return lax.axis_index("expert"), lax.axis_index("context"), lax.axis_index("dp")


def remote(src, dst, send_sem, recv_sem, device):
    return pltpu.make_async_remote_copy(
        src_ref=src,
        dst_ref=dst,
        send_sem=send_sem,
        recv_sem=recv_sem,
        device_id=device,
        device_id_type=MESH,
    )


def greet(devices):
    barrier = pltpu.get_barrier_semaphore()
    for device in devices:
        pl.semaphore_signal(barrier, inc=1, device_id=device, device_id_type=MESH)
    pl.semaphore_wait(barrier, len(devices))


def context_peers(sizes, place):
    e, c, d = place
    pairs = sizes[1] // 2
    outer, inner = c // 2, c % 2
    peers = [(e, outer * 2 + 1 - inner, d)]
    for k in range(1, pairs):
        peers.append((e, lax.rem(outer + k, pairs) * 2 + inner, d))
    return peers


def expert_peers(sizes, place):
    e, c, d = place
    return [(lax.rem(e + j, sizes[0]), c, d) for j in range(1, sizes[0])]


class ContextGather:
    def __init__(self, sizes, place, own, slot, send, recv):
        e, c, d = place
        self.pairs = sizes[1] // 2
        self.place, self.own, self.slot = place, own, slot
        self.send, self.recv = send, recv
        self.outer, self.inner = c // 2, c % 2
        self.peers = context_peers(sizes, place)
        self.copies = []
        self.forwards = []

    def start(self):
        for k in [*range(1, self.pairs), 0]:
            copy = remote(
                self.own, self.slot(self.place[1]), self.send(k), self.recv(k), self.peers[k]
            )
            copy.start()
            self.copies.append((k, copy))

    def origin(self, k):
        return lax.rem(self.outer - k + self.pairs, self.pairs) * 2 + self.inner

    def forward(self):
        for k, copy in self.copies:
            if k > 0:
                copy.wait_recv()
                block = self.slot(self.origin(k))
                n = self.pairs - 1 + k
                onward = remote(block, block, self.send(n), self.recv(n), self.peers[0])
                onward.start()
                self.forwards.append(onward)

    def finish(self):
        for k, copy in self.copies:
            if k == 0:
                copy.wait_recv()
            copy.wait_send()
        for copy in self.forwards:
            copy.wait()


def gather_kernel(
    sizes, a_ref, o_ref, x_ref, ag_ref, og_ref, xg_ref, local, s_a, r_a, s_b, r_b, s_o, r_o, s_x, r_x
):
    n_e, n_c, n_d = sizes
    place = e, c, d = position()
    pairs = n_c // 2
    keep = [
        pltpu.make_async_copy(a_ref.at[c], ag_ref.at[e, c, d], local.at[0]),
        pltpu.make_async_copy(o_ref, og_ref.at[e, c, d], local.at[1]),
        pltpu.make_async_copy(x_ref, xg_ref.at[c], local.at[2]),
    ]
    for copy in keep:
        copy.start()
    c_peers = [(e, lax.rem(c + k, n_c), d) for k in range(1, n_c)]
    d_peers = [(e, c, lax.rem(d + k, n_d)) for k in range(1, n_d)]
    e_peers = expert_peers(sizes, place)
    greet(c_peers + d_peers + e_peers)
    turn = []
    for k in range(1, n_c):
        copy = remote(
            a_ref.at[lax.rem(c + k, n_c)],
            ag_ref.at[e, c, d],
            s_a.at[k - 1],
            r_a.at[k - 1],
            c_peers[k - 1],
        )
        copy.start()
        turn.append(copy)
    rows = ContextGather(
        sizes, place, x_ref, lambda j: xg_ref.at[j], lambda k: s_x.at[k], lambda k: r_x.at[k]
    )
    rows.start()

    def spread(own, slot, send, recv, base):
        along = []
        for k in range(1, n_d):
            copy = remote(
                own, slot(e, d), send.at[base + k - 1], recv.at[base + k - 1], d_peers[k - 1]
            )
            copy.start()
            along.append(copy)
        across = []
        for j in range(1, n_e):
            n = base + n_d - 1 + (j - 1) * n_d
            copy = remote(own, slot(e, d), send.at[n], recv.at[n], e_peers[j - 1])
            copy.start()
            across.append(copy)
        return along, across

    def onward(parts, slot, send, recv, base):
        along, across = parts
        for k in range(1, n_d):
            along[k - 1].wait_recv()
            block = slot(e, lax.rem(d - k + n_d, n_d))
            for j in range(1, n_e):
                n = base + n_d - 1 + (j - 1) * n_d + k
                copy = remote(block, block, send.at[n], recv.at[n], e_peers[j - 1])
                copy.start()
                across.append(copy)

    o_slot = lambda j, k: og_ref.at[j, c, k]
    a_slot = lambda j, k: ag_ref.at[j, :, k]
    o_parts = spread(o_ref, o_slot, s_o, r_o, 0)
    for copy in turn:
        copy.wait()
    for copy in keep:
        copy.wait()
    a_parts = spread(ag_ref.at[e, :, d], a_slot, s_b, r_b, 0)
    onward(o_parts, o_slot, s_o, r_o, 0)
    rows.forward()
    for copy in o_parts[1]:
        copy.wait_recv()
    base = (n_d - 1) + (n_e - 1) * n_d
    whole = ContextGather(
        sizes,
        place,
        og_ref.at[:, c],
        lambda j: og_ref.at[:, j],
        lambda k: s_o.at[base + k],
        lambda k: r_o.at[base + k],
    )
    whole.start()
    onward(a_parts, a_slot, s_b, r_b, 0)
    whole.forward()
    for copy in a_parts[1]:
        copy.wait()
    for copy in [*a_parts[0], *o_parts[0], *o_parts[1]]:
        copy.wait_send()
    rows.finish()
    whole.finish()


def gather_first(sizes, a_part, o_part, x_part):
    n_e, n_c, n_d = sizes
    dma = pltpu.SemaphoreType.DMA
    spread = (n_d - 1) + (n_e - 1) * n_d
    counts = [n_c - 1, n_c - 1, spread, spread, spread + n_c - 1, spread + n_c - 1, n_c - 1, n_c - 1]
    anywhere = pl.BlockSpec(memory_space=pl.ANY)
    return pl.pallas_call(
        functools.partial(gather_kernel, sizes),
        out_shape=(
            jax.ShapeDtypeStruct((n_e, n_c, n_d, *a_part.shape[1:]), BF16),
            jax.ShapeDtypeStruct((n_e, n_c, n_d, *o_part.shape), BF16),
            jax.ShapeDtypeStruct((n_c, *x_part.shape), BF16),
        ),
        in_specs=[anywhere] * 3,
        out_specs=(anywhere,) * 3,
        scratch_shapes=[dma((3,))] + [dma((n,)) for n in counts],
        compiler_params=pltpu.CompilerParams(collective_id=0, has_side_effects=True),
        name="gather_first",
    )(a_part, o_part, x_part)


def softmax_pair(left, right):
    top = jnp.maximum(left, right)
    left, right = jnp.exp(left - top), jnp.exp(right - top)
    total = left + right
    return left / total, right / total


def route_parts(routes_t, routes, small, n_ff, n_all, slots):
    rows = routes.shape[0]
    hot = lax.broadcasted_iota(jnp.int32, (LANES, rows), 0)
    marks = [(hot == routes_t[k : k + 1, :]) & (hot < n_ff) for k in range(2)]
    both = (marks[0] | marks[1]).astype(F32)
    earlier = lax.broadcasted_iota(jnp.int32, (rows, rows), 0) < lax.broadcasted_iota(
        jnp.int32, (rows, rows), 1
    )
    rank = dot(both.astype(BF16), earlier.astype(F32).astype(BF16))
    number = lax.broadcasted_iota(jnp.int32, (slots, rows), 0).astype(F32)
    tables = []
    for k in range(2):
        wanted = jnp.where(marks[k], rank, -1.0)
        tables.append(
            jnp.concatenate(
                [(number == wanted[j : j + 1, :]).astype(F32) for j in range(n_ff)], axis=0
            ).astype(BF16)
        )
    lane = lax.broadcasted_iota(jnp.int32, (rows, LANES), 1)
    picks = [(lane == routes[:, k : k + 1]).astype(F32) for k in range(2)]
    chosen = [
        jnp.sum(jnp.where(picks[k] > 0, small, 0.0), axis=1, keepdims=True) for k in range(2)
    ]
    w_pair = softmax_pair(chosen[0], chosen[1])
    first = softmax_pair(small[:, n_all : n_all + 1], small[:, n_all + 1 : n_all + 2])
    second = softmax_pair(small[:, n_all + 2 : n_all + 3], small[:, n_all + 3 : n_all + 4])
    return tables, picks, w_pair, first, second


def front_kernel(
    sizes,
    cfg,
    xg_ref,
    xown_ref,
    wqkv_ref,
    wo_ref,
    wsm_ref,
    vec_ref,
    dcol_ref,
    drow_ref,
    routes_ref,
    routest_ref,
    prev_ref,
    g_ref,
    a1_ref,
    qt_ref,
    kh_ref,
    vh_ref,
    mixed_ref,
    h_ref,
    a2_ref,
    small_ref,
    p_ref,
    slots_ref,
    o_scr,
    vt_scr,
    p_scr,
    sbuf,
    xin,
    p_sem,
    s_o,
    r_o,
    s_x,
    r_x,
    s_g,
    r_g,
    l_g,
):
    n_e, n_c, n_d = sizes
    hp, n_ff, n_all, n_loc, slots = cfg
    hc = hp * HEAD_DIM
    place = e, c, d = position()
    length = xg_ref.shape[0]
    rows = length // n_c
    c_all = [(e, lax.rem(c + k, n_c), d) for k in range(1, n_c)]
    e_peers = expert_peers(sizes, place)
    greet(c_all + e_peers)

    gain_one = vec_ref[0:1, :]
    for b in range(n_c):
        part = pl.ds(b * rows, rows)
        x = xg_ref[part, :].astype(F32)
        inverse = lax.rsqrt(jnp.mean(x * x, axis=-1, keepdims=True) + EPS)
        a1_ref[part, :] = (x * inverse * gain_one).astype(BF16)
    a1 = a1_ref[...]
    wqkv = wqkv_ref[...]
    q_t = dot(wqkv[:, :hc], a1, 0, 1).astype(BF16) * jnp.asarray(HEAD_DIM**-0.5, BF16)
    qt_ref[...] = q_t
    kv = dot(a1, wqkv[:, hc:]).astype(BF16)
    for j in range(hp):
        kh_ref[j] = kv[:, j * HEAD_DIM : (j + 1) * HEAD_DIM]
        vh_ref[j] = kv[:, hc + j * HEAD_DIM : hc + (j + 1) * HEAD_DIM]
    vt_scr[...] = dot(wqkv[:, 2 * hc :], a1, 0, 1).astype(BF16)

    turn = 0
    p_copies = {}
    for b in reversed(range(n_c)):
        reach = (b + 1) * rows
        key_place = lax.broadcasted_iota(jnp.int32, (reach, rows), 0)
        q_place = lax.broadcasted_iota(jnp.int32, (reach, rows), 1) + b * rows
        allowed = (dcol_ref[:reach, :] == drow_ref[:, b * rows : reach]) & (key_place <= q_place)
        bias = jnp.where(allowed, 0.0, -1e30)
        for j in range(hp):
            head = slice(j * HEAD_DIM, (j + 1) * HEAD_DIM)
            scores = dot(kh_ref[j, :reach, :], qt_ref[head, b * rows : reach]) + bias
            top = jnp.max(scores, axis=0, keepdims=True)
            exponent = jnp.exp(scores - top)
            total = jnp.sum(exponent, axis=0, keepdims=True)
            rounded = (exponent * (1.0 / total)).astype(BF16)
            slot = turn % 2
            if turn >= 2:
                p_copies[turn - 2].wait()
            p_scr[slot, :reach, :] = rounded
            copy = pltpu.make_async_copy(
                p_scr.at[slot, pl.ds(0, reach)], p_ref.at[j, b, pl.ds(0, reach)], p_sem.at[slot]
            )
            copy.start()
            p_copies[turn] = copy
            turn += 1
            o_scr[b, head, :] = dot(vt_scr[head, :reach], rounded).astype(BF16)

        @pl.when(c != b)
        def _():
            remote(
                o_scr.at[b], mixed_ref.at[c], s_o.at[b], r_o.at[c], (e, b, d)
            ).start()

    for n in range(max(0, turn - 2), turn):
        p_copies[n].wait()
    mixed_ref[pl.ds(c, 1)] = o_scr[pl.ds(c, 1)]
    for b in range(n_c):

        @pl.when(c != b)
        def _():
            copy = remote(o_scr.at[b], mixed_ref.at[b], s_o.at[b], r_o.at[b], (e, b, d))
            copy.wait_send()
            copy.wait_recv()

    mixed = mixed_ref[...].reshape(n_c * hc, rows)
    h = xown_ref[...].astype(F32) + dot(mixed, wo_ref[...], 0, 0)
    h_ref[...] = h
    inverse = lax.rsqrt(jnp.mean(h * h, axis=-1, keepdims=True) + EPS)
    a2 = (h * inverse * vec_ref[1:2, :]).astype(BF16)
    a2_ref[...] = a2
    small = dot(a2, wsm_ref[...]) + prev_ref[...]
    small_ref[...] = small
    tables, _, w_pair, _, _ = route_parts(
        routest_ref[...], routes_ref[...], small, n_ff, n_all, slots
    )
    per = n_loc * slots
    crossing = {}
    gathers = {}
    g = g_ref[...]
    for t in range(2):
        if t == 0:
            block = dot(tables[0] + tables[1], a2).astype(BF16)
        else:
            block = dot(tables[0], (w_pair[0] * g).astype(BF16)) + dot(
                tables[1], (w_pair[1] * g).astype(BF16)
            )
            block = block.astype(BF16)
        for k in range(n_e):
            sbuf[t, k] = block[k * per : (k + 1) * per, :]
        for j in range(1, n_e):
            n = t * n_e + j
            copy = remote(
                sbuf.at[t, lax.rem(e + j, n_e)],
                xin.at[t, e],
                s_x.at[n],
                r_x.at[n],
                e_peers[j - 1],
            )
            copy.start()
            crossing[t, j] = copy

        def gather(j, own, t=t):
            src = lax.rem(e - j + n_e, n_e)
            base = (t * n_e + j) * (n_c - 1)
            keep = pltpu.make_async_copy(own, slots_ref.at[c, t, src], l_g.at[t * n_e + j])
            keep.start()
            made = ContextGather(
                sizes,
                place,
                own,
                lambda k: slots_ref.at[k, t, src],
                lambda k: s_g.at[base + k],
                lambda k: r_g.at[base + k],
            )
            made.start()
            gathers[t, j] = (made, keep)

        gather(0, sbuf.at[t, e])
        crossing[t, 0] = gather
    for t in range(2):
        for j in range(1, n_e):
            crossing[t, j].wait_recv()
            crossing[t, 0](j, xin.at[t, lax.rem(e - j + n_e, n_e)])
    for made, _ in gathers.values():
        made.forward()
    for made, keep in gathers.values():
        made.finish()
        keep.wait()
    for t in range(2):
        for j in range(1, n_e):
            crossing[t, j].wait_send()


def front(sizes, cfg, *operands):
    n_e, n_c, n_d = sizes
    hp, n_ff, n_all, n_loc, slots = cfg
    hc = hp * HEAD_DIM
    length = operands[0].shape[0]
    rows = length // n_c
    per = n_loc * slots
    dma = pltpu.SemaphoreType.DMA
    vmem = pl.BlockSpec(memory_space=pltpu.VMEM)
    anywhere = pl.BlockSpec(memory_space=pl.ANY)
    shape = jax.ShapeDtypeStruct
    gathers = 2 * n_e * (n_c - 1)
    return pl.pallas_call(
        functools.partial(front_kernel, sizes, cfg),
        out_shape=(
            shape((length, D), BF16),
            shape((hc, length), BF16),
            shape((hp, length, HEAD_DIM), BF16),
            shape((hp, length, HEAD_DIM), BF16),
            shape((n_c, hc, rows), BF16),
            shape((rows, D), F32),
            shape((rows, D), BF16),
            shape((rows, LANES), F32),
            shape((hp, n_c, length, rows), BF16),
            shape((n_c, 2, n_e, per, D), BF16),
        ),
        in_specs=[vmem] * len(operands),
        out_specs=(vmem,) * 8 + (anywhere,) * 2,
        scratch_shapes=[
            pltpu.VMEM((n_c, hc, rows), BF16),
            pltpu.VMEM((hc, length), BF16),
            pltpu.VMEM((2, length, rows), BF16),
            pltpu.VMEM((2, n_e, per, D), BF16),
            pltpu.VMEM((2, n_e, per, D), BF16),
            dma((2,)),
            dma((n_c,)),
            dma((n_c,)),
            dma((2 * n_e,)),
            dma((2 * n_e,)),
            dma((gathers,)),
            dma((gathers,)),
            dma((2 * n_e,)),
        ],
        compiler_params=pltpu.CompilerParams(
            collective_id=1, has_side_effects=True, vmem_limit_bytes=VMEM_LIMIT
        ),
        name="front",
    )(*operands)


def expert_kernel(x_ref, dy_ref, w_ref, out_ref, gw_ref, total):
    step = pl.program_id(1)
    parts = w_ref.shape[0]
    x = x_ref[...].reshape(-1, D)
    dy = dy_ref[...].reshape(-1, D)
    block = out_ref.shape[0:1] + out_ref.shape[2:]
    gate, up, down = [
        jnp.concatenate([w_ref[k, n, 0] for k in range(parts)], axis=1) for n in range(3)
    ]
    gate_pre = dot(x, gate)
    up_pre = dot(x, up)
    sig = jax.nn.sigmoid(gate_pre)
    hidden = (gate_pre * sig * up_pre).astype(BF16)
    result = dot(hidden, down, 1, 1).astype(BF16)
    out_ref[:, 0] = result.reshape(block)
    d_hidden = dot(dy, down)
    d_gate = (d_hidden * up_pre * sig * (1.0 + gate_pre * (1.0 - sig))).astype(BF16)
    d_up = (d_hidden * gate_pre * sig).astype(BF16)
    d_x = dot(d_gate, gate, 1, 1) + dot(d_up, up, 1, 1)
    out_ref[:, 1] = d_x.astype(BF16).reshape(block)
    grads = (dot(x, d_gate, 0, 0), dot(x, d_up, 0, 0), dot(dy, hidden, 0, 0))

    @pl.when(step == 0)
    def _():
        for n in range(3):
            total[n] = grads[n]

    @pl.when(step > 0)
    def _():
        for n in range(3):
            total[n] += grads[n]

    @pl.when(step == pl.num_programs(1) - 1)
    def _():
        width = gate.shape[1] // parts
        for n in range(3):
            for k in range(parts):
                gw_ref[k, n, 0] = total[n, :, k * width : (k + 1) * width].astype(BF16)


def experts_pass(gathered, weights):
    n_c, _, n_e, n_loc, slots, _ = gathered.shape
    parts, _, _, _, units = weights.shape
    take = max(1, min(n_c, 512 // (n_e * slots)))
    return pl.pallas_call(
        expert_kernel,
        grid=(n_loc, n_c // take),
        out_shape=(
            jax.ShapeDtypeStruct(gathered.shape, BF16),
            jax.ShapeDtypeStruct(weights.shape, BF16),
        ),
        in_specs=[
            pl.BlockSpec((take, 1, n_e, 1, slots, D), lambda i, j: (j, 0, 0, i, 0, 0)),
            pl.BlockSpec((take, 1, n_e, 1, slots, D), lambda i, j: (j, 1, 0, i, 0, 0)),
            pl.BlockSpec((parts, 3, 1, D, units), lambda i, j: (0, 0, i, 0, 0)),
        ],
        out_specs=(
            pl.BlockSpec((take, 2, n_e, 1, slots, D), lambda i, j: (j, 0, 0, i, 0, 0)),
            pl.BlockSpec((parts, 3, 1, D, units), lambda i, j: (0, 0, i, 0, 0)),
        ),
        scratch_shapes=[pltpu.VMEM((3, D, parts * units), F32)],
        compiler_params=pltpu.CompilerParams(
            dimension_semantics=("arbitrary", "arbitrary"), vmem_limit_bytes=VMEM_LIMIT
        ),
        name="experts_pass",
    )(gathered, gathered, weights)


def back_kernel(
    sizes,
    cfg,
    res_ref,
    h_ref,
    a2_ref,
    small_ref,
    g_ref,
    routes_ref,
    routest_ref,
    wo_ref,
    wqkv_ref,
    wsm_ref,
    vec_ref,
    mixed_ref,
    a1_ref,
    qt_ref,
    kh_ref,
    vh_ref,
    p_ref,
    x_ref,
    block_ref,
    dx_ref,
    dprev_ref,
    gqkv_ref,
    go_ref,
    gsmall_ref,
    inn,
    osum,
    outr,
    back,
    xsum,
    stage,
    dhg,
    dht_scr,
    p_scr,
    dk_acc,
    dv_acc,
    dqt,
    dqkv,
    da_in,
    da_sum,
    da_out,
    l_sem,
    s_in,
    r_in,
    s_out,
    r_out,
    s_x,
    r_x,
    s_g,
    r_g,
    p_sem,
    s_d,
    r_d,
):
    n_e, n_c, n_d = sizes
    hp, n_ff, n_all, n_loc, slots = cfg
    hc = hp * HEAD_DIM
    place = e, c, d = position()
    pairs = n_c // 2
    outer, inner = c // 2, c % 2
    rows = h_ref.shape[0]
    length = rows * n_c
    peers = context_peers(sizes, place)
    e_peers = expert_peers(sizes, place)

    in_vmem = len(stage.shape) == 5
    if in_vmem:
        take = pltpu.make_async_copy(res_ref.at[:, inner], stage, l_sem.at[0])
        take.start()
    greet(peers + e_peers)

    def load(ref, slot=0):
        if in_vmem:
            return ref[...].astype(F32)
        copy = pltpu.make_async_copy(ref, stage.at[slot], l_sem.at[0])
        copy.start()
        copy.wait()
        return stage[slot].astype(F32)

    def own_part(there, t, src):
        if in_vmem:
            return stage[there, t, src].astype(F32)
        return load(res_ref.at[there, inner, t, src])

    def store(ref, value):
        if in_vmem:
            ref[...] = value
        else:
            stage[3] = value
            copy = pltpu.make_async_copy(stage.at[3], ref, l_sem.at[0])
            copy.start()
            copy.wait()

    pieces = [(t, j) for j in [*range(1, n_e), 0] for t in range(2)]
    first_copies = {}
    for t, j in pieces:
        src = lax.rem(e + j, n_e)
        for k in [*range(1, pairs), 0]:
            n = (t * n_e + j) * pairs + k
            there = lax.rem(outer + k, pairs)
            copy = remote(
                res_ref.at[there, 1 - inner, t, src],
                inn.at[there, t, src],
                s_in.at[n],
                r_in.at[n],
                peers[0],
            )
            copy.start()
            first_copies[t, j, k] = copy
    if in_vmem:
        take.wait()
    second = {}
    for t, j in pieces:
        src = lax.rem(e + j, n_e)
        for k in range(1, pairs):
            n = (t * n_e + j) * pairs + k
            there = lax.rem(outer + k, pairs)
            first_copies[t, j, k].wait_recv()
            total = own_part(there, t, src) + load(inn.at[there, t, src], 1)
            store(osum.at[k - 1, t, src], total.astype(BF16))
            copy = remote(
                osum.at[k - 1, t, src], outr.at[k - 1, t, src], s_out.at[n], r_out.at[n], peers[k]
            )
            copy.start()
            second[t, j, k] = copy
    home = {}
    for t, j in pieces:
        src = lax.rem(e + j, n_e)
        first_copies[t, j, 0].wait_recv()
        total = own_part(outer, t, src) + load(inn.at[outer, t, src], 1)
        for k in range(1, pairs):
            second[t, j, k].wait_recv()
            total = total + load(outr.at[k - 1, t, src], 2)
        if j == 0:
            back[t, e] = total.astype(BF16)
        else:
            xsum[t, src] = total.astype(BF16)
            n = t * n_e + j
            copy = remote(
                xsum.at[t, src], back.at[t, e], s_x.at[n], r_x.at[n], e_peers[j - 1]
            )
            copy.start()
            home[t, j] = copy

    h = h_ref[...]
    a2 = a2_ref[...].astype(F32)
    g = g_ref[...]
    small = small_ref[...]
    value_one, value_two = vec_ref[2:3, :], vec_ref[3:4, :]
    tables, picks, w_pair, first, other = route_parts(
        routest_ref[...], routes_ref[...], small, n_ff, n_all, slots
    )
    copy_on, one_on, two_on = [
        [picks[k][:, n_ff + n : n_ff + n + 1] for k in range(2)] for n in (1, 2, 3)
    ]
    g_a2 = jnp.sum(g * a2, axis=1, keepdims=True)
    g_one = jnp.sum(g * value_one, axis=1, keepdims=True)
    g_two = jnp.sum(g * value_two, axis=1, keepdims=True)
    alpha = [copy_on[k] + one_on[k] * first[0] + two_on[k] * other[0] for k in range(2)]
    a_weight = alpha[0] * w_pair[0] + alpha[1] * w_pair[1]
    one_weight = one_on[0] * w_pair[0] + one_on[1] * w_pair[1]
    two_weight = two_on[0] * w_pair[0] + two_on[1] * w_pair[1]
    for copy in home.values():
        copy.wait_recv()
    returned = [back[t].reshape(n_ff * slots, D) for t in range(2)]
    block = h
    d_weight = []
    for k in range(2):
        routed = dot(tables[k], returned[0], 0, 0)
        picked = (
            routed
            + alpha[k] * a2
            + (one_on[k] * first[1]) * value_one
            + (two_on[k] * other[1]) * value_two
        )
        block = block + w_pair[k] * picked
        d_weight.append(jnp.sum(g * picked, axis=1, keepdims=True))
    block_ref[...] = block
    center = w_pair[0] * d_weight[0] + w_pair[1] * d_weight[1]
    d_logits = (
        picks[0] * (w_pair[0] * (d_weight[0] - center))
        + picks[1] * (w_pair[1] * (d_weight[1] - center))
    )
    dprev_ref[...] = d_logits
    lane = lax.broadcasted_iota(jnp.int32, (rows, LANES), 1)
    d_small = d_logits
    for base, pair, weight, g_value in (
        (n_all, first, one_weight, g_one),
        (n_all + 2, other, two_weight, g_two),
    ):
        d_pair = (weight * g_a2, weight * g_value)
        middle = pair[0] * d_pair[0] + pair[1] * d_pair[1]
        for k in range(2):
            d_small = d_small + jnp.where(lane == base + k, pair[k] * (d_pair[k] - middle), 0.0)
    d_small = d_small.astype(BF16)
    d_const_one = jnp.sum((first[1] * one_weight) * g, axis=0, keepdims=True)
    d_const_two = jnp.sum((other[1] * two_weight) * g, axis=0, keepdims=True)
    d_a2 = (
        dot(tables[0] + tables[1], returned[1], 0, 0)
        + a_weight * g
        + dot(d_small, wsm_ref[...], 1, 1)
    )
    gain_two = vec_ref[1:2, :]
    inverse_two = lax.rsqrt(jnp.mean(h * h, axis=-1, keepdims=True) + EPS)
    d_gain_two = jnp.sum(d_a2 * h * inverse_two, axis=0, keepdims=True)
    scaled = gain_two * d_a2
    d_h = (
        g
        + inverse_two * scaled
        - h * inverse_two**3 * jnp.mean(scaled * h, axis=-1, keepdims=True)
    )
    d_hb = d_h.astype(BF16)
    dhg[pl.ds(c, 1)] = d_hb[None]
    gather = ContextGather(
        sizes,
        place,
        dhg.at[c],
        lambda k: dhg.at[k],
        lambda k: s_g.at[k],
        lambda k: r_g.at[k],
    )
    gather.start()
    dx_ref[...] = d_h
    go_ref[...] = dot(mixed_ref[...].reshape(n_c * hc, rows), d_hb)[:D]
    g_small = dot(a2_ref[...], d_small, 0, 0)
    dk_acc[...] = jnp.zeros_like(dk_acc)
    dv_acc[...] = jnp.zeros_like(dv_acc)
    order = [(b, j) for b in reversed(range(n_c)) for j in range(hp)]

    def fetch(n):
        b, j = order[n]
        reach = pl.ds(0, (b + 1) * rows)
        return pltpu.make_async_copy(p_ref.at[j, b, reach], p_scr.at[n % 2, reach], p_sem.at[n % 2])

    fetch(0).start()
    gather.forward()
    gather.finish()
    wo_part = wo_ref[pl.ds(pl.multiple_of(c * hc, hc), hc), :]
    for b in range(n_c):
        dht_scr[:, b * rows : (b + 1) * rows] = dot(wo_part, dhg[b], 1, 1).astype(BF16)
    for n, (b, j) in enumerate(order):
        reach = (b + 1) * rows
        head = slice(j * HEAD_DIM, (j + 1) * HEAD_DIM)
        mine_q = slice(b * rows, reach)
        if n + 1 < len(order):
            fetch(n + 1).start()
        fetch(n).wait()
        rounded = p_scr[n % 2, :reach, :]
        prob = rounded.astype(F32)
        d_o = dht_scr[head, mine_q]
        d_prob = dot(vh_ref[j, :reach, :], d_o)
        delta = jnp.sum(prob * d_prob, axis=0, keepdims=True)
        d_scores = (prob * (d_prob - delta)).astype(BF16)
        dqt[head, mine_q] = dot(kh_ref[j, :reach, :], d_scores, 0, 0) * HEAD_DIM**-0.5
        dk_acc[j, :reach, :] += dot(d_scores, qt_ref[head, mine_q], 1, 1)
        dv_acc[j, :reach, :] += dot(rounded, d_o, 1, 1)
    dqkv[:, :hc] = dqt[...].T.astype(BF16)
    for j in range(hp):
        at = j * HEAD_DIM
        dqkv[:, hc + at : hc + at + HEAD_DIM] = dk_acc[j].astype(BF16)
        dqkv[:, 2 * hc + at : 2 * hc + at + HEAD_DIM] = dv_acc[j].astype(BF16)
    d_all = dqkv[...]
    wqkv = wqkv_ref[...]
    for b in range(n_c):
        dhg[b] = dot(d_all[b * rows : (b + 1) * rows], wqkv, 1, 1).astype(BF16)
    to_pair = []
    for k in [*range(1, pairs), 0]:
        there = lax.rem(outer + k, pairs)
        copy = remote(
            dhg.at[there * 2 + 1 - inner], da_in.at[there], s_d.at[k], r_d.at[k], peers[0]
        )
        copy.start()
        to_pair.append((k, copy))
    along = []
    for k, copy in to_pair:
        if k == 0:
            continue
        there = lax.rem(outer + k, pairs)
        copy.wait_recv()
        da_sum[k - 1] = (
            dhg[there * 2 + inner].astype(F32) + da_in[there].astype(F32)
        ).astype(BF16)
        onward = remote(
            da_sum.at[k - 1],
            da_out.at[k - 1],
            s_d.at[pairs + k - 1],
            r_d.at[pairs + k - 1],
            peers[k],
        )
        onward.start()
        along.append(onward)
    gqkv_ref[...] = dot(a1_ref[...], d_all, 0, 0)
    to_pair[-1][1].wait_recv()
    d_a1 = dhg[c].astype(F32) + da_in[outer].astype(F32)
    for k, copy in enumerate(along):
        copy.wait_recv()
        d_a1 = d_a1 + da_out[k].astype(F32)
    x = x_ref[...].astype(F32)
    gain_one = vec_ref[0:1, :]
    inverse_one = lax.rsqrt(jnp.mean(x * x, axis=-1, keepdims=True) + EPS)
    d_gain_one = jnp.sum(d_a1 * x * inverse_one, axis=0, keepdims=True)
    scaled = gain_one * d_a1
    dx_ref[...] += inverse_one * scaled - x * inverse_one**3 * jnp.mean(
        scaled * x, axis=-1, keepdims=True
    )
    spot = lax.broadcasted_iota(jnp.int32, (LANES, D), 0)
    tall = jnp.zeros((LANES, D), F32)
    for n, row in enumerate((d_const_one, d_const_two, d_gain_one, d_gain_two)):
        tall = tall + jnp.where(spot == n_all + 4 + n, row, 0.0)
    gsmall_ref[...] = g_small + tall.T
    for copy in first_copies.values():
        copy.wait_send()
    for copy in second.values():
        copy.wait_send()
    for copy in home.values():
        copy.wait_send()
    for _, copy in to_pair:
        copy.wait_send()
    for copy in along:
        copy.wait_send()


def backward(sizes, cfg, *operands):
    n_e, n_c, n_d = sizes
    hp, n_ff, n_all, n_loc, slots = cfg
    hc = hp * HEAD_DIM
    rows = operands[1].shape[0]
    length = rows * n_c
    pairs = n_c // 2
    per = n_loc * slots
    dma = pltpu.SemaphoreType.DMA
    vmem = pl.BlockSpec(memory_space=pltpu.VMEM)
    anywhere = pl.BlockSpec(memory_space=pl.ANY)
    shape = jax.ShapeDtypeStruct
    n_in = 2 * n_e * pairs
    n_more = max(1, pairs - 1)
    in_specs = [vmem] * len(operands)
    in_specs[0] = anywhere
    in_specs[16] = anywhere
    arriving = [(pairs, 2, n_e, per, D), (n_more, 2, n_e, per, D), (n_more, 2, n_e, per, D)]
    roomy = 2 * pairs * n_e * per * D <= 2**21
    held = [pltpu.VMEM(dims, BF16) for dims in arriving] if roomy else []
    extra = [] if roomy else [shape(dims, BF16) for dims in arriving]
    stage = pltpu.VMEM(arriving[0] if roomy else (4, per, D), BF16)
    return pl.pallas_call(
        functools.partial(back_kernel, sizes, cfg),
        out_shape=(
            shape((rows, D), F32),
            shape((rows, D), F32),
            shape((rows, LANES), F32),
            shape((D, 3 * hc), F32),
            shape((D, D), F32),
            shape((D, LANES), F32),
            *extra,
        ),
        in_specs=in_specs,
        out_specs=(vmem,) * 6 + (anywhere,) * len(extra),
        scratch_shapes=[
            *held,
            pltpu.VMEM((2, n_e, per, D), BF16),
            pltpu.VMEM((2, n_e, per, D), BF16),
            stage,
            pltpu.VMEM((n_c, rows, D), BF16),
            pltpu.VMEM((hc, length), BF16),
            pltpu.VMEM((2, length, rows), BF16),
            pltpu.VMEM((hp, length, HEAD_DIM), F32),
            pltpu.VMEM((hp, length, HEAD_DIM), F32),
            pltpu.VMEM((hc, length), F32),
            pltpu.VMEM((length, 3 * hc), BF16),
            pltpu.VMEM((pairs, rows, D), BF16),
            pltpu.VMEM((n_more, rows, D), BF16),
            pltpu.VMEM((n_more, rows, D), BF16),
            dma((1,)),
            dma((n_in,)),
            dma((n_in,)),
            dma((n_in,)),
            dma((n_in,)),
            dma((2 * n_e,)),
            dma((2 * n_e,)),
            dma((n_c - 1,)),
            dma((n_c - 1,)),
            dma((2,)),
            dma((n_c,)),
            dma((n_c,)),
        ],
        compiler_params=pltpu.CompilerParams(
            collective_id=2, has_side_effects=True, vmem_limit_bytes=VMEM_LIMIT
        ),
        name="backward",
    )(*operands)[:6]


def pad_to(array, axis, size):
    widths = [(0, 0)] * array.ndim
    widths[axis] = (0, size - array.shape[axis])
    return jnp.pad(array, widths)


def body(
    tokens,
    doc_ids,
    routes,
    prev_logits,
    cotangent,
    w_query,
    w_key,
    w_value,
    w_out,
    w_router,
    const_coef,
    const_value,
    norm_gains,
    expert_gate,
    expert_up,
    expert_down,
):
    sizes = n_e, n_c, n_d = tuple(lax.axis_size(axis) for axis in ALL_AXES)
    rows = tokens.shape[1]
    length = doc_ids.shape[1]
    n_loc, _, units = expert_gate.shape
    n_ff = n_loc * n_e
    n_all = w_router.shape[1]
    slots = rows // 4
    hp = -(-HEADS // n_c)
    hc = hp * HEAD_DIM
    cfg = (hp, n_ff, n_all, n_loc, slots)
    w_rows = w_query.shape[0]
    w_pad = -(-w_rows // 16) * 16
    width = -(-(3 * hc + SMALL) // LANES) * LANES

    pieces = jnp.stack([expert_gate, expert_up, expert_down]).astype(BF16)
    gathered_w = lax.all_gather(pieces, "dp", axis=0)

    small_w = jnp.concatenate([w_router, const_coef, const_value, norm_gains], axis=1).astype(BF16)
    slices = [
        pad_to(w.astype(BF16), 1, n_c * hc).reshape(w_rows, n_c, hc)
        for w in (w_query, w_key, w_value)
    ]
    slices.append(
        jnp.broadcast_to(
            pad_to(small_w, 1, width - 3 * hc)[:, None, :], (w_rows, n_c, width - 3 * hc)
        )
    )
    a_part = pad_to(jnp.concatenate(slices, axis=2).transpose(1, 0, 2), 1, w_pad)
    o_part = pad_to(w_out.astype(BF16), 0, w_pad)
    a_all, o_all, x_all = gather_first(sizes, a_part, o_part, tokens[0])
    a_all = a_all[:, :, :, :w_rows].reshape(D, width)
    wqkv = a_all[:, : 3 * hc]
    small_w = a_all[:, 3 * hc : 3 * hc + SMALL]
    wsm = pad_to(small_w, 1, LANES)
    wo = pad_to(o_all[:, :, :, :w_rows].reshape(D, D), 0, n_c * hc)
    lines = small_w[:, n_all + 4 : n_all + 8].astype(F32).T
    vec = pad_to(jnp.concatenate([lines[2:4], lines[0:2]], axis=0), 0, 8)

    documents = doc_ids[0]
    route_rows = routes[0]
    routes_t = pad_to(route_rows.T, 0, 8)
    prev = pad_to(prev_logits[0], 1, LANES)
    upstream = cotangent[0]
    (a1, q_t, k_h, v_h, mixed, h, a2, small, probs, gathered) = front(
        sizes,
        cfg,
        x_all.reshape(length, D),
        tokens[0],
        wqkv,
        wo,
        wsm,
        vec,
        documents[:, None],
        documents[None, :],
        route_rows,
        routes_t,
        prev,
        upstream,
    )
    if units % LANES:
        flat = gathered_w.transpose(1, 2, 3, 0, 4).reshape(1, 3, n_loc, D, n_d * units)
    else:
        flat = gathered_w
    results, grads = experts_pass(gathered.reshape(n_c, 2, n_e, n_loc, slots, D), flat)
    if units % LANES:
        grads = grads.reshape(3, n_loc, D, n_d, units).transpose(3, 0, 1, 2, 4)
    expert_grads = lax.psum_scatter(grads, "dp", scatter_dimension=0, tiled=False).astype(F32)

    block_rows, d_x, d_prev, g_qkv, g_o, g_small = backward(
        sizes,
        cfg,
        results.reshape(n_c // 2, 2, 2, n_e, n_loc * slots, D),
        h,
        a2,
        small,
        upstream,
        route_rows,
        routes_t,
        wo,
        wqkv,
        wsm,
        vec,
        mixed,
        a1,
        q_t,
        k_h,
        v_h,
        probs,
        tokens[0],
    )
    own = lax.psum_scatter(
        jnp.concatenate([g_o.astype(BF16), g_small.astype(BF16)], axis=1),
        ALL_AXES,
        scatter_dimension=0,
        tiled=True,
    ).astype(F32)
    blocks = (
        g_qkv.astype(BF16)
        .reshape(n_e, n_c, n_d, w_rows, 3 * hc)
        .transpose(0, 2, 1, 3, 4)
        .reshape(n_e * n_d * n_c * w_rows, 3 * hc)
    )
    mine = lax.psum_scatter(blocks, ("expert", "dp"), scatter_dimension=0, tiled=True)
    mine = lax.all_to_all(
        mine.reshape(n_c, w_rows, 3 * hc), "context", split_axis=0, concat_axis=0, tiled=True
    ).astype(F32)
    q_grad, k_grad, v_grad = [
        mine[:, :, n * hc : (n + 1) * hc].transpose(1, 0, 2).reshape(w_rows, n_c * hc)[:, :D]
        for n in range(3)
    ]
    s_own = own[:, D:]
    return (
        block_rows[None],
        d_x[None],
        d_prev[None, :, :n_all],
        q_grad,
        k_grad,
        v_grad,
        own[:, :D],
        s_own[:, :n_all],
        s_own[:, n_all : n_all + 4],
        s_own[:, n_all + 4 : n_all + 6],
        s_own[:, n_all + 6 : n_all + 8],
        expert_grads[0],
        expert_grads[1],
        expert_grads[2],
    )


def solution(mesh):
    rows = P(("expert", "dp"), "context", None)
    weights = P(ALL_AXES, None)
    units = P("expert", None, ("context", "dp"))
    return jax.shard_map(
        body,
        mesh=mesh,
        in_specs=(rows, P(("expert", "dp"), None), rows, rows, rows)
        + (weights,) * 8
        + (units,) * 3,
        out_specs=(rows,) * 3 + (weights,) * 8 + (units,) * 3,
        check_vma=False,
    )
```

```python
import functools

import jax
import jax.numpy as jnp
from jax import lax
from jax.experimental import pallas as pl
from jax.experimental.pallas import tpu as pltpu
from jax.sharding import PartitionSpec as P

D = 768
HEADS = 12
HEAD_DIM = 64
EPS = 1e-06
SMALL = 64
LANES = 128
VMEM_LIMIT = 63 * 2**20
MESH = pl.DeviceIdType.MESH
F32 = jnp.float32
BF16 = jnp.bfloat16
ALL_AXES = ("expert", "context", "dp")


def dot(left, right, left_dim=1, right_dim=0):
    return lax.dot_general(
        left, right, (((left_dim,), (right_dim,)), ((), ())), preferred_element_type=F32
    )


def position():
    return lax.axis_index("expert"), lax.axis_index("context"), lax.axis_index("dp")


def remote(src, dst, send_sem, recv_sem, device):
    return pltpu.make_async_remote_copy(
        src_ref=src,
        dst_ref=dst,
        send_sem=send_sem,
        recv_sem=recv_sem,
        device_id=device,
        device_id_type=MESH,
    )


def greet(devices):
    barrier = pltpu.get_barrier_semaphore()
    for device in devices:
        pl.semaphore_signal(barrier, inc=1, device_id=device, device_id_type=MESH)
    pl.semaphore_wait(barrier, len(devices))


def context_peers(sizes, place):
    e, c, d = place
    pairs = sizes[1] // 2
    outer, inner = c // 2, c % 2
    peers = [(e, outer * 2 + 1 - inner, d)]
    for k in range(1, pairs):
        peers.append((e, lax.rem(outer + k, pairs) * 2 + inner, d))
    return peers


def expert_peers(sizes, place):
    e, c, d = place
    return [(lax.rem(e + j, sizes[0]), c, d) for j in range(1, sizes[0])]


class Courier:
    def __init__(self, send, recv):
        self.send, self.recv = send, recv
        self.copies = []

    def carry(self, src, dst, device):
        n = len(self.copies)
        copy = remote(src, dst, self.send.at[n], self.recv.at[n], device)
        copy.start()
        self.copies.append(copy)
        return copy

    def finish(self):
        for copy in self.copies:
            copy.wait_send()


def up_to(count, step):
    return -(-count // step) * step


class ContextGather:
    def __init__(self, sizes, place, own, slot, send, recv):
        e, c, d = place
        self.pairs = sizes[1] // 2
        self.place, self.own, self.slot = place, own, slot
        self.send, self.recv = send, recv
        self.outer, self.inner = c // 2, c % 2
        self.peers = context_peers(sizes, place)
        self.copies = []
        self.forwards = []

    def start(self):
        for k in [*range(1, self.pairs), 0]:
            copy = remote(
                self.own, self.slot(self.place[1]), self.send(k), self.recv(k), self.peers[k]
            )
            copy.start()
            self.copies.append((k, copy))

    def origin(self, k):
        return lax.rem(self.outer - k + self.pairs, self.pairs) * 2 + self.inner

    def forward(self):
        for k, copy in self.copies:
            if k > 0:
                copy.wait_recv()
                block = self.slot(self.origin(k))
                n = self.pairs - 1 + k
                onward = remote(block, block, self.send(n), self.recv(n), self.peers[0])
                onward.start()
                self.forwards.append(onward)

    def finish(self):
        for k, copy in self.copies:
            if k == 0:
                copy.wait_recv()
            copy.wait_send()
        for copy in self.forwards:
            copy.wait()


def gather_kernel(
    sizes, a_ref, o_ref, x_ref, ag_ref, og_ref, xg_ref, local, s_a, r_a, s_b, r_b, s_o, r_o, s_x, r_x
):
    n_e, n_c, n_d = sizes
    place = e, c, d = position()
    pairs = n_c // 2
    keep = [
        pltpu.make_async_copy(a_ref.at[c], ag_ref.at[e, c, d], local.at[0]),
        pltpu.make_async_copy(o_ref, og_ref.at[e, c, d], local.at[1]),
        pltpu.make_async_copy(x_ref, xg_ref.at[c], local.at[2]),
    ]
    for copy in keep:
        copy.start()
    c_peers = [(e, lax.rem(c + k, n_c), d) for k in range(1, n_c)]
    d_peers = [(e, c, lax.rem(d + k, n_d)) for k in range(1, n_d)]
    e_peers = expert_peers(sizes, place)
    greet(c_peers + d_peers + e_peers)
    turn = []
    for k in range(1, n_c):
        copy = remote(
            a_ref.at[lax.rem(c + k, n_c)],
            ag_ref.at[e, c, d],
            s_a.at[k - 1],
            r_a.at[k - 1],
            c_peers[k - 1],
        )
        copy.start()
        turn.append(copy)
    rows = ContextGather(
        sizes, place, x_ref, lambda j: xg_ref.at[j], lambda k: s_x.at[k], lambda k: r_x.at[k]
    )
    rows.start()

    def spread(own, slot, send, recv, base):
        along = []
        for k in range(1, n_d):
            copy = remote(
                own, slot(e, d), send.at[base + k - 1], recv.at[base + k - 1], d_peers[k - 1]
            )
            copy.start()
            along.append(copy)
        across = []
        for j in range(1, n_e):
            n = base + n_d - 1 + (j - 1) * n_d
            copy = remote(own, slot(e, d), send.at[n], recv.at[n], e_peers[j - 1])
            copy.start()
            across.append(copy)
        return along, across

    def onward(parts, slot, send, recv, base):
        along, across = parts
        for k in range(1, n_d):
            along[k - 1].wait_recv()
            block = slot(e, lax.rem(d - k + n_d, n_d))
            for j in range(1, n_e):
                n = base + n_d - 1 + (j - 1) * n_d + k
                copy = remote(block, block, send.at[n], recv.at[n], e_peers[j - 1])
                copy.start()
                across.append(copy)

    o_slot = lambda j, k: og_ref.at[j, c, k]
    a_slot = lambda j, k: ag_ref.at[j, :, k]
    o_parts = spread(o_ref, o_slot, s_o, r_o, 0)
    for copy in turn:
        copy.wait()
    for copy in keep:
        copy.wait()
    a_parts = spread(ag_ref.at[e, :, d], a_slot, s_b, r_b, 0)
    onward(o_parts, o_slot, s_o, r_o, 0)
    rows.forward()
    for copy in o_parts[1]:
        copy.wait_recv()
    base = (n_d - 1) + (n_e - 1) * n_d
    whole = ContextGather(
        sizes,
        place,
        og_ref.at[:, c],
        lambda j: og_ref.at[:, j],
        lambda k: s_o.at[base + k],
        lambda k: r_o.at[base + k],
    )
    whole.start()
    onward(a_parts, a_slot, s_b, r_b, 0)
    whole.forward()
    for copy in a_parts[1]:
        copy.wait()
    for copy in [*a_parts[0], *o_parts[0], *o_parts[1]]:
        copy.wait_send()
    rows.finish()
    whole.finish()


def gather_first(sizes, a_part, o_part, x_part):
    n_e, n_c, n_d = sizes
    dma = pltpu.SemaphoreType.DMA
    spread = (n_d - 1) + (n_e - 1) * n_d
    counts = [n_c - 1, n_c - 1, spread, spread, spread + n_c - 1, spread + n_c - 1, n_c - 1, n_c - 1]
    anywhere = pl.BlockSpec(memory_space=pl.ANY)
    return pl.pallas_call(
        functools.partial(gather_kernel, sizes),
        out_shape=(
            jax.ShapeDtypeStruct((n_e, n_c, n_d, *a_part.shape[1:]), BF16),
            jax.ShapeDtypeStruct((n_e, n_c, n_d, *o_part.shape), BF16),
            jax.ShapeDtypeStruct((n_c, *x_part.shape), BF16),
        ),
        in_specs=[anywhere] * 3,
        out_specs=(anywhere,) * 3,
        scratch_shapes=[dma((3,))] + [dma((n,)) for n in counts],
        compiler_params=pltpu.CompilerParams(collective_id=0, has_side_effects=True),
        name="gather_first",
    )(a_part, o_part, x_part)


def softmax_pair(left, right):
    top = jnp.maximum(left, right)
    left, right = jnp.exp(left - top), jnp.exp(right - top)
    total = left + right
    return left / total, right / total


def route_parts(routes_t, routes, small, n_ff, n_all, slots):
    rows = routes.shape[0]
    hot = lax.broadcasted_iota(jnp.int32, (LANES, rows), 0)
    marks = [(hot == routes_t[k : k + 1, :]) & (hot < n_ff) for k in range(2)]
    both = (marks[0] | marks[1]).astype(F32)
    earlier = lax.broadcasted_iota(jnp.int32, (rows, rows), 0) < lax.broadcasted_iota(
        jnp.int32, (rows, rows), 1
    )
    rank = dot(both.astype(BF16), earlier.astype(F32).astype(BF16))
    number = lax.broadcasted_iota(jnp.int32, (slots, rows), 0).astype(F32)
    tables = []
    for k in range(2):
        wanted = jnp.where(marks[k], rank, -1.0)
        tables.append(
            jnp.concatenate(
                [(number == wanted[j : j + 1, :]).astype(F32) for j in range(n_ff)], axis=0
            ).astype(BF16)
        )
    lane = lax.broadcasted_iota(jnp.int32, (rows, LANES), 1)
    picks = [(lane == routes[:, k : k + 1]).astype(F32) for k in range(2)]
    chosen = [
        jnp.sum(jnp.where(picks[k] > 0, small, 0.0), axis=1, keepdims=True) for k in range(2)
    ]
    w_pair = softmax_pair(chosen[0], chosen[1])
    first = softmax_pair(small[:, n_all : n_all + 1], small[:, n_all + 1 : n_all + 2])
    second = softmax_pair(small[:, n_all + 2 : n_all + 3], small[:, n_all + 3 : n_all + 4])
    return tables, picks, w_pair, first, second


def front_kernel(
    sizes,
    cfg,
    xg_ref,
    xown_ref,
    wqkv_ref,
    wo_ref,
    wsm_ref,
    vec_ref,
    dcol_ref,
    drow_ref,
    routes_ref,
    routest_ref,
    prev_ref,
    g_ref,
    a1_ref,
    qt_ref,
    kh_ref,
    vh_ref,
    mixed_ref,
    h_ref,
    a2_ref,
    small_ref,
    p_ref,
    slots_ref,
    o_scr,
    vt_scr,
    p_scr,
    sbuf,
    xin,
    p_sem,
    s_o,
    r_o,
    s_x,
    r_x,
    s_g,
    r_g,
    l_g,
):
    n_e, n_c, n_d = sizes
    hp, n_ff, n_all, n_loc, slots = cfg
    hc = hp * HEAD_DIM
    place = e, c, d = position()
    length = xg_ref.shape[0]
    rows = length // n_c
    c_all = [(e, lax.rem(c + k, n_c), d) for k in range(1, n_c)]
    e_peers = expert_peers(sizes, place)
    greet(c_all + e_peers)

    gain_one = vec_ref[0:1, :]
    for b in range(n_c):
        part = pl.ds(b * rows, rows)
        x = xg_ref[part, :].astype(F32)
        inverse = lax.rsqrt(jnp.mean(x * x, axis=-1, keepdims=True) + EPS)
        a1_ref[part, :] = (x * inverse * gain_one).astype(BF16)
    a1 = a1_ref[...]
    wqkv = wqkv_ref[...]
    q_t = dot(wqkv[:, :hc], a1, 0, 1).astype(BF16) * jnp.asarray(HEAD_DIM**-0.5, BF16)
    qt_ref[...] = q_t
    kv = dot(a1, wqkv[:, hc:]).astype(BF16)
    for j in range(hp):
        kh_ref[j] = kv[:, j * HEAD_DIM : (j + 1) * HEAD_DIM]
        vh_ref[j] = kv[:, hc + j * HEAD_DIM : hc + (j + 1) * HEAD_DIM]
    vt_scr[...] = dot(wqkv[:, 2 * hc :], a1, 0, 1).astype(BF16)

    turn = 0
    p_copies = {}
    for b in reversed(range(n_c)):
        reach = (b + 1) * rows
        key_place = lax.broadcasted_iota(jnp.int32, (reach, rows), 0)
        q_place = lax.broadcasted_iota(jnp.int32, (reach, rows), 1) + b * rows
        allowed = (dcol_ref[:reach, :] == drow_ref[:, b * rows : reach]) & (key_place <= q_place)
        bias = jnp.where(allowed, 0.0, -1e30)
        for j in range(hp):
            head = slice(j * HEAD_DIM, (j + 1) * HEAD_DIM)
            scores = dot(kh_ref[j, :reach, :], qt_ref[head, b * rows : reach]) + bias
            top = jnp.max(scores, axis=0, keepdims=True)
            exponent = jnp.exp(scores - top)
            total = jnp.sum(exponent, axis=0, keepdims=True)
            rounded = (exponent * (1.0 / total)).astype(BF16)
            slot = turn % 2
            if turn >= 2:
                p_copies[turn - 2].wait()
            p_scr[slot, :reach, :] = rounded
            copy = pltpu.make_async_copy(
                p_scr.at[slot, pl.ds(0, reach)], p_ref.at[j, b, pl.ds(0, reach)], p_sem.at[slot]
            )
            copy.start()
            p_copies[turn] = copy
            turn += 1
            o_scr[b, head, :] = dot(vt_scr[head, :reach], rounded).astype(BF16)

        @pl.when(c != b)
        def _():
            remote(
                o_scr.at[b], mixed_ref.at[c], s_o.at[b], r_o.at[c], (e, b, d)
            ).start()

    for n in range(max(0, turn - 2), turn):
        p_copies[n].wait()
    mixed_ref[pl.ds(c, 1)] = o_scr[pl.ds(c, 1)]
    for b in range(n_c):

        @pl.when(c != b)
        def _():
            copy = remote(o_scr.at[b], mixed_ref.at[b], s_o.at[b], r_o.at[b], (e, b, d))
            copy.wait_send()
            copy.wait_recv()

    mixed = mixed_ref[...].reshape(n_c * hc, rows)
    h = xown_ref[...].astype(F32) + dot(mixed, wo_ref[...], 0, 0)
    h_ref[...] = h
    inverse = lax.rsqrt(jnp.mean(h * h, axis=-1, keepdims=True) + EPS)
    a2 = (h * inverse * vec_ref[1:2, :]).astype(BF16)
    a2_ref[...] = a2
    small = dot(a2, wsm_ref[...]) + prev_ref[...]
    small_ref[...] = small
    tables, _, w_pair, _, _ = route_parts(
        routest_ref[...], routes_ref[...], small, n_ff, n_all, slots
    )
    per = n_loc * slots
    crossing = {}
    gathers = {}
    g = g_ref[...]
    for t in range(2):
        if t == 0:
            block = dot(tables[0] + tables[1], a2).astype(BF16)
        else:
            block = dot(tables[0], (w_pair[0] * g).astype(BF16)) + dot(
                tables[1], (w_pair[1] * g).astype(BF16)
            )
            block = block.astype(BF16)
        for k in range(n_e):
            sbuf[t, k] = block[k * per : (k + 1) * per, :]
        for j in range(1, n_e):
            n = t * n_e + j
            copy = remote(
                sbuf.at[t, lax.rem(e + j, n_e)],
                xin.at[t, e],
                s_x.at[n],
                r_x.at[n],
                e_peers[j - 1],
            )
            copy.start()
            crossing[t, j] = copy

        def gather(j, own, t=t):
            src = lax.rem(e - j + n_e, n_e)
            base = (t * n_e + j) * (n_c - 1)
            keep = pltpu.make_async_copy(own, slots_ref.at[c, t, src], l_g.at[t * n_e + j])
            keep.start()
            made = ContextGather(
                sizes,
                place,
                own,
                lambda k: slots_ref.at[k, t, src],
                lambda k: s_g.at[base + k],
                lambda k: r_g.at[base + k],
            )
            made.start()
            gathers[t, j] = (made, keep)

        gather(0, sbuf.at[t, e])
        crossing[t, 0] = gather
    for t in range(2):
        for j in range(1, n_e):
            crossing[t, j].wait_recv()
            crossing[t, 0](j, xin.at[t, lax.rem(e - j + n_e, n_e)])
    for made, _ in gathers.values():
        made.forward()
    for made, keep in gathers.values():
        made.finish()
        keep.wait()
    for t in range(2):
        for j in range(1, n_e):
            crossing[t, j].wait_send()


def front(sizes, cfg, *operands):
    n_e, n_c, n_d = sizes
    hp, n_ff, n_all, n_loc, slots = cfg
    hc = hp * HEAD_DIM
    length = operands[0].shape[0]
    rows = length // n_c
    per = n_loc * slots
    dma = pltpu.SemaphoreType.DMA
    vmem = pl.BlockSpec(memory_space=pltpu.VMEM)
    anywhere = pl.BlockSpec(memory_space=pl.ANY)
    shape = jax.ShapeDtypeStruct
    gathers = 2 * n_e * (n_c - 1)
    return pl.pallas_call(
        functools.partial(front_kernel, sizes, cfg),
        out_shape=(
            shape((length, D), BF16),
            shape((hc, length), BF16),
            shape((hp, length, HEAD_DIM), BF16),
            shape((hp, length, HEAD_DIM), BF16),
            shape((n_c, hc, rows), BF16),
            shape((rows, D), F32),
            shape((rows, D), BF16),
            shape((rows, LANES), F32),
            shape((hp, n_c, length, rows), BF16),
            shape((n_c, 2, n_e, per, D), BF16),
        ),
        in_specs=[vmem] * len(operands),
        out_specs=(vmem,) * 8 + (anywhere,) * 2,
        scratch_shapes=[
            pltpu.VMEM((n_c, hc, rows), BF16),
            pltpu.VMEM((hc, length), BF16),
            pltpu.VMEM((2, length, rows), BF16),
            pltpu.VMEM((2, n_e, per, D), BF16),
            pltpu.VMEM((2, n_e, per, D), BF16),
            dma((2,)),
            dma((n_c,)),
            dma((n_c,)),
            dma((2 * n_e,)),
            dma((2 * n_e,)),
            dma((gathers,)),
            dma((gathers,)),
            dma((2 * n_e,)),
        ],
        compiler_params=pltpu.CompilerParams(
            collective_id=1, has_side_effects=True, vmem_limit_bytes=VMEM_LIMIT
        ),
        name="front",
    )(*operands)


def expert_kernel(x_ref, dy_ref, w_ref, out_ref, gw_ref, total):
    step = pl.program_id(1)
    parts = w_ref.shape[0]
    x = x_ref[...].reshape(-1, D)
    dy = dy_ref[...].reshape(-1, D)
    block = out_ref.shape[0:1] + out_ref.shape[2:]
    gate, up, down = [
        jnp.concatenate([w_ref[k, n, 0] for k in range(parts)], axis=1) for n in range(3)
    ]
    gate_pre = dot(x, gate)
    up_pre = dot(x, up)
    sig = jax.nn.sigmoid(gate_pre)
    hidden = (gate_pre * sig * up_pre).astype(BF16)
    result = dot(hidden, down, 1, 1).astype(BF16)
    out_ref[:, 0] = result.reshape(block)
    d_hidden = dot(dy, down)
    d_gate = (d_hidden * up_pre * sig * (1.0 + gate_pre * (1.0 - sig))).astype(BF16)
    d_up = (d_hidden * gate_pre * sig).astype(BF16)
    d_x = dot(d_gate, gate, 1, 1) + dot(d_up, up, 1, 1)
    out_ref[:, 1] = d_x.astype(BF16).reshape(block)
    grads = (dot(x, d_gate, 0, 0), dot(x, d_up, 0, 0), dot(dy, hidden, 0, 0))

    @pl.when(step == 0)
    def _():
        for n in range(3):
            total[n] = grads[n]

    @pl.when(step > 0)
    def _():
        for n in range(3):
            total[n] += grads[n]

    @pl.when(step == pl.num_programs(1) - 1)
    def _():
        width = gate.shape[1] // parts
        for n in range(3):
            for k in range(parts):
                gw_ref[k, n, 0] = total[n, :, k * width : (k + 1) * width].astype(BF16)


def experts_pass(gathered, weights):
    n_c, _, n_e, n_loc, slots, _ = gathered.shape
    parts, _, _, _, units = weights.shape
    take = max(1, min(n_c, 512 // (n_e * slots)))
    return pl.pallas_call(
        expert_kernel,
        grid=(n_loc, n_c // take),
        out_shape=(
            jax.ShapeDtypeStruct(gathered.shape, BF16),
            jax.ShapeDtypeStruct(weights.shape, BF16),
        ),
        in_specs=[
            pl.BlockSpec((take, 1, n_e, 1, slots, D), lambda i, j: (j, 0, 0, i, 0, 0)),
            pl.BlockSpec((take, 1, n_e, 1, slots, D), lambda i, j: (j, 1, 0, i, 0, 0)),
            pl.BlockSpec((parts, 3, 1, D, units), lambda i, j: (0, 0, i, 0, 0)),
        ],
        out_specs=(
            pl.BlockSpec((take, 2, n_e, 1, slots, D), lambda i, j: (j, 0, 0, i, 0, 0)),
            pl.BlockSpec((parts, 3, 1, D, units), lambda i, j: (0, 0, i, 0, 0)),
        ),
        scratch_shapes=[pltpu.VMEM((3, D, parts * units), F32)],
        compiler_params=pltpu.CompilerParams(
            dimension_semantics=("arbitrary", "arbitrary"), vmem_limit_bytes=VMEM_LIMIT
        ),
        name="experts_pass",
    )(gathered, gathered, weights)


def back_kernel(
    sizes,
    cfg,
    res_ref,
    h_ref,
    a2_ref,
    small_ref,
    g_ref,
    routes_ref,
    routest_ref,
    wo_ref,
    wqkv_ref,
    wsm_ref,
    vec_ref,
    mixed_ref,
    a1_ref,
    qt_ref,
    kh_ref,
    vh_ref,
    p_ref,
    xg_ref,
    gw_ref,
    block_ref,
    dx_ref,
    dprev_ref,
    gq_ref,
    gk_ref,
    gv_ref,
    go_ref,
    gsmall_ref,
    egate_ref,
    eup_ref,
    edown_ref,
    inn,
    osum,
    outr,
    back,
    xsum,
    stage,
    dhg,
    dht_scr,
    p_scr,
    dk_acc,
    dv_acc,
    dqt,
    dqkv,
    da_in,
    da_sum,
    da_out,
    x_scr,
    ew_own,
    ew_in,
    t_send,
    t_recv,
    t_z,
    t_zr,
    t_c,
    t_cr,
    o_own,
    o_in,
    o_sum,
    o_out,
    o_x,
    o_xr,
    o_z,
    o_zr,
    l_sem,
    s_in,
    r_in,
    s_out,
    r_out,
    s_x,
    r_x,
    s_g,
    r_g,
    p_sem,
    s_d,
    r_d,
    s_w,
    r_w,
    s_t,
    r_t,
    s_q,
    r_q,
):
    n_e, n_c, n_d = sizes
    hp, n_ff, n_all, n_loc, slots = cfg
    hc = hp * HEAD_DIM
    place = e, c, d = position()
    pairs = n_c // 2
    outer, inner = c // 2, c % 2
    rows = h_ref.shape[0]
    w_rows = go_ref.shape[0]
    shift = 3 * hc % LANES
    chunks = up_to(3 * hc + SMALL, LANES) // LANES
    d_peers = [(e, c, lax.rem(d + k, n_d)) for k in range(1, n_d)]
    length = rows * n_c
    peers = context_peers(sizes, place)
    e_peers = expert_peers(sizes, place)

    in_vmem = len(stage.shape) == 5
    if in_vmem:
        take = pltpu.make_async_copy(res_ref.at[:, inner], stage, l_sem.at[0])
        take.start()
    bring = pltpu.make_async_copy(gw_ref, ew_own, l_sem.at[1])
    bring.start()

    def fetch_x(b, slot):
        return pltpu.make_async_copy(xg_ref.at[b], x_scr.at[slot], l_sem.at[2 + slot])

    fetch_x(c, 2).start()
    fetch_x(0, 0).start()
    greet(peers + e_peers + d_peers)

    def expert_send(way, step, src):
        there = d + 1 if way == 0 else d - 1
        return remote(
            src,
            ew_in.at[way, step - 1],
            s_w.at[way, step - 1],
            r_w.at[way, step - 1],
            (e, c, there),
        )

    def expert_place(way):
        return d if way == 0 else n_d - 1 - d

    def add_own(way, step, part):
        size = ew_own.shape[1]
        tile = size // 8 if size % 128 == 0 else size

        def one(n, carry):
            at = pl.ds(pl.multiple_of(n * tile, tile), tile)
            total = ew_in[way, step - 1, at, :].astype(F32) + ew_own[part, at, :].astype(F32)
            ew_in[way, step - 1, at, :] = total.astype(BF16)
            return carry

        lax.fori_loop(0, size // tile, one, 0)

    def expert_step(step):
        for way in range(2):
            at = expert_place(way)
            far = n_d + at - step
            part = far if way == 0 else n_d - 1 - far

            @pl.when(at == 0)
            def _():
                expert_send(way, step, ew_own.at[part]).start()

            if step > 1:

                @pl.when((at > 0) & (at < step))
                def _():
                    src = ew_in.at[way, step - 2]
                    expert_send(way, step - 1, src).wait_recv()
                    add_own(way, step - 1, part)
                    expert_send(way, step, src).start()

    def expert_end():
        last = n_d - 1
        for way in range(2):

            @pl.when(expert_place(way) > 0)
            def _():
                expert_send(way, last, ew_own.at[0]).wait_recv()

        size = ew_own.shape[1] // 3
        for n, ref in enumerate((egate_ref, eup_ref, edown_ref)):
            at = pl.ds(n * size, size)
            ref[...] = ew_own[d, at, :].astype(F32)
            for way in range(2):

                @pl.when(expert_place(way) > 0)
                def _():
                    ref[...] += ew_in[way, last - 1, at, :].astype(F32)

        for way in range(2):
            for step in range(1, n_d):

                @pl.when(expert_place(way) < step)
                def _():
                    expert_send(way, step, ew_own.at[0]).wait_send()

    bring.wait()
    expert_step(1)

    def load(ref, slot=0):
        if in_vmem:
            return ref[...].astype(F32)
        copy = pltpu.make_async_copy(ref, stage.at[slot], l_sem.at[0])
        copy.start()
        copy.wait()
        return stage[slot].astype(F32)

    def own_part(there, t, src):
        if in_vmem:
            return stage[there, t, src].astype(F32)
        return load(res_ref.at[there, inner, t, src])

    def store(ref, value):
        if in_vmem:
            ref[...] = value
        else:
            stage[3] = value
            copy = pltpu.make_async_copy(stage.at[3], ref, l_sem.at[0])
            copy.start()
            copy.wait()

    pieces = [(t, j) for j in [*range(1, n_e), 0] for t in range(2)]
    first_copies = {}
    for t, j in pieces:
        src = lax.rem(e + j, n_e)
        for k in [*range(1, pairs), 0]:
            n = (t * n_e + j) * pairs + k
            there = lax.rem(outer + k, pairs)
            copy = remote(
                res_ref.at[there, 1 - inner, t, src],
                inn.at[there, t, src],
                s_in.at[n],
                r_in.at[n],
                peers[0],
            )
            copy.start()
            first_copies[t, j, k] = copy
    if in_vmem:
        take.wait()
    second = {}
    for t, j in pieces:
        src = lax.rem(e + j, n_e)
        for k in range(1, pairs):
            n = (t * n_e + j) * pairs + k
            there = lax.rem(outer + k, pairs)
            first_copies[t, j, k].wait_recv()
            total = own_part(there, t, src) + load(inn.at[there, t, src], 1)
            store(osum.at[k - 1, t, src], total.astype(BF16))
            copy = remote(
                osum.at[k - 1, t, src], outr.at[k - 1, t, src], s_out.at[n], r_out.at[n], peers[k]
            )
            copy.start()
            second[t, j, k] = copy
    home = {}
    for t, j in pieces:
        src = lax.rem(e + j, n_e)
        first_copies[t, j, 0].wait_recv()
        total = own_part(outer, t, src) + load(inn.at[outer, t, src], 1)
        for k in range(1, pairs):
            second[t, j, k].wait_recv()
            total = total + load(outr.at[k - 1, t, src], 2)
        if j == 0:
            back[t, e] = total.astype(BF16)
        else:
            xsum[t, src] = total.astype(BF16)
            n = t * n_e + j
            copy = remote(
                xsum.at[t, src], back.at[t, e], s_x.at[n], r_x.at[n], e_peers[j - 1]
            )
            copy.start()
            home[t, j] = copy

    h = h_ref[...]
    a2 = a2_ref[...].astype(F32)
    g = g_ref[...]
    small = small_ref[...]
    value_one, value_two = vec_ref[2:3, :], vec_ref[3:4, :]
    tables, picks, w_pair, first, other = route_parts(
        routest_ref[...], routes_ref[...], small, n_ff, n_all, slots
    )
    copy_on, one_on, two_on = [
        [picks[k][:, n_ff + n : n_ff + n + 1] for k in range(2)] for n in (1, 2, 3)
    ]
    g_a2 = jnp.sum(g * a2, axis=1, keepdims=True)
    g_one = jnp.sum(g * value_one, axis=1, keepdims=True)
    g_two = jnp.sum(g * value_two, axis=1, keepdims=True)
    alpha = [copy_on[k] + one_on[k] * first[0] + two_on[k] * other[0] for k in range(2)]
    a_weight = alpha[0] * w_pair[0] + alpha[1] * w_pair[1]
    one_weight = one_on[0] * w_pair[0] + one_on[1] * w_pair[1]
    two_weight = two_on[0] * w_pair[0] + two_on[1] * w_pair[1]
    for copy in home.values():
        copy.wait_recv()
    returned = [back[t].reshape(n_ff * slots, D) for t in range(2)]
    block = h
    d_weight = []
    for k in range(2):
        routed = dot(tables[k], returned[0], 0, 0)
        picked = (
            routed
            + alpha[k] * a2
            + (one_on[k] * first[1]) * value_one
            + (two_on[k] * other[1]) * value_two
        )
        block = block + w_pair[k] * picked
        d_weight.append(jnp.sum(g * picked, axis=1, keepdims=True))
    block_ref[...] = block
    center = w_pair[0] * d_weight[0] + w_pair[1] * d_weight[1]
    d_logits = (
        picks[0] * (w_pair[0] * (d_weight[0] - center))
        + picks[1] * (w_pair[1] * (d_weight[1] - center))
    )
    dprev_ref[...] = d_logits[:, :n_all]
    lane = lax.broadcasted_iota(jnp.int32, (rows, LANES), 1)
    d_small = d_logits
    for base, pair, weight, g_value in (
        (n_all, first, one_weight, g_one),
        (n_all + 2, other, two_weight, g_two),
    ):
        d_pair = (weight * g_a2, weight * g_value)
        middle = pair[0] * d_pair[0] + pair[1] * d_pair[1]
        for k in range(2):
            d_small = d_small + jnp.where(lane == base + k, pair[k] * (d_pair[k] - middle), 0.0)
    d_small = d_small.astype(BF16)
    d_const_one = jnp.sum((first[1] * one_weight) * g, axis=0, keepdims=True)
    d_const_two = jnp.sum((other[1] * two_weight) * g, axis=0, keepdims=True)
    d_a2 = (
        dot(tables[0] + tables[1], returned[1], 0, 0)
        + a_weight * g
        + dot(d_small, wsm_ref[...], 1, 1)
    )
    gain_two = vec_ref[1:2, :]
    inverse_two = lax.rsqrt(jnp.mean(h * h, axis=-1, keepdims=True) + EPS)
    d_gain_two = jnp.sum(d_a2 * h * inverse_two, axis=0, keepdims=True)
    scaled = gain_two * d_a2
    d_h = (
        g
        + inverse_two * scaled
        - h * inverse_two**3 * jnp.mean(scaled * h, axis=-1, keepdims=True)
    )
    d_hb = d_h.astype(BF16)
    dhg[pl.ds(c, 1)] = d_hb[None]
    gather = ContextGather(
        sizes,
        place,
        dhg.at[c],
        lambda k: dhg.at[k],
        lambda k: s_g.at[k],
        lambda k: r_g.at[k],
    )
    gather.start()
    dx_ref[...] = d_h
    if n_d > 2:
        expert_step(2)
    g_o = dot(mixed_ref[...].reshape(n_c * hc, rows), d_hb)
    run = n_d * w_rows
    for b in range(n_c):
        for k in range(n_e):
            o_own[b, k, :run, :] = g_o[(k * n_c + b) * run : (k * n_c + b + 1) * run].astype(BF16)
    parcel = Courier(s_q, r_q)
    o_pair = {}
    for k in [*range(1, pairs), 0]:
        there = lax.rem(outer + k, pairs)
        o_pair[k] = parcel.carry(
            o_own.at[there * 2 + 1 - inner], o_in.at[there], peers[0]
        )
    o_state = {}

    def o_outer():
        o_state["outer"] = []
        for k in range(1, pairs):
            there = lax.rem(outer + k, pairs)
            o_pair[k].wait_recv()
            o_sum[k - 1] = (
                o_own[there * 2 + inner].astype(F32) + o_in[there].astype(F32)
            ).astype(BF16)
            o_state["outer"].append(
                parcel.carry(o_sum.at[k - 1], o_out.at[k - 1], peers[k])
            )

    def o_across():
        o_pair[0].wait_recv()
        total = o_own[c].astype(F32) + o_in[outer].astype(F32)
        for k, copy in enumerate(o_state["outer"]):
            copy.wait_recv()
            total = total + o_out[k].astype(F32)
        o_x[...] = total.astype(BF16)
        o_state["across"] = [
            parcel.carry(o_x.at[lax.rem(e + j, n_e)], o_xr.at[j - 1], e_peers[j - 1])
            for j in range(1, n_e)
        ]

    def o_along():
        total = o_x[e].astype(F32)
        for j, copy in enumerate(o_state["across"]):
            copy.wait_recv()
            total = total + o_xr[j].astype(F32)
        for k in range(n_d):
            o_z[k, :w_rows, :] = total[k * w_rows : (k + 1) * w_rows].astype(BF16)
        o_state["along"] = [
            parcel.carry(o_z.at[lax.rem(d + k, n_d)], o_zr.at[k - 1], d_peers[k - 1])
            for k in range(1, n_d)
        ]

    def o_end():
        total = o_z[d].astype(F32)
        for k, copy in enumerate(o_state["along"]):
            copy.wait_recv()
            total = total + o_zr[k].astype(F32)
        go_ref[...] = total[:w_rows]
        parcel.finish()

    if shift:
        d_small = jnp.concatenate(
            [jnp.zeros((rows, shift), BF16), d_small[:, : LANES - shift]], axis=1
        )
    g_small = dot(a2_ref[...], d_small, 0, 0)
    dk_acc[...] = jnp.zeros_like(dk_acc)
    dv_acc[...] = jnp.zeros_like(dv_acc)
    order = [(b, j) for b in reversed(range(n_c)) for j in range(hp)]

    def fetch(n):
        b, j = order[n]
        reach = pl.ds(0, (b + 1) * rows)
        return pltpu.make_async_copy(p_ref.at[j, b, reach], p_scr.at[n % 2, reach], p_sem.at[n % 2])

    fetch(0).start()
    gather.forward()
    gather.finish()
    o_outer()
    wo_part = wo_ref[pl.ds(pl.multiple_of(c * hc, hc), hc), :]
    for b in range(n_c):
        dht_scr[:, b * rows : (b + 1) * rows] = dot(wo_part, dhg[b], 1, 1).astype(BF16)
    for n, (b, j) in enumerate(order):
        reach = (b + 1) * rows
        head = slice(j * HEAD_DIM, (j + 1) * HEAD_DIM)
        mine_q = slice(b * rows, reach)
        if n == len(order) // 4:
            o_across()
        if n == len(order) // 2:
            o_along()
        if n + 1 < len(order):
            fetch(n + 1).start()
        fetch(n).wait()
        rounded = p_scr[n % 2, :reach, :]
        prob = rounded.astype(F32)
        d_o = dht_scr[head, mine_q]
        d_prob = dot(vh_ref[j, :reach, :], d_o)
        delta = jnp.sum(prob * d_prob, axis=0, keepdims=True)
        d_scores = (prob * (d_prob - delta)).astype(BF16)
        dqt[head, mine_q] = dot(kh_ref[j, :reach, :], d_scores, 0, 0) * HEAD_DIM**-0.5
        dk_acc[j, :reach, :] += dot(d_scores, qt_ref[head, mine_q], 1, 1)
        dv_acc[j, :reach, :] += dot(rounded, d_o, 1, 1)
    dqkv[:, :hc] = dqt[...].T.astype(BF16)
    for j in range(hp):
        at = j * HEAD_DIM
        dqkv[:, hc + at : hc + at + HEAD_DIM] = dk_acc[j].astype(BF16)
        dqkv[:, 2 * hc + at : 2 * hc + at + HEAD_DIM] = dv_acc[j].astype(BF16)
    dqkv[:, 3 * hc :] = jnp.zeros((length, dqkv.shape[1] - 3 * hc), BF16)
    d_all = dqkv[...]
    bag = Courier(s_t, r_t)
    across = {}
    g_all = dot(a1_ref[...], d_all, 0, 0)
    half = D // n_e

    def send_chunk(k, value):
        for n in range(n_e):
            t_send[k, n] = value[n * half : (n + 1) * half].astype(BF16)
        across[k] = [
            bag.carry(t_send.at[k, lax.rem(e + j, n_e)], t_recv.at[k, j - 1], e_peers[j - 1])
            for j in range(1, n_e)
        ]

    for k in range(chunks - 1):
        send_chunk(k, g_all[:, k * LANES : (k + 1) * LANES])
    for step in range(3, n_d):
        expert_step(step)
    wqkv = wqkv_ref[...]
    gain_one = vec_ref[0:1, :]
    d_gain_one = jnp.zeros((1, D), F32)
    for b in range(n_c):
        part = dot(d_all[b * rows : (b + 1) * rows, : 3 * hc], wqkv, 1, 1)
        dhg[b] = part.astype(BF16)
        if b + 1 < n_c:
            fetch_x(b + 1, (b + 1) % 2).start()
        fetch_x(b, b % 2).wait()
        x = x_scr[b % 2].astype(F32)
        inverse = lax.rsqrt(jnp.mean(x * x, axis=-1, keepdims=True) + EPS)
        d_gain_one = d_gain_one + jnp.sum(part * x * inverse, axis=0, keepdims=True)
    to_pair = []
    for k in [*range(1, pairs), 0]:
        there = lax.rem(outer + k, pairs)
        copy = remote(
            dhg.at[there * 2 + 1 - inner], da_in.at[there], s_d.at[k], r_d.at[k], peers[0]
        )
        copy.start()
        to_pair.append((k, copy))
    spot = lax.broadcasted_iota(jnp.int32, (LANES, D), 0)
    tall = jnp.zeros((LANES, D), F32)
    for n, row in enumerate((d_const_one, d_const_two, d_gain_one, d_gain_two)):
        tall = tall + jnp.where(spot == shift + n_all + 4 + n, row, 0.0)
    send_chunk(chunks - 1, g_all[:, (chunks - 1) * LANES :] + g_small + tall.T)
    along = []
    for k, copy in to_pair:
        if k == 0:
            continue
        there = lax.rem(outer + k, pairs)
        copy.wait_recv()
        da_sum[k - 1] = (
            dhg[there * 2 + inner].astype(F32) + da_in[there].astype(F32)
        ).astype(BF16)
        onward = remote(
            da_sum.at[k - 1],
            da_out.at[k - 1],
            s_d.at[pairs + k - 1],
            r_d.at[pairs + k - 1],
            peers[k],
        )
        onward.start()
        along.append(onward)
    down = {}
    for k in range(chunks):
        total = t_send[k, e].astype(F32)
        for j, copy in enumerate(across[k]):
            copy.wait_recv()
            total = total + t_recv[k, j].astype(F32)
        for n in range(n_d):
            t_z[k, n, : n_c * w_rows, :] = jnp.concatenate(
                [
                    total[(b * n_d + n) * w_rows : (b * n_d + n + 1) * w_rows]
                    for b in range(n_c)
                ],
                axis=0,
            ).astype(BF16)
        down[k] = [
            bag.carry(t_z.at[k, lax.rem(d + n, n_d)], t_zr.at[k, n - 1], d_peers[n - 1])
            for n in range(1, n_d)
        ]
    o_end()
    to_pair[-1][1].wait_recv()
    d_a1 = dhg[c].astype(F32) + da_in[outer].astype(F32)
    for k, copy in enumerate(along):
        copy.wait_recv()
        d_a1 = d_a1 + da_out[k].astype(F32)
    fetch_x(c, 2).wait()
    x = x_scr[2].astype(F32)
    inverse_one = lax.rsqrt(jnp.mean(x * x, axis=-1, keepdims=True) + EPS)
    scaled = gain_one * d_a1
    dx_ref[...] += inverse_one * scaled - x * inverse_one**3 * jnp.mean(
        scaled * x, axis=-1, keepdims=True
    )
    for k in range(chunks):
        total = t_z[k, d].astype(F32)
        for n, copy in enumerate(down[k]):
            copy.wait_recv()
            total = total + t_zr[k, n].astype(F32)
        for b in range(n_c):
            t_c[b, k, :w_rows, :] = total[b * w_rows : (b + 1) * w_rows]
    t_cr[pl.ds(c, 1)] = t_c[pl.ds(c, 1)]
    turned = [
        bag.carry(t_c.at[lax.rem(c + k, n_c)], t_cr.at[c], (e, lax.rem(c + k, n_c), d))
        for k in range(1, n_c)
    ]
    expert_end()
    for copy in turned:
        copy.wait_recv()
    s_total = jnp.zeros((w_rows, SMALL), F32)
    for b in range(n_c):
        line = jnp.concatenate([t_cr[b, k] for k in range(chunks)], axis=1)[:w_rows]
        for n, ref in enumerate((gq_ref, gk_ref, gv_ref)):
            width = min(hc, D - b * hc)
            if width > 0:
                ref[:, b * hc : b * hc + width] = line[:, n * hc : n * hc + width]
        s_total = s_total + line[:, 3 * hc : 3 * hc + SMALL]
    gsmall_ref[...] = s_total
    bag.finish()
    for copy in first_copies.values():
        copy.wait_send()
    for copy in second.values():
        copy.wait_send()
    for copy in home.values():
        copy.wait_send()
    for _, copy in to_pair:
        copy.wait_send()
    for copy in along:
        copy.wait_send()


def backward(sizes, cfg, *operands):
    n_e, n_c, n_d = sizes
    hp, n_ff, n_all, n_loc, slots = cfg
    hc = hp * HEAD_DIM
    rows = operands[1].shape[0]
    length = rows * n_c
    pairs = n_c // 2
    per = n_loc * slots
    dma = pltpu.SemaphoreType.DMA
    vmem = pl.BlockSpec(memory_space=pltpu.VMEM)
    anywhere = pl.BlockSpec(memory_space=pl.ANY)
    shape = jax.ShapeDtypeStruct
    n_in = 2 * n_e * pairs
    part = operands[18].shape[1]
    w_rows = D // (n_e * n_c * n_d)
    chunks = up_to(3 * hc + SMALL, LANES) // LANES
    run = up_to(n_d * w_rows, 16)
    turn = up_to(n_c * w_rows, 16)
    few = up_to(w_rows, 16)
    few_wide = up_to(w_rows, 8)
    bags = chunks * (n_e - 1 + n_d - 1) + n_c - 1
    parcels = 2 * pairs - 1 + n_e - 1 + n_d - 1
    n_more = max(1, pairs - 1)
    in_specs = [vmem] * len(operands)
    in_specs[0] = anywhere
    in_specs[16] = in_specs[17] = in_specs[18] = anywhere
    arriving = [(pairs, 2, n_e, per, D), (n_more, 2, n_e, per, D), (n_more, 2, n_e, per, D)]
    roomy = 2 * pairs * n_e * per * D <= 2**21
    held = [pltpu.VMEM(dims, BF16) for dims in arriving] if roomy else []
    extra = [] if roomy else [shape(dims, BF16) for dims in arriving]
    stage = pltpu.VMEM(arriving[0] if roomy else (4, per, D), BF16)
    return pl.pallas_call(
        functools.partial(back_kernel, sizes, cfg),
        out_shape=(
            shape((rows, D), F32),
            shape((rows, D), F32),
            shape((rows, n_all), F32),
            *[shape((w_rows, D), F32)] * 4,
            shape((w_rows, SMALL), F32),
            *[shape((part // 3, LANES), F32)] * 3,
            *extra,
        ),
        in_specs=in_specs,
        out_specs=(vmem,) * 11 + (anywhere,) * len(extra),
        scratch_shapes=[
            *held,
            pltpu.VMEM((2, n_e, per, D), BF16),
            pltpu.VMEM((2, n_e, per, D), BF16),
            stage,
            pltpu.VMEM((n_c, rows, D), BF16),
            pltpu.VMEM((hc, length), BF16),
            pltpu.VMEM((2, length, rows), BF16),
            pltpu.VMEM((hp, length, HEAD_DIM), F32),
            pltpu.VMEM((hp, length, HEAD_DIM), F32),
            pltpu.VMEM((hc, length), F32),
            pltpu.VMEM((length, chunks * LANES), BF16),
            pltpu.VMEM((pairs, rows, D), BF16),
            pltpu.VMEM((n_more, rows, D), BF16),
            pltpu.VMEM((n_more, rows, D), BF16),
            pltpu.VMEM((3, rows, D), BF16),
            pltpu.VMEM((n_d, part, LANES), BF16),
            pltpu.VMEM((2, n_d - 1, part, LANES), BF16),
            pltpu.VMEM((chunks, n_e, D // n_e, LANES), BF16),
            pltpu.VMEM((chunks, n_e - 1, D // n_e, LANES), BF16),
            pltpu.VMEM((chunks, n_d, turn, LANES), BF16),
            pltpu.VMEM((chunks, n_d - 1, turn, LANES), BF16),
            pltpu.VMEM((n_c, chunks, few_wide, LANES), F32),
            pltpu.VMEM((n_c, chunks, few_wide, LANES), F32),
            pltpu.VMEM((n_c, n_e, run, D), BF16),
            pltpu.VMEM((pairs, n_e, run, D), BF16),
            pltpu.VMEM((n_more, n_e, run, D), BF16),
            pltpu.VMEM((n_more, n_e, run, D), BF16),
            pltpu.VMEM((n_e, run, D), BF16),
            pltpu.VMEM((n_e - 1, run, D), BF16),
            pltpu.VMEM((n_d, few, D), BF16),
            pltpu.VMEM((n_d - 1, few, D), BF16),
            dma((5,)),
            dma((n_in,)),
            dma((n_in,)),
            dma((n_in,)),
            dma((n_in,)),
            dma((2 * n_e,)),
            dma((2 * n_e,)),
            dma((n_c - 1,)),
            dma((n_c - 1,)),
            dma((2,)),
            dma((n_c,)),
            dma((n_c,)),
            dma((2, n_d - 1)),
            dma((2, n_d - 1)),
            dma((bags,)),
            dma((bags,)),
            dma((parcels,)),
            dma((parcels,)),
        ],
        compiler_params=pltpu.CompilerParams(
            collective_id=2, has_side_effects=True, vmem_limit_bytes=VMEM_LIMIT
        ),
        name="backward",
    )(*operands)[:11]


def pad_to(array, axis, size):
    widths = [(0, 0)] * array.ndim
    widths[axis] = (0, size - array.shape[axis])
    return jnp.pad(array, widths)


def body(
    tokens,
    doc_ids,
    routes,
    prev_logits,
    cotangent,
    w_query,
    w_key,
    w_value,
    w_out,
    w_router,
    const_coef,
    const_value,
    norm_gains,
    expert_gate,
    expert_up,
    expert_down,
):
    sizes = n_e, n_c, n_d = tuple(lax.axis_size(axis) for axis in ALL_AXES)
    rows = tokens.shape[1]
    length = doc_ids.shape[1]
    n_loc, _, units = expert_gate.shape
    n_ff = n_loc * n_e
    n_all = w_router.shape[1]
    slots = rows // 4
    hp = -(-HEADS // n_c)
    hc = hp * HEAD_DIM
    cfg = (hp, n_ff, n_all, n_loc, slots)
    w_rows = w_query.shape[0]
    w_pad = -(-w_rows // 16) * 16
    width = -(-(3 * hc + SMALL) // LANES) * LANES

    pieces = jnp.stack([expert_gate, expert_up, expert_down]).astype(BF16)
    gathered_w = lax.all_gather(pieces, "dp", axis=0)

    small_w = jnp.concatenate([w_router, const_coef, const_value, norm_gains], axis=1).astype(BF16)
    slices = [
        pad_to(w.astype(BF16), 1, n_c * hc).reshape(w_rows, n_c, hc)
        for w in (w_query, w_key, w_value)
    ]
    slices.append(
        jnp.broadcast_to(
            pad_to(small_w, 1, width - 3 * hc)[:, None, :], (w_rows, n_c, width - 3 * hc)
        )
    )
    a_part = pad_to(jnp.concatenate(slices, axis=2).transpose(1, 0, 2), 1, w_pad)
    o_part = pad_to(w_out.astype(BF16), 0, w_pad)
    a_all, o_all, x_all = gather_first(sizes, a_part, o_part, tokens[0])
    a_all = a_all[:, :, :, :w_rows].reshape(D, width)
    wqkv = a_all[:, : 3 * hc]
    small_w = a_all[:, 3 * hc : 3 * hc + SMALL]
    wsm = pad_to(small_w, 1, LANES)
    wo = pad_to(o_all[:, :, :, :w_rows].reshape(D, D), 0, n_c * hc)
    lines = small_w[:, n_all + 4 : n_all + 8].astype(F32).T
    vec = pad_to(jnp.concatenate([lines[2:4], lines[0:2]], axis=0), 0, 8)

    documents = doc_ids[0]
    route_rows = routes[0]
    routes_t = pad_to(route_rows.T, 0, 8)
    prev = pad_to(prev_logits[0], 1, LANES)
    upstream = cotangent[0]
    (a1, q_t, k_h, v_h, mixed, h, a2, small, probs, gathered) = front(
        sizes,
        cfg,
        x_all.reshape(length, D),
        tokens[0],
        wqkv,
        wo,
        wsm,
        vec,
        documents[:, None],
        documents[None, :],
        route_rows,
        routes_t,
        prev,
        upstream,
    )
    if units % LANES:
        flat = gathered_w.transpose(1, 2, 3, 0, 4).reshape(1, 3, n_loc, D, n_d * units)
    else:
        flat = gathered_w
    results, grads = experts_pass(gathered.reshape(n_c, 2, n_e, n_loc, slots, D), flat)
    if units % LANES:
        grads = grads.reshape(3, n_loc, D, n_d, units).transpose(3, 0, 1, 2, 4)
    (block_rows, d_x, d_prev, q_grad, k_grad, v_grad, o_grad, s_grad, *expert_grads) = backward(
        sizes,
        cfg,
        results.reshape(n_c // 2, 2, 2, n_e, n_loc * slots, D),
        h,
        a2,
        small,
        upstream,
        route_rows,
        routes_t,
        wo,
        wqkv,
        wsm,
        vec,
        mixed,
        a1,
        q_t,
        k_h,
        v_h,
        probs,
        x_all,
        grads.reshape(n_d, 3 * n_loc * D * units // LANES, LANES),
    )
    return (
        block_rows[None],
        d_x[None],
        d_prev[None],
        q_grad,
        k_grad,
        v_grad,
        o_grad,
        s_grad[:, :n_all],
        s_grad[:, n_all : n_all + 4],
        s_grad[:, n_all + 4 : n_all + 6],
        s_grad[:, n_all + 6 : n_all + 8],
        *[part.reshape(n_loc, D, units) for part in expert_grads],
    )


def solution(mesh):
    rows = P(("expert", "dp"), "context", None)
    weights = P(ALL_AXES, None)
    units = P("expert", None, ("context", "dp"))
    return jax.shard_map(
        body,
        mesh=mesh,
        in_specs=(rows, P(("expert", "dp"), None), rows, rows, rows)
        + (weights,) * 8
        + (units,) * 3,
        out_specs=(rows,) * 3 + (weights,) * 8 + (units,) * 3,
        check_vma=False,
    )
```

```python
import functools

import jax
import jax.numpy as jnp
from jax import lax
from jax.experimental import pallas as pl
from jax.experimental.pallas import tpu as pltpu
from jax.sharding import PartitionSpec as P

D = 768
HEADS = 12
HEAD_DIM = 64
EPS = 1e-06
SMALL = 64
LANES = 128
VMEM_LIMIT = 63 * 2**20
MESH = pl.DeviceIdType.MESH
F32 = jnp.float32
BF16 = jnp.bfloat16
ALL_AXES = ("expert", "context", "dp")


def dot(left, right, left_dim=1, right_dim=0):
    return lax.dot_general(
        left, right, (((left_dim,), (right_dim,)), ((), ())), preferred_element_type=F32
    )


def position():
    return lax.axis_index("expert"), lax.axis_index("context"), lax.axis_index("dp")


def remote(src, dst, send_sem, recv_sem, device):
    return pltpu.make_async_remote_copy(
        src_ref=src,
        dst_ref=dst,
        send_sem=send_sem,
        recv_sem=recv_sem,
        device_id=device,
        device_id_type=MESH,
    )


def greet(devices):
    barrier = pltpu.get_barrier_semaphore()
    for device in devices:
        pl.semaphore_signal(barrier, inc=1, device_id=device, device_id_type=MESH)
    pl.semaphore_wait(barrier, len(devices))


def context_peers(sizes, place):
    e, c, d = place
    pairs = sizes[1] // 2
    outer, inner = c // 2, c % 2
    peers = [(e, outer * 2 + 1 - inner, d)]
    for k in range(1, pairs):
        peers.append((e, lax.rem(outer + k, pairs) * 2 + inner, d))
    return peers


def expert_peers(sizes, place):
    e, c, d = place
    return [(lax.rem(e + j, sizes[0]), c, d) for j in range(1, sizes[0])]


def crossing_only(sizes, n_loc, place):
    _, there, _ = homes(sizes, n_loc, place)
    return [device for j, (_, device) in enumerate(there) if j // n_loc and j % n_loc]


def homes(sizes, n_loc, place):
    n_e, n_c, n_d = sizes
    e, c, d = place
    size = n_d // n_loc
    group, seat = d // size, lax.rem(d, size)
    there, back = [], []
    for j in range(n_e * n_loc):
        je, jg = j // n_loc, j % n_loc
        to_e, to_g = lax.rem(e + je, n_e), lax.rem(group + jg, n_loc)
        from_e, from_g = lax.rem(e - je + n_e, n_e), lax.rem(group - jg + n_loc, n_loc)
        there.append((to_e * n_loc + to_g, (to_e, c, to_g * size + seat)))
        back.append(from_e * n_loc + from_g)
    return e * n_loc + group, there, back


class Courier:
    def __init__(self, send, recv):
        self.send, self.recv = send, recv
        self.copies = []

    def carry(self, src, dst, device):
        n = len(self.copies)
        copy = remote(src, dst, self.send.at[n], self.recv.at[n], device)
        copy.start()
        self.copies.append(copy)
        return copy

    def finish(self):
        for copy in self.copies:
            copy.wait_send()


def up_to(count, step):
    return -(-count // step) * step


class ContextGather:
    def __init__(self, sizes, place, own, slot, send, recv):
        e, c, d = place
        self.pairs = sizes[1] // 2
        self.place, self.own, self.slot = place, own, slot
        self.send, self.recv = send, recv
        self.outer, self.inner = c // 2, c % 2
        self.peers = context_peers(sizes, place)
        self.copies = []
        self.forwards = []

    def start(self):
        for k in [*range(1, self.pairs), 0]:
            copy = remote(
                self.own, self.slot(self.place[1]), self.send(k), self.recv(k), self.peers[k]
            )
            copy.start()
            self.copies.append((k, copy))

    def origin(self, k):
        return lax.rem(self.outer - k + self.pairs, self.pairs) * 2 + self.inner

    def forward(self):
        for k, copy in self.copies:
            if k > 0:
                copy.wait_recv()
                block = self.slot(self.origin(k))
                n = self.pairs - 1 + k
                onward = remote(block, block, self.send(n), self.recv(n), self.peers[0])
                onward.start()
                self.forwards.append(onward)

    def finish(self):
        for k, copy in self.copies:
            if k == 0:
                copy.wait_recv()
            copy.wait_send()
        for copy in self.forwards:
            copy.wait()


class Spread:
    def __init__(self, sizes, place, courier, own, slot):
        self.sizes, self.place, self.courier = sizes, place, courier
        self.slot = slot
        n_e, n_c, n_d = sizes
        e, c, d = place
        self.across_to = expert_peers(sizes, place)
        self.along = [
            courier.carry(own, slot(e, d), (e, c, lax.rem(d + k, n_d))) for k in range(1, n_d)
        ]
        self.across = [courier.carry(own, slot(e, d), device) for device in self.across_to]

    def onward(self):
        e, c, d = self.place
        n_d = self.sizes[2]
        for k in range(1, n_d):
            self.along[k - 1].wait_recv()
            block = self.slot(e, lax.rem(d - k + n_d, n_d))
            for device in self.across_to:
                self.across.append(self.courier.carry(block, block, device))

    def arrive(self):
        for copy in self.across:
            copy.wait_recv()


def spread_count(sizes):
    n_e, n_c, n_d = sizes
    return (n_d - 1) + (n_e - 1) * n_d


def softmax_pair(left, right):
    top = jnp.maximum(left, right)
    left, right = jnp.exp(left - top), jnp.exp(right - top)
    total = left + right
    return left / total, right / total


def tall(array, height):
    return jnp.concatenate(
        [array, jnp.zeros((height - array.shape[0], *array.shape[1:]), array.dtype)], axis=0
    )


def route_parts(routes_t, small, n_ff, n_all, slots):
    rows = routes_t.shape[1]
    routes = tall(routes_t.astype(F32), LANES).T
    hot = lax.broadcasted_iota(jnp.int32, (LANES, rows), 0)
    marks = [(hot == routes_t[k : k + 1, :]) & (hot < n_ff) for k in range(2)]
    both = (marks[0] | marks[1]).astype(F32)
    earlier = lax.broadcasted_iota(jnp.int32, (rows, rows), 0) < lax.broadcasted_iota(
        jnp.int32, (rows, rows), 1
    )
    rank = dot(both.astype(BF16), earlier.astype(F32).astype(BF16))
    number = lax.broadcasted_iota(jnp.int32, (slots, rows), 0).astype(F32)
    tables = []
    for k in range(2):
        wanted = jnp.where(marks[k], rank, -1.0)
        tables.append(
            jnp.concatenate(
                [(number == wanted[j : j + 1, :]).astype(F32) for j in range(n_ff)], axis=0
            ).astype(BF16)
        )
    lane = lax.broadcasted_iota(jnp.int32, (rows, LANES), 1)
    picks = [(lane.astype(F32) == routes[:, k : k + 1]).astype(F32) for k in range(2)]
    chosen = [
        jnp.sum(jnp.where(picks[k] > 0, small, 0.0), axis=1, keepdims=True) for k in range(2)
    ]
    w_pair = softmax_pair(chosen[0], chosen[1])
    first = softmax_pair(small[:, n_all : n_all + 1], small[:, n_all + 1 : n_all + 2])
    second = softmax_pair(small[:, n_all + 2 : n_all + 3], small[:, n_all + 3 : n_all + 4])
    return tables, picks, w_pair, first, second


def front_kernel(
    sizes,
    cfg,
    wq_ref,
    wk_ref,
    wv_ref,
    wout_ref,
    router_ref,
    coef_ref,
    value_ref,
    gains_ref,
    xown_ref,
    gate_ref,
    up_ref,
    down_ref,
    drow_ref,
    routest_ref,
    prev_ref,
    g_ref,
    xg_ref,
    wqkv_ref,
    wo_ref,
    wsm_ref,
    vec_ref,
    a1_ref,
    qt_ref,
    kh_ref,
    vh_ref,
    mixed_ref,
    h_ref,
    a2_ref,
    small_ref,
    p_ref,
    slots_ref,
    ew_ref,
    small_scr,
    a_ref,
    ow_ref,
    ag,
    og,
    ew_own,
    o_scr,
    vt_scr,
    p_scr,
    sbuf,
    xin,
    p_sem,
    s_o,
    r_o,
    s_x,
    r_x,
    s_g,
    r_g,
    l_g,
    s_c,
    r_c,
    s_ow,
    r_ow,
    s_xg,
    r_xg,
):
    n_e, n_c, n_d = sizes
    hp, n_ff, n_all, n_loc, slots = cfg
    hc = hp * HEAD_DIM
    place = e, c, d = position()
    rows = xown_ref.shape[0]
    length = rows * n_c
    c_all = [(e, lax.rem(c + k, n_c), d) for k in range(1, n_c)]
    n_s = n_e * n_loc
    me, there, back = homes(sizes, n_loc, place)
    d_peers = [(e, c, lax.rem(d + k, n_d)) for k in range(1, n_d)]
    w_rows = wq_ref.shape[0]
    small_scr[...] = jnp.zeros_like(small_scr)
    at = 0
    for ref in (router_ref, coef_ref, value_ref, gains_ref):
        small_scr[at : at + ref.shape[0], :w_rows] = ref[...]
        at += ref.shape[0]
    w_small = small_scr[...].T[:w_rows, : a_ref.shape[2] - 3 * hc].astype(BF16)
    a_ref[...] = jnp.zeros_like(a_ref)
    ow_ref[...] = jnp.zeros_like(ow_ref)
    ow_ref[:w_rows, :] = wout_ref[...].astype(BF16)
    for b in range(n_c):
        for n, ref in enumerate((wq_ref, wk_ref, wv_ref)):
            wide = min(hc, D - b * hc)
            if wide > 0:
                a_ref[b, :w_rows, n * hc : n * hc + wide] = ref[:, b * hc : b * hc + wide].astype(
                    BF16
                )
        a_ref[b, :w_rows, 3 * hc :] = w_small
    greet(c_all + d_peers + expert_peers(sizes, place) + crossing_only(sizes, n_loc, place))
    post = Courier(s_c, r_c)
    turned = [
        post.carry(a_ref.at[lax.rem(c + k, n_c)], ag.at[e, c, d], device)
        for k, device in enumerate(c_all, 1)
    ]
    x_rows = ContextGather(
        sizes,
        place,
        xown_ref,
        lambda k: xg_ref.at[k],
        lambda k: s_xg.at[k],
        lambda k: r_xg.at[k],
    )
    x_rows.start()
    ow_spread = Spread(sizes, place, post, ow_ref, lambda j, k: og.at[j, c, k])
    ag[e, c, d] = a_ref[c]
    og[e, c, d] = ow_ref[...]
    xg_ref[pl.ds(c, 1)] = xown_ref[...][None]
    for n, ref in enumerate((gate_ref, up_ref, down_ref)):
        size = ref.shape[1]
        ew_own[:, n * size : (n + 1) * size, :] = ref[...].astype(BF16)
    for copy in turned:
        copy.wait_recv()
    a_spread = Spread(sizes, place, post, ag.at[e, :, d], lambda j, k: ag.at[j, :, k])
    size = n_d // n_loc
    group, seat = d // size, lax.rem(d, size)
    mates = [(e, c, group * size + lax.rem(seat + k, size)) for k in range(1, size)]
    keep_w = pltpu.make_async_copy(ew_own.at[group], ew_ref.at[d], l_g.at[2 * n_s])
    keep_w.start()
    w_near = [post.carry(ew_own.at[group], ew_ref.at[d], device) for device in mates]
    w_far = []
    for k in range(1, n_loc):
        to = lax.rem(group + k, n_loc)
        w_far.append(post.carry(ew_own.at[to], ew_ref.at[d], (e, c, to * size + seat)))

    def pass_weights():
        for k, copy in enumerate(w_far, 1):
            copy.wait_recv()
            block = ew_ref.at[lax.rem(group - k + n_loc, n_loc) * size + seat]
            w_near.extend([post.carry(block, block, device) for device in mates])

    ow_spread.onward()
    x_rows.forward()
    ow_spread.arrive()
    ow_rows = ContextGather(
        sizes,
        place,
        og.at[:, c],
        lambda k: og.at[:, k],
        lambda k: s_ow.at[k],
        lambda k: r_ow.at[k],
    )
    ow_rows.start()
    a_spread.onward()
    x_rows.finish()
    a_spread.arrive()

    padded = a_ref.shape[1]
    at_row = lax.broadcasted_iota(jnp.int32, (D // n_e, n_c * n_d * padded), 0)
    at_slab = lax.broadcasted_iota(jnp.int32, (D // n_e, n_c * n_d * padded), 1)
    unpad = jnp.where(
        at_slab == at_row // w_rows * padded + lax.rem(at_row, w_rows), 1.0, 0.0
    ).astype(BF16)
    weights = jnp.concatenate(
        [dot(unpad, ag[k].reshape(n_c * n_d * padded, ag.shape[-1])) for k in range(n_e)], axis=0
    )
    wqkv = weights[:, : 3 * hc].astype(BF16)
    wqkv_ref[...] = wqkv
    w_small = jnp.concatenate(
        [weights[:, 3 * hc : 3 * hc + SMALL], jnp.zeros((D, LANES - SMALL), F32)], axis=1
    )
    wsm_ref[...] = w_small.astype(BF16)
    w_lines = w_small.T
    vec_ref[0:2, :] = w_lines[n_all + 6 : n_all + 8, :]
    vec_ref[2:4, :] = w_lines[n_all + 4 : n_all + 6, :]
    vec_ref[4:8, :] = jnp.zeros((4, D), F32)

    gain_one = vec_ref[0:1, :]
    for b in range(n_c):
        x = xg_ref[b].astype(F32)
        inverse = lax.rsqrt(jnp.mean(x * x, axis=-1, keepdims=True) + EPS)
        a1_ref[b * rows : (b + 1) * rows, :] = (x * inverse * gain_one).astype(BF16)
    a1 = a1_ref[...]
    ow_rows.forward()
    q_t = dot(wqkv[:, :hc], a1, 0, 1).astype(BF16) * jnp.asarray(HEAD_DIM**-0.5, BF16)
    qt_ref[...] = q_t
    kv = dot(a1, wqkv[:, hc:]).astype(BF16)
    for j in range(hp):
        kh_ref[j] = kv[:, j * HEAD_DIM : (j + 1) * HEAD_DIM]
        vh_ref[j] = kv[:, hc + j * HEAD_DIM : hc + (j + 1) * HEAD_DIM]
    vt_scr[...] = dot(wqkv[:, 2 * hc :], a1, 0, 1).astype(BF16)

    documents = drow_ref[...].astype(F32)
    document_of = jnp.broadcast_to(documents, (LANES, length)).T[:, :1]
    turn = 0
    p_copies = {}
    for b in reversed(range(n_c)):
        reach = (b + 1) * rows
        key_place = lax.broadcasted_iota(jnp.int32, (reach, rows), 0)
        q_place = lax.broadcasted_iota(jnp.int32, (reach, rows), 1) + b * rows
        allowed = (document_of[:reach] == documents[:, b * rows : reach]) & (key_place <= q_place)
        bias = jnp.where(allowed, 0.0, -1e30)
        for j in range(hp):
            head = slice(j * HEAD_DIM, (j + 1) * HEAD_DIM)
            scores = dot(kh_ref[j, :reach, :], qt_ref[head, b * rows : reach]) + bias
            top = jnp.max(scores, axis=0, keepdims=True)
            exponent = jnp.exp(scores - top)
            total = jnp.sum(exponent, axis=0, keepdims=True)
            rounded = (exponent * (1.0 / total)).astype(BF16)
            slot = turn % 2
            if turn >= 2:
                p_copies[turn - 2].wait()
            p_scr[slot, :reach, :] = rounded
            copy = pltpu.make_async_copy(
                p_scr.at[slot, pl.ds(0, reach)], p_ref.at[j, b, pl.ds(0, reach)], p_sem.at[slot]
            )
            copy.start()
            p_copies[turn] = copy
            turn += 1
            o_scr[b, head, :] = dot(vt_scr[head, :reach], rounded).astype(BF16)

        @pl.when(c != b)
        def _():
            remote(
                o_scr.at[b], mixed_ref.at[c], s_o.at[b], r_o.at[c], (e, b, d)
            ).start()

    pass_weights()
    for n in range(max(0, turn - 2), turn):
        p_copies[n].wait()
    ow_rows.finish()
    if n_c * hc > D:
        wo_ref[D:, :] = jnp.zeros((n_c * hc - D, D), BF16)
    for k in range(n_e):
        wo_ref[k * (D // n_e) : (k + 1) * (D // n_e), :] = dot(
            unpad, og[k].reshape(n_c * n_d * padded, D)
        ).astype(BF16)
    mixed_ref[pl.ds(c, 1)] = o_scr[pl.ds(c, 1)]
    for b in range(n_c):

        @pl.when(c != b)
        def _():
            copy = remote(o_scr.at[b], mixed_ref.at[b], s_o.at[b], r_o.at[b], (e, b, d))
            copy.wait_send()
            copy.wait_recv()

    mixed = mixed_ref[...].reshape(n_c * hc, rows)
    h = xown_ref[...].astype(F32) + dot(mixed, wo_ref[...], 0, 0)
    h_ref[...] = h
    inverse = lax.rsqrt(jnp.mean(h * h, axis=-1, keepdims=True) + EPS)
    a2 = (h * inverse * vec_ref[1:2, :]).astype(BF16)
    a2_ref[...] = a2
    small = dot(a2, wsm_ref[...]) + tall(prev_ref[...], LANES).T
    small_ref[...] = small
    tables, _, w_pair, _, _ = route_parts(routest_ref[...], small, n_ff, n_all, slots)
    crossing = {}
    gathers = {}
    g = g_ref[...]
    for t in range(2):
        if t == 0:
            block = dot(tables[0] + tables[1], a2).astype(BF16)
        else:
            block = dot(tables[0], (w_pair[0] * g).astype(BF16)) + dot(
                tables[1], (w_pair[1] * g).astype(BF16)
            )
            block = block.astype(BF16)
        for k in range(n_s):
            sbuf[t, k] = block[k * slots : (k + 1) * slots, :]
        for j in reversed(range(1, n_s)):
            n = t * n_s + j
            part, device = there[j]
            copy = remote(sbuf.at[t, part], xin.at[t, me], s_x.at[n], r_x.at[n], device)
            copy.start()
            crossing[t, j] = copy

        def gather(j, own, t=t):
            src = back[j]
            base = (t * n_s + j) * (n_c - 1)
            keep = pltpu.make_async_copy(own, slots_ref.at[c, t, src], l_g.at[t * n_s + j])
            keep.start()
            made = ContextGather(
                sizes,
                place,
                own,
                lambda k: slots_ref.at[k, t, src],
                lambda k: s_g.at[base + k],
                lambda k: r_g.at[base + k],
            )
            made.start()
            gathers[t, j] = (made, keep)

        gather(0, sbuf.at[t, me])
        crossing[t, 0] = gather
    for t in range(2):
        for j in range(1, n_s):
            crossing[t, j].wait_recv()
            crossing[t, 0](j, xin.at[t, back[j]])
    for made, _ in gathers.values():
        made.forward()
    for made, keep in gathers.values():
        made.finish()
        keep.wait()
    for t in range(2):
        for j in range(1, n_s):
            crossing[t, j].wait_send()
    for copy in w_near:
        copy.wait_recv()
    keep_w.wait()
    post.finish()


def front(sizes, cfg, *operands):
    n_e, n_c, n_d = sizes
    hp, n_ff, n_all, n_loc, slots = cfg
    hc = hp * HEAD_DIM
    rows = operands[8].shape[0]
    length = rows * n_c
    padded = up_to(operands[0].shape[0], 16)
    width = up_to(3 * hc + SMALL, LANES)
    part = operands[9].shape[1]
    posts = (n_c - 1) + 2 * spread_count(sizes) + n_d - 1
    n_s = n_e * n_loc
    dma = pltpu.SemaphoreType.DMA
    vmem = pl.BlockSpec(memory_space=pltpu.VMEM)
    anywhere = pl.BlockSpec(memory_space=pl.ANY)
    shape = jax.ShapeDtypeStruct
    gathers = 2 * n_s * (n_c - 1)
    return pl.pallas_call(
        functools.partial(front_kernel, sizes, cfg),
        out_shape=(
            shape((n_c, rows, D), BF16),
            shape((D, 3 * hc), BF16),
            shape((n_c * hc, D), BF16),
            shape((D, LANES), BF16),
            shape((8, D), F32),
            shape((length, D), BF16),
            shape((hc, length), BF16),
            shape((hp, length, HEAD_DIM), BF16),
            shape((hp, length, HEAD_DIM), BF16),
            shape((n_c, hc, rows), BF16),
            shape((rows, D), F32),
            shape((rows, D), BF16),
            shape((rows, LANES), F32),
            shape((hp, n_c, length, rows), BF16),
            shape((n_c, 2, n_s, slots, D), BF16),
            shape((n_d, 3 * part, LANES), BF16),
        ),
        in_specs=[vmem] * len(operands),
        out_specs=(vmem,) * 13 + (anywhere,) * 3,
        scratch_shapes=[
            pltpu.VMEM((LANES, LANES), F32),
            pltpu.VMEM((n_c, padded, width), BF16),
            pltpu.VMEM((padded, D), BF16),
            pltpu.VMEM((n_e, n_c, n_d, padded, width), BF16),
            pltpu.VMEM((n_e, n_c, n_d, padded, D), BF16),
            pltpu.VMEM((n_loc, 3 * part, LANES), BF16),
            pltpu.VMEM((n_c, hc, rows), BF16),
            pltpu.VMEM((hc, length), BF16),
            pltpu.VMEM((2, length, rows), BF16),
            pltpu.VMEM((2, n_s, slots, D), BF16),
            pltpu.VMEM((2, n_s, slots, D), BF16),
            dma((2,)),
            dma((n_c,)),
            dma((n_c,)),
            dma((2 * n_s,)),
            dma((2 * n_s,)),
            dma((gathers,)),
            dma((gathers,)),
            dma((2 * n_s + 1,)),
            dma((posts,)),
            dma((posts,)),
            *[dma((n_c - 1,))] * 4,
        ],
        compiler_params=pltpu.CompilerParams(
            collective_id=0, has_side_effects=True, vmem_limit_bytes=VMEM_LIMIT
        ),
        name="front",
    )(*operands)


def expert_kernel(x_ref, dy_ref, w_ref, out_ref, gw_ref, total):
    step = pl.program_id(0)
    parts = w_ref.shape[0]
    x = x_ref[...].reshape(-1, D)
    dy = dy_ref[...].reshape(-1, D)
    block = out_ref.shape[0:1] + out_ref.shape[2:]
    gate, up, down = [
        jnp.concatenate([w_ref[k, n] for k in range(parts)], axis=1) for n in range(3)
    ]
    gate_pre = dot(x, gate)
    up_pre = dot(x, up)
    sig = jax.nn.sigmoid(gate_pre)
    hidden = (gate_pre * sig * up_pre).astype(BF16)
    result = dot(hidden, down, 1, 1).astype(BF16)
    out_ref[:, 0] = result.reshape(block)
    d_hidden = dot(dy, down)
    d_gate = (d_hidden * up_pre * sig * (1.0 + gate_pre * (1.0 - sig))).astype(BF16)
    d_up = (d_hidden * gate_pre * sig).astype(BF16)
    d_x = dot(d_gate, gate, 1, 1) + dot(d_up, up, 1, 1)
    out_ref[:, 1] = d_x.astype(BF16).reshape(block)
    grads = (dot(x, d_gate, 0, 0), dot(x, d_up, 0, 0), dot(dy, hidden, 0, 0))

    @pl.when(step == 0)
    def _():
        for n in range(3):
            total[n] = grads[n]

    @pl.when(step > 0)
    def _():
        for n in range(3):
            total[n] += grads[n]

    @pl.when(step == pl.num_programs(0) - 1)
    def _():
        width = gate.shape[1] // parts
        for n in range(3):
            for k in range(parts):
                gw_ref[k, n] = total[n, :, k * width : (k + 1) * width].astype(BF16)


def experts_pass(gathered, weights):
    n_c, _, n_s, slots, _ = gathered.shape
    parts, _, _, units = weights.shape
    take = max(1, min(n_c, 512 // (n_s * slots)))
    return pl.pallas_call(
        expert_kernel,
        grid=(n_c // take,),
        out_shape=(
            jax.ShapeDtypeStruct(gathered.shape, BF16),
            jax.ShapeDtypeStruct(weights.shape, BF16),
        ),
        in_specs=[
            pl.BlockSpec((take, 1, n_s, slots, D), lambda i: (i, 0, 0, 0, 0)),
            pl.BlockSpec((take, 1, n_s, slots, D), lambda i: (i, 1, 0, 0, 0)),
            pl.BlockSpec((parts, 3, D, units), lambda i: (0, 0, 0, 0)),
        ],
        out_specs=(
            pl.BlockSpec((take, 2, n_s, slots, D), lambda i: (i, 0, 0, 0, 0)),
            pl.BlockSpec((parts, 3, D, units), lambda i: (0, 0, 0, 0)),
        ),
        scratch_shapes=[pltpu.VMEM((3, D, parts * units), F32)],
        compiler_params=pltpu.CompilerParams(
            dimension_semantics=("arbitrary",), vmem_limit_bytes=VMEM_LIMIT
        ),
        name="experts_pass",
    )(gathered, gathered, weights)


def back_kernel(
    sizes,
    cfg,
    res_ref,
    h_ref,
    a2_ref,
    small_ref,
    g_ref,
    routest_ref,
    wo_ref,
    wqkv_ref,
    wsm_ref,
    vec_ref,
    mixed_ref,
    a1_ref,
    qt_ref,
    kh_ref,
    vh_ref,
    p_ref,
    xg_ref,
    gw_ref,
    block_ref,
    dx_ref,
    dprev_ref,
    gq_ref,
    gk_ref,
    gv_ref,
    go_ref,
    grouter_ref,
    gcoef_ref,
    gvalue_ref,
    ggains_ref,
    egate_ref,
    eup_ref,
    edown_ref,
    inn,
    osum,
    outr,
    back,
    xsum,
    stage,
    dhg,
    dht_scr,
    p_scr,
    dk_acc,
    dv_acc,
    dqt,
    dqkv,
    da_in,
    da_sum,
    da_out,
    x_scr,
    ew_own,
    ew_in,
    ew_mid,
    ew_out,
    t_send,
    t_recv,
    t_z,
    t_zr,
    t_c,
    t_cr,
    o_own,
    o_in,
    o_sum,
    o_out,
    o_x,
    o_xr,
    o_z,
    o_zr,
    l_sem,
    s_in,
    r_in,
    s_out,
    r_out,
    s_x,
    r_x,
    s_g,
    r_g,
    p_sem,
    s_d,
    r_d,
    s_w,
    r_w,
    s_t,
    r_t,
    s_q,
    r_q,
):
    n_e, n_c, n_d = sizes
    hp, n_ff, n_all, n_loc, slots = cfg
    hc = hp * HEAD_DIM
    place = e, c, d = position()
    pairs = n_c // 2
    outer, inner = c // 2, c % 2
    rows = h_ref.shape[0]
    w_rows = go_ref.shape[0]
    shift = 3 * hc % LANES
    chunks = up_to(3 * hc + SMALL, LANES) // LANES
    d_peers = [(e, c, lax.rem(d + k, n_d)) for k in range(1, n_d)]
    length = rows * n_c
    peers = context_peers(sizes, place)
    e_peers = expert_peers(sizes, place)

    in_vmem = len(stage.shape) == 5
    if in_vmem:
        take = pltpu.make_async_copy(res_ref.at[:, inner], stage, l_sem.at[0])
        take.start()
    bring = pltpu.make_async_copy(gw_ref, ew_own, l_sem.at[1])
    bring.start()

    def fetch_x(b, slot):
        return pltpu.make_async_copy(xg_ref.at[b], x_scr.at[slot], l_sem.at[2 + slot])

    fetch_x(c, 2).start()
    fetch_x(0, 0).start()
    n_s = n_e * n_loc
    me, there_s, _ = homes(sizes, n_loc, place)
    greet(peers + e_peers + d_peers + crossing_only(sizes, n_loc, place))

    size = n_d // n_loc
    group, seat = d // size, lax.rem(d, size)
    mates = [(e, c, group * size + lax.rem(seat + k, size)) for k in range(1, size)]
    others = [lax.rem(group + k, n_loc) for k in range(1, n_loc)]
    freight = Courier(s_w, r_w)
    e_near = {}
    e_far = []

    def expert_start():
        for k, mate in enumerate(mates):
            for r, other in enumerate(others):
                e_near[k, r] = freight.carry(
                    ew_own.at[other * size + lax.rem(seat + k + 1, size)], ew_mid.at[k, r], mate
                )
            e_near[k, -1] = freight.carry(ew_own.at[mate[2]], ew_in.at[k], mate)

    def expert_cross():
        for r, other in enumerate(others):
            target = other * size + seat
            for k in range(size - 1):
                e_near[k, r].wait_recv()

            def one(n, carry):
                at = pl.ds(pl.multiple_of(n * tile, tile), tile)
                total = ew_own[target, at, :].astype(F32)
                for k in range(size - 1):
                    total = total + ew_mid[k, r, at, :].astype(F32)
                ew_out[r, at, :] = total.astype(BF16)
                return carry

            tile = ew_own.shape[1] // 9
            lax.fori_loop(0, 9, one, 0)
            e_far.append(freight.carry(ew_out.at[r], ew_in.at[size - 1 + r], (e, c, target)))

    def expert_end():
        for k in range(size - 1):
            e_near[k, -1].wait_recv()
        for copy in e_far:
            copy.wait_recv()
        part = ew_own.shape[1] // 3
        for n, ref in enumerate((egate_ref, eup_ref, edown_ref)):
            at = slice(n * part, (n + 1) * part)
            total = ew_own[d, at, :].astype(F32)
            for k in range(size - 1):
                total = total + ew_in[k, at, :].astype(F32)
            ref[pl.ds(group, 1)] = total[None]
            for r in range(n_loc - 1):
                ref[pl.ds(lax.rem(group - r - 1 + n_loc, n_loc), 1)] = ew_in[
                    size - 1 + r, at, :
                ].astype(F32)[None]
        freight.finish()

    bring.wait()
    expert_start()

    def load(ref, slot=0):
        if in_vmem:
            return ref[...].astype(F32)
        copy = pltpu.make_async_copy(ref, stage.at[slot], l_sem.at[0])
        copy.start()
        copy.wait()
        return stage[slot].astype(F32)

    def own_part(there, t, src):
        if in_vmem:
            return stage[there, t, src].astype(F32)
        return load(res_ref.at[there, inner, t, src])

    def store(ref, value):
        if in_vmem:
            ref[...] = value
        else:
            stage[3] = value
            copy = pltpu.make_async_copy(stage.at[3], ref, l_sem.at[0])
            copy.start()
            copy.wait()

    pieces = [(t, j) for j in [*reversed(range(1, n_s)), 0] for t in range(2)]
    first_copies = {}
    for t, j in pieces:
        src = there_s[j][0]
        for k in [*range(1, pairs), 0]:
            n = (t * n_s + j) * pairs + k
            there = lax.rem(outer + k, pairs)
            copy = remote(
                res_ref.at[there, 1 - inner, t, src],
                inn.at[there, t, src],
                s_in.at[n],
                r_in.at[n],
                peers[0],
            )
            copy.start()
            first_copies[t, j, k] = copy
    if in_vmem:
        take.wait()
    second = {}
    for t, j in pieces:
        src = there_s[j][0]
        for k in range(1, pairs):
            n = (t * n_s + j) * pairs + k
            there = lax.rem(outer + k, pairs)
            first_copies[t, j, k].wait_recv()
            total = own_part(there, t, src) + load(inn.at[there, t, src], 1)
            store(osum.at[k - 1, t, src], total.astype(BF16))
            copy = remote(
                osum.at[k - 1, t, src], outr.at[k - 1, t, src], s_out.at[n], r_out.at[n], peers[k]
            )
            copy.start()
            second[t, j, k] = copy
    home = {}
    for t, j in pieces:
        src = there_s[j][0]
        first_copies[t, j, 0].wait_recv()
        total = own_part(outer, t, src) + load(inn.at[outer, t, src], 1)
        for k in range(1, pairs):
            second[t, j, k].wait_recv()
            total = total + load(outr.at[k - 1, t, src], 2)
        if j == 0:
            back[t, me] = total.astype(BF16)
        else:
            xsum[t, src] = total.astype(BF16)
            n = t * n_s + j
            copy = remote(
                xsum.at[t, src], back.at[t, me], s_x.at[n], r_x.at[n], there_s[j][1]
            )
            copy.start()
            home[t, j] = copy

    expert_cross()
    h = h_ref[...]
    a2 = a2_ref[...].astype(F32)
    g = g_ref[...]
    small = small_ref[...]
    value_one, value_two = vec_ref[2:3, :], vec_ref[3:4, :]
    tables, picks, w_pair, first, other = route_parts(
        routest_ref[...], small, n_ff, n_all, slots
    )
    copy_on, one_on, two_on = [
        [picks[k][:, n_ff + n : n_ff + n + 1] for k in range(2)] for n in (1, 2, 3)
    ]
    g_a2 = jnp.sum(g * a2, axis=1, keepdims=True)
    g_one = jnp.sum(g * value_one, axis=1, keepdims=True)
    g_two = jnp.sum(g * value_two, axis=1, keepdims=True)
    alpha = [copy_on[k] + one_on[k] * first[0] + two_on[k] * other[0] for k in range(2)]
    a_weight = alpha[0] * w_pair[0] + alpha[1] * w_pair[1]
    one_weight = one_on[0] * w_pair[0] + one_on[1] * w_pair[1]
    two_weight = two_on[0] * w_pair[0] + two_on[1] * w_pair[1]
    for copy in home.values():
        copy.wait_recv()
    returned = [back[t].reshape(n_ff * slots, D) for t in range(2)]
    block = h
    d_weight = []
    for k in range(2):
        routed = dot(tables[k], returned[0], 0, 0)
        picked = (
            routed
            + alpha[k] * a2
            + (one_on[k] * first[1]) * value_one
            + (two_on[k] * other[1]) * value_two
        )
        block = block + w_pair[k] * picked
        d_weight.append(jnp.sum(g * picked, axis=1, keepdims=True))
    block_ref[...] = block
    center = w_pair[0] * d_weight[0] + w_pair[1] * d_weight[1]
    d_logits = (
        picks[0] * (w_pair[0] * (d_weight[0] - center))
        + picks[1] * (w_pair[1] * (d_weight[1] - center))
    )
    dprev_ref[...] = d_logits.T[:n_all, :]
    lane = lax.broadcasted_iota(jnp.int32, (rows, LANES), 1)
    d_small = d_logits
    for base, pair, weight, g_value in (
        (n_all, first, one_weight, g_one),
        (n_all + 2, other, two_weight, g_two),
    ):
        d_pair = (weight * g_a2, weight * g_value)
        middle = pair[0] * d_pair[0] + pair[1] * d_pair[1]
        for k in range(2):
            d_small = d_small + jnp.where(lane == base + k, pair[k] * (d_pair[k] - middle), 0.0)
    d_small = d_small.astype(BF16)
    d_const_one = jnp.sum((first[1] * one_weight) * g, axis=0, keepdims=True)
    d_const_two = jnp.sum((other[1] * two_weight) * g, axis=0, keepdims=True)
    d_a2 = (
        dot(tables[0] + tables[1], returned[1], 0, 0)
        + a_weight * g
        + dot(d_small, wsm_ref[...], 1, 1)
    )
    gain_two = vec_ref[1:2, :]
    inverse_two = lax.rsqrt(jnp.mean(h * h, axis=-1, keepdims=True) + EPS)
    d_gain_two = jnp.sum(d_a2 * h * inverse_two, axis=0, keepdims=True)
    scaled = gain_two * d_a2
    d_h = (
        g
        + inverse_two * scaled
        - h * inverse_two**3 * jnp.mean(scaled * h, axis=-1, keepdims=True)
    )
    d_hb = d_h.astype(BF16)
    dhg[pl.ds(c, 1)] = d_hb[None]
    gather = ContextGather(
        sizes,
        place,
        dhg.at[c],
        lambda k: dhg.at[k],
        lambda k: s_g.at[k],
        lambda k: r_g.at[k],
    )
    gather.start()
    dx_ref[...] = d_h
    g_o = dot(mixed_ref[...].reshape(n_c * hc, rows), d_hb)
    run = n_d * w_rows
    for b in range(n_c):
        for k in range(n_e):
            o_own[b, k, :run, :] = g_o[(k * n_c + b) * run : (k * n_c + b + 1) * run].astype(BF16)
    parcel = Courier(s_q, r_q)
    o_pair = {}
    for k in [*range(1, pairs), 0]:
        there = lax.rem(outer + k, pairs)
        o_pair[k] = parcel.carry(
            o_own.at[there * 2 + 1 - inner], o_in.at[there], peers[0]
        )
    o_state = {}

    def o_outer():
        o_state["outer"] = []
        for k in range(1, pairs):
            there = lax.rem(outer + k, pairs)
            o_pair[k].wait_recv()
            o_sum[k - 1] = (
                o_own[there * 2 + inner].astype(F32) + o_in[there].astype(F32)
            ).astype(BF16)
            o_state["outer"].append(
                parcel.carry(o_sum.at[k - 1], o_out.at[k - 1], peers[k])
            )

    def o_across():
        o_pair[0].wait_recv()
        total = o_own[c].astype(F32) + o_in[outer].astype(F32)
        for k, copy in enumerate(o_state["outer"]):
            copy.wait_recv()
            total = total + o_out[k].astype(F32)
        o_x[...] = total.astype(BF16)
        o_state["across"] = [
            parcel.carry(o_x.at[lax.rem(e + j, n_e)], o_xr.at[j - 1], e_peers[j - 1])
            for j in range(1, n_e)
        ]

    def o_along():
        total = o_x[e].astype(F32)
        for j, copy in enumerate(o_state["across"]):
            copy.wait_recv()
            total = total + o_xr[j].astype(F32)
        for k in range(n_d):
            o_z[k, :w_rows, :] = total[k * w_rows : (k + 1) * w_rows].astype(BF16)
        o_state["along"] = [
            parcel.carry(o_z.at[lax.rem(d + k, n_d)], o_zr.at[k - 1], d_peers[k - 1])
            for k in range(1, n_d)
        ]

    def o_end():
        total = o_z[d].astype(F32)
        for k, copy in enumerate(o_state["along"]):
            copy.wait_recv()
            total = total + o_zr[k].astype(F32)
        go_ref[...] = total[:w_rows]
        parcel.finish()

    if shift:
        d_small = jnp.concatenate(
            [jnp.zeros((rows, shift), BF16), d_small[:, : LANES - shift]], axis=1
        )
    g_small = dot(a2_ref[...], d_small, 0, 0)
    dk_acc[...] = jnp.zeros_like(dk_acc)
    dv_acc[...] = jnp.zeros_like(dv_acc)
    order = [(b, j) for b in reversed(range(n_c)) for j in range(hp)]

    def fetch(n):
        b, j = order[n]
        reach = pl.ds(0, (b + 1) * rows)
        return pltpu.make_async_copy(p_ref.at[j, b, reach], p_scr.at[n % 2, reach], p_sem.at[n % 2])

    fetch(0).start()
    gather.forward()
    gather.finish()
    o_outer()
    wo_part = wo_ref[pl.ds(pl.multiple_of(c * hc, hc), hc), :]
    for b in range(n_c):
        dht_scr[:, b * rows : (b + 1) * rows] = dot(wo_part, dhg[b], 1, 1).astype(BF16)
    for n, (b, j) in enumerate(order):
        reach = (b + 1) * rows
        head = slice(j * HEAD_DIM, (j + 1) * HEAD_DIM)
        mine_q = slice(b * rows, reach)
        if n == len(order) // 4:
            o_across()
        if n == len(order) // 2:
            o_along()
        if n + 1 < len(order):
            fetch(n + 1).start()
        fetch(n).wait()
        rounded = p_scr[n % 2, :reach, :]
        prob = rounded.astype(F32)
        d_o = dht_scr[head, mine_q]
        d_prob = dot(vh_ref[j, :reach, :], d_o)
        delta = jnp.sum(prob * d_prob, axis=0, keepdims=True)
        d_scores = (prob * (d_prob - delta)).astype(BF16)
        dqt[head, mine_q] = dot(kh_ref[j, :reach, :], d_scores, 0, 0) * HEAD_DIM**-0.5
        dk_acc[j, :reach, :] += dot(d_scores, qt_ref[head, mine_q], 1, 1)
        dv_acc[j, :reach, :] += dot(rounded, d_o, 1, 1)
    dqkv[:, :hc] = dqt[...].T.astype(BF16)
    for j in range(hp):
        at = j * HEAD_DIM
        dqkv[:, hc + at : hc + at + HEAD_DIM] = dk_acc[j].astype(BF16)
        dqkv[:, 2 * hc + at : 2 * hc + at + HEAD_DIM] = dv_acc[j].astype(BF16)
    dqkv[:, 3 * hc :] = jnp.zeros((length, dqkv.shape[1] - 3 * hc), BF16)
    d_all = dqkv[...]
    bag = Courier(s_t, r_t)
    across = {}
    g_all = dot(a1_ref[...], d_all, 0, 0)
    half = D // n_e

    def send_chunk(k, value):
        for n in range(n_e):
            t_send[k, n] = value[n * half : (n + 1) * half].astype(BF16)
        across[k] = [
            bag.carry(t_send.at[k, lax.rem(e + j, n_e)], t_recv.at[k, j - 1], e_peers[j - 1])
            for j in range(1, n_e)
        ]

    for k in range(chunks - 1):
        send_chunk(k, g_all[:, k * LANES : (k + 1) * LANES])
    wqkv = wqkv_ref[...]
    gain_one = vec_ref[0:1, :]
    d_gain_one = jnp.zeros((1, D), F32)
    for b in range(n_c):
        part = dot(d_all[b * rows : (b + 1) * rows, : 3 * hc], wqkv, 1, 1)
        dhg[b] = part.astype(BF16)
        if b + 1 < n_c:
            fetch_x(b + 1, (b + 1) % 2).start()
        fetch_x(b, b % 2).wait()
        x = x_scr[b % 2].astype(F32)
        inverse = lax.rsqrt(jnp.mean(x * x, axis=-1, keepdims=True) + EPS)
        d_gain_one = d_gain_one + jnp.sum(part * x * inverse, axis=0, keepdims=True)
    to_pair = []
    for k in [*range(1, pairs), 0]:
        there = lax.rem(outer + k, pairs)
        copy = remote(
            dhg.at[there * 2 + 1 - inner], da_in.at[there], s_d.at[k], r_d.at[k], peers[0]
        )
        copy.start()
        to_pair.append((k, copy))
    spot = lax.broadcasted_iota(jnp.int32, (LANES, D), 0)
    lines = jnp.zeros((LANES, D), F32)
    for n, row in enumerate((d_const_one, d_const_two, d_gain_one, d_gain_two)):
        lines = lines + jnp.where(spot == shift + n_all + 4 + n, row, 0.0)
    send_chunk(chunks - 1, g_all[:, (chunks - 1) * LANES :] + g_small + lines.T)
    along = []
    for k, copy in to_pair:
        if k == 0:
            continue
        there = lax.rem(outer + k, pairs)
        copy.wait_recv()
        da_sum[k - 1] = (
            dhg[there * 2 + inner].astype(F32) + da_in[there].astype(F32)
        ).astype(BF16)
        onward = remote(
            da_sum.at[k - 1],
            da_out.at[k - 1],
            s_d.at[pairs + k - 1],
            r_d.at[pairs + k - 1],
            peers[k],
        )
        onward.start()
        along.append(onward)
    down = {}
    for k in range(chunks):
        total = t_send[k, e].astype(F32)
        for j, copy in enumerate(across[k]):
            copy.wait_recv()
            total = total + t_recv[k, j].astype(F32)
        for n in range(n_d):
            t_z[k, n, : n_c * w_rows, :] = jnp.concatenate(
                [
                    total[(b * n_d + n) * w_rows : (b * n_d + n + 1) * w_rows]
                    for b in range(n_c)
                ],
                axis=0,
            ).astype(BF16)
        down[k] = [
            bag.carry(t_z.at[k, lax.rem(d + n, n_d)], t_zr.at[k, n - 1], d_peers[n - 1])
            for n in range(1, n_d)
        ]
    o_end()
    to_pair[-1][1].wait_recv()
    d_a1 = dhg[c].astype(F32) + da_in[outer].astype(F32)
    for k, copy in enumerate(along):
        copy.wait_recv()
        d_a1 = d_a1 + da_out[k].astype(F32)
    fetch_x(c, 2).wait()
    x = x_scr[2].astype(F32)
    inverse_one = lax.rsqrt(jnp.mean(x * x, axis=-1, keepdims=True) + EPS)
    scaled = gain_one * d_a1
    dx_ref[...] += inverse_one * scaled - x * inverse_one**3 * jnp.mean(
        scaled * x, axis=-1, keepdims=True
    )
    for k in range(chunks):
        total = t_z[k, d].astype(F32)
        for n, copy in enumerate(down[k]):
            copy.wait_recv()
            total = total + t_zr[k, n].astype(F32)
        for b in range(n_c):
            t_c[b, k, :w_rows, :] = total[b * w_rows : (b + 1) * w_rows]
    t_cr[pl.ds(c, 1)] = t_c[pl.ds(c, 1)]
    turned = [
        bag.carry(t_c.at[lax.rem(c + k, n_c)], t_cr.at[c], (e, lax.rem(c + k, n_c), d))
        for k in range(1, n_c)
    ]
    expert_end()
    for copy in turned:
        copy.wait_recv()
    s_total = jnp.zeros((w_rows, SMALL), F32)
    for b in range(n_c):
        line = jnp.concatenate([t_cr[b, k] for k in range(chunks)], axis=1)[:w_rows]
        for n, ref in enumerate((gq_ref, gk_ref, gv_ref)):
            width = min(hc, D - b * hc)
            if width > 0:
                ref[:, b * hc : b * hc + width] = line[:, n * hc : n * hc + width]
        s_total = s_total + line[:, 3 * hc : 3 * hc + SMALL]
    s_lines = jnp.concatenate([s_total, jnp.zeros((w_rows, LANES - SMALL), F32)], axis=1)
    s_lines = tall(s_lines, LANES).T
    at = 0
    for ref in (grouter_ref, gcoef_ref, gvalue_ref, ggains_ref):
        ref[...] = s_lines[at : at + ref.shape[0], :w_rows]
        at += ref.shape[0]
    bag.finish()
    for copy in first_copies.values():
        copy.wait_send()
    for copy in second.values():
        copy.wait_send()
    for copy in home.values():
        copy.wait_send()
    for _, copy in to_pair:
        copy.wait_send()
    for copy in along:
        copy.wait_send()


def backward(sizes, cfg, *operands):
    n_e, n_c, n_d = sizes
    hp, n_ff, n_all, n_loc, slots = cfg
    hc = hp * HEAD_DIM
    rows = operands[1].shape[0]
    length = rows * n_c
    pairs = n_c // 2
    per = slots
    dma = pltpu.SemaphoreType.DMA
    vmem = pl.BlockSpec(memory_space=pltpu.VMEM)
    anywhere = pl.BlockSpec(memory_space=pl.ANY)
    shape = jax.ShapeDtypeStruct
    n_s = n_e * n_loc
    n_in = 2 * n_s * pairs
    part = operands[17].shape[1]
    w_rows = D // (n_e * n_c * n_d)
    chunks = up_to(3 * hc + SMALL, LANES) // LANES
    run = up_to(n_d * w_rows, 16)
    turn = up_to(n_c * w_rows, 16)
    few = up_to(w_rows, 16)
    few_wide = up_to(w_rows, 8)
    size = n_d // n_loc
    loads = (size - 1) * n_loc + n_loc - 1
    bags = chunks * (n_e - 1 + n_d - 1) + n_c - 1
    parcels = 2 * pairs - 1 + n_e - 1 + n_d - 1
    n_more = max(1, pairs - 1)
    in_specs = [vmem] * len(operands)
    in_specs[0] = anywhere
    in_specs[15] = in_specs[16] = in_specs[17] = anywhere
    arriving = [(pairs, 2, n_s, per, D), (n_more, 2, n_s, per, D), (n_more, 2, n_s, per, D)]
    roomy = 2 * pairs * n_s * per * D <= 2**21
    held = [pltpu.VMEM(dims, BF16) for dims in arriving] if roomy else []
    extra = [] if roomy else [shape(dims, BF16) for dims in arriving]
    stage = pltpu.VMEM(arriving[0] if roomy else (4, per, D), BF16)
    return pl.pallas_call(
        functools.partial(back_kernel, sizes, cfg),
        out_shape=(
            shape((rows, D), F32),
            shape((rows, D), F32),
            shape((n_all, rows), F32),
            *[shape((w_rows, D), F32)] * 4,
            *[shape((n, w_rows), F32) for n in (n_all, 4, 2, 2)],
            *[shape((n_loc, part // 3, LANES), F32)] * 3,
            *extra,
        ),
        in_specs=in_specs,
        out_specs=(vmem,) * 14 + (anywhere,) * len(extra),
        scratch_shapes=[
            *held,
            pltpu.VMEM((2, n_s, per, D), BF16),
            pltpu.VMEM((2, n_s, per, D), BF16),
            stage,
            pltpu.VMEM((n_c, rows, D), BF16),
            pltpu.VMEM((hc, length), BF16),
            pltpu.VMEM((2, length, rows), BF16),
            pltpu.VMEM((hp, length, HEAD_DIM), F32),
            pltpu.VMEM((hp, length, HEAD_DIM), F32),
            pltpu.VMEM((hc, length), F32),
            pltpu.VMEM((length, chunks * LANES), BF16),
            pltpu.VMEM((pairs, rows, D), BF16),
            pltpu.VMEM((n_more, rows, D), BF16),
            pltpu.VMEM((n_more, rows, D), BF16),
            pltpu.VMEM((3, rows, D), BF16),
            pltpu.VMEM((n_d, part, LANES), BF16),
            pltpu.VMEM((size + n_loc - 2, part, LANES), BF16),
            pltpu.VMEM((max(1, size - 1), max(1, n_loc - 1), part, LANES), BF16),
            pltpu.VMEM((max(1, n_loc - 1), part, LANES), BF16),
            pltpu.VMEM((chunks, n_e, D // n_e, LANES), BF16),
            pltpu.VMEM((chunks, n_e - 1, D // n_e, LANES), BF16),
            pltpu.VMEM((chunks, n_d, turn, LANES), BF16),
            pltpu.VMEM((chunks, n_d - 1, turn, LANES), BF16),
            pltpu.VMEM((n_c, chunks, few_wide, LANES), F32),
            pltpu.VMEM((n_c, chunks, few_wide, LANES), F32),
            pltpu.VMEM((n_c, n_e, run, D), BF16),
            pltpu.VMEM((pairs, n_e, run, D), BF16),
            pltpu.VMEM((n_more, n_e, run, D), BF16),
            pltpu.VMEM((n_more, n_e, run, D), BF16),
            pltpu.VMEM((n_e, run, D), BF16),
            pltpu.VMEM((n_e - 1, run, D), BF16),
            pltpu.VMEM((n_d, few, D), BF16),
            pltpu.VMEM((n_d - 1, few, D), BF16),
            dma((5,)),
            dma((n_in,)),
            dma((n_in,)),
            dma((n_in,)),
            dma((n_in,)),
            dma((2 * n_s,)),
            dma((2 * n_s,)),
            dma((n_c - 1,)),
            dma((n_c - 1,)),
            dma((2,)),
            dma((n_c,)),
            dma((n_c,)),
            dma((loads,)),
            dma((loads,)),
            dma((bags,)),
            dma((bags,)),
            dma((parcels,)),
            dma((parcels,)),
        ],
        compiler_params=pltpu.CompilerParams(
            collective_id=1, has_side_effects=True, vmem_limit_bytes=VMEM_LIMIT
        ),
        name="backward",
    )(*operands)[:14]


def hand_out_kernel(*refs):
    count = (len(refs) - 2) // 3
    sources, results, held = refs[:count], refs[count : 2 * count], refs[2 * count : 3 * count]
    in_sems, out_sems = refs[-2:]
    takes = [pltpu.make_async_copy(sources[n], held[n], in_sems.at[n]) for n in range(count)]
    gives = [pltpu.make_async_copy(held[n], results[n], out_sems.at[n]) for n in range(count)]
    for copy in takes:
        copy.start()
    for take, give in zip(takes, gives):
        take.wait()
        give.start()
    for copy in gives:
        copy.wait()


def hand_out(results):
    anywhere = pl.BlockSpec(memory_space=pl.ANY)
    dma = pltpu.SemaphoreType.DMA((len(results),))
    return pl.pallas_call(
        hand_out_kernel,
        out_shape=tuple(jax.ShapeDtypeStruct(r.shape, r.dtype) for r in results),
        in_specs=[anywhere] * len(results),
        out_specs=(anywhere,) * len(results),
        scratch_shapes=[*[pltpu.VMEM(r.shape, r.dtype) for r in results], dma, dma],
        compiler_params=pltpu.CompilerParams(vmem_limit_bytes=VMEM_LIMIT),
        name="hand_out",
    )(*results)


def body(
    tokens,
    doc_ids,
    routes,
    prev_logits,
    cotangent,
    w_query,
    w_key,
    w_value,
    w_out,
    w_router,
    const_coef,
    const_value,
    norm_gains,
    expert_gate,
    expert_up,
    expert_down,
):
    sizes = n_e, n_c, n_d = tuple(lax.axis_size(axis) for axis in ALL_AXES)
    rows = tokens.shape[1]
    length = doc_ids.shape[1]
    n_loc, _, units = expert_gate.shape
    n_ff = n_loc * n_e
    n_all = w_router.shape[1]
    slots = rows // 4
    hp = -(-HEADS // n_c)
    cfg = (hp, n_ff, n_all, n_loc, slots)
    routes_t = routes[0].T
    upstream = cotangent[0]
    (
        x_all,
        wqkv,
        wo,
        wsm,
        vec,
        a1,
        q_t,
        k_h,
        v_h,
        mixed,
        h,
        a2,
        small,
        probs,
        gathered,
        gathered_w,
    ) = front(
        sizes,
        cfg,
        w_query,
        w_key,
        w_value,
        w_out,
        w_router.T,
        const_coef.T,
        const_value.T,
        norm_gains.T,
        tokens[0],
        *[
            w.reshape(n_loc, D * units // LANES, LANES)
            for w in (expert_gate, expert_up, expert_down)
        ],
        doc_ids,
        routes_t,
        prev_logits[0].T,
        upstream,
    )
    gathered_w = gathered_w.reshape(n_d, 3, D, units)
    if units % LANES:
        flat = gathered_w.transpose(1, 2, 0, 3).reshape(1, 3, D, n_d * units)
    else:
        flat = gathered_w
    results, grads = experts_pass(gathered, flat)
    if units % LANES:
        grads = grads.reshape(3, D, n_d, units).transpose(2, 0, 1, 3)
    results = backward(
        sizes,
        cfg,
        results.reshape(n_c // 2, 2, 2, n_e * n_loc, slots, D),
        h,
        a2,
        small,
        upstream,
        routes_t,
        wo,
        wqkv,
        wsm,
        vec,
        mixed,
        a1,
        q_t,
        k_h,
        v_h,
        probs,
        x_all,
        grads.reshape(n_d, 3 * D * units // LANES, LANES),
    )
    block_rows, d_x, d_prev, *square = hand_out(results)
    narrow = square[4:8]
    return (
        block_rows[None],
        d_x[None],
        d_prev.T[None],
        *square[:4],
        *[grad.T for grad in narrow],
        *[grad.reshape(n_loc, D, units) for grad in square[8:]],
    )


def solution(mesh):
    rows = P(("expert", "dp"), "context", None)
    weights = P(ALL_AXES, None)
    units = P("expert", None, ("context", "dp"))
    return jax.shard_map(
        body,
        mesh=mesh,
        in_specs=(rows, P(("expert", "dp"), None), rows, rows, rows)
        + (weights,) * 8
        + (units,) * 3,
        out_specs=(rows,) * 3 + (weights,) * 8 + (units,) * 3,
        check_vma=False,
    )
```

```python
import functools

import jax
import jax.numpy as jnp
from jax import lax
from jax.experimental import pallas as pl
from jax.experimental.pallas import tpu as pltpu
from jax.sharding import PartitionSpec as P

D = 768
HEADS = 12
HEAD_DIM = 64
EPS = 1e-06
SMALL = 64
LANES = 128
VMEM_LIMIT = 63 * 2**20
MESH = pl.DeviceIdType.MESH
F32 = jnp.float32
BF16 = jnp.bfloat16
ALL_AXES = ("expert", "context", "dp")


def dot(left, right, left_dim=1, right_dim=0):
    return lax.dot_general(
        left, right, (((left_dim,), (right_dim,)), ((), ())), preferred_element_type=F32
    )


def position():
    return lax.axis_index("expert"), lax.axis_index("context"), lax.axis_index("dp")


def remote(src, dst, send_sem, recv_sem, device):
    return pltpu.make_async_remote_copy(
        src_ref=src,
        dst_ref=dst,
        send_sem=send_sem,
        recv_sem=recv_sem,
        device_id=device,
        device_id_type=MESH,
    )


def hail(devices):
    barrier = pltpu.get_barrier_semaphore()
    for device in devices:
        pl.semaphore_signal(barrier, inc=1, device_id=device, device_id_type=MESH)


def await_hails(devices):
    pl.semaphore_wait(pltpu.get_barrier_semaphore(), len(devices))


def context_peers(sizes, place):
    e, c, d = place
    pairs = sizes[1] // 2
    outer, inner = c // 2, c % 2
    peers = [(e, outer * 2 + 1 - inner, d)]
    for k in range(1, pairs):
        peers.append((e, lax.rem(outer + k, pairs) * 2 + inner, d))
    return peers


def expert_peers(sizes, place):
    e, c, d = place
    return [(lax.rem(e + j, sizes[0]), c, d) for j in range(1, sizes[0])]


def crossing_only(sizes, n_loc, place):
    _, there, _ = homes(sizes, n_loc, place)
    return [device for j, (_, device) in enumerate(there) if j // n_loc and j % n_loc]


def homes(sizes, n_loc, place):
    n_e, n_c, n_d = sizes
    e, c, d = place
    size = n_d // n_loc
    group, seat = d // size, lax.rem(d, size)
    there, back = [], []
    for j in range(n_e * n_loc):
        je, jg = j // n_loc, j % n_loc
        to_e, to_g = lax.rem(e + je, n_e), lax.rem(group + jg, n_loc)
        from_e, from_g = lax.rem(e - je + n_e, n_e), lax.rem(group - jg + n_loc, n_loc)
        there.append((to_e * n_loc + to_g, (to_e, c, to_g * size + seat)))
        back.append(from_e * n_loc + from_g)
    return e * n_loc + group, there, back


class Courier:
    def __init__(self, send, recv):
        self.send, self.recv = send, recv
        self.copies = []

    def carry(self, src, dst, device):
        n = len(self.copies)
        copy = remote(src, dst, self.send.at[n], self.recv.at[n], device)
        copy.start()
        self.copies.append(copy)
        return copy

    def finish(self):
        for copy in self.copies:
            copy.wait_send()


def up_to(count, step):
    return -(-count // step) * step


class ContextGather:
    def __init__(self, sizes, place, own, slot, send, recv):
        e, c, d = place
        self.pairs = sizes[1] // 2
        self.place, self.own, self.slot = place, own, slot
        self.send, self.recv = send, recv
        self.outer, self.inner = c // 2, c % 2
        self.peers = context_peers(sizes, place)
        self.copies = []
        self.forwards = []

    def start(self):
        for k in [*range(1, self.pairs), 0]:
            copy = remote(
                self.own, self.slot(self.place[1]), self.send(k), self.recv(k), self.peers[k]
            )
            copy.start()
            self.copies.append((k, copy))

    def origin(self, k):
        return lax.rem(self.outer - k + self.pairs, self.pairs) * 2 + self.inner

    def forward(self):
        for k, copy in self.copies:
            if k > 0:
                copy.wait_recv()
                block = self.slot(self.origin(k))
                n = self.pairs - 1 + k
                onward = remote(block, block, self.send(n), self.recv(n), self.peers[0])
                onward.start()
                self.forwards.append(onward)

    def finish(self):
        for k, copy in self.copies:
            if k == 0:
                copy.wait_recv()
            copy.wait_send()
        for copy in self.forwards:
            copy.wait()


class Spread:
    def __init__(self, sizes, place, courier, own, slot):
        self.sizes, self.place, self.courier = sizes, place, courier
        self.slot = slot
        n_e, n_c, n_d = sizes
        e, c, d = place
        self.across_to = expert_peers(sizes, place)
        self.along = [
            courier.carry(own, slot(e, d), (e, c, lax.rem(d + k, n_d))) for k in range(1, n_d)
        ]
        self.across = [courier.carry(own, slot(e, d), device) for device in self.across_to]

    def onward(self):
        e, c, d = self.place
        n_d = self.sizes[2]
        for k in range(1, n_d):
            self.along[k - 1].wait_recv()
            block = self.slot(e, lax.rem(d - k + n_d, n_d))
            for device in self.across_to:
                self.across.append(self.courier.carry(block, block, device))

    def arrive(self):
        for copy in self.across:
            copy.wait_recv()


def spread_count(sizes):
    n_e, n_c, n_d = sizes
    return (n_d - 1) + (n_e - 1) * n_d


def softmax_pair(left, right):
    top = jnp.maximum(left, right)
    left, right = jnp.exp(left - top), jnp.exp(right - top)
    total = left + right
    return left / total, right / total


def tall(array, height):
    return jnp.concatenate(
        [array, jnp.zeros((height - array.shape[0], *array.shape[1:]), array.dtype)], axis=0
    )


def route_parts(routes_t, small, n_ff, n_all, slots):
    rows = routes_t.shape[1]
    routes = tall(routes_t.astype(F32), LANES).T
    hot = lax.broadcasted_iota(jnp.int32, (LANES, rows), 0)
    marks = [(hot == routes_t[k : k + 1, :]) & (hot < n_ff) for k in range(2)]
    both = (marks[0] | marks[1]).astype(F32)
    earlier = lax.broadcasted_iota(jnp.int32, (rows, rows), 0) < lax.broadcasted_iota(
        jnp.int32, (rows, rows), 1
    )
    rank = dot(both.astype(BF16), earlier.astype(F32).astype(BF16))
    number = lax.broadcasted_iota(jnp.int32, (slots, rows), 0).astype(F32)
    tables = []
    for k in range(2):
        wanted = jnp.where(marks[k], rank, -1.0)
        tables.append(
            jnp.concatenate(
                [(number == wanted[j : j + 1, :]).astype(F32) for j in range(n_ff)], axis=0
            ).astype(BF16)
        )
    lane = lax.broadcasted_iota(jnp.int32, (rows, LANES), 1)
    picks = [(lane.astype(F32) == routes[:, k : k + 1]).astype(F32) for k in range(2)]
    chosen = [
        jnp.sum(jnp.where(picks[k] > 0, small, 0.0), axis=1, keepdims=True) for k in range(2)
    ]
    w_pair = softmax_pair(chosen[0], chosen[1])
    first = softmax_pair(small[:, n_all : n_all + 1], small[:, n_all + 1 : n_all + 2])
    second = softmax_pair(small[:, n_all + 2 : n_all + 3], small[:, n_all + 3 : n_all + 4])
    return tables, picks, w_pair, first, second


def front_kernel(
    sizes,
    cfg,
    wq_ref,
    wk_ref,
    wv_ref,
    wout_ref,
    router_ref,
    coef_ref,
    value_ref,
    gains_ref,
    xown_ref,
    gate_ref,
    up_ref,
    down_ref,
    drow_ref,
    routest_ref,
    prev_ref,
    g_ref,
    xg_ref,
    wqkv_ref,
    wo_ref,
    wsm_ref,
    vec_ref,
    a1_ref,
    qt_ref,
    kh_ref,
    vh_ref,
    mixed_ref,
    h_ref,
    a2_ref,
    small_ref,
    back_ref,
    gw_ref,
    p_ref,
    slots_ref,
    res,
    inn,
    osum,
    outr,
    stage,
    blk,
    gate_scr,
    up_scr,
    hid_scr,
    acc_scr,
    ew_ref,
    small_scr,
    a_ref,
    ow_ref,
    ag,
    og,
    ew_own,
    o_scr,
    vt_scr,
    p_scr,
    sbuf,
    xin,
    p_sem,
    s_o,
    r_o,
    s_x,
    r_x,
    s_g,
    r_g,
    l_g,
    s_c,
    r_c,
    s_ow,
    r_ow,
    s_xg,
    r_xg,
    b_sem,
    s_in,
    r_in,
    s_out,
    r_out,
    s_h,
    r_h,
):
    n_e, n_c, n_d = sizes
    hp, n_ff, n_all, n_loc, slots = cfg
    hc = hp * HEAD_DIM
    place = e, c, d = position()
    rows = xown_ref.shape[0]
    length = rows * n_c
    c_all = [(e, lax.rem(c + k, n_c), d) for k in range(1, n_c)]
    n_s = n_e * n_loc
    me, there, back = homes(sizes, n_loc, place)
    d_peers = [(e, c, lax.rem(d + k, n_d)) for k in range(1, n_d)]
    neighbours = (
        c_all + d_peers + expert_peers(sizes, place) + crossing_only(sizes, n_loc, place)
    )
    hail(neighbours)
    w_rows = wq_ref.shape[0]
    small_scr[...] = jnp.zeros_like(small_scr)
    at = 0
    for ref in (router_ref, coef_ref, value_ref, gains_ref):
        small_scr[at : at + ref.shape[0], :w_rows] = ref[...]
        at += ref.shape[0]
    w_small = small_scr[...].T[:w_rows, : a_ref.shape[2] - 3 * hc].astype(BF16)
    a_ref[...] = jnp.zeros_like(a_ref)
    ow_ref[...] = jnp.zeros_like(ow_ref)
    ow_ref[:w_rows, :] = wout_ref[...].astype(BF16)
    for b in range(n_c):
        for n, ref in enumerate((wq_ref, wk_ref, wv_ref)):
            wide = min(hc, D - b * hc)
            if wide > 0:
                a_ref[b, :w_rows, n * hc : n * hc + wide] = ref[:, b * hc : b * hc + wide].astype(
                    BF16
                )
        a_ref[b, :w_rows, 3 * hc :] = w_small
    await_hails(neighbours)
    post = Courier(s_c, r_c)
    turned = [
        post.carry(a_ref.at[lax.rem(c + k, n_c)], ag.at[e, c, d], device)
        for k, device in enumerate(c_all, 1)
    ]
    x_rows = ContextGather(
        sizes,
        place,
        xown_ref,
        lambda k: xg_ref.at[k],
        lambda k: s_xg.at[k],
        lambda k: r_xg.at[k],
    )
    x_rows.start()
    ow_spread = Spread(sizes, place, post, ow_ref, lambda j, k: og.at[j, c, k])
    ag[e, c, d] = a_ref[c]
    og[e, c, d] = ow_ref[...]
    xg_ref[pl.ds(c, 1)] = xown_ref[...][None]
    for n, ref in enumerate((gate_ref, up_ref, down_ref)):
        ew_own[:, n] = ref[...].astype(BF16)
    for copy in turned:
        copy.wait_recv()
    a_spread = Spread(sizes, place, post, ag.at[e, :, d], lambda j, k: ag.at[j, :, k])
    size = n_d // n_loc
    group, seat = d // size, lax.rem(d, size)
    mates = [(e, c, group * size + lax.rem(seat + k, size)) for k in range(1, size)]
    keep_w = pltpu.make_async_copy(ew_own.at[group], ew_ref.at[d], l_g.at[2 * n_s])
    keep_w.start()
    w_far = {}
    for n in range(3):
        for k in range(1, n_loc):
            to = lax.rem(group + k, n_loc)
            w_far[n, k] = post.carry(
                ew_own.at[to, n], ew_ref.at[d, n], (e, c, to * size + seat)
            )
    w_near = [post.carry(ew_own.at[group], ew_ref.at[d], device) for device in mates]

    def pass_weights(n):
        for k in range(1, n_loc):
            w_far[n, k].wait_recv()
            block = ew_ref.at[lax.rem(group - k + n_loc, n_loc) * size + seat, n]
            w_near.extend([post.carry(block, block, device) for device in mates])

    ow_spread.onward()
    x_rows.forward()
    ow_spread.arrive()
    ow_rows = ContextGather(
        sizes,
        place,
        og.at[:, c],
        lambda k: og.at[:, k],
        lambda k: s_ow.at[k],
        lambda k: r_ow.at[k],
    )
    ow_rows.start()
    a_spread.onward()
    x_rows.finish()
    a_spread.arrive()

    padded = a_ref.shape[1]
    at_row = lax.broadcasted_iota(jnp.int32, (D // n_e, n_c * n_d * padded), 0)
    at_slab = lax.broadcasted_iota(jnp.int32, (D // n_e, n_c * n_d * padded), 1)
    unpad = jnp.where(
        at_slab == at_row // w_rows * padded + lax.rem(at_row, w_rows), 1.0, 0.0
    ).astype(BF16)
    weights = jnp.concatenate(
        [dot(unpad, ag[k].reshape(n_c * n_d * padded, ag.shape[-1])) for k in range(n_e)], axis=0
    )
    wqkv = weights[:, : 3 * hc].astype(BF16)
    wqkv_ref[...] = wqkv
    w_small = jnp.concatenate(
        [weights[:, 3 * hc : 3 * hc + SMALL], jnp.zeros((D, LANES - SMALL), F32)], axis=1
    )
    wsm_ref[...] = w_small.astype(BF16)
    w_lines = w_small.T
    vec_ref[0:2, :] = w_lines[n_all + 6 : n_all + 8, :]
    vec_ref[2:4, :] = w_lines[n_all + 4 : n_all + 6, :]
    vec_ref[4:8, :] = jnp.zeros((4, D), F32)

    gain_one = vec_ref[0:1, :]
    for b in range(n_c):
        x = xg_ref[b].astype(F32)
        inverse = lax.rsqrt(jnp.mean(x * x, axis=-1, keepdims=True) + EPS)
        a1_ref[b * rows : (b + 1) * rows, :] = (x * inverse * gain_one).astype(BF16)
    a1 = a1_ref[...]
    ow_rows.forward()
    q_t = dot(wqkv[:, :hc], a1, 0, 1).astype(BF16) * jnp.asarray(HEAD_DIM**-0.5, BF16)
    qt_ref[...] = q_t
    kv = dot(a1, wqkv[:, hc:]).astype(BF16)
    for j in range(hp):
        kh_ref[j] = kv[:, j * HEAD_DIM : (j + 1) * HEAD_DIM]
        vh_ref[j] = kv[:, hc + j * HEAD_DIM : hc + (j + 1) * HEAD_DIM]
    vt_scr[...] = dot(wqkv[:, 2 * hc :], a1, 0, 1).astype(BF16)

    pass_weights(0)
    documents = drow_ref[...].astype(F32)
    document_of = jnp.broadcast_to(documents, (LANES, length)).T[:, :1]
    turn = 0
    p_copies = {}
    for b in reversed(range(n_c)):
        reach = (b + 1) * rows
        key_place = lax.broadcasted_iota(jnp.int32, (reach, rows), 0)
        q_place = lax.broadcasted_iota(jnp.int32, (reach, rows), 1) + b * rows
        allowed = (document_of[:reach] == documents[:, b * rows : reach]) & (key_place <= q_place)
        bias = jnp.where(allowed, 0.0, -1e30)
        for j in range(hp):
            head = slice(j * HEAD_DIM, (j + 1) * HEAD_DIM)
            scores = dot(kh_ref[j, :reach, :], qt_ref[head, b * rows : reach]) + bias
            top = jnp.max(scores, axis=0, keepdims=True)
            exponent = jnp.exp(scores - top)
            total = jnp.sum(exponent, axis=0, keepdims=True)
            rounded = (exponent * (1.0 / total)).astype(BF16)
            slot = turn % 2
            if turn >= 2:
                p_copies[turn - 2].wait()
            p_scr[slot, :reach, :] = rounded
            copy = pltpu.make_async_copy(
                p_scr.at[slot, pl.ds(0, reach)], p_ref.at[j, b, pl.ds(0, reach)], p_sem.at[slot]
            )
            copy.start()
            p_copies[turn] = copy
            turn += 1
            o_scr[b, head, :] = dot(vt_scr[head, :reach], rounded).astype(BF16)

        @pl.when(c != b)
        def _():
            remote(
                o_scr.at[b], mixed_ref.at[c], s_o.at[b], r_o.at[c], (e, b, d)
            ).start()

    pass_weights(1)
    for n in range(max(0, turn - 2), turn):
        p_copies[n].wait()
    ow_rows.finish()
    if n_c * hc > D:
        wo_ref[D:, :] = jnp.zeros((n_c * hc - D, D), BF16)
    for k in range(n_e):
        wo_ref[k * (D // n_e) : (k + 1) * (D // n_e), :] = dot(
            unpad, og[k].reshape(n_c * n_d * padded, D)
        ).astype(BF16)
    mixed_ref[pl.ds(c, 1)] = o_scr[pl.ds(c, 1)]
    for b in range(n_c):

        @pl.when(c != b)
        def _():
            copy = remote(o_scr.at[b], mixed_ref.at[b], s_o.at[b], r_o.at[b], (e, b, d))
            copy.wait_send()
            copy.wait_recv()

    mixed = mixed_ref[...].reshape(n_c * hc, rows)
    h = xown_ref[...].astype(F32) + dot(mixed, wo_ref[...], 0, 0)
    h_ref[...] = h
    inverse = lax.rsqrt(jnp.mean(h * h, axis=-1, keepdims=True) + EPS)
    a2 = (h * inverse * vec_ref[1:2, :]).astype(BF16)
    a2_ref[...] = a2
    small = dot(a2, wsm_ref[...]) + tall(prev_ref[...], LANES).T
    small_ref[...] = small
    tables, _, w_pair, _, _ = route_parts(routest_ref[...], small, n_ff, n_all, slots)
    crossing = {}
    gathers = {}
    g = g_ref[...]
    for t in range(2):
        if t == 0:
            block = dot(tables[0] + tables[1], a2).astype(BF16)
        else:
            block = dot(tables[0], (w_pair[0] * g).astype(BF16)) + dot(
                tables[1], (w_pair[1] * g).astype(BF16)
            )
            block = block.astype(BF16)
        for k in range(n_s):
            sbuf[t, k] = block[k * slots : (k + 1) * slots, :]
        for j in reversed(range(1, n_s)):
            n = t * n_s + j
            part, device = there[j]
            copy = remote(sbuf.at[t, part], xin.at[t, me], s_x.at[n], r_x.at[n], device)
            copy.start()
            crossing[t, j] = copy

        def gather(j, own, t=t):
            src = back[j]
            base = (t * n_s + j) * (n_c - 1)
            keep = pltpu.make_async_copy(own, slots_ref.at[c, t, src], l_g.at[t * n_s + j])
            keep.start()
            made = ContextGather(
                sizes,
                place,
                own,
                lambda k: slots_ref.at[k, t, src],
                lambda k: s_g.at[base + k],
                lambda k: r_g.at[base + k],
            )
            made.start()
            gathers[t, j] = (made, keep)

        gather(0, sbuf.at[t, me])
        crossing[t, 0] = gather
    for t in range(2):
        for j in range(1, n_s):
            crossing[t, j].wait_recv()
            crossing[t, 0](j, xin.at[t, back[j]])
        if t == 0:
            pass_weights(2)

    def gathered(t):
        for j in range(n_s):
            gathers[t, j][0].forward()
        for j in range(n_s):
            gathers[t, j][0].finish()
            gathers[t, j][1].wait()

    roomy = len(stage.shape) == 2
    take = blk.shape[1]
    blocks = n_c // take
    pairs = n_c // 2
    outer, inner = c // 2, c % 2
    peers = context_peers(sizes, place)

    def load_rows(t, n):
        if roomy:
            return slots_ref[n * take : (n + 1) * take, t].reshape(-1, D)
        copy = pltpu.make_async_copy(slots_ref.at[pl.ds(n * take, take), t], blk.at[t], b_sem.at[0])
        copy.start()
        copy.wait()
        return blk[t].reshape(-1, D)

    def store_rows(t, n, value):
        value = value.astype(BF16).reshape(take, n_s, slots, D)
        if roomy:
            res[n * take : (n + 1) * take, t] = value
        else:
            blk[2] = value
            copy = pltpu.make_async_copy(blk.at[2], res.at[pl.ds(n * take, take), t], b_sem.at[0])
            copy.start()
            copy.wait()

    def load(ref, slot=0):
        if roomy:
            return ref[...].astype(F32)
        copy = pltpu.make_async_copy(ref, stage.at[slot], b_sem.at[0])
        copy.start()
        copy.wait()
        return stage[slot].astype(F32)

    def store(ref, value):
        if roomy:
            ref[...] = value
        else:
            stage[3] = value
            copy = pltpu.make_async_copy(stage.at[3], ref, b_sem.at[0])
            copy.start()
            copy.wait()

    order = [*reversed(range(1, n_s)), 0]
    to_pair, along, home = {}, {}, {}

    def sum_pair(t):
        for j in order:
            src = there[j][0]
            for k in [*range(1, pairs), 0]:
                n = (t * n_s + j) * pairs + k
                far = lax.rem(outer + k, pairs)
                copy = remote(
                    res.at[far * 2 + 1 - inner, t, src],
                    inn.at[far, t, src],
                    s_in.at[n],
                    r_in.at[n],
                    peers[0],
                )
                copy.start()
                to_pair[t, j, k] = copy

    def sum_along(t):
        for j in order:
            src = there[j][0]
            for k in range(1, pairs):
                n = (t * n_s + j) * pairs + k
                far = lax.rem(outer + k, pairs)
                to_pair[t, j, k].wait_recv()
                value = load(res.at[far * 2 + inner, t, src]) + load(inn.at[far, t, src], 1)
                store(osum.at[k - 1, t, src], value.astype(BF16))
                copy = remote(
                    osum.at[k - 1, t, src],
                    outr.at[k - 1, t, src],
                    s_out.at[n],
                    r_out.at[n],
                    peers[k],
                )
                copy.start()
                along[t, j, k] = copy

    def send_home(t):
        for j in order:
            src, device = there[j]
            to_pair[t, j, 0].wait_recv()
            value = load(res.at[c, t, src]) + load(inn.at[outer, t, src], 1)
            for k in range(1, pairs):
                along[t, j, k].wait_recv()
                value = value + load(outr.at[k - 1, t, src], 2)
            if j == 0:
                back_ref[t, me] = value.astype(BF16)
            else:
                xin[t, src] = value.astype(BF16)
                n = t * n_s + j
                copy = remote(xin.at[t, src], back_ref.at[t, me], s_h.at[n], r_h.at[n], device)
                copy.start()
                home[t, j] = copy

    gathered(0)
    for copy in w_near:
        copy.wait_recv()
    keep_w.wait()
    parts, units = ew_ref.shape[0], ew_ref.shape[3]
    gate, up, down = [
        jnp.concatenate([ew_ref[k, n] for k in range(parts)], axis=1) for n in range(3)
    ]
    def hidden_of(n):
        x = load_rows(0, n)
        gate_pre = dot(x, gate)
        up_pre = dot(x, up)
        return gate_pre, up_pre, (gate_pre * jax.nn.sigmoid(gate_pre) * up_pre).astype(BF16)

    for n in range(blocks):
        gate_pre, up_pre, hidden = hidden_of(n)
        if blocks == 1:
            gate_scr[...] = gate_pre
            up_scr[...] = up_pre
            hid_scr[...] = hidden
        store_rows(0, n, dot(hidden, down, 1, 1))
    sum_pair(0)
    gathered(1)
    for n in range(blocks):
        dy = load_rows(1, n)
        d_hidden = dot(dy, down)
        if n == 0:
            sum_along(0)
        if blocks == 1:
            gate_pre, up_pre, hidden = gate_scr[...], up_scr[...], hid_scr[...]
        else:
            gate_pre, up_pre, hidden = hidden_of(n)
        sig = jax.nn.sigmoid(gate_pre)
        d_gate = (d_hidden * up_pre * sig * (1.0 + gate_pre * (1.0 - sig))).astype(BF16)
        d_up = (d_hidden * gate_pre * sig).astype(BF16)
        store_rows(1, n, dot(d_gate, gate, 1, 1) + dot(d_up, up, 1, 1))
        if n == blocks - 1:
            sum_pair(1)
        x = load_rows(0, n)
        for m, (left, right) in enumerate(((x, d_gate), (x, d_up), (dy, hidden))):
            part = dot(left, right, 0, 0)
            if blocks > 1:
                if n > 0:
                    part = part + acc_scr[m]
                if n < blocks - 1:
                    acc_scr[m] = part
            if n == blocks - 1:
                for k in range(parts):
                    gw_ref[k, m] = part[:, k * units : (k + 1) * units].astype(BF16)
            if n == blocks - 1 and m == 0:
                sum_along(1)
            if n == blocks - 1 and m == 1:
                send_home(0)
    send_home(1)
    for copy in home.values():
        copy.wait()
    for copy in [*to_pair.values(), *along.values()]:
        copy.wait_send()
    for t in range(2):
        for j in range(1, n_s):
            crossing[t, j].wait_send()
    post.finish()


def front(sizes, cfg, *operands):
    n_e, n_c, n_d = sizes
    hp, n_ff, n_all, n_loc, slots = cfg
    hc = hp * HEAD_DIM
    rows = operands[8].shape[0]
    length = rows * n_c
    padded = up_to(operands[0].shape[0], 16)
    width = up_to(3 * hc + SMALL, LANES)
    units = operands[9].shape[2]
    size = n_d // n_loc
    posts = (n_c - 1) + 2 * spread_count(sizes) + size - 1 + 3 * (n_loc - 1) * size
    n_s = n_e * n_loc
    dma = pltpu.SemaphoreType.DMA
    vmem = pl.BlockSpec(memory_space=pltpu.VMEM)
    anywhere = pl.BlockSpec(memory_space=pl.ANY)
    shape = jax.ShapeDtypeStruct
    gathers = 2 * n_s * (n_c - 1)
    pairs = n_c // 2
    more = max(1, pairs - 1)
    wide = [(n_c, 2), (n_c, 2), (pairs, 2), (more, 2), (more, 2)]
    wide = [(*dims, n_s, slots, D) for dims in wide]
    roomy = n_c * n_s * slots * D <= 2**20
    held = [pltpu.VMEM(dims, BF16) for dims in wide] if roomy else []
    extra = [] if roomy else [shape(dims, BF16) for dims in wide]
    take = n_c if n_c * n_s * slots <= 1024 else max(1, 512 // (n_s * slots))
    return pl.pallas_call(
        functools.partial(front_kernel, sizes, cfg),
        out_shape=(
            shape((n_c, rows, D), BF16),
            shape((D, 3 * hc), BF16),
            shape((n_c * hc, D), BF16),
            shape((D, LANES), BF16),
            shape((8, D), F32),
            shape((length, D), BF16),
            shape((hc, length), BF16),
            shape((hp, length, HEAD_DIM), BF16),
            shape((hp, length, HEAD_DIM), BF16),
            shape((n_c, hc, rows), BF16),
            shape((rows, D), F32),
            shape((rows, D), BF16),
            shape((rows, LANES), F32),
            shape((2, n_s, slots, D), BF16),
            shape((n_d, 3, D, units), BF16),
            shape((hp, n_c, length, rows), BF16),
            *extra,
        ),
        in_specs=[vmem] * len(operands),
        out_specs=(vmem,) * 15 + (anywhere,) * (1 + len(extra)),
        scratch_shapes=[
            *held,
            pltpu.VMEM((8, LANES) if roomy else (4, slots, D), BF16),
            pltpu.VMEM((3, take, n_s, *((8, LANES) if roomy else (slots, D))), BF16),
            *[
                pltpu.VMEM((n_c * n_s * slots, n_d * units) if take == n_c else (16, LANES), kind)
                for kind in (F32, F32, BF16)
            ],
            pltpu.VMEM((3, D, n_d * units) if take < n_c else (8, LANES), F32),
            pltpu.VMEM((n_d, 3, D, units), BF16),
            pltpu.VMEM((LANES, LANES), F32),
            pltpu.VMEM((n_c, padded, width), BF16),
            pltpu.VMEM((padded, D), BF16),
            pltpu.VMEM((n_e, n_c, n_d, padded, width), BF16),
            pltpu.VMEM((n_e, n_c, n_d, padded, D), BF16),
            pltpu.VMEM((n_loc, 3, D, units), BF16),
            pltpu.VMEM((n_c, hc, rows), BF16),
            pltpu.VMEM((hc, length), BF16),
            pltpu.VMEM((2, length, rows), BF16),
            pltpu.VMEM((2, n_s, slots, D), BF16),
            pltpu.VMEM((2, n_s, slots, D), BF16),
            dma((2,)),
            dma((n_c,)),
            dma((n_c,)),
            dma((2 * n_s,)),
            dma((2 * n_s,)),
            dma((gathers,)),
            dma((gathers,)),
            dma((2 * n_s + 1,)),
            dma((posts,)),
            dma((posts,)),
            *[dma((n_c - 1,))] * 4,
            dma((1,)),
            *[dma((2 * n_s * pairs,))] * 4,
            *[dma((2 * n_s,))] * 2,
        ],
        compiler_params=pltpu.CompilerParams(
            collective_id=0, has_side_effects=True, vmem_limit_bytes=VMEM_LIMIT
        ),
        name="front",
    )(*operands)


def back_kernel(
    sizes,
    cfg,
    ret_ref,
    h_ref,
    a2_ref,
    small_ref,
    g_ref,
    routest_ref,
    wo_ref,
    wqkv_ref,
    wsm_ref,
    vec_ref,
    mixed_ref,
    a1_ref,
    qt_ref,
    kh_ref,
    vh_ref,
    p_ref,
    xg_ref,
    gw_ref,
    block_ref,
    dx_ref,
    dprev_ref,
    gq_ref,
    gk_ref,
    gv_ref,
    go_ref,
    grouter_ref,
    gcoef_ref,
    gvalue_ref,
    ggains_ref,
    egate_ref,
    eup_ref,
    edown_ref,
    dhg,
    dht_scr,
    p_scr,
    dk_acc,
    dv_acc,
    dqt,
    dqkv,
    da_in,
    da_sum,
    da_out,
    x_scr,
    ew_own,
    ew_in,
    ew_mid,
    ew_out,
    t_send,
    t_recv,
    t_z,
    t_zr,
    t_c,
    t_cr,
    o_own,
    o_in,
    o_sum,
    o_out,
    o_x,
    o_xr,
    o_z,
    o_zr,
    l_sem,
    s_g,
    r_g,
    p_sem,
    s_d,
    r_d,
    s_w,
    r_w,
    s_t,
    r_t,
    s_q,
    r_q,
):
    n_e, n_c, n_d = sizes
    hp, n_ff, n_all, n_loc, slots = cfg
    hc = hp * HEAD_DIM
    place = e, c, d = position()
    pairs = n_c // 2
    outer, inner = c // 2, c % 2
    rows = h_ref.shape[0]
    w_rows = go_ref.shape[0]
    shift = 3 * hc % LANES
    chunks = up_to(3 * hc + SMALL, LANES) // LANES
    d_peers = [(e, c, lax.rem(d + k, n_d)) for k in range(1, n_d)]
    length = rows * n_c
    peers = context_peers(sizes, place)
    e_peers = expert_peers(sizes, place)

    bring = pltpu.make_async_copy(gw_ref, ew_own, l_sem.at[1])
    bring.start()

    def fetch_x(b, slot):
        return pltpu.make_async_copy(xg_ref.at[b], x_scr.at[slot], l_sem.at[2 + slot])

    fetch_x(c, 2).start()
    fetch_x(0, 0).start()
    hail(peers + e_peers + d_peers)

    size = n_d // n_loc
    group, seat = d // size, lax.rem(d, size)
    mates = [(e, c, group * size + lax.rem(seat + k, size)) for k in range(1, size)]
    others = [lax.rem(group + k, n_loc) for k in range(1, n_loc)]
    freight = Courier(s_w, r_w)
    e_near = {}
    e_far = []

    def expert_start():
        for k, mate in enumerate(mates):
            for r, other in enumerate(others):
                e_near[k, r] = freight.carry(
                    ew_own.at[other * size + lax.rem(seat + k + 1, size)], ew_mid.at[k, r], mate
                )

    def expert_cross():
        for k, mate in enumerate(mates):
            e_near[k, -1] = freight.carry(ew_own.at[mate[2]], ew_in.at[k], mate)
        for r, other in enumerate(others):
            target = other * size + seat
            for k in range(size - 1):
                e_near[k, r].wait_recv()

            def one(n, carry):
                at = pl.ds(pl.multiple_of(n * tile, tile), tile)
                total = ew_own[target, at, :].astype(F32)
                for k in range(size - 1):
                    total = total + ew_mid[k, r, at, :].astype(F32)
                ew_out[r, at, :] = total.astype(BF16)
                return carry

            tile = ew_own.shape[1] // 9
            lax.fori_loop(0, 9, one, 0)
            e_far.append(freight.carry(ew_out.at[r], ew_in.at[size - 1 + r], (e, c, target)))

    def expert_end():
        for k in range(size - 1):
            e_near[k, -1].wait_recv()
        for copy in e_far:
            copy.wait_recv()
        part = ew_own.shape[1] // 3
        for n, ref in enumerate((egate_ref, eup_ref, edown_ref)):
            at = slice(n * part, (n + 1) * part)
            total = ew_own[d, at, :].astype(F32)
            for k in range(size - 1):
                total = total + ew_in[k, at, :].astype(F32)
            ref[pl.ds(group, 1)] = total[None]
            for r in range(n_loc - 1):
                ref[pl.ds(lax.rem(group - r - 1 + n_loc, n_loc), 1)] = ew_in[
                    size - 1 + r, at, :
                ].astype(F32)[None]
        freight.finish()

    await_hails(peers + e_peers + d_peers)
    bring.wait()
    expert_start()
    h = h_ref[...]
    a2 = a2_ref[...].astype(F32)
    g = g_ref[...]
    small = small_ref[...]
    value_one, value_two = vec_ref[2:3, :], vec_ref[3:4, :]
    tables, picks, w_pair, first, other = route_parts(
        routest_ref[...], small, n_ff, n_all, slots
    )
    copy_on, one_on, two_on = [
        [picks[k][:, n_ff + n : n_ff + n + 1] for k in range(2)] for n in (1, 2, 3)
    ]
    g_a2 = jnp.sum(g * a2, axis=1, keepdims=True)
    g_one = jnp.sum(g * value_one, axis=1, keepdims=True)
    g_two = jnp.sum(g * value_two, axis=1, keepdims=True)
    alpha = [copy_on[k] + one_on[k] * first[0] + two_on[k] * other[0] for k in range(2)]
    a_weight = alpha[0] * w_pair[0] + alpha[1] * w_pair[1]
    one_weight = one_on[0] * w_pair[0] + one_on[1] * w_pair[1]
    two_weight = two_on[0] * w_pair[0] + two_on[1] * w_pair[1]
    returned = [ret_ref[t].reshape(n_ff * slots, D) for t in range(2)]
    block = h
    d_weight = []
    for k in range(2):
        routed = dot(tables[k], returned[0], 0, 0)
        picked = (
            routed
            + alpha[k] * a2
            + (one_on[k] * first[1]) * value_one
            + (two_on[k] * other[1]) * value_two
        )
        block = block + w_pair[k] * picked
        d_weight.append(jnp.sum(g * picked, axis=1, keepdims=True))
    block_ref[...] = block
    center = w_pair[0] * d_weight[0] + w_pair[1] * d_weight[1]
    d_logits = (
        picks[0] * (w_pair[0] * (d_weight[0] - center))
        + picks[1] * (w_pair[1] * (d_weight[1] - center))
    )
    dprev_ref[...] = d_logits.T[:n_all, :]
    lane = lax.broadcasted_iota(jnp.int32, (rows, LANES), 1)
    d_small = d_logits
    for base, pair, weight, g_value in (
        (n_all, first, one_weight, g_one),
        (n_all + 2, other, two_weight, g_two),
    ):
        d_pair = (weight * g_a2, weight * g_value)
        middle = pair[0] * d_pair[0] + pair[1] * d_pair[1]
        for k in range(2):
            d_small = d_small + jnp.where(lane == base + k, pair[k] * (d_pair[k] - middle), 0.0)
    d_small = d_small.astype(BF16)
    d_const_one = jnp.sum((first[1] * one_weight) * g, axis=0, keepdims=True)
    d_const_two = jnp.sum((other[1] * two_weight) * g, axis=0, keepdims=True)
    d_a2 = (
        dot(tables[0] + tables[1], returned[1], 0, 0)
        + a_weight * g
        + dot(d_small, wsm_ref[...], 1, 1)
    )
    gain_two = vec_ref[1:2, :]
    inverse_two = lax.rsqrt(jnp.mean(h * h, axis=-1, keepdims=True) + EPS)
    d_gain_two = jnp.sum(d_a2 * h * inverse_two, axis=0, keepdims=True)
    scaled = gain_two * d_a2
    d_h = (
        g
        + inverse_two * scaled
        - h * inverse_two**3 * jnp.mean(scaled * h, axis=-1, keepdims=True)
    )
    d_hb = d_h.astype(BF16)
    dhg[pl.ds(c, 1)] = d_hb[None]
    gather = ContextGather(
        sizes,
        place,
        dhg.at[c],
        lambda k: dhg.at[k],
        lambda k: s_g.at[k],
        lambda k: r_g.at[k],
    )
    gather.start()
    dx_ref[...] = d_h
    expert_cross()
    g_o = dot(mixed_ref[...].reshape(n_c * hc, rows), d_hb)
    run = n_d * w_rows
    for b in range(n_c):
        for k in range(n_e):
            o_own[b, k, :run, :] = g_o[(k * n_c + b) * run : (k * n_c + b + 1) * run].astype(BF16)
    parcel = Courier(s_q, r_q)
    o_pair = {}
    for k in [*range(1, pairs), 0]:
        there = lax.rem(outer + k, pairs)
        o_pair[k] = parcel.carry(
            o_own.at[there * 2 + 1 - inner], o_in.at[there], peers[0]
        )
    o_state = {}

    def o_outer():
        o_state["outer"] = []
        for k in range(1, pairs):
            there = lax.rem(outer + k, pairs)
            o_pair[k].wait_recv()
            o_sum[k - 1] = (
                o_own[there * 2 + inner].astype(F32) + o_in[there].astype(F32)
            ).astype(BF16)
            o_state["outer"].append(
                parcel.carry(o_sum.at[k - 1], o_out.at[k - 1], peers[k])
            )

    def o_across():
        o_pair[0].wait_recv()
        total = o_own[c].astype(F32) + o_in[outer].astype(F32)
        for k, copy in enumerate(o_state["outer"]):
            copy.wait_recv()
            total = total + o_out[k].astype(F32)
        o_x[...] = total.astype(BF16)
        o_state["across"] = [
            parcel.carry(o_x.at[lax.rem(e + j, n_e)], o_xr.at[j - 1], e_peers[j - 1])
            for j in range(1, n_e)
        ]

    def o_along():
        total = o_x[e].astype(F32)
        for j, copy in enumerate(o_state["across"]):
            copy.wait_recv()
            total = total + o_xr[j].astype(F32)
        for k in range(n_d):
            o_z[k, :w_rows, :] = total[k * w_rows : (k + 1) * w_rows].astype(BF16)
        o_state["along"] = [
            parcel.carry(o_z.at[lax.rem(d + k, n_d)], o_zr.at[k - 1], d_peers[k - 1])
            for k in range(1, n_d)
        ]

    def o_end():
        total = o_z[d].astype(F32)
        for k, copy in enumerate(o_state["along"]):
            copy.wait_recv()
            total = total + o_zr[k].astype(F32)
        go_ref[...] = total[:w_rows]
        parcel.finish()

    if shift:
        d_small = jnp.concatenate(
            [jnp.zeros((rows, shift), BF16), d_small[:, : LANES - shift]], axis=1
        )
    g_small = dot(a2_ref[...], d_small, 0, 0)
    dk_acc[...] = jnp.zeros_like(dk_acc)
    dv_acc[...] = jnp.zeros_like(dv_acc)
    order = [(b, j) for b in reversed(range(n_c)) for j in range(hp)]

    def fetch(n):
        b, j = order[n]
        reach = pl.ds(0, (b + 1) * rows)
        return pltpu.make_async_copy(p_ref.at[j, b, reach], p_scr.at[n % 2, reach], p_sem.at[n % 2])

    fetch(0).start()
    gather.forward()
    gather.finish()
    o_outer()
    wo_part = wo_ref[pl.ds(pl.multiple_of(c * hc, hc), hc), :]
    for b in range(n_c):
        dht_scr[:, b * rows : (b + 1) * rows] = dot(wo_part, dhg[b], 1, 1).astype(BF16)
    for n, (b, j) in enumerate(order):
        reach = (b + 1) * rows
        head = slice(j * HEAD_DIM, (j + 1) * HEAD_DIM)
        mine_q = slice(b * rows, reach)
        if n == len(order) // 4:
            o_across()
        if n == len(order) // 2:
            o_along()
        if n + 1 < len(order):
            fetch(n + 1).start()
        fetch(n).wait()
        rounded = p_scr[n % 2, :reach, :]
        prob = rounded.astype(F32)
        d_o = dht_scr[head, mine_q]
        d_prob = dot(vh_ref[j, :reach, :], d_o)
        delta = jnp.sum(prob * d_prob, axis=0, keepdims=True)
        d_scores = (prob * (d_prob - delta)).astype(BF16)
        dqt[head, mine_q] = dot(kh_ref[j, :reach, :], d_scores, 0, 0) * HEAD_DIM**-0.5
        dk_acc[j, :reach, :] += dot(d_scores, qt_ref[head, mine_q], 1, 1)
        dv_acc[j, :reach, :] += dot(rounded, d_o, 1, 1)
    dqkv[:, :hc] = dqt[...].T.astype(BF16)
    for j in range(hp):
        at = j * HEAD_DIM
        dqkv[:, hc + at : hc + at + HEAD_DIM] = dk_acc[j].astype(BF16)
        dqkv[:, 2 * hc + at : 2 * hc + at + HEAD_DIM] = dv_acc[j].astype(BF16)
    dqkv[:, 3 * hc :] = jnp.zeros((length, dqkv.shape[1] - 3 * hc), BF16)
    d_all = dqkv[...]
    bag = Courier(s_t, r_t)
    across = {}
    g_all = dot(a1_ref[...], d_all, 0, 0)
    half = D // n_e

    def send_chunk(k, value):
        for n in range(n_e):
            t_send[k, n] = value[n * half : (n + 1) * half].astype(BF16)
        across[k] = [
            bag.carry(t_send.at[k, lax.rem(e + j, n_e)], t_recv.at[k, j - 1], e_peers[j - 1])
            for j in range(1, n_e)
        ]

    for k in range(chunks - 1):
        send_chunk(k, g_all[:, k * LANES : (k + 1) * LANES])
    wqkv = wqkv_ref[...]
    gain_one = vec_ref[0:1, :]
    d_gain_one = jnp.zeros((1, D), F32)
    for b in range(n_c):
        part = dot(d_all[b * rows : (b + 1) * rows, : 3 * hc], wqkv, 1, 1)
        dhg[b] = part.astype(BF16)
        if b + 1 < n_c:
            fetch_x(b + 1, (b + 1) % 2).start()
        fetch_x(b, b % 2).wait()
        x = x_scr[b % 2].astype(F32)
        inverse = lax.rsqrt(jnp.mean(x * x, axis=-1, keepdims=True) + EPS)
        d_gain_one = d_gain_one + jnp.sum(part * x * inverse, axis=0, keepdims=True)
    to_pair = []
    for k in [*range(1, pairs), 0]:
        there = lax.rem(outer + k, pairs)
        copy = remote(
            dhg.at[there * 2 + 1 - inner], da_in.at[there], s_d.at[k], r_d.at[k], peers[0]
        )
        copy.start()
        to_pair.append((k, copy))
    spot = lax.broadcasted_iota(jnp.int32, (LANES, D), 0)
    lines = jnp.zeros((LANES, D), F32)
    for n, row in enumerate((d_const_one, d_const_two, d_gain_one, d_gain_two)):
        lines = lines + jnp.where(spot == shift + n_all + 4 + n, row, 0.0)
    send_chunk(chunks - 1, g_all[:, (chunks - 1) * LANES :] + g_small + lines.T)
    along = []
    for k, copy in to_pair:
        if k == 0:
            continue
        there = lax.rem(outer + k, pairs)
        copy.wait_recv()
        da_sum[k - 1] = (
            dhg[there * 2 + inner].astype(F32) + da_in[there].astype(F32)
        ).astype(BF16)
        onward = remote(
            da_sum.at[k - 1],
            da_out.at[k - 1],
            s_d.at[pairs + k - 1],
            r_d.at[pairs + k - 1],
            peers[k],
        )
        onward.start()
        along.append(onward)
    down = {}
    for k in range(chunks):
        total = t_send[k, e].astype(F32)
        for j, copy in enumerate(across[k]):
            copy.wait_recv()
            total = total + t_recv[k, j].astype(F32)
        for n in range(n_d):
            t_z[k, n, : n_c * w_rows, :] = jnp.concatenate(
                [
                    total[(b * n_d + n) * w_rows : (b * n_d + n + 1) * w_rows]
                    for b in range(n_c)
                ],
                axis=0,
            ).astype(BF16)
        down[k] = [
            bag.carry(t_z.at[k, lax.rem(d + n, n_d)], t_zr.at[k, n - 1], d_peers[n - 1])
            for n in range(1, n_d)
        ]
    o_end()
    to_pair[-1][1].wait_recv()
    d_a1 = dhg[c].astype(F32) + da_in[outer].astype(F32)
    for k, copy in enumerate(along):
        copy.wait_recv()
        d_a1 = d_a1 + da_out[k].astype(F32)
    fetch_x(c, 2).wait()
    x = x_scr[2].astype(F32)
    inverse_one = lax.rsqrt(jnp.mean(x * x, axis=-1, keepdims=True) + EPS)
    scaled = gain_one * d_a1
    dx_ref[...] += inverse_one * scaled - x * inverse_one**3 * jnp.mean(
        scaled * x, axis=-1, keepdims=True
    )
    for k in range(chunks):
        total = t_z[k, d].astype(F32)
        for n, copy in enumerate(down[k]):
            copy.wait_recv()
            total = total + t_zr[k, n].astype(F32)
        for b in range(n_c):
            t_c[b, k, :w_rows, :] = total[b * w_rows : (b + 1) * w_rows]
    t_cr[pl.ds(c, 1)] = t_c[pl.ds(c, 1)]
    turned = [
        bag.carry(t_c.at[lax.rem(c + k, n_c)], t_cr.at[c], (e, lax.rem(c + k, n_c), d))
        for k in range(1, n_c)
    ]
    expert_end()
    for copy in turned:
        copy.wait_recv()
    s_total = jnp.zeros((w_rows, SMALL), F32)
    for b in range(n_c):
        line = jnp.concatenate([t_cr[b, k] for k in range(chunks)], axis=1)[:w_rows]
        for n, ref in enumerate((gq_ref, gk_ref, gv_ref)):
            width = min(hc, D - b * hc)
            if width > 0:
                ref[:, b * hc : b * hc + width] = line[:, n * hc : n * hc + width]
        s_total = s_total + line[:, 3 * hc : 3 * hc + SMALL]
    s_lines = jnp.concatenate([s_total, jnp.zeros((w_rows, LANES - SMALL), F32)], axis=1)
    s_lines = tall(s_lines, LANES).T
    at = 0
    for ref in (grouter_ref, gcoef_ref, gvalue_ref, ggains_ref):
        ref[...] = s_lines[at : at + ref.shape[0], :w_rows]
        at += ref.shape[0]
    bag.finish()
    for _, copy in to_pair:
        copy.wait_send()
    for copy in along:
        copy.wait_send()


def backward(sizes, cfg, *operands):
    n_e, n_c, n_d = sizes
    hp, n_ff, n_all, n_loc, slots = cfg
    hc = hp * HEAD_DIM
    rows = operands[1].shape[0]
    length = rows * n_c
    pairs = n_c // 2
    dma = pltpu.SemaphoreType.DMA
    vmem = pl.BlockSpec(memory_space=pltpu.VMEM)
    anywhere = pl.BlockSpec(memory_space=pl.ANY)
    shape = jax.ShapeDtypeStruct
    part = operands[17].shape[1]
    w_rows = D // (n_e * n_c * n_d)
    chunks = up_to(3 * hc + SMALL, LANES) // LANES
    run = up_to(n_d * w_rows, 16)
    turn = up_to(n_c * w_rows, 16)
    few = up_to(w_rows, 16)
    few_wide = up_to(w_rows, 8)
    size = n_d // n_loc
    loads = (size - 1) * n_loc + n_loc - 1
    bags = chunks * (n_e - 1 + n_d - 1) + n_c - 1
    parcels = 2 * pairs - 1 + n_e - 1 + n_d - 1
    n_more = max(1, pairs - 1)
    in_specs = [vmem] * len(operands)
    in_specs[15] = in_specs[16] = in_specs[17] = anywhere
    return pl.pallas_call(
        functools.partial(back_kernel, sizes, cfg),
        out_shape=(
            shape((rows, D), F32),
            shape((rows, D), F32),
            shape((n_all, rows), F32),
            *[shape((w_rows, D), F32)] * 4,
            *[shape((n, w_rows), F32) for n in (n_all, 4, 2, 2)],
            *[shape((n_loc, part // 3, LANES), F32)] * 3,
        ),
        in_specs=in_specs,
        out_specs=(vmem,) * 14,
        scratch_shapes=[
            pltpu.VMEM((n_c, rows, D), BF16),
            pltpu.VMEM((hc, length), BF16),
            pltpu.VMEM((2, length, rows), BF16),
            pltpu.VMEM((hp, length, HEAD_DIM), F32),
            pltpu.VMEM((hp, length, HEAD_DIM), F32),
            pltpu.VMEM((hc, length), F32),
            pltpu.VMEM((length, chunks * LANES), BF16),
            pltpu.VMEM((pairs, rows, D), BF16),
            pltpu.VMEM((n_more, rows, D), BF16),
            pltpu.VMEM((n_more, rows, D), BF16),
            pltpu.VMEM((3, rows, D), BF16),
            pltpu.VMEM((n_d, part, LANES), BF16),
            pltpu.VMEM((size + n_loc - 2, part, LANES), BF16),
            pltpu.VMEM((max(1, size - 1), max(1, n_loc - 1), part, LANES), BF16),
            pltpu.VMEM((max(1, n_loc - 1), part, LANES), BF16),
            pltpu.VMEM((chunks, n_e, D // n_e, LANES), BF16),
            pltpu.VMEM((chunks, n_e - 1, D // n_e, LANES), BF16),
            pltpu.VMEM((chunks, n_d, turn, LANES), BF16),
            pltpu.VMEM((chunks, n_d - 1, turn, LANES), BF16),
            pltpu.VMEM((n_c, chunks, few_wide, LANES), F32),
            pltpu.VMEM((n_c, chunks, few_wide, LANES), F32),
            pltpu.VMEM((n_c, n_e, run, D), BF16),
            pltpu.VMEM((pairs, n_e, run, D), BF16),
            pltpu.VMEM((n_more, n_e, run, D), BF16),
            pltpu.VMEM((n_more, n_e, run, D), BF16),
            pltpu.VMEM((n_e, run, D), BF16),
            pltpu.VMEM((n_e - 1, run, D), BF16),
            pltpu.VMEM((n_d, few, D), BF16),
            pltpu.VMEM((n_d - 1, few, D), BF16),
            dma((5,)),
            dma((n_c - 1,)),
            dma((n_c - 1,)),
            dma((2,)),
            dma((n_c,)),
            dma((n_c,)),
            dma((loads,)),
            dma((loads,)),
            dma((bags,)),
            dma((bags,)),
            dma((parcels,)),
            dma((parcels,)),
        ],
        compiler_params=pltpu.CompilerParams(
            collective_id=1, has_side_effects=True, vmem_limit_bytes=VMEM_LIMIT
        ),
        name="backward",
    )(*operands)


def hand_out_kernel(*refs):
    count = (len(refs) - 2) // 3
    sources, results, held = refs[:count], refs[count : 2 * count], refs[2 * count : 3 * count]
    in_sems, out_sems = refs[-2:]
    takes = [pltpu.make_async_copy(sources[n], held[n], in_sems.at[n]) for n in range(count)]
    gives = [pltpu.make_async_copy(held[n], results[n], out_sems.at[n]) for n in range(count)]
    for copy in takes:
        copy.start()
    for take, give in zip(takes, gives):
        take.wait()
        give.start()
    for copy in gives:
        copy.wait()


def hand_out(results):
    anywhere = pl.BlockSpec(memory_space=pl.ANY)
    dma = pltpu.SemaphoreType.DMA((len(results),))
    return pl.pallas_call(
        hand_out_kernel,
        out_shape=tuple(jax.ShapeDtypeStruct(r.shape, r.dtype) for r in results),
        in_specs=[anywhere] * len(results),
        out_specs=(anywhere,) * len(results),
        scratch_shapes=[*[pltpu.VMEM(r.shape, r.dtype) for r in results], dma, dma],
        compiler_params=pltpu.CompilerParams(vmem_limit_bytes=VMEM_LIMIT),
        name="hand_out",
    )(*results)


def body(
    tokens,
    doc_ids,
    routes,
    prev_logits,
    cotangent,
    w_query,
    w_key,
    w_value,
    w_out,
    w_router,
    const_coef,
    const_value,
    norm_gains,
    expert_gate,
    expert_up,
    expert_down,
):
    sizes = n_e, n_c, n_d = tuple(lax.axis_size(axis) for axis in ALL_AXES)
    rows = tokens.shape[1]
    length = doc_ids.shape[1]
    n_loc, _, units = expert_gate.shape
    n_ff = n_loc * n_e
    n_all = w_router.shape[1]
    slots = rows // 4
    hp = -(-HEADS // n_c)
    cfg = (hp, n_ff, n_all, n_loc, slots)
    routes_t = routes[0].T
    upstream = cotangent[0]
    (
        x_all,
        wqkv,
        wo,
        wsm,
        vec,
        a1,
        q_t,
        k_h,
        v_h,
        mixed,
        h,
        a2,
        small,
        returned,
        grads,
        probs,
        *_,
    ) = front(
        sizes,
        cfg,
        w_query,
        w_key,
        w_value,
        w_out,
        w_router.T,
        const_coef.T,
        const_value.T,
        norm_gains.T,
        tokens[0],
        expert_gate,
        expert_up,
        expert_down,
        doc_ids,
        routes_t,
        prev_logits[0].T,
        upstream,
    )
    results = backward(
        sizes,
        cfg,
        returned,
        h,
        a2,
        small,
        upstream,
        routes_t,
        wo,
        wqkv,
        wsm,
        vec,
        mixed,
        a1,
        q_t,
        k_h,
        v_h,
        probs,
        x_all,
        grads.reshape(n_d, 3 * D * units // LANES, LANES),
    )
    block_rows, d_x, d_prev, *square = hand_out(results)
    narrow = square[4:8]
    return (
        block_rows[None],
        d_x[None],
        d_prev.T[None],
        *square[:4],
        *[grad.T for grad in narrow],
        *[grad.reshape(n_loc, D, units) for grad in square[8:]],
    )


def solution(mesh):
    rows = P(("expert", "dp"), "context", None)
    weights = P(ALL_AXES, None)
    units = P("expert", None, ("context", "dp"))
    return jax.shard_map(
        body,
        mesh=mesh,
        in_specs=(rows, P(("expert", "dp"), None), rows, rows, rows)
        + (weights,) * 8
        + (units,) * 3,
        out_specs=(rows,) * 3 + (weights,) * 8 + (units,) * 3,
        check_vma=False,
    )
```

```python
import functools

import jax
import jax.numpy as jnp
from jax import lax
from jax.experimental import pallas as pl
from jax.experimental.pallas import tpu as pltpu
from jax.sharding import PartitionSpec as P

D = 768
HEADS = 12
HEAD_DIM = 64
EPS = 1e-06
SMALL = 64
LANES = 128
VMEM_LIMIT = 63 * 2**20
MESH = pl.DeviceIdType.MESH
F32 = jnp.float32
BF16 = jnp.bfloat16
ALL_AXES = ("expert", "context", "dp")


def dot(left, right, left_dim=1, right_dim=0):
    return lax.dot_general(
        left, right, (((left_dim,), (right_dim,)), ((), ())), preferred_element_type=F32
    )


def position():
    return lax.axis_index("expert"), lax.axis_index("context"), lax.axis_index("dp")


def remote(src, dst, send_sem, recv_sem, device):
    return pltpu.make_async_remote_copy(
        src_ref=src,
        dst_ref=dst,
        send_sem=send_sem,
        recv_sem=recv_sem,
        device_id=device,
        device_id_type=MESH,
    )


def hail(devices):
    barrier = pltpu.get_barrier_semaphore()
    for device in devices:
        pl.semaphore_signal(barrier, inc=1, device_id=device, device_id_type=MESH)


def await_hails(devices):
    pl.semaphore_wait(pltpu.get_barrier_semaphore(), len(devices))


def context_peers(sizes, place):
    e, c, d = place
    pairs = sizes[1] // 2
    outer, inner = c // 2, c % 2
    peers = [(e, outer * 2 + 1 - inner, d)]
    for k in range(1, pairs):
        peers.append((e, lax.rem(outer + k, pairs) * 2 + inner, d))
    return peers


def expert_peers(sizes, place):
    e, c, d = place
    return [(lax.rem(e + j, sizes[0]), c, d) for j in range(1, sizes[0])]


def crossing_only(sizes, n_loc, place):
    _, there, _ = homes(sizes, n_loc, place)
    return [device for j, (_, device) in enumerate(there) if j // n_loc and j % n_loc]


def homes(sizes, n_loc, place):
    n_e, n_c, n_d = sizes
    e, c, d = place
    size = n_d // n_loc
    group, seat = d // size, lax.rem(d, size)
    there, back = [], []
    for j in range(n_e * n_loc):
        je, jg = j // n_loc, j % n_loc
        to_e, to_g = lax.rem(e + je, n_e), lax.rem(group + jg, n_loc)
        from_e, from_g = lax.rem(e - je + n_e, n_e), lax.rem(group - jg + n_loc, n_loc)
        there.append((to_e * n_loc + to_g, (to_e, c, to_g * size + seat)))
        back.append(from_e * n_loc + from_g)
    return e * n_loc + group, there, back


class Courier:
    def __init__(self, send, recv):
        self.send, self.recv = send, recv
        self.copies = []

    def carry(self, src, dst, device):
        n = len(self.copies)
        copy = remote(src, dst, self.send.at[n], self.recv.at[n], device)
        copy.start()
        self.copies.append(copy)
        return copy

    def finish(self):
        for copy in self.copies:
            copy.wait_send()


def up_to(count, step):
    return -(-count // step) * step


class ContextGather:
    def __init__(self, sizes, place, own, slot, send, recv):
        e, c, d = place
        self.pairs = sizes[1] // 2
        self.place, self.own, self.slot = place, own, slot
        self.send, self.recv = send, recv
        self.outer, self.inner = c // 2, c % 2
        self.peers = context_peers(sizes, place)
        self.copies = []
        self.forwards = []

    def start(self):
        for k in [*range(1, self.pairs), 0]:
            copy = remote(
                self.own, self.slot(self.place[1]), self.send(k), self.recv(k), self.peers[k]
            )
            copy.start()
            self.copies.append((k, copy))

    def origin(self, k):
        return lax.rem(self.outer - k + self.pairs, self.pairs) * 2 + self.inner

    def forward(self):
        for k, copy in self.copies:
            if k > 0:
                copy.wait_recv()
                block = self.slot(self.origin(k))
                n = self.pairs - 1 + k
                onward = remote(block, block, self.send(n), self.recv(n), self.peers[0])
                onward.start()
                self.forwards.append(onward)

    def finish(self):
        for k, copy in self.copies:
            if k == 0:
                copy.wait_recv()
            copy.wait_send()
        for copy in self.forwards:
            copy.wait()


class Spread:
    def __init__(self, sizes, place, courier, own, slot):
        self.sizes, self.place, self.courier = sizes, place, courier
        self.slot = slot
        n_e, n_c, n_d = sizes
        e, c, d = place
        self.across_to = expert_peers(sizes, place)
        self.along = [
            courier.carry(own, slot(e, d), (e, c, lax.rem(d + k, n_d))) for k in range(1, n_d)
        ]
        self.across = [courier.carry(own, slot(e, d), device) for device in self.across_to]

    def onward(self):
        e, c, d = self.place
        n_d = self.sizes[2]
        for k in range(1, n_d):
            self.along[k - 1].wait_recv()
            block = self.slot(e, lax.rem(d - k + n_d, n_d))
            for device in self.across_to:
                self.across.append(self.courier.carry(block, block, device))

    def arrive(self):
        for copy in self.across:
            copy.wait_recv()


def spread_count(sizes):
    n_e, n_c, n_d = sizes
    return (n_d - 1) + (n_e - 1) * n_d


def softmax_pair(left, right):
    top = jnp.maximum(left, right)
    left, right = jnp.exp(left - top), jnp.exp(right - top)
    total = left + right
    return left / total, right / total


def tall(array, height):
    if array.shape[0] == height:
        return array
    return jnp.concatenate(
        [array, jnp.zeros((height - array.shape[0], *array.shape[1:]), array.dtype)], axis=0
    )


def route_parts(routes_t, small, n_ff, n_all, slots):
    rows = routes_t.shape[1]
    routes = tall(routes_t.astype(F32), LANES).T
    hot = lax.broadcasted_iota(jnp.int32, (LANES, rows), 0)
    marks = [(hot == routes_t[k : k + 1, :]) & (hot < n_ff) for k in range(2)]
    both = (marks[0] | marks[1]).astype(F32)
    earlier = lax.broadcasted_iota(jnp.int32, (rows, rows), 0) < lax.broadcasted_iota(
        jnp.int32, (rows, rows), 1
    )
    rank = dot(both.astype(BF16), earlier.astype(F32).astype(BF16))
    number = lax.broadcasted_iota(jnp.int32, (slots, rows), 0).astype(F32)
    tables = []
    for k in range(2):
        wanted = jnp.where(marks[k], rank, -1.0)
        tables.append(
            jnp.concatenate(
                [(number == wanted[j : j + 1, :]).astype(F32) for j in range(n_ff)], axis=0
            ).astype(BF16)
        )
    lane = lax.broadcasted_iota(jnp.int32, (rows, LANES), 1)
    picks = [(lane.astype(F32) == routes[:, k : k + 1]).astype(F32) for k in range(2)]
    chosen = [
        jnp.sum(jnp.where(picks[k] > 0, small, 0.0), axis=1, keepdims=True) for k in range(2)
    ]
    w_pair = softmax_pair(chosen[0], chosen[1])
    first = softmax_pair(small[:, n_all : n_all + 1], small[:, n_all + 1 : n_all + 2])
    second = softmax_pair(small[:, n_all + 2 : n_all + 3], small[:, n_all + 3 : n_all + 4])
    return tables, picks, w_pair, first, second


def front_kernel(
    sizes,
    cfg,
    wq_ref,
    wk_ref,
    wv_ref,
    wout_ref,
    router_ref,
    coef_ref,
    value_ref,
    gains_ref,
    xown_ref,
    gate_ref,
    up_ref,
    down_ref,
    drow_ref,
    routest_ref,
    prev_ref,
    g_ref,
    xg_out,
    wqkv_out,
    wo_out,
    wsm_out,
    vec_out,
    a1_out,
    qt_out,
    kh_out,
    vh_out,
    mixed_out,
    h_out,
    a2_out,
    small_out,
    gw_out,
    back_ref,
    p_ref,
    slots_ref,
    res,
    inn,
    osum,
    outr,
    stage,
    blk,
    gate_scr,
    up_scr,
    hid_scr,
    acc_scr,
    ew_ref,
    small_scr,
    row_scr,
    a_ref,
    ow_ref,
    ag,
    og,
    ew_own,
    o_scr,
    vt_scr,
    p_scr,
    sbuf,
    xin,
    p_sem,
    s_o,
    r_o,
    s_x,
    r_x,
    s_g,
    r_g,
    l_g,
    s_c,
    r_c,
    s_ow,
    r_ow,
    s_xg,
    r_xg,
    b_sem,
    s_in,
    r_in,
    s_out,
    r_out,
    s_h,
    r_h,
    xg_ref,
    wqkv_ref,
    wo_ref,
    wsm_ref,
    vec_ref,
    a1_ref,
    qt_ref,
    kh_ref,
    vh_ref,
    mixed_ref,
    h_ref,
    a2_ref,
    small_ref,
    gw_ref,
    o_sem,
):
    n_e, n_c, n_d = sizes
    hp, n_ff, n_all, n_loc, slots = cfg
    hc = hp * HEAD_DIM
    place = e, c, d = position()
    rows = xown_ref.shape[0]
    length = rows * n_c
    c_all = [(e, lax.rem(c + k, n_c), d) for k in range(1, n_c)]
    n_s = n_e * n_loc
    me, there, back = homes(sizes, n_loc, place)
    d_peers = [(e, c, lax.rem(d + k, n_d)) for k in range(1, n_d)]
    neighbours = (
        c_all + d_peers + expert_peers(sizes, place) + crossing_only(sizes, n_loc, place)
    )
    hail(neighbours)
    leaving = []

    def leave(*pairs_of):
        for src, dst in pairs_of:
            copy = pltpu.make_async_copy(src, dst, o_sem.at[len(leaving)])
            copy.start()
            leaving.append(copy)

    w_rows = wq_ref.shape[0]
    small_scr[...] = jnp.zeros_like(small_scr)
    at = 0
    for ref in (router_ref, coef_ref, value_ref, gains_ref):
        small_scr[at : at + ref.shape[0], :w_rows] = ref[...]
        at += ref.shape[0]
    width = row_scr.shape[1]
    w_small = small_scr[...].T[:w_rows, :SMALL]

    def stack(rows_of, tiles, height):
        parts = [rows_of(k * LANES) for k in range(tiles)]
        return tall(jnp.concatenate(parts, axis=0), height).astype(BF16)

    ow_ref[...] = stack(lambda at: wout_ref[:, at : at + LANES], D // LANES, ow_ref.shape[0])
    row_scr[...] = jnp.zeros_like(row_scr)
    row_scr[:w_rows, 3 * hc : 3 * hc + SMALL] = w_small
    for b in range(n_c):
        for n, ref in enumerate((wq_ref, wk_ref, wv_ref)):
            wide = max(0, min(hc, D - b * hc))
            if wide > 0:
                row_scr[:w_rows, n * hc : n * hc + wide] = ref[:, b * hc : b * hc + wide]
            if wide < hc:
                row_scr[:w_rows, n * hc + wide : (n + 1) * hc] = jnp.zeros((w_rows, hc - wide), F32)
        a_ref[b] = stack(
            lambda at: row_scr[:w_rows, at : at + LANES], width // LANES, a_ref.shape[1]
        )
    await_hails(neighbours)
    post = Courier(s_c, r_c)
    turned = [
        post.carry(a_ref.at[lax.rem(c + k, n_c)], ag.at[e, c, d], device)
        for k, device in enumerate(c_all, 1)
    ]
    x_rows = ContextGather(
        sizes,
        place,
        xown_ref,
        lambda k: xg_ref.at[k],
        lambda k: s_xg.at[k],
        lambda k: r_xg.at[k],
    )
    x_rows.start()
    ow_spread = Spread(sizes, place, post, ow_ref, lambda j, k: og.at[j, c, k])
    ag[e, c, d] = a_ref[c]
    og[e, c, d] = ow_ref[...]
    xg_ref[pl.ds(c, 1)] = xown_ref[...][None]
    for n, ref in enumerate((gate_ref, up_ref, down_ref)):
        ew_own[:, n] = ref[...].astype(BF16)
    for copy in turned:
        copy.wait_recv()
    a_spread = Spread(sizes, place, post, ag.at[e, :, d], lambda j, k: ag.at[j, :, k])
    size = n_d // n_loc
    group, seat = d // size, lax.rem(d, size)
    mates = [(e, c, group * size + lax.rem(seat + k, size)) for k in range(1, size)]
    keep_w = pltpu.make_async_copy(ew_own.at[group], ew_ref.at[d], l_g.at[2 * n_s])
    keep_w.start()
    w_far = {}
    for n in range(3):
        for k in range(1, n_loc):
            to = lax.rem(group + k, n_loc)
            w_far[n, k] = post.carry(
                ew_own.at[to, n], ew_ref.at[d, n], (e, c, to * size + seat)
            )
    w_near = [post.carry(ew_own.at[group], ew_ref.at[d], device) for device in mates]

    def pass_weights(n):
        for k in range(1, n_loc):
            w_far[n, k].wait_recv()
            block = ew_ref.at[lax.rem(group - k + n_loc, n_loc) * size + seat, n]
            w_near.extend([post.carry(block, block, device) for device in mates])

    ow_spread.onward()
    x_rows.forward()
    ow_spread.arrive()
    ow_rows = ContextGather(
        sizes,
        place,
        og.at[:, c],
        lambda k: og.at[:, k],
        lambda k: s_ow.at[k],
        lambda k: r_ow.at[k],
    )
    ow_rows.start()
    a_spread.onward()
    x_rows.finish()
    leave((xg_ref, xg_out))
    a_spread.arrive()

    def unstack(slabs, tiles):
        height = slabs.shape[2]
        slabs = slabs.reshape(n_c * n_d, height, LANES)
        if w_rows % 8 == 0:
            wide = [slabs[n].astype(F32) for n in range(n_c * n_d)]
            return jnp.concatenate(
                [
                    jnp.concatenate([w[k * w_rows : (k + 1) * w_rows] for w in wide], axis=0)
                    for k in range(tiles)
                ],
                axis=1,
            )
        flat = slabs.reshape(n_c * n_d * height, LANES)
        at_row = lax.broadcasted_iota(jnp.int32, (D // n_e, flat.shape[0]), 0)
        at_slab = lax.broadcasted_iota(jnp.int32, (D // n_e, flat.shape[0]), 1)
        first = at_row // w_rows * height + lax.rem(at_row, w_rows)
        return jnp.concatenate(
            [
                dot(jnp.where(at_slab == first + k * w_rows, 1.0, 0.0).astype(BF16), flat)
                for k in range(tiles)
            ],
            axis=1,
        )

    weights = jnp.concatenate([unstack(ag[k], width // LANES) for k in range(n_e)], axis=0)
    wqkv = weights[:, : 3 * hc].astype(BF16)
    wqkv_ref[...] = wqkv
    w_small = jnp.concatenate(
        [weights[:, 3 * hc : 3 * hc + SMALL], jnp.zeros((D, LANES - SMALL), F32)], axis=1
    )
    wsm_ref[...] = w_small.astype(BF16)
    w_lines = w_small.T
    vec_ref[0:2, :] = w_lines[n_all + 6 : n_all + 8, :]
    vec_ref[2:4, :] = w_lines[n_all + 4 : n_all + 6, :]
    vec_ref[4:8, :] = jnp.zeros((4, D), F32)

    gain_one = vec_ref[0:1, :]
    for b in range(n_c):
        x = xg_ref[b].astype(F32)
        inverse = lax.rsqrt(jnp.mean(x * x, axis=-1, keepdims=True) + EPS)
        a1_ref[b * rows : (b + 1) * rows, :] = (x * inverse * gain_one).astype(BF16)
    a1 = a1_ref[...]
    leave((a1_ref, a1_out), (wqkv_ref, wqkv_out), (wsm_ref, wsm_out), (vec_ref, vec_out))
    ow_rows.forward()
    q_t = dot(wqkv[:, :hc], a1, 0, 1).astype(BF16) * jnp.asarray(HEAD_DIM**-0.5, BF16)
    qt_ref[...] = q_t
    kv = dot(a1, wqkv[:, hc:]).astype(BF16)
    for j in range(hp):
        kh_ref[j] = kv[:, j * HEAD_DIM : (j + 1) * HEAD_DIM]
        vh_ref[j] = kv[:, hc + j * HEAD_DIM : hc + (j + 1) * HEAD_DIM]
    vt_scr[...] = dot(wqkv[:, 2 * hc :], a1, 0, 1).astype(BF16)

    leave((qt_ref, qt_out), (kh_ref, kh_out), (vh_ref, vh_out))
    pass_weights(0)
    documents = drow_ref[...].astype(F32)
    document_of = jnp.broadcast_to(documents, (LANES, length)).T[:, :1]
    turn = 0
    p_copies = {}
    for b in reversed(range(n_c)):
        reach = (b + 1) * rows
        key_place = lax.broadcasted_iota(jnp.int32, (reach, rows), 0)
        q_place = lax.broadcasted_iota(jnp.int32, (reach, rows), 1) + b * rows
        allowed = (document_of[:reach] == documents[:, b * rows : reach]) & (key_place <= q_place)
        bias = jnp.where(allowed, 0.0, -1e30)
        for j in range(hp):
            head = slice(j * HEAD_DIM, (j + 1) * HEAD_DIM)
            scores = dot(kh_ref[j, :reach, :], qt_ref[head, b * rows : reach]) + bias
            top = jnp.max(scores, axis=0, keepdims=True)
            exponent = jnp.exp(scores - top)
            total = jnp.sum(exponent, axis=0, keepdims=True)
            rounded = (exponent * (1.0 / total)).astype(BF16)
            slot = turn % 2
            if turn >= 2:
                p_copies[turn - 2].wait()
            p_scr[slot, :reach, :] = rounded
            copy = pltpu.make_async_copy(
                p_scr.at[slot, pl.ds(0, reach)], p_ref.at[j, b, pl.ds(0, reach)], p_sem.at[slot]
            )
            copy.start()
            p_copies[turn] = copy
            turn += 1
            o_scr[b, head, :] = dot(vt_scr[head, :reach], rounded).astype(BF16)

        @pl.when(c != b)
        def _():
            remote(
                o_scr.at[b], mixed_ref.at[c], s_o.at[b], r_o.at[c], (e, b, d)
            ).start()

    pass_weights(1)
    for n in range(max(0, turn - 2), turn):
        p_copies[n].wait()
    ow_rows.finish()
    if n_c * hc > D:
        wo_ref[D:, :] = jnp.zeros((n_c * hc - D, D), BF16)
    for k in range(n_e):
        wo_ref[k * (D // n_e) : (k + 1) * (D // n_e), :] = unstack(og[k], D // LANES).astype(BF16)
    mixed_ref[pl.ds(c, 1)] = o_scr[pl.ds(c, 1)]
    for b in range(n_c):

        @pl.when(c != b)
        def _():
            copy = remote(o_scr.at[b], mixed_ref.at[b], s_o.at[b], r_o.at[b], (e, b, d))
            copy.wait_send()
            copy.wait_recv()

    leave((wo_ref, wo_out), (mixed_ref, mixed_out))
    mixed = mixed_ref[...].reshape(n_c * hc, rows)
    h = xown_ref[...].astype(F32) + dot(mixed, wo_ref[...], 0, 0)
    h_ref[...] = h
    inverse = lax.rsqrt(jnp.mean(h * h, axis=-1, keepdims=True) + EPS)
    a2 = (h * inverse * vec_ref[1:2, :]).astype(BF16)
    a2_ref[...] = a2
    small = dot(a2, wsm_ref[...]) + tall(prev_ref[...], LANES).T
    small_ref[...] = small
    leave((h_ref, h_out), (a2_ref, a2_out), (small_ref, small_out))
    tables, _, w_pair, _, _ = route_parts(routest_ref[...], small, n_ff, n_all, slots)
    crossing = {}
    gathers = {}
    g = g_ref[...]
    for t in range(2):
        if t == 0:
            block = dot(tables[0] + tables[1], a2).astype(BF16)
        else:
            block = dot(tables[0], (w_pair[0] * g).astype(BF16)) + dot(
                tables[1], (w_pair[1] * g).astype(BF16)
            )
            block = block.astype(BF16)
        for k in range(n_s):
            sbuf[t, k] = block[k * slots : (k + 1) * slots, :]
        for j in reversed(range(1, n_s)):
            n = t * n_s + j
            part, device = there[j]
            copy = remote(sbuf.at[t, part], xin.at[t, me], s_x.at[n], r_x.at[n], device)
            copy.start()
            crossing[t, j] = copy

        def gather(j, own, t=t):
            src = back[j]
            base = (t * n_s + j) * (n_c - 1)
            keep = pltpu.make_async_copy(own, slots_ref.at[c, t, src], l_g.at[t * n_s + j])
            keep.start()
            made = ContextGather(
                sizes,
                place,
                own,
                lambda k: slots_ref.at[k, t, src],
                lambda k: s_g.at[base + k],
                lambda k: r_g.at[base + k],
            )
            made.start()
            gathers[t, j] = (made, keep)

        gather(0, sbuf.at[t, me])
        crossing[t, 0] = gather
    for t in range(2):
        for j in range(1, n_s):
            crossing[t, j].wait_recv()
            crossing[t, 0](j, xin.at[t, back[j]])
        if t == 0:
            pass_weights(2)

    def gathered(t):
        for j in range(n_s):
            gathers[t, j][0].forward()
        for j in range(n_s):
            gathers[t, j][0].finish()
            gathers[t, j][1].wait()

    roomy = len(stage.shape) == 2
    take = blk.shape[1]
    blocks = n_c // take
    pairs = n_c // 2
    outer, inner = c // 2, c % 2
    peers = context_peers(sizes, place)

    def load_rows(t, n):
        if roomy:
            return slots_ref[n * take : (n + 1) * take, t].reshape(-1, D)
        copy = pltpu.make_async_copy(slots_ref.at[pl.ds(n * take, take), t], blk.at[t], b_sem.at[0])
        copy.start()
        copy.wait()
        return blk[t].reshape(-1, D)

    def store_rows(t, n, value):
        value = value.astype(BF16).reshape(take, n_s, slots, D)
        if roomy:
            res[n * take : (n + 1) * take, t] = value
        else:
            blk[2] = value
            copy = pltpu.make_async_copy(blk.at[2], res.at[pl.ds(n * take, take), t], b_sem.at[0])
            copy.start()
            copy.wait()

    def load(ref, slot=0):
        if roomy:
            return ref[...].astype(F32)
        copy = pltpu.make_async_copy(ref, stage.at[slot], b_sem.at[0])
        copy.start()
        copy.wait()
        return stage[slot].astype(F32)

    def store(ref, value):
        if roomy:
            ref[...] = value
        else:
            stage[3] = value
            copy = pltpu.make_async_copy(stage.at[3], ref, b_sem.at[0])
            copy.start()
            copy.wait()

    order = [*reversed(range(1, n_s)), 0]
    to_pair, along, home = {}, {}, {}

    def sum_pair(t):
        for j in order:
            src = there[j][0]
            for k in [*range(1, pairs), 0]:
                n = (t * n_s + j) * pairs + k
                far = lax.rem(outer + k, pairs)
                copy = remote(
                    res.at[far * 2 + 1 - inner, t, src],
                    inn.at[far, t, src],
                    s_in.at[n],
                    r_in.at[n],
                    peers[0],
                )
                copy.start()
                to_pair[t, j, k] = copy

    def sum_along(t):
        for j in order:
            src = there[j][0]
            for k in range(1, pairs):
                n = (t * n_s + j) * pairs + k
                far = lax.rem(outer + k, pairs)
                to_pair[t, j, k].wait_recv()
                value = load(res.at[far * 2 + inner, t, src]) + load(inn.at[far, t, src], 1)
                store(osum.at[k - 1, t, src], value.astype(BF16))
                copy = remote(
                    osum.at[k - 1, t, src],
                    outr.at[k - 1, t, src],
                    s_out.at[n],
                    r_out.at[n],
                    peers[k],
                )
                copy.start()
                along[t, j, k] = copy

    def send_home(t):
        for j in order:
            src, device = there[j]
            to_pair[t, j, 0].wait_recv()
            value = load(res.at[c, t, src]) + load(inn.at[outer, t, src], 1)
            for k in range(1, pairs):
                along[t, j, k].wait_recv()
                value = value + load(outr.at[k - 1, t, src], 2)
            if j == 0:
                back_ref[t, me] = value.astype(BF16)
            else:
                xin[t, src] = value.astype(BF16)
                n = t * n_s + j
                copy = remote(xin.at[t, src], back_ref.at[t, me], s_h.at[n], r_h.at[n], device)
                copy.start()
                home[t, j] = copy

    gathered(0)
    for copy in w_near:
        copy.wait_recv()
    keep_w.wait()
    parts, units = ew_ref.shape[0], ew_ref.shape[3]
    gate, up, down = [
        jnp.concatenate([ew_ref[k, n] for k in range(parts)], axis=1) for n in range(3)
    ]
    def hidden_of(n):
        x = load_rows(0, n)
        gate_pre = dot(x, gate)
        up_pre = dot(x, up)
        return gate_pre, up_pre, (gate_pre * jax.nn.sigmoid(gate_pre) * up_pre).astype(BF16)

    for n in range(blocks):
        gate_pre, up_pre, hidden = hidden_of(n)
        if blocks == 1:
            gate_scr[...] = gate_pre
            up_scr[...] = up_pre
            hid_scr[...] = hidden
        store_rows(0, n, dot(hidden, down, 1, 1))
    sum_pair(0)
    gathered(1)
    for n in range(blocks):
        dy = load_rows(1, n)
        d_hidden = dot(dy, down)
        if n == 0:
            sum_along(0)
        if blocks == 1:
            gate_pre, up_pre, hidden = gate_scr[...], up_scr[...], hid_scr[...]
        else:
            gate_pre, up_pre, hidden = hidden_of(n)
        sig = jax.nn.sigmoid(gate_pre)
        d_gate = (d_hidden * up_pre * sig * (1.0 + gate_pre * (1.0 - sig))).astype(BF16)
        d_up = (d_hidden * gate_pre * sig).astype(BF16)
        store_rows(1, n, dot(d_gate, gate, 1, 1) + dot(d_up, up, 1, 1))
        if n == blocks - 1:
            sum_pair(1)
        x = load_rows(0, n)
        for m, (left, right) in enumerate(((x, d_gate), (x, d_up), (dy, hidden))):
            part = dot(left, right, 0, 0)
            if blocks > 1:
                if n > 0:
                    part = part + acc_scr[m]
                if n < blocks - 1:
                    acc_scr[m] = part
            if n == blocks - 1:
                for k in range(parts):
                    gw_ref[k, m] = part[:, k * units : (k + 1) * units].astype(BF16)
                leave((gw_ref.at[:, m], gw_out.at[:, m]))
            if n == blocks - 1 and m == 0:
                sum_along(1)
            if n == blocks - 1 and m == 1:
                send_home(0)
    send_home(1)
    for copy in home.values():
        copy.wait()
    for copy in [*to_pair.values(), *along.values()]:
        copy.wait_send()
    for t in range(2):
        for j in range(1, n_s):
            crossing[t, j].wait_send()
    post.finish()
    for copy in leaving:
        copy.wait()


def front(sizes, cfg, *operands):
    n_e, n_c, n_d = sizes
    hp, n_ff, n_all, n_loc, slots = cfg
    hc = hp * HEAD_DIM
    rows = operands[8].shape[0]
    length = rows * n_c
    w_rows = operands[0].shape[0]
    width = up_to(3 * hc + SMALL, LANES)
    a_rows = up_to(width // LANES * w_rows, 16)
    o_rows = up_to(D // LANES * w_rows, 16)
    units = operands[9].shape[2]
    size = n_d // n_loc
    posts = (n_c - 1) + 2 * spread_count(sizes) + size - 1 + 3 * (n_loc - 1) * size
    n_s = n_e * n_loc
    dma = pltpu.SemaphoreType.DMA
    vmem = pl.BlockSpec(memory_space=pltpu.VMEM)
    anywhere = pl.BlockSpec(memory_space=pl.ANY)
    shape = jax.ShapeDtypeStruct
    gathers = 2 * n_s * (n_c - 1)
    pairs = n_c // 2
    more = max(1, pairs - 1)
    wide = [(n_c, 2), (n_c, 2), (pairs, 2), (more, 2), (more, 2)]
    wide = [(*dims, n_s, slots, D) for dims in wide]
    roomy = n_c * n_s * slots * D <= 2**20
    held = [pltpu.VMEM(dims, BF16) for dims in wide] if roomy else []
    extra = [] if roomy else [shape(dims, BF16) for dims in wide]
    take = n_c if n_c * n_s * slots <= 1024 else max(1, 512 // (n_s * slots))
    kept = (
        shape((n_c, rows, D), BF16),
        shape((D, 3 * hc), BF16),
        shape((n_c * hc, D), BF16),
        shape((D, LANES), BF16),
        shape((8, D), F32),
        shape((length, D), BF16),
        shape((hc, length), BF16),
        shape((hp, length, HEAD_DIM), BF16),
        shape((hp, length, HEAD_DIM), BF16),
        shape((n_c, hc, rows), BF16),
        shape((rows, D), F32),
        shape((rows, D), BF16),
        shape((rows, LANES), F32),
        shape((n_d, 3, D, units), BF16),
    )
    return pl.pallas_call(
        functools.partial(front_kernel, sizes, cfg),
        out_shape=(
            *kept,
            shape((2, n_s, slots, D), BF16),
            shape((hp, n_c, length, rows), BF16),
            *extra,
        ),
        in_specs=[vmem] * len(operands),
        out_specs=(anywhere,) * len(kept) + (vmem,) + (anywhere,) * (1 + len(extra)),
        scratch_shapes=[
            *held,
            pltpu.VMEM((8, LANES) if roomy else (4, slots, D), BF16),
            pltpu.VMEM((3, take, n_s, *((8, LANES) if roomy else (slots, D))), BF16),
            *[
                pltpu.VMEM((n_c * n_s * slots, n_d * units) if take == n_c else (16, LANES), kind)
                for kind in (F32, F32, BF16)
            ],
            pltpu.VMEM((3, D, n_d * units) if take < n_c else (8, LANES), F32),
            pltpu.VMEM((n_d, 3, D, units), BF16),
            pltpu.VMEM((LANES, LANES), F32),
            pltpu.VMEM((up_to(w_rows, 8), width), F32),
            pltpu.VMEM((n_c, a_rows, LANES), BF16),
            pltpu.VMEM((o_rows, LANES), BF16),
            pltpu.VMEM((n_e, n_c, n_d, a_rows, LANES), BF16),
            pltpu.VMEM((n_e, n_c, n_d, o_rows, LANES), BF16),
            pltpu.VMEM((n_loc, 3, D, units), BF16),
            pltpu.VMEM((n_c, hc, rows), BF16),
            pltpu.VMEM((hc, length), BF16),
            pltpu.VMEM((2, length, rows), BF16),
            pltpu.VMEM((2, n_s, slots, D), BF16),
            pltpu.VMEM((2, n_s, slots, D), BF16),
            dma((2,)),
            dma((n_c,)),
            dma((n_c,)),
            dma((2 * n_s,)),
            dma((2 * n_s,)),
            dma((gathers,)),
            dma((gathers,)),
            dma((2 * n_s + 1,)),
            dma((posts,)),
            dma((posts,)),
            *[dma((n_c - 1,))] * 4,
            dma((1,)),
            *[dma((2 * n_s * pairs,))] * 4,
            *[dma((2 * n_s,))] * 2,
            *[pltpu.VMEM(k.shape, k.dtype) for k in kept],
            dma((len(kept) + 2,)),
        ],
        compiler_params=pltpu.CompilerParams(
            collective_id=0, has_side_effects=True, vmem_limit_bytes=VMEM_LIMIT
        ),
        name="front",
    )(*operands)


def back_kernel(
    sizes,
    cfg,
    ret_ref,
    h_ref,
    a2_ref,
    small_ref,
    g_ref,
    routest_ref,
    wo_in,
    wqkv_in,
    wsm_ref,
    vec_ref,
    mixed_in,
    a1_in,
    qt_in,
    kh_in,
    vh_in,
    p_ref,
    xg_ref,
    gw_ref,
    block_ref,
    dx_ref,
    dprev_ref,
    gq_ref,
    gk_ref,
    gv_ref,
    go_ref,
    grouter_ref,
    gcoef_ref,
    gvalue_ref,
    ggains_ref,
    egate_ref,
    eup_ref,
    edown_ref,
    dhg,
    dht_scr,
    p_scr,
    dk_acc,
    dv_acc,
    dqt,
    dqkv,
    da_in,
    da_sum,
    da_out,
    x_scr,
    ew_own,
    ew_in,
    ew_mid,
    ew_out,
    t_send,
    t_recv,
    t_z,
    t_zr,
    t_c,
    t_cr,
    o_own,
    o_in,
    o_sum,
    o_out,
    o_x,
    o_xr,
    o_z,
    o_zr,
    l_sem,
    s_g,
    r_g,
    p_sem,
    s_d,
    r_d,
    s_w,
    r_w,
    s_t,
    r_t,
    s_q,
    r_q,
    wo_ref,
    wqkv_ref,
    mixed_ref,
    a1_ref,
    qt_ref,
    kh_ref,
    vh_ref,
    i_sem,
):
    n_e, n_c, n_d = sizes
    hp, n_ff, n_all, n_loc, slots = cfg
    hc = hp * HEAD_DIM
    place = e, c, d = position()
    pairs = n_c // 2
    outer, inner = c // 2, c % 2
    rows = h_ref.shape[0]
    w_rows = go_ref.shape[0]
    shift = 3 * hc % LANES
    chunks = up_to(3 * hc + SMALL, LANES) // LANES
    d_peers = [(e, c, lax.rem(d + k, n_d)) for k in range(1, n_d)]
    length = rows * n_c
    peers = context_peers(sizes, place)
    e_peers = expert_peers(sizes, place)

    bring = pltpu.make_async_copy(gw_ref, ew_own, l_sem.at[1])
    bring.start()

    def fetch_x(b, slot):
        return pltpu.make_async_copy(xg_ref.at[b], x_scr.at[slot], l_sem.at[2 + slot])

    early = {}
    for name, src, dst in (
        ("mixed", mixed_in, mixed_ref),
        ("wo", wo_in, wo_ref),
        ("kh", kh_in, kh_ref),
        ("vh", vh_in, vh_ref),
        ("qt", qt_in, qt_ref),
        ("a1", a1_in, a1_ref),
        ("wqkv", wqkv_in, wqkv_ref),
    ):
        early[name] = pltpu.make_async_copy(src, dst, i_sem.at[len(early)])
        early[name].start()
    fetch_x(c, 2).start()
    fetch_x(0, 0).start()
    hail(peers + e_peers + d_peers)

    size = n_d // n_loc
    group, seat = d // size, lax.rem(d, size)
    mates = [(e, c, group * size + lax.rem(seat + k, size)) for k in range(1, size)]
    others = [lax.rem(group + k, n_loc) for k in range(1, n_loc)]
    freight = Courier(s_w, r_w)
    e_near = {}
    e_far = []

    def expert_start():
        for k, mate in enumerate(mates):
            for r, other in enumerate(others):
                e_near[k, r] = freight.carry(
                    ew_own.at[other * size + lax.rem(seat + k + 1, size)], ew_mid.at[k, r], mate
                )

    def expert_cross():
        for r, other in enumerate(others):
            target = other * size + seat
            for k in range(size - 1):
                e_near[k, r].wait_recv()

            def one(n, carry):
                at = pl.ds(pl.multiple_of(n * tile, tile), tile)
                total = ew_own[target, at, :].astype(F32)
                for k in range(size - 1):
                    total = total + ew_mid[k, r, at, :].astype(F32)
                ew_out[r, at, :] = total.astype(BF16)
                return carry

            tile = ew_own.shape[1] // 9
            lax.fori_loop(0, 9, one, 0)
            e_far.append(freight.carry(ew_out.at[r], ew_in.at[size - 1 + r], (e, c, target)))
        for k, mate in enumerate(mates):
            e_near[k, -1] = freight.carry(ew_own.at[mate[2]], ew_in.at[k], mate)

    def expert_end():
        for k in range(size - 1):
            e_near[k, -1].wait_recv()
        for copy in e_far:
            copy.wait_recv()
        part = ew_own.shape[1] // 3
        for n, ref in enumerate((egate_ref, eup_ref, edown_ref)):
            at = slice(n * part, (n + 1) * part)
            total = ew_own[d, at, :].astype(F32)
            for k in range(size - 1):
                total = total + ew_in[k, at, :].astype(F32)
            ref[pl.ds(group, 1)] = total[None]
            for r in range(n_loc - 1):
                ref[pl.ds(lax.rem(group - r - 1 + n_loc, n_loc), 1)] = ew_in[
                    size - 1 + r, at, :
                ].astype(F32)[None]
        freight.finish()

    await_hails(peers + e_peers + d_peers)
    bring.wait()
    expert_start()
    h = h_ref[...]
    a2 = a2_ref[...].astype(F32)
    g = g_ref[...]
    small = small_ref[...]
    value_one, value_two = vec_ref[2:3, :], vec_ref[3:4, :]
    tables, picks, w_pair, first, other = route_parts(
        routest_ref[...], small, n_ff, n_all, slots
    )
    copy_on, one_on, two_on = [
        [picks[k][:, n_ff + n : n_ff + n + 1] for k in range(2)] for n in (1, 2, 3)
    ]
    g_a2 = jnp.sum(g * a2, axis=1, keepdims=True)
    g_one = jnp.sum(g * value_one, axis=1, keepdims=True)
    g_two = jnp.sum(g * value_two, axis=1, keepdims=True)
    alpha = [copy_on[k] + one_on[k] * first[0] + two_on[k] * other[0] for k in range(2)]
    a_weight = alpha[0] * w_pair[0] + alpha[1] * w_pair[1]
    one_weight = one_on[0] * w_pair[0] + one_on[1] * w_pair[1]
    two_weight = two_on[0] * w_pair[0] + two_on[1] * w_pair[1]
    returned = [ret_ref[t].reshape(n_ff * slots, D) for t in range(2)]
    block = h
    d_weight = []
    for k in range(2):
        routed = dot(tables[k], returned[0], 0, 0)
        picked = (
            routed
            + alpha[k] * a2
            + (one_on[k] * first[1]) * value_one
            + (two_on[k] * other[1]) * value_two
        )
        block = block + w_pair[k] * picked
        d_weight.append(jnp.sum(g * picked, axis=1, keepdims=True))
    block_ref[...] = block
    center = w_pair[0] * d_weight[0] + w_pair[1] * d_weight[1]
    d_logits = (
        picks[0] * (w_pair[0] * (d_weight[0] - center))
        + picks[1] * (w_pair[1] * (d_weight[1] - center))
    )
    dprev_ref[...] = d_logits.T[:n_all, :]
    lane = lax.broadcasted_iota(jnp.int32, (rows, LANES), 1)
    d_small = d_logits
    for base, pair, weight, g_value in (
        (n_all, first, one_weight, g_one),
        (n_all + 2, other, two_weight, g_two),
    ):
        d_pair = (weight * g_a2, weight * g_value)
        middle = pair[0] * d_pair[0] + pair[1] * d_pair[1]
        for k in range(2):
            d_small = d_small + jnp.where(lane == base + k, pair[k] * (d_pair[k] - middle), 0.0)
    d_small = d_small.astype(BF16)
    d_const_one = jnp.sum((first[1] * one_weight) * g, axis=0, keepdims=True)
    d_const_two = jnp.sum((other[1] * two_weight) * g, axis=0, keepdims=True)
    d_a2 = (
        dot(tables[0] + tables[1], returned[1], 0, 0)
        + a_weight * g
        + dot(d_small, wsm_ref[...], 1, 1)
    )
    gain_two = vec_ref[1:2, :]
    inverse_two = lax.rsqrt(jnp.mean(h * h, axis=-1, keepdims=True) + EPS)
    d_gain_two = jnp.sum(d_a2 * h * inverse_two, axis=0, keepdims=True)
    scaled = gain_two * d_a2
    d_h = (
        g
        + inverse_two * scaled
        - h * inverse_two**3 * jnp.mean(scaled * h, axis=-1, keepdims=True)
    )
    d_hb = d_h.astype(BF16)
    dhg[pl.ds(c, 1)] = d_hb[None]
    gather = ContextGather(
        sizes,
        place,
        dhg.at[c],
        lambda k: dhg.at[k],
        lambda k: s_g.at[k],
        lambda k: r_g.at[k],
    )
    gather.start()
    dx_ref[...] = d_h
    expert_cross()
    early["mixed"].wait()
    g_o = dot(mixed_ref[...].reshape(n_c * hc, rows), d_hb)
    run = n_d * w_rows
    for b in range(n_c):
        for k in range(n_e):
            o_own[b, k, :run, :] = g_o[(k * n_c + b) * run : (k * n_c + b + 1) * run].astype(BF16)
    parcel = Courier(s_q, r_q)
    o_pair = {}
    for k in [*range(1, pairs), 0]:
        there = lax.rem(outer + k, pairs)
        o_pair[k] = parcel.carry(
            o_own.at[there * 2 + 1 - inner], o_in.at[there], peers[0]
        )
    o_state = {}

    def o_outer():
        o_state["outer"] = []
        for k in range(1, pairs):
            there = lax.rem(outer + k, pairs)
            o_pair[k].wait_recv()
            o_sum[k - 1] = (
                o_own[there * 2 + inner].astype(F32) + o_in[there].astype(F32)
            ).astype(BF16)
            o_state["outer"].append(
                parcel.carry(o_sum.at[k - 1], o_out.at[k - 1], peers[k])
            )

    def o_across():
        o_pair[0].wait_recv()
        total = o_own[c].astype(F32) + o_in[outer].astype(F32)
        for k, copy in enumerate(o_state["outer"]):
            copy.wait_recv()
            total = total + o_out[k].astype(F32)
        o_x[...] = total.astype(BF16)
        o_state["across"] = [
            parcel.carry(o_x.at[lax.rem(e + j, n_e)], o_xr.at[j - 1], e_peers[j - 1])
            for j in range(1, n_e)
        ]

    def o_along():
        total = o_x[e].astype(F32)
        for j, copy in enumerate(o_state["across"]):
            copy.wait_recv()
            total = total + o_xr[j].astype(F32)
        for k in range(n_d):
            o_z[k, :w_rows, :] = total[k * w_rows : (k + 1) * w_rows].astype(BF16)
        o_state["along"] = [
            parcel.carry(o_z.at[lax.rem(d + k, n_d)], o_zr.at[k - 1], d_peers[k - 1])
            for k in range(1, n_d)
        ]

    def o_end():
        total = o_z[d].astype(F32)
        for k, copy in enumerate(o_state["along"]):
            copy.wait_recv()
            total = total + o_zr[k].astype(F32)
        go_ref[...] = total[:w_rows]
        parcel.finish()

    if shift:
        d_small = jnp.concatenate(
            [jnp.zeros((rows, shift), BF16), d_small[:, : LANES - shift]], axis=1
        )
    g_small = dot(a2_ref[...], d_small, 0, 0)
    dk_acc[...] = jnp.zeros_like(dk_acc)
    dv_acc[...] = jnp.zeros_like(dv_acc)
    order = [(b, j) for b in reversed(range(n_c)) for j in range(hp)]

    def fetch(n):
        b, j = order[n]
        reach = pl.ds(0, (b + 1) * rows)
        return pltpu.make_async_copy(p_ref.at[j, b, reach], p_scr.at[n % 2, reach], p_sem.at[n % 2])

    fetch(0).start()
    gather.forward()
    gather.finish()
    o_outer()
    for name in ("wo", "kh", "vh", "qt"):
        early[name].wait()
    wo_part = wo_ref[pl.ds(pl.multiple_of(c * hc, hc), hc), :]
    for b in range(n_c):
        dht_scr[:, b * rows : (b + 1) * rows] = dot(wo_part, dhg[b], 1, 1).astype(BF16)
    for n, (b, j) in enumerate(order):
        reach = (b + 1) * rows
        head = slice(j * HEAD_DIM, (j + 1) * HEAD_DIM)
        mine_q = slice(b * rows, reach)
        if n == len(order) // 4:
            o_across()
        if n == len(order) // 2:
            o_along()
        if n + 1 < len(order):
            fetch(n + 1).start()
        fetch(n).wait()
        rounded = p_scr[n % 2, :reach, :]
        prob = rounded.astype(F32)
        d_o = dht_scr[head, mine_q]
        d_prob = dot(vh_ref[j, :reach, :], d_o)
        delta = jnp.sum(prob * d_prob, axis=0, keepdims=True)
        d_scores = (prob * (d_prob - delta)).astype(BF16)
        dqt[head, mine_q] = dot(kh_ref[j, :reach, :], d_scores, 0, 0) * HEAD_DIM**-0.5
        dk_acc[j, :reach, :] += dot(d_scores, qt_ref[head, mine_q], 1, 1)
        dv_acc[j, :reach, :] += dot(rounded, d_o, 1, 1)
    dqkv[:, :hc] = dqt[...].T.astype(BF16)
    for j in range(hp):
        at = j * HEAD_DIM
        dqkv[:, hc + at : hc + at + HEAD_DIM] = dk_acc[j].astype(BF16)
        dqkv[:, 2 * hc + at : 2 * hc + at + HEAD_DIM] = dv_acc[j].astype(BF16)
    dqkv[:, 3 * hc :] = jnp.zeros((length, dqkv.shape[1] - 3 * hc), BF16)
    d_all = dqkv[...]
    bag = Courier(s_t, r_t)
    across = {}
    early["a1"].wait()
    early["wqkv"].wait()
    g_all = dot(a1_ref[...], d_all, 0, 0)
    half = D // n_e

    def send_chunk(k, value):
        for n in range(n_e):
            t_send[k, n] = value[n * half : (n + 1) * half].astype(BF16)
        across[k] = [
            bag.carry(t_send.at[k, lax.rem(e + j, n_e)], t_recv.at[k, j - 1], e_peers[j - 1])
            for j in range(1, n_e)
        ]

    for k in range(chunks - 1):
        send_chunk(k, g_all[:, k * LANES : (k + 1) * LANES])
    wqkv = wqkv_ref[...]
    gain_one = vec_ref[0:1, :]
    d_gain_one = jnp.zeros((1, D), F32)
    for b in range(n_c):
        part = dot(d_all[b * rows : (b + 1) * rows, : 3 * hc], wqkv, 1, 1)
        dhg[b] = part.astype(BF16)
        if b + 1 < n_c:
            fetch_x(b + 1, (b + 1) % 2).start()
        fetch_x(b, b % 2).wait()
        x = x_scr[b % 2].astype(F32)
        inverse = lax.rsqrt(jnp.mean(x * x, axis=-1, keepdims=True) + EPS)
        d_gain_one = d_gain_one + jnp.sum(part * x * inverse, axis=0, keepdims=True)
    to_pair = []
    for k in [*range(1, pairs), 0]:
        there = lax.rem(outer + k, pairs)
        copy = remote(
            dhg.at[there * 2 + 1 - inner], da_in.at[there], s_d.at[k], r_d.at[k], peers[0]
        )
        copy.start()
        to_pair.append((k, copy))
    spot = lax.broadcasted_iota(jnp.int32, (LANES, D), 0)
    lines = jnp.zeros((LANES, D), F32)
    for n, row in enumerate((d_const_one, d_const_two, d_gain_one, d_gain_two)):
        lines = lines + jnp.where(spot == shift + n_all + 4 + n, row, 0.0)
    send_chunk(chunks - 1, g_all[:, (chunks - 1) * LANES :] + g_small + lines.T)
    along = []
    for k, copy in to_pair:
        if k == 0:
            continue
        there = lax.rem(outer + k, pairs)
        copy.wait_recv()
        da_sum[k - 1] = (
            dhg[there * 2 + inner].astype(F32) + da_in[there].astype(F32)
        ).astype(BF16)
        onward = remote(
            da_sum.at[k - 1],
            da_out.at[k - 1],
            s_d.at[pairs + k - 1],
            r_d.at[pairs + k - 1],
            peers[k],
        )
        onward.start()
        along.append(onward)
    down = {}
    for k in range(chunks):
        total = t_send[k, e].astype(F32)
        for j, copy in enumerate(across[k]):
            copy.wait_recv()
            total = total + t_recv[k, j].astype(F32)
        for n in range(n_d):
            t_z[k, n, : n_c * w_rows, :] = jnp.concatenate(
                [
                    total[(b * n_d + n) * w_rows : (b * n_d + n + 1) * w_rows]
                    for b in range(n_c)
                ],
                axis=0,
            ).astype(BF16)
        down[k] = [
            bag.carry(t_z.at[k, lax.rem(d + n, n_d)], t_zr.at[k, n - 1], d_peers[n - 1])
            for n in range(1, n_d)
        ]
    o_end()
    to_pair[-1][1].wait_recv()
    d_a1 = dhg[c].astype(F32) + da_in[outer].astype(F32)
    for k, copy in enumerate(along):
        copy.wait_recv()
        d_a1 = d_a1 + da_out[k].astype(F32)
    fetch_x(c, 2).wait()
    x = x_scr[2].astype(F32)
    inverse_one = lax.rsqrt(jnp.mean(x * x, axis=-1, keepdims=True) + EPS)
    scaled = gain_one * d_a1
    dx_ref[...] += inverse_one * scaled - x * inverse_one**3 * jnp.mean(
        scaled * x, axis=-1, keepdims=True
    )
    for k in range(chunks):
        total = t_z[k, d].astype(F32)
        for n, copy in enumerate(down[k]):
            copy.wait_recv()
            total = total + t_zr[k, n].astype(F32)
        for b in range(n_c):
            t_c[b, k, :w_rows, :] = total[b * w_rows : (b + 1) * w_rows]
    t_cr[pl.ds(c, 1)] = t_c[pl.ds(c, 1)]
    turned = [
        bag.carry(t_c.at[lax.rem(c + k, n_c)], t_cr.at[c], (e, lax.rem(c + k, n_c), d))
        for k in range(1, n_c)
    ]
    expert_end()
    for copy in turned:
        copy.wait_recv()
    s_total = jnp.zeros((w_rows, SMALL), F32)
    for b in range(n_c):
        line = jnp.concatenate([t_cr[b, k] for k in range(chunks)], axis=1)[:w_rows]
        for n, ref in enumerate((gq_ref, gk_ref, gv_ref)):
            width = min(hc, D - b * hc)
            if width > 0:
                ref[:, b * hc : b * hc + width] = line[:, n * hc : n * hc + width]
        s_total = s_total + line[:, 3 * hc : 3 * hc + SMALL]
    s_lines = jnp.concatenate([s_total, jnp.zeros((w_rows, LANES - SMALL), F32)], axis=1)
    s_lines = tall(s_lines, LANES).T
    at = 0
    for ref in (grouter_ref, gcoef_ref, gvalue_ref, ggains_ref):
        ref[...] = s_lines[at : at + ref.shape[0], :w_rows]
        at += ref.shape[0]
    bag.finish()
    for _, copy in to_pair:
        copy.wait_send()
    for copy in along:
        copy.wait_send()


def backward(sizes, cfg, *operands):
    n_e, n_c, n_d = sizes
    hp, n_ff, n_all, n_loc, slots = cfg
    hc = hp * HEAD_DIM
    rows = operands[1].shape[0]
    length = rows * n_c
    pairs = n_c // 2
    dma = pltpu.SemaphoreType.DMA
    vmem = pl.BlockSpec(memory_space=pltpu.VMEM)
    anywhere = pl.BlockSpec(memory_space=pl.ANY)
    shape = jax.ShapeDtypeStruct
    part = operands[17].shape[1]
    w_rows = D // (n_e * n_c * n_d)
    chunks = up_to(3 * hc + SMALL, LANES) // LANES
    run = up_to(n_d * w_rows, 16)
    turn = up_to(n_c * w_rows, 16)
    few = up_to(w_rows, 16)
    few_wide = up_to(w_rows, 8)
    size = n_d // n_loc
    loads = (size - 1) * n_loc + n_loc - 1
    bags = chunks * (n_e - 1 + n_d - 1) + n_c - 1
    parcels = 2 * pairs - 1 + n_e - 1 + n_d - 1
    n_more = max(1, pairs - 1)
    in_specs = [vmem] * len(operands)
    in_specs[15] = in_specs[16] = in_specs[17] = anywhere
    late = [operands[n] for n in (6, 7, 10, 11, 12, 13, 14)]
    for n in (6, 7, 10, 11, 12, 13, 14):
        in_specs[n] = anywhere
    return pl.pallas_call(
        functools.partial(back_kernel, sizes, cfg),
        out_shape=(
            shape((rows, D), F32),
            shape((rows, D), F32),
            shape((n_all, rows), F32),
            *[shape((w_rows, D), F32)] * 4,
            *[shape((n, w_rows), F32) for n in (n_all, 4, 2, 2)],
            *[shape((n_loc, part // 3, LANES), F32)] * 3,
        ),
        in_specs=in_specs,
        out_specs=(vmem,) * 14,
        scratch_shapes=[
            pltpu.VMEM((n_c, rows, D), BF16),
            pltpu.VMEM((hc, length), BF16),
            pltpu.VMEM((2, length, rows), BF16),
            pltpu.VMEM((hp, length, HEAD_DIM), F32),
            pltpu.VMEM((hp, length, HEAD_DIM), F32),
            pltpu.VMEM((hc, length), F32),
            pltpu.VMEM((length, chunks * LANES), BF16),
            pltpu.VMEM((pairs, rows, D), BF16),
            pltpu.VMEM((n_more, rows, D), BF16),
            pltpu.VMEM((n_more, rows, D), BF16),
            pltpu.VMEM((3, rows, D), BF16),
            pltpu.VMEM((n_d, part, LANES), BF16),
            pltpu.VMEM((size + n_loc - 2, part, LANES), BF16),
            pltpu.VMEM((max(1, size - 1), max(1, n_loc - 1), part, LANES), BF16),
            pltpu.VMEM((max(1, n_loc - 1), part, LANES), BF16),
            pltpu.VMEM((chunks, n_e, D // n_e, LANES), BF16),
            pltpu.VMEM((chunks, n_e - 1, D // n_e, LANES), BF16),
            pltpu.VMEM((chunks, n_d, turn, LANES), BF16),
            pltpu.VMEM((chunks, n_d - 1, turn, LANES), BF16),
            pltpu.VMEM((n_c, chunks, few_wide, LANES), F32),
            pltpu.VMEM((n_c, chunks, few_wide, LANES), F32),
            pltpu.VMEM((n_c, n_e, run, D), BF16),
            pltpu.VMEM((pairs, n_e, run, D), BF16),
            pltpu.VMEM((n_more, n_e, run, D), BF16),
            pltpu.VMEM((n_more, n_e, run, D), BF16),
            pltpu.VMEM((n_e, run, D), BF16),
            pltpu.VMEM((n_e - 1, run, D), BF16),
            pltpu.VMEM((n_d, few, D), BF16),
            pltpu.VMEM((n_d - 1, few, D), BF16),
            dma((5,)),
            dma((n_c - 1,)),
            dma((n_c - 1,)),
            dma((2,)),
            dma((n_c,)),
            dma((n_c,)),
            dma((loads,)),
            dma((loads,)),
            dma((bags,)),
            dma((bags,)),
            dma((parcels,)),
            dma((parcels,)),
            *[pltpu.VMEM(w.shape, w.dtype) for w in late],
            dma((len(late),)),
        ],
        compiler_params=pltpu.CompilerParams(
            collective_id=1, has_side_effects=True, vmem_limit_bytes=VMEM_LIMIT
        ),
        name="backward",
    )(*operands)


def hand_out_kernel(*refs):
    count = (len(refs) - 2) // 3
    sources, results, held = refs[:count], refs[count : 2 * count], refs[2 * count : 3 * count]
    in_sems, out_sems = refs[-2:]
    takes = [pltpu.make_async_copy(sources[n], held[n], in_sems.at[n]) for n in range(count)]
    gives = [pltpu.make_async_copy(held[n], results[n], out_sems.at[n]) for n in range(count)]
    for copy in takes:
        copy.start()
    for take, give in zip(takes, gives):
        take.wait()
        give.start()
    for copy in gives:
        copy.wait()


def hand_out(results):
    anywhere = pl.BlockSpec(memory_space=pl.ANY)
    dma = pltpu.SemaphoreType.DMA((len(results),))
    return pl.pallas_call(
        hand_out_kernel,
        out_shape=tuple(jax.ShapeDtypeStruct(r.shape, r.dtype) for r in results),
        in_specs=[anywhere] * len(results),
        out_specs=(anywhere,) * len(results),
        scratch_shapes=[*[pltpu.VMEM(r.shape, r.dtype) for r in results], dma, dma],
        compiler_params=pltpu.CompilerParams(vmem_limit_bytes=VMEM_LIMIT),
        name="hand_out",
    )(*results)


def body(
    tokens,
    doc_ids,
    routes,
    prev_logits,
    cotangent,
    w_query,
    w_key,
    w_value,
    w_out,
    w_router,
    const_coef,
    const_value,
    norm_gains,
    expert_gate,
    expert_up,
    expert_down,
):
    sizes = n_e, n_c, n_d = tuple(lax.axis_size(axis) for axis in ALL_AXES)
    rows = tokens.shape[1]
    length = doc_ids.shape[1]
    n_loc, _, units = expert_gate.shape
    n_ff = n_loc * n_e
    n_all = w_router.shape[1]
    slots = rows // 4
    hp = -(-HEADS // n_c)
    cfg = (hp, n_ff, n_all, n_loc, slots)
    routes_t = routes[0].T
    upstream = cotangent[0]
    (
        x_all,
        wqkv,
        wo,
        wsm,
        vec,
        a1,
        q_t,
        k_h,
        v_h,
        mixed,
        h,
        a2,
        small,
        grads,
        returned,
        probs,
        *_,
    ) = front(
        sizes,
        cfg,
        w_query,
        w_key,
        w_value,
        w_out,
        w_router.T,
        const_coef.T,
        const_value.T,
        norm_gains.T,
        tokens[0],
        expert_gate,
        expert_up,
        expert_down,
        doc_ids,
        routes_t,
        prev_logits[0].T,
        upstream,
    )
    results = backward(
        sizes,
        cfg,
        returned,
        h,
        a2,
        small,
        upstream,
        routes_t,
        wo,
        wqkv,
        wsm,
        vec,
        mixed,
        a1,
        q_t,
        k_h,
        v_h,
        probs,
        x_all,
        grads.reshape(n_d, 3 * D * units // LANES, LANES),
    )
    block_rows, d_x, d_prev, *square = hand_out(results)
    narrow = square[4:8]
    return (
        block_rows[None],
        d_x[None],
        d_prev.T[None],
        *square[:4],
        *[grad.T for grad in narrow],
        *[grad.reshape(n_loc, D, units) for grad in square[8:]],
    )


def solution(mesh):
    rows = P(("expert", "dp"), "context", None)
    weights = P(ALL_AXES, None)
    units = P("expert", None, ("context", "dp"))
    return jax.shard_map(
        body,
        mesh=mesh,
        in_specs=(rows, P(("expert", "dp"), None), rows, rows, rows)
        + (weights,) * 8
        + (units,) * 3,
        out_specs=(rows,) * 3 + (weights,) * 8 + (units,) * 3,
        check_vma=False,
    )
```

```python
import functools

import jax
import jax.numpy as jnp
from jax import lax
from jax.experimental import pallas as pl
from jax.experimental.pallas import tpu as pltpu
from jax.sharding import PartitionSpec as P

D = 768
HEADS = 12
HEAD_DIM = 64
EPS = 1e-06
SMALL = 64
LANES = 128
VMEM_LIMIT = 63 * 2**20
MESH = pl.DeviceIdType.MESH
F32 = jnp.float32
BF16 = jnp.bfloat16
ALL_AXES = ("expert", "context", "dp")


def dot(left, right, left_dim=1, right_dim=0):
    return lax.dot_general(
        left, right, (((left_dim,), (right_dim,)), ((), ())), preferred_element_type=F32
    )


def position():
    return lax.axis_index("expert"), lax.axis_index("context"), lax.axis_index("dp")


def remote(src, dst, send_sem, recv_sem, device):
    return pltpu.make_async_remote_copy(
        src_ref=src,
        dst_ref=dst,
        send_sem=send_sem,
        recv_sem=recv_sem,
        device_id=device,
        device_id_type=MESH,
    )


def hail(devices):
    barrier = pltpu.get_barrier_semaphore()
    for device in devices:
        pl.semaphore_signal(barrier, inc=1, device_id=device, device_id_type=MESH)


def await_hails(devices):
    pl.semaphore_wait(pltpu.get_barrier_semaphore(), len(devices))


def context_peers(sizes, place):
    e, c, d = place
    pairs = sizes[1] // 2
    outer, inner = c // 2, c % 2
    peers = [(e, outer * 2 + 1 - inner, d)]
    for k in range(1, pairs):
        peers.append((e, lax.rem(outer + k, pairs) * 2 + inner, d))
    return peers


def expert_peers(sizes, place):
    e, c, d = place
    return [(lax.rem(e + j, sizes[0]), c, d) for j in range(1, sizes[0])]


def crossing_only(sizes, n_loc, place):
    _, there, _ = homes(sizes, n_loc, place)
    return [device for j, (_, device) in enumerate(there) if j // n_loc and j % n_loc]


def homes(sizes, n_loc, place):
    n_e, n_c, n_d = sizes
    e, c, d = place
    size = n_d // n_loc
    group, seat = d // size, lax.rem(d, size)
    there, back = [], []
    for j in range(n_e * n_loc):
        je, jg = j // n_loc, j % n_loc
        to_e, to_g = lax.rem(e + je, n_e), lax.rem(group + jg, n_loc)
        from_e, from_g = lax.rem(e - je + n_e, n_e), lax.rem(group - jg + n_loc, n_loc)
        there.append((to_e * n_loc + to_g, (to_e, c, to_g * size + seat)))
        back.append(from_e * n_loc + from_g)
    return e * n_loc + group, there, back


class Courier:
    def __init__(self, send, recv):
        self.send, self.recv = send, recv
        self.copies = []

    def carry(self, src, dst, device):
        n = len(self.copies)
        copy = remote(src, dst, self.send.at[n], self.recv.at[n], device)
        copy.start()
        self.copies.append(copy)
        return copy

    def finish(self):
        for copy in self.copies:
            copy.wait_send()


def up_to(count, step):
    return -(-count // step) * step


class ContextGather:
    def __init__(self, sizes, place, own, slot, send, recv):
        e, c, d = place
        self.pairs = sizes[1] // 2
        self.place, self.own, self.slot = place, own, slot
        self.send, self.recv = send, recv
        self.outer, self.inner = c // 2, c % 2
        self.peers = context_peers(sizes, place)
        self.copies = []
        self.forwards = []

    def start(self):
        for k in [*range(1, self.pairs), 0]:
            copy = remote(
                self.own, self.slot(self.place[1]), self.send(k), self.recv(k), self.peers[k]
            )
            copy.start()
            self.copies.append((k, copy))

    def origin(self, k):
        return lax.rem(self.outer - k + self.pairs, self.pairs) * 2 + self.inner

    def forward(self):
        for k, copy in self.copies:
            if k > 0:
                copy.wait_recv()
                block = self.slot(self.origin(k))
                n = self.pairs - 1 + k
                onward = remote(block, block, self.send(n), self.recv(n), self.peers[0])
                onward.start()
                self.forwards.append(onward)

    def finish(self):
        for k, copy in self.copies:
            if k == 0:
                copy.wait_recv()
            copy.wait_send()
        for copy in self.forwards:
            copy.wait()


class Spread:
    def __init__(self, sizes, place, courier, own, slot):
        self.sizes, self.place, self.courier = sizes, place, courier
        self.slot = slot
        n_e, n_c, n_d = sizes
        e, c, d = place
        self.across_to = expert_peers(sizes, place)
        self.along = [
            courier.carry(own, slot(e, d), (e, c, lax.rem(d + k, n_d))) for k in range(1, n_d)
        ]
        self.across = [courier.carry(own, slot(e, d), device) for device in self.across_to]

    def onward(self):
        e, c, d = self.place
        n_d = self.sizes[2]
        for k in range(1, n_d):
            self.along[k - 1].wait_recv()
            block = self.slot(e, lax.rem(d - k + n_d, n_d))
            for device in self.across_to:
                self.across.append(self.courier.carry(block, block, device))

    def arrive(self):
        for copy in self.across:
            copy.wait_recv()


def spread_count(sizes):
    n_e, n_c, n_d = sizes
    return (n_d - 1) + (n_e - 1) * n_d


def softmax_pair(left, right):
    top = jnp.maximum(left, right)
    left, right = jnp.exp(left - top), jnp.exp(right - top)
    total = left + right
    return left / total, right / total


def tall(array, height):
    if array.shape[0] == height:
        return array
    return jnp.concatenate(
        [array, jnp.zeros((height - array.shape[0], *array.shape[1:]), array.dtype)], axis=0
    )


def route_parts(routes_t, small, n_ff, n_all, slots):
    rows = routes_t.shape[1]
    routes = tall(routes_t.astype(F32), LANES).T
    hot = lax.broadcasted_iota(jnp.int32, (LANES, rows), 0)
    marks = [(hot == routes_t[k : k + 1, :]) & (hot < n_ff) for k in range(2)]
    both = (marks[0] | marks[1]).astype(F32)
    earlier = lax.broadcasted_iota(jnp.int32, (rows, rows), 0) < lax.broadcasted_iota(
        jnp.int32, (rows, rows), 1
    )
    rank = dot(both.astype(BF16), earlier.astype(F32).astype(BF16))
    number = lax.broadcasted_iota(jnp.int32, (slots, rows), 0).astype(F32)
    tables = []
    for k in range(2):
        wanted = jnp.where(marks[k], rank, -1.0)
        tables.append(
            jnp.concatenate(
                [(number == wanted[j : j + 1, :]).astype(F32) for j in range(n_ff)], axis=0
            ).astype(BF16)
        )
    lane = lax.broadcasted_iota(jnp.int32, (rows, LANES), 1)
    picks = [(lane.astype(F32) == routes[:, k : k + 1]).astype(F32) for k in range(2)]
    chosen = [
        jnp.sum(jnp.where(picks[k] > 0, small, 0.0), axis=1, keepdims=True) for k in range(2)
    ]
    w_pair = softmax_pair(chosen[0], chosen[1])
    first = softmax_pair(small[:, n_all : n_all + 1], small[:, n_all + 1 : n_all + 2])
    second = softmax_pair(small[:, n_all + 2 : n_all + 3], small[:, n_all + 3 : n_all + 4])
    return tables, picks, w_pair, first, second


def front_kernel(
    sizes,
    cfg,
    wq_ref,
    wk_ref,
    wv_ref,
    wout_ref,
    router_ref,
    coef_ref,
    value_ref,
    gains_ref,
    xown_ref,
    gate_ref,
    up_ref,
    down_ref,
    drow_ref,
    routest_ref,
    prev_ref,
    g_ref,
    xg_out,
    wqkv_out,
    wo_out,
    wsm_out,
    vec_out,
    a1_out,
    qt_out,
    kh_out,
    vh_out,
    mixed_out,
    h_out,
    a2_out,
    small_out,
    gw_out,
    back_ref,
    p_ref,
    slots_ref,
    res,
    inn,
    osum,
    outr,
    stage,
    blk,
    gate_scr,
    up_scr,
    hid_scr,
    acc_scr,
    ew_ref,
    small_scr,
    row_scr,
    a_ref,
    ow_ref,
    ag,
    og,
    ew_own,
    o_scr,
    vt_scr,
    p_scr,
    sbuf,
    xin,
    p_sem,
    s_o,
    r_o,
    s_x,
    r_x,
    s_g,
    r_g,
    l_g,
    s_c,
    r_c,
    s_ow,
    r_ow,
    s_xg,
    r_xg,
    b_sem,
    s_in,
    r_in,
    s_out,
    r_out,
    s_h,
    r_h,
    xg_ref,
    wqkv_ref,
    wo_ref,
    wsm_ref,
    vec_ref,
    a1_ref,
    qt_ref,
    kh_ref,
    vh_ref,
    mixed_ref,
    h_ref,
    a2_ref,
    small_ref,
    gw_ref,
    o_sem,
):
    n_e, n_c, n_d = sizes
    hp, n_ff, n_all, n_loc, slots = cfg
    hc = hp * HEAD_DIM
    place = e, c, d = position()
    rows = xown_ref.shape[0]
    length = rows * n_c
    c_all = [(e, lax.rem(c + k, n_c), d) for k in range(1, n_c)]
    n_s = n_e * n_loc
    me, there, back = homes(sizes, n_loc, place)
    d_peers = [(e, c, lax.rem(d + k, n_d)) for k in range(1, n_d)]
    neighbours = (
        c_all + d_peers + expert_peers(sizes, place) + crossing_only(sizes, n_loc, place)
    )
    hail(neighbours)
    leaving = []

    def leave(*pairs_of):
        for src, dst in pairs_of:
            copy = pltpu.make_async_copy(src, dst, o_sem.at[len(leaving)])
            copy.start()
            leaving.append(copy)

    w_rows = wq_ref.shape[0]
    small_scr[...] = jnp.zeros_like(small_scr)
    at = 0
    for ref in (router_ref, coef_ref, value_ref, gains_ref):
        small_scr[at : at + ref.shape[0], :w_rows] = ref[...]
        at += ref.shape[0]
    width = row_scr.shape[1]
    w_small = small_scr[...].T[:w_rows, :SMALL]

    def stack(rows_of, tiles, height):
        parts = [rows_of(k * LANES) for k in range(tiles)]
        return tall(jnp.concatenate(parts, axis=0), height).astype(BF16)

    ow_ref[...] = stack(lambda at: wout_ref[:, at : at + LANES], D // LANES, ow_ref.shape[0])
    row_scr[...] = jnp.zeros_like(row_scr)
    row_scr[:w_rows, 3 * hc : 3 * hc + SMALL] = w_small
    for b in range(n_c):
        for n, ref in enumerate((wq_ref, wk_ref, wv_ref)):
            wide = max(0, min(hc, D - b * hc))
            if wide > 0:
                row_scr[:w_rows, n * hc : n * hc + wide] = ref[:, b * hc : b * hc + wide]
            if wide < hc:
                row_scr[:w_rows, n * hc + wide : (n + 1) * hc] = jnp.zeros((w_rows, hc - wide), F32)
        a_ref[b] = stack(
            lambda at: row_scr[:w_rows, at : at + LANES], width // LANES, a_ref.shape[1]
        )
    await_hails(neighbours)
    post = Courier(s_c, r_c)
    turned = [
        post.carry(a_ref.at[lax.rem(c + k, n_c)], ag.at[e, c, d], device)
        for k, device in enumerate(c_all, 1)
    ]
    x_rows = ContextGather(
        sizes,
        place,
        xown_ref,
        lambda k: xg_ref.at[k],
        lambda k: s_xg.at[k],
        lambda k: r_xg.at[k],
    )
    x_rows.start()
    ow_spread = Spread(sizes, place, post, ow_ref, lambda j, k: og.at[j, c, k])
    ag[e, c, d] = a_ref[c]
    og[e, c, d] = ow_ref[...]
    xg_ref[pl.ds(c, 1)] = xown_ref[...][None]
    for n, ref in enumerate((gate_ref, up_ref, down_ref)):
        ew_own[:, n] = ref[...].astype(BF16)
    for copy in turned:
        copy.wait_recv()
    a_spread = Spread(sizes, place, post, ag.at[e, :, d], lambda j, k: ag.at[j, :, k])
    size = n_d // n_loc
    group, seat = d // size, lax.rem(d, size)
    mates = [(e, c, group * size + lax.rem(seat + k, size)) for k in range(1, size)]
    keep_w = pltpu.make_async_copy(ew_own.at[group], ew_ref.at[d], l_g.at[2 * n_s])
    keep_w.start()
    w_far = {}
    for n in range(3):
        for k in range(1, n_loc):
            to = lax.rem(group + k, n_loc)
            w_far[n, k] = post.carry(
                ew_own.at[to, n], ew_ref.at[d, n], (e, c, to * size + seat)
            )
    w_near = [post.carry(ew_own.at[group], ew_ref.at[d], device) for device in mates]

    def pass_weights(n):
        for k in range(1, n_loc):
            w_far[n, k].wait_recv()
            block = ew_ref.at[lax.rem(group - k + n_loc, n_loc) * size + seat, n]
            w_near.extend([post.carry(block, block, device) for device in mates])

    ow_spread.onward()
    x_rows.forward()
    ow_spread.arrive()
    ow_rows = ContextGather(
        sizes,
        place,
        og.at[:, c],
        lambda k: og.at[:, k],
        lambda k: s_ow.at[k],
        lambda k: r_ow.at[k],
    )
    ow_rows.start()
    a_spread.onward()
    x_rows.finish()
    leave((xg_ref, xg_out))
    a_spread.arrive()

    def unstack(slabs, tiles):
        height = slabs.shape[2]
        slabs = slabs.reshape(n_c * n_d, height, LANES)
        if w_rows % 8 == 0:
            wide = [slabs[n].astype(F32) for n in range(n_c * n_d)]
            return jnp.concatenate(
                [
                    jnp.concatenate([w[k * w_rows : (k + 1) * w_rows] for w in wide], axis=0)
                    for k in range(tiles)
                ],
                axis=1,
            )
        flat = slabs.reshape(n_c * n_d * height, LANES)
        at_row = lax.broadcasted_iota(jnp.int32, (D // n_e, flat.shape[0]), 0)
        at_slab = lax.broadcasted_iota(jnp.int32, (D // n_e, flat.shape[0]), 1)
        first = at_row // w_rows * height + lax.rem(at_row, w_rows)
        return jnp.concatenate(
            [
                dot(jnp.where(at_slab == first + k * w_rows, 1.0, 0.0).astype(BF16), flat)
                for k in range(tiles)
            ],
            axis=1,
        )

    weights = jnp.concatenate([unstack(ag[k], width // LANES) for k in range(n_e)], axis=0)
    wqkv = weights[:, : 3 * hc].astype(BF16)
    wqkv_ref[...] = wqkv
    w_small = jnp.concatenate(
        [weights[:, 3 * hc : 3 * hc + SMALL], jnp.zeros((D, LANES - SMALL), F32)], axis=1
    )
    wsm_ref[...] = w_small.astype(BF16)
    w_lines = w_small.T
    vec_ref[0:2, :] = w_lines[n_all + 6 : n_all + 8, :]
    vec_ref[2:4, :] = w_lines[n_all + 4 : n_all + 6, :]
    vec_ref[4:8, :] = jnp.zeros((4, D), F32)

    gain_one = vec_ref[0:1, :]
    for b in range(n_c):
        x = xg_ref[b].astype(F32)
        inverse = lax.rsqrt(jnp.mean(x * x, axis=-1, keepdims=True) + EPS)
        a1_ref[b * rows : (b + 1) * rows, :] = (x * inverse * gain_one).astype(BF16)
    a1 = a1_ref[...]
    leave((a1_ref, a1_out), (wqkv_ref, wqkv_out), (wsm_ref, wsm_out), (vec_ref, vec_out))
    ow_rows.forward()
    q_t = dot(wqkv[:, :hc], a1, 0, 1).astype(BF16) * jnp.asarray(HEAD_DIM**-0.5, BF16)
    qt_ref[...] = q_t
    kv = dot(a1, wqkv[:, hc:]).astype(BF16)
    for j in range(hp):
        kh_ref[j] = kv[:, j * HEAD_DIM : (j + 1) * HEAD_DIM]
        vh_ref[j] = kv[:, hc + j * HEAD_DIM : hc + (j + 1) * HEAD_DIM]
    vt_scr[...] = dot(wqkv[:, 2 * hc :], a1, 0, 1).astype(BF16)

    leave((qt_ref, qt_out), (kh_ref, kh_out), (vh_ref, vh_out))
    pass_weights(0)
    documents = drow_ref[...].astype(F32)
    document_of = jnp.broadcast_to(documents, (LANES, length)).T[:, :1]
    turn = 0
    p_copies = {}
    for b in reversed(range(n_c)):
        reach = (b + 1) * rows
        key_place = lax.broadcasted_iota(jnp.int32, (reach, rows), 0)
        q_place = lax.broadcasted_iota(jnp.int32, (reach, rows), 1) + b * rows
        allowed = (document_of[:reach] == documents[:, b * rows : reach]) & (key_place <= q_place)
        bias = jnp.where(allowed, 0.0, -1e30)
        for j in range(hp):
            head = slice(j * HEAD_DIM, (j + 1) * HEAD_DIM)
            scores = dot(kh_ref[j, :reach, :], qt_ref[head, b * rows : reach]) + bias
            top = jnp.max(scores, axis=0, keepdims=True)
            exponent = jnp.exp(scores - top)
            total = jnp.sum(exponent, axis=0, keepdims=True)
            rounded = (exponent * (1.0 / total)).astype(BF16)
            slot = turn % 2
            if turn >= 2:
                p_copies[turn - 2].wait()
            p_scr[slot, :reach, :] = rounded
            copy = pltpu.make_async_copy(
                p_scr.at[slot, pl.ds(0, reach)], p_ref.at[j, b, pl.ds(0, reach)], p_sem.at[slot]
            )
            copy.start()
            p_copies[turn] = copy
            turn += 1
            o_scr[b, head, :] = dot(vt_scr[head, :reach], rounded).astype(BF16)

        @pl.when(c != b)
        def _():
            remote(
                o_scr.at[b], mixed_ref.at[c], s_o.at[b], r_o.at[c], (e, b, d)
            ).start()

    pass_weights(1)
    for n in range(max(0, turn - 2), turn):
        p_copies[n].wait()
    ow_rows.finish()
    if n_c * hc > D:
        wo_ref[D:, :] = jnp.zeros((n_c * hc - D, D), BF16)
    for k in range(n_e):
        wo_ref[k * (D // n_e) : (k + 1) * (D // n_e), :] = unstack(og[k], D // LANES).astype(BF16)
    mixed_ref[pl.ds(c, 1)] = o_scr[pl.ds(c, 1)]
    for b in range(n_c):

        @pl.when(c != b)
        def _():
            copy = remote(o_scr.at[b], mixed_ref.at[b], s_o.at[b], r_o.at[b], (e, b, d))
            copy.wait_send()
            copy.wait_recv()

    leave((wo_ref, wo_out), (mixed_ref, mixed_out))
    mixed = mixed_ref[...].reshape(n_c * hc, rows)
    h = xown_ref[...].astype(F32) + dot(mixed, wo_ref[...], 0, 0)
    h_ref[...] = h
    inverse = lax.rsqrt(jnp.mean(h * h, axis=-1, keepdims=True) + EPS)
    a2 = (h * inverse * vec_ref[1:2, :]).astype(BF16)
    a2_ref[...] = a2
    small = dot(a2, wsm_ref[...]) + tall(prev_ref[...], LANES).T
    small_ref[...] = small
    leave((h_ref, h_out), (a2_ref, a2_out), (small_ref, small_out))
    tables, _, w_pair, _, _ = route_parts(routest_ref[...], small, n_ff, n_all, slots)
    crossing = {}
    gathers = {}
    g = g_ref[...]
    for t in range(2):
        if t == 0:
            block = dot(tables[0] + tables[1], a2).astype(BF16)
        else:
            block = dot(tables[0], (w_pair[0] * g).astype(BF16)) + dot(
                tables[1], (w_pair[1] * g).astype(BF16)
            )
            block = block.astype(BF16)
        for k in range(n_s):
            sbuf[t, k] = block[k * slots : (k + 1) * slots, :]
        for j in reversed(range(1, n_s)):
            n = t * n_s + j
            part, device = there[j]
            copy = remote(sbuf.at[t, part], xin.at[t, me], s_x.at[n], r_x.at[n], device)
            copy.start()
            crossing[t, j] = copy

        def gather(j, own, t=t):
            src = back[j]
            base = (t * n_s + j) * (n_c - 1)
            keep = pltpu.make_async_copy(own, slots_ref.at[c, t, src], l_g.at[t * n_s + j])
            keep.start()
            made = ContextGather(
                sizes,
                place,
                own,
                lambda k: slots_ref.at[k, t, src],
                lambda k: s_g.at[base + k],
                lambda k: r_g.at[base + k],
            )
            made.start()
            gathers[t, j] = (made, keep)

        gather(0, sbuf.at[t, me])
        crossing[t, 0] = gather
    for t in range(2):
        for j in range(1, n_s):
            crossing[t, j].wait_recv()
            crossing[t, 0](j, xin.at[t, back[j]])
        if t == 0:
            pass_weights(2)

    def gathered(t):
        for j in range(n_s):
            gathers[t, j][0].forward()
        for j in range(n_s):
            gathers[t, j][0].finish()
            gathers[t, j][1].wait()

    roomy = len(stage.shape) == 2
    take = blk.shape[1]
    blocks = n_c // take
    pairs = n_c // 2
    outer, inner = c // 2, c % 2
    peers = context_peers(sizes, place)

    def load_rows(t, n):
        if roomy:
            return slots_ref[n * take : (n + 1) * take, t].reshape(-1, D)
        copy = pltpu.make_async_copy(slots_ref.at[pl.ds(n * take, take), t], blk.at[t], b_sem.at[0])
        copy.start()
        copy.wait()
        return blk[t].reshape(-1, D)

    def store_rows(t, n, value):
        value = value.astype(BF16).reshape(take, n_s, slots, D)
        if roomy:
            res[n * take : (n + 1) * take, t] = value
        else:
            blk[2] = value
            copy = pltpu.make_async_copy(blk.at[2], res.at[pl.ds(n * take, take), t], b_sem.at[0])
            copy.start()
            copy.wait()

    def load(ref, slot=0):
        if roomy:
            return ref[...].astype(F32)
        copy = pltpu.make_async_copy(ref, stage.at[slot], b_sem.at[0])
        copy.start()
        copy.wait()
        return stage[slot].astype(F32)

    def store(ref, value):
        if roomy:
            ref[...] = value
        else:
            stage[3] = value
            copy = pltpu.make_async_copy(stage.at[3], ref, b_sem.at[0])
            copy.start()
            copy.wait()

    order = [*reversed(range(1, n_s)), 0]
    to_pair, along, home = {}, {}, {}

    def sum_pair(t):
        for j in order:
            src = there[j][0]
            for k in [*range(1, pairs), 0]:
                n = (t * n_s + j) * pairs + k
                far = lax.rem(outer + k, pairs)
                copy = remote(
                    res.at[far * 2 + 1 - inner, t, src],
                    inn.at[far, t, src],
                    s_in.at[n],
                    r_in.at[n],
                    peers[0],
                )
                copy.start()
                to_pair[t, j, k] = copy

    def sum_along(t):
        for j in order:
            src = there[j][0]
            for k in range(1, pairs):
                n = (t * n_s + j) * pairs + k
                far = lax.rem(outer + k, pairs)
                to_pair[t, j, k].wait_recv()
                value = load(res.at[far * 2 + inner, t, src]) + load(inn.at[far, t, src], 1)
                store(osum.at[k - 1, t, src], value.astype(BF16))
                copy = remote(
                    osum.at[k - 1, t, src],
                    outr.at[k - 1, t, src],
                    s_out.at[n],
                    r_out.at[n],
                    peers[k],
                )
                copy.start()
                along[t, j, k] = copy

    def send_home(t):
        for j in order:
            src, device = there[j]
            to_pair[t, j, 0].wait_recv()
            value = load(res.at[c, t, src]) + load(inn.at[outer, t, src], 1)
            for k in range(1, pairs):
                along[t, j, k].wait_recv()
                value = value + load(outr.at[k - 1, t, src], 2)
            if j == 0:
                back_ref[t, me] = value.astype(BF16)
            else:
                xin[t, src] = value.astype(BF16)
                n = t * n_s + j
                copy = remote(xin.at[t, src], back_ref.at[t, me], s_h.at[n], r_h.at[n], device)
                copy.start()
                home[t, j] = copy

    gathered(0)
    for copy in w_near:
        copy.wait_recv()
    keep_w.wait()
    parts, units = ew_ref.shape[0], ew_ref.shape[3]
    gate, up, down = [
        jnp.concatenate([ew_ref[k, n] for k in range(parts)], axis=1) for n in range(3)
    ]
    def hidden_of(n):
        x = load_rows(0, n)
        gate_pre = dot(x, gate)
        up_pre = dot(x, up)
        return gate_pre, up_pre, (gate_pre * jax.nn.sigmoid(gate_pre) * up_pre).astype(BF16)

    for n in range(blocks):
        gate_pre, up_pre, hidden = hidden_of(n)
        if blocks == 1:
            gate_scr[...] = gate_pre
            up_scr[...] = up_pre
            hid_scr[...] = hidden
        store_rows(0, n, dot(hidden, down, 1, 1))
    sum_pair(0)
    gathered(1)
    for n in range(blocks):
        dy = load_rows(1, n)
        d_hidden = dot(dy, down)
        if n == 0:
            sum_along(0)
        if blocks == 1:
            gate_pre, up_pre, hidden = gate_scr[...], up_scr[...], hid_scr[...]
        else:
            gate_pre, up_pre, hidden = hidden_of(n)
        sig = jax.nn.sigmoid(gate_pre)
        d_gate = (d_hidden * up_pre * sig * (1.0 + gate_pre * (1.0 - sig))).astype(BF16)
        d_up = (d_hidden * gate_pre * sig).astype(BF16)
        store_rows(1, n, dot(d_gate, gate, 1, 1) + dot(d_up, up, 1, 1))
        if n == blocks - 1:
            sum_pair(1)
        x = load_rows(0, n)
        for m, (left, right) in enumerate(((x, d_gate), (x, d_up), (dy, hidden))):
            part = dot(left, right, 0, 0)
            if blocks > 1:
                if n > 0:
                    part = part + acc_scr[m]
                if n < blocks - 1:
                    acc_scr[m] = part
            if n == blocks - 1:
                for k in range(parts):
                    gw_ref[k, m] = part[:, k * units : (k + 1) * units].astype(BF16)
                leave((gw_ref.at[:, m], gw_out.at[:, m]))
            if n == blocks - 1 and m == 0:
                sum_along(1)
            if n == blocks - 1 and m == 1:
                send_home(0)
    send_home(1)
    for copy in home.values():
        copy.wait()
    for copy in [*to_pair.values(), *along.values()]:
        copy.wait_send()
    for t in range(2):
        for j in range(1, n_s):
            crossing[t, j].wait_send()
    post.finish()
    for copy in leaving:
        copy.wait()


def front(sizes, cfg, *operands):
    n_e, n_c, n_d = sizes
    hp, n_ff, n_all, n_loc, slots = cfg
    hc = hp * HEAD_DIM
    rows = operands[8].shape[0]
    length = rows * n_c
    w_rows = operands[0].shape[0]
    width = up_to(3 * hc + SMALL, LANES)
    a_rows = up_to(width // LANES * w_rows, 16)
    o_rows = up_to(D // LANES * w_rows, 16)
    units = operands[9].shape[2]
    size = n_d // n_loc
    posts = (n_c - 1) + 2 * spread_count(sizes) + size - 1 + 3 * (n_loc - 1) * size
    n_s = n_e * n_loc
    dma = pltpu.SemaphoreType.DMA
    vmem = pl.BlockSpec(memory_space=pltpu.VMEM)
    anywhere = pl.BlockSpec(memory_space=pl.ANY)
    shape = jax.ShapeDtypeStruct
    gathers = 2 * n_s * (n_c - 1)
    pairs = n_c // 2
    more = max(1, pairs - 1)
    wide = [(n_c, 2), (n_c, 2), (pairs, 2), (more, 2), (more, 2)]
    wide = [(*dims, n_s, slots, D) for dims in wide]
    roomy = n_c * n_s * slots * D <= 2**20
    held = [pltpu.VMEM(dims, BF16) for dims in wide] if roomy else []
    extra = [] if roomy else [shape(dims, BF16) for dims in wide]
    take = n_c if n_c * n_s * slots <= 1024 else max(1, 512 // (n_s * slots))
    kept = (
        shape((n_c, rows, D), BF16),
        shape((D, 3 * hc), BF16),
        shape((n_c * hc, D), BF16),
        shape((D, LANES), BF16),
        shape((8, D), F32),
        shape((length, D), BF16),
        shape((hc, length), BF16),
        shape((hp, length, HEAD_DIM), BF16),
        shape((hp, length, HEAD_DIM), BF16),
        shape((n_c, hc, rows), BF16),
        shape((rows, D), F32),
        shape((rows, D), BF16),
        shape((rows, LANES), F32),
        shape((n_d, 3, D, units), BF16),
    )
    return pl.pallas_call(
        functools.partial(front_kernel, sizes, cfg),
        out_shape=(
            *kept,
            shape((2, n_s, slots, D), BF16),
            shape((hp, n_c, length, rows), BF16),
            *extra,
        ),
        in_specs=[vmem] * len(operands),
        out_specs=(anywhere,) * len(kept) + (vmem,) + (anywhere,) * (1 + len(extra)),
        scratch_shapes=[
            *held,
            pltpu.VMEM((8, LANES) if roomy else (4, slots, D), BF16),
            pltpu.VMEM((3, take, n_s, *((8, LANES) if roomy else (slots, D))), BF16),
            *[
                pltpu.VMEM((n_c * n_s * slots, n_d * units) if take == n_c else (16, LANES), kind)
                for kind in (F32, F32, BF16)
            ],
            pltpu.VMEM((3, D, n_d * units) if take < n_c else (8, LANES), F32),
            pltpu.VMEM((n_d, 3, D, units), BF16),
            pltpu.VMEM((LANES, LANES), F32),
            pltpu.VMEM((up_to(w_rows, 8), width), F32),
            pltpu.VMEM((n_c, a_rows, LANES), BF16),
            pltpu.VMEM((o_rows, LANES), BF16),
            pltpu.VMEM((n_e, n_c, n_d, a_rows, LANES), BF16),
            pltpu.VMEM((n_e, n_c, n_d, o_rows, LANES), BF16),
            pltpu.VMEM((n_loc, 3, D, units), BF16),
            pltpu.VMEM((n_c, hc, rows), BF16),
            pltpu.VMEM((hc, length), BF16),
            pltpu.VMEM((2, length, rows), BF16),
            pltpu.VMEM((2, n_s, slots, D), BF16),
            pltpu.VMEM((2, n_s, slots, D), BF16),
            dma((2,)),
            dma((n_c,)),
            dma((n_c,)),
            dma((2 * n_s,)),
            dma((2 * n_s,)),
            dma((gathers,)),
            dma((gathers,)),
            dma((2 * n_s + 1,)),
            dma((posts,)),
            dma((posts,)),
            *[dma((n_c - 1,))] * 4,
            dma((1,)),
            *[dma((2 * n_s * pairs,))] * 4,
            *[dma((2 * n_s,))] * 2,
            *[pltpu.VMEM(k.shape, k.dtype) for k in kept],
            dma((len(kept) + 2,)),
        ],
        compiler_params=pltpu.CompilerParams(
            collective_id=0, has_side_effects=True, vmem_limit_bytes=VMEM_LIMIT
        ),
        name="front",
    )(*operands)


def back_kernel(
    sizes,
    cfg,
    ret_ref,
    h_ref,
    a2_ref,
    small_ref,
    g_ref,
    routest_ref,
    wo_in,
    wqkv_in,
    wsm_ref,
    vec_ref,
    mixed_in,
    a1_in,
    qt_in,
    kh_in,
    vh_in,
    p_ref,
    xg_ref,
    gw_ref,
    block_ref,
    dx_ref,
    dprev_ref,
    gq_ref,
    gk_ref,
    gv_ref,
    go_ref,
    grouter_ref,
    gcoef_ref,
    gvalue_ref,
    ggains_ref,
    egate_ref,
    eup_ref,
    edown_ref,
    dhg,
    dht_scr,
    p_scr,
    dk_acc,
    dv_acc,
    dqt,
    dqkv,
    da_in,
    da_sum,
    da_out,
    x_scr,
    ew_own,
    ew_in,
    ew_mid,
    ew_out,
    t_send,
    t_recv,
    t_z,
    t_zr,
    t_c,
    t_cr,
    o_own,
    o_in,
    o_sum,
    o_out,
    o_x,
    o_xr,
    o_z,
    o_zr,
    l_sem,
    s_g,
    r_g,
    p_sem,
    s_d,
    r_d,
    s_w,
    r_w,
    s_t,
    r_t,
    s_q,
    r_q,
    wo_ref,
    wqkv_ref,
    mixed_ref,
    a1_ref,
    qt_ref,
    kh_ref,
    vh_ref,
    i_sem,
):
    n_e, n_c, n_d = sizes
    hp, n_ff, n_all, n_loc, slots = cfg
    hc = hp * HEAD_DIM
    place = e, c, d = position()
    pairs = n_c // 2
    outer, inner = c // 2, c % 2
    rows = h_ref.shape[0]
    w_rows = go_ref.shape[0]
    shift = 3 * hc % LANES
    chunks = up_to(3 * hc + SMALL, LANES) // LANES
    d_peers = [(e, c, lax.rem(d + k, n_d)) for k in range(1, n_d)]
    length = rows * n_c
    peers = context_peers(sizes, place)
    e_peers = expert_peers(sizes, place)

    bring = pltpu.make_async_copy(gw_ref, ew_own, l_sem.at[1])
    bring.start()

    def fetch_x(b, slot):
        return pltpu.make_async_copy(xg_ref.at[b], x_scr.at[slot], l_sem.at[2 + slot])

    early = {}
    for name, src, dst in (
        ("mixed", mixed_in, mixed_ref),
        ("wo", wo_in, wo_ref),
        ("kh", kh_in, kh_ref),
        ("vh", vh_in, vh_ref),
        ("qt", qt_in, qt_ref),
        ("a1", a1_in, a1_ref),
        ("wqkv", wqkv_in, wqkv_ref),
    ):
        early[name] = pltpu.make_async_copy(src, dst, i_sem.at[len(early)])
        early[name].start()
    fetch_x(c, 2).start()
    blocks = []
    for k in [*range(1, pairs), 0]:
        there = lax.rem(outer + k, pairs)
        blocks.extend([(k, there, there * 2 + 1 - inner), (None, there, there * 2 + inner)])
    fetch_x(blocks[0][2], 0).start()
    hail(peers + e_peers + d_peers)

    size = n_d // n_loc
    group, seat = d // size, lax.rem(d, size)
    mates = [(e, c, group * size + lax.rem(seat + k, size)) for k in range(1, size)]
    others = [lax.rem(group + k, n_loc) for k in range(1, n_loc)]
    freight = Courier(s_w, r_w)
    e_near = {}
    e_far = []

    def expert_start():
        for k, mate in enumerate(mates):
            for r, other in enumerate(others):
                e_near[k, r] = freight.carry(
                    ew_own.at[other * size + lax.rem(seat + k + 1, size)], ew_mid.at[k, r], mate
                )

    def expert_cross():
        for r, other in enumerate(others):
            target = other * size + seat
            for k in range(size - 1):
                e_near[k, r].wait_recv()

            def one(n, carry):
                at = pl.ds(pl.multiple_of(n * tile, tile), tile)
                total = ew_own[target, at, :].astype(F32)
                for k in range(size - 1):
                    total = total + ew_mid[k, r, at, :].astype(F32)
                ew_out[r, at, :] = total.astype(BF16)
                return carry

            tile = ew_own.shape[1] // 9
            lax.fori_loop(0, 9, one, 0)
            e_far.append(freight.carry(ew_out.at[r], ew_in.at[size - 1 + r], (e, c, target)))
        for k, mate in enumerate(mates):
            e_near[k, -1] = freight.carry(ew_own.at[mate[2]], ew_in.at[k], mate)

    def expert_end():
        for k in range(size - 1):
            e_near[k, -1].wait_recv()
        for copy in e_far:
            copy.wait_recv()
        part = ew_own.shape[1] // 3
        for n, ref in enumerate((egate_ref, eup_ref, edown_ref)):
            at = slice(n * part, (n + 1) * part)
            total = ew_own[d, at, :].astype(F32)
            for k in range(size - 1):
                total = total + ew_in[k, at, :].astype(F32)
            ref[pl.ds(group, 1)] = total[None]
            for r in range(n_loc - 1):
                ref[pl.ds(lax.rem(group - r - 1 + n_loc, n_loc), 1)] = ew_in[
                    size - 1 + r, at, :
                ].astype(F32)[None]
        freight.finish()

    await_hails(peers + e_peers + d_peers)
    bring.wait()
    expert_start()
    h = h_ref[...]
    a2 = a2_ref[...].astype(F32)
    g = g_ref[...]
    small = small_ref[...]
    value_one, value_two = vec_ref[2:3, :], vec_ref[3:4, :]
    tables, picks, w_pair, first, other = route_parts(
        routest_ref[...], small, n_ff, n_all, slots
    )
    copy_on, one_on, two_on = [
        [picks[k][:, n_ff + n : n_ff + n + 1] for k in range(2)] for n in (1, 2, 3)
    ]
    g_a2 = jnp.sum(g * a2, axis=1, keepdims=True)
    g_one = jnp.sum(g * value_one, axis=1, keepdims=True)
    g_two = jnp.sum(g * value_two, axis=1, keepdims=True)
    alpha = [copy_on[k] + one_on[k] * first[0] + two_on[k] * other[0] for k in range(2)]
    a_weight = alpha[0] * w_pair[0] + alpha[1] * w_pair[1]
    one_weight = one_on[0] * w_pair[0] + one_on[1] * w_pair[1]
    two_weight = two_on[0] * w_pair[0] + two_on[1] * w_pair[1]
    returned = [ret_ref[t].reshape(n_ff * slots, D) for t in range(2)]
    block = h
    d_weight = []
    for k in range(2):
        routed = dot(tables[k], returned[0], 0, 0)
        picked = (
            routed
            + alpha[k] * a2
            + (one_on[k] * first[1]) * value_one
            + (two_on[k] * other[1]) * value_two
        )
        block = block + w_pair[k] * picked
        d_weight.append(jnp.sum(g * picked, axis=1, keepdims=True))
    block_ref[...] = block
    center = w_pair[0] * d_weight[0] + w_pair[1] * d_weight[1]
    d_logits = (
        picks[0] * (w_pair[0] * (d_weight[0] - center))
        + picks[1] * (w_pair[1] * (d_weight[1] - center))
    )
    dprev_ref[...] = d_logits.T[:n_all, :]
    lane = lax.broadcasted_iota(jnp.int32, (rows, LANES), 1)
    d_small = d_logits
    for base, pair, weight, g_value in (
        (n_all, first, one_weight, g_one),
        (n_all + 2, other, two_weight, g_two),
    ):
        d_pair = (weight * g_a2, weight * g_value)
        middle = pair[0] * d_pair[0] + pair[1] * d_pair[1]
        for k in range(2):
            d_small = d_small + jnp.where(lane == base + k, pair[k] * (d_pair[k] - middle), 0.0)
    d_small = d_small.astype(BF16)
    d_const_one = jnp.sum((first[1] * one_weight) * g, axis=0, keepdims=True)
    d_const_two = jnp.sum((other[1] * two_weight) * g, axis=0, keepdims=True)
    d_a2 = (
        dot(tables[0] + tables[1], returned[1], 0, 0)
        + a_weight * g
        + dot(d_small, wsm_ref[...], 1, 1)
    )
    gain_two = vec_ref[1:2, :]
    inverse_two = lax.rsqrt(jnp.mean(h * h, axis=-1, keepdims=True) + EPS)
    d_gain_two = jnp.sum(d_a2 * h * inverse_two, axis=0, keepdims=True)
    scaled = gain_two * d_a2
    d_h = (
        g
        + inverse_two * scaled
        - h * inverse_two**3 * jnp.mean(scaled * h, axis=-1, keepdims=True)
    )
    d_hb = d_h.astype(BF16)
    dhg[pl.ds(c, 1)] = d_hb[None]
    gather = ContextGather(
        sizes,
        place,
        dhg.at[c],
        lambda k: dhg.at[k],
        lambda k: s_g.at[k],
        lambda k: r_g.at[k],
    )
    gather.start()
    dx_ref[...] = d_h
    early["mixed"].wait()
    g_o = dot(mixed_ref[...].reshape(n_c * hc, rows), d_hb)
    run = n_d * w_rows
    for b in range(n_c):
        for k in range(n_e):
            o_own[b, k, :run, :] = g_o[(k * n_c + b) * run : (k * n_c + b + 1) * run].astype(BF16)
    parcel = Courier(s_q, r_q)
    o_pair = {}
    for k in [*range(1, pairs), 0]:
        there = lax.rem(outer + k, pairs)
        o_pair[k] = parcel.carry(
            o_own.at[there * 2 + 1 - inner], o_in.at[there], peers[0]
        )
    o_state = {}

    def o_outer():
        o_state["outer"] = []
        for k in range(1, pairs):
            there = lax.rem(outer + k, pairs)
            o_pair[k].wait_recv()
            o_sum[k - 1] = (
                o_own[there * 2 + inner].astype(F32) + o_in[there].astype(F32)
            ).astype(BF16)
            o_state["outer"].append(
                parcel.carry(o_sum.at[k - 1], o_out.at[k - 1], peers[k])
            )

    def o_across():
        o_pair[0].wait_recv()
        total = o_own[c].astype(F32) + o_in[outer].astype(F32)
        for k, copy in enumerate(o_state["outer"]):
            copy.wait_recv()
            total = total + o_out[k].astype(F32)
        o_x[...] = total.astype(BF16)
        o_state["across"] = [
            parcel.carry(o_x.at[lax.rem(e + j, n_e)], o_xr.at[j - 1], e_peers[j - 1])
            for j in range(1, n_e)
        ]

    def o_along():
        total = o_x[e].astype(F32)
        for j, copy in enumerate(o_state["across"]):
            copy.wait_recv()
            total = total + o_xr[j].astype(F32)
        for k in range(n_d):
            o_z[k, :w_rows, :] = total[k * w_rows : (k + 1) * w_rows].astype(BF16)
        o_state["along"] = [
            parcel.carry(o_z.at[lax.rem(d + k, n_d)], o_zr.at[k - 1], d_peers[k - 1])
            for k in range(1, n_d)
        ]

    def o_end():
        total = o_z[d].astype(F32)
        for k, copy in enumerate(o_state["along"]):
            copy.wait_recv()
            total = total + o_zr[k].astype(F32)
        go_ref[...] = total[:w_rows]
        parcel.finish()

    if shift:
        d_small = jnp.concatenate(
            [jnp.zeros((rows, shift), BF16), d_small[:, : LANES - shift]], axis=1
        )
    g_small = dot(a2_ref[...], d_small, 0, 0)
    dk_acc[...] = jnp.zeros_like(dk_acc)
    dv_acc[...] = jnp.zeros_like(dv_acc)
    order = [(b, j) for b in reversed(range(n_c)) for j in range(hp)]

    def fetch(n):
        b, j = order[n]
        reach = pl.ds(0, (b + 1) * rows)
        return pltpu.make_async_copy(p_ref.at[j, b, reach], p_scr.at[n % 2, reach], p_sem.at[n % 2])

    fetch(0).start()
    expert_cross()
    gather.forward()
    gather.finish()
    o_outer()
    for name in ("wo", "kh", "vh", "qt"):
        early[name].wait()
    wo_part = wo_ref[pl.ds(pl.multiple_of(c * hc, hc), hc), :]
    for b in range(n_c):
        dht_scr[:, b * rows : (b + 1) * rows] = dot(wo_part, dhg[b], 1, 1).astype(BF16)
    for n, (b, j) in enumerate(order):
        reach = (b + 1) * rows
        head = slice(j * HEAD_DIM, (j + 1) * HEAD_DIM)
        mine_q = slice(b * rows, reach)
        if n == len(order) // 4:
            o_across()
        if n == len(order) // 2:
            o_along()
        if n + 1 < len(order):
            fetch(n + 1).start()
        fetch(n).wait()
        rounded = p_scr[n % 2, :reach, :]
        prob = rounded.astype(F32)
        d_o = dht_scr[head, mine_q]
        d_prob = dot(vh_ref[j, :reach, :], d_o)
        delta = jnp.sum(prob * d_prob, axis=0, keepdims=True)
        d_scores = (prob * (d_prob - delta)).astype(BF16)
        dqt[head, mine_q] = dot(kh_ref[j, :reach, :], d_scores, 0, 0) * HEAD_DIM**-0.5
        dk_acc[j, :reach, :] += dot(d_scores, qt_ref[head, mine_q], 1, 1)
        dv_acc[j, :reach, :] += dot(rounded, d_o, 1, 1)
    dqkv[:, :hc] = dqt[...].T.astype(BF16)
    for j in range(hp):
        at = j * HEAD_DIM
        dqkv[:, hc + at : hc + at + HEAD_DIM] = dk_acc[j].astype(BF16)
        dqkv[:, 2 * hc + at : 2 * hc + at + HEAD_DIM] = dv_acc[j].astype(BF16)
    dqkv[:, 3 * hc :] = jnp.zeros((length, dqkv.shape[1] - 3 * hc), BF16)
    d_all = dqkv[...]
    bag = Courier(s_t, r_t)
    across = {}
    early["a1"].wait()
    early["wqkv"].wait()
    g_all = dot(a1_ref[...], d_all, 0, 0)
    half = D // n_e

    def send_chunk(k, value):
        for n in range(n_e):
            t_send[k, n] = value[n * half : (n + 1) * half].astype(BF16)
        across[k] = [
            bag.carry(t_send.at[k, lax.rem(e + j, n_e)], t_recv.at[k, j - 1], e_peers[j - 1])
            for j in range(1, n_e)
        ]

    for k in range(chunks - 1):
        send_chunk(k, g_all[:, k * LANES : (k + 1) * LANES])
    wqkv = wqkv_ref[...]
    gain_one = vec_ref[0:1, :]
    d_gain_one = jnp.zeros((1, D), F32)
    to_pair = []
    for n, (k, there, b) in enumerate(blocks):
        if n + 1 < n_c:
            fetch_x(blocks[n + 1][2], (n + 1) % 2).start()
        here = pl.ds(pl.multiple_of(b * rows, rows), rows)
        part = dot(dqkv[here, : 3 * hc], wqkv, 1, 1)
        dhg[pl.ds(b, 1)] = part.astype(BF16)[None]
        if k is not None:
            copy = remote(dhg.at[b], da_in.at[there], s_d.at[k], r_d.at[k], peers[0])
            copy.start()
            to_pair.append((k, copy))
        fetch_x(b, n % 2).wait()
        x = x_scr[n % 2].astype(F32)
        inverse = lax.rsqrt(jnp.mean(x * x, axis=-1, keepdims=True) + EPS)
        d_gain_one = d_gain_one + jnp.sum(part * x * inverse, axis=0, keepdims=True)
    spot = lax.broadcasted_iota(jnp.int32, (LANES, D), 0)
    lines = jnp.zeros((LANES, D), F32)
    for n, row in enumerate((d_const_one, d_const_two, d_gain_one, d_gain_two)):
        lines = lines + jnp.where(spot == shift + n_all + 4 + n, row, 0.0)
    send_chunk(chunks - 1, g_all[:, (chunks - 1) * LANES :] + g_small + lines.T)
    along = []
    for k, copy in to_pair:
        if k == 0:
            continue
        there = lax.rem(outer + k, pairs)
        copy.wait_recv()
        da_sum[k - 1] = (
            dhg[there * 2 + inner].astype(F32) + da_in[there].astype(F32)
        ).astype(BF16)
        onward = remote(
            da_sum.at[k - 1],
            da_out.at[k - 1],
            s_d.at[pairs + k - 1],
            r_d.at[pairs + k - 1],
            peers[k],
        )
        onward.start()
        along.append(onward)
    down = {}
    for k in range(chunks):
        total = t_send[k, e].astype(F32)
        for j, copy in enumerate(across[k]):
            copy.wait_recv()
            total = total + t_recv[k, j].astype(F32)
        for n in range(n_d):
            t_z[k, n, : n_c * w_rows, :] = jnp.concatenate(
                [
                    total[(b * n_d + n) * w_rows : (b * n_d + n + 1) * w_rows]
                    for b in range(n_c)
                ],
                axis=0,
            ).astype(BF16)
        down[k] = [
            bag.carry(t_z.at[k, lax.rem(d + n, n_d)], t_zr.at[k, n - 1], d_peers[n - 1])
            for n in range(1, n_d)
        ]
    o_end()
    to_pair[-1][1].wait_recv()
    d_a1 = dhg[c].astype(F32) + da_in[outer].astype(F32)
    for k, copy in enumerate(along):
        copy.wait_recv()
        d_a1 = d_a1 + da_out[k].astype(F32)
    fetch_x(c, 2).wait()
    x = x_scr[2].astype(F32)
    inverse_one = lax.rsqrt(jnp.mean(x * x, axis=-1, keepdims=True) + EPS)
    scaled = gain_one * d_a1
    dx_ref[...] += inverse_one * scaled - x * inverse_one**3 * jnp.mean(
        scaled * x, axis=-1, keepdims=True
    )
    for k in range(chunks):
        total = t_z[k, d].astype(F32)
        for n, copy in enumerate(down[k]):
            copy.wait_recv()
            total = total + t_zr[k, n].astype(F32)
        for b in range(n_c):
            t_c[b, k, :w_rows, :] = total[b * w_rows : (b + 1) * w_rows]
    t_cr[pl.ds(c, 1)] = t_c[pl.ds(c, 1)]
    turned = [
        bag.carry(t_c.at[lax.rem(c + k, n_c)], t_cr.at[c], (e, lax.rem(c + k, n_c), d))
        for k in range(1, n_c)
    ]
    expert_end()
    for copy in turned:
        copy.wait_recv()
    s_total = jnp.zeros((w_rows, SMALL), F32)
    for b in range(n_c):
        line = jnp.concatenate([t_cr[b, k] for k in range(chunks)], axis=1)[:w_rows]
        for n, ref in enumerate((gq_ref, gk_ref, gv_ref)):
            width = min(hc, D - b * hc)
            if width > 0:
                ref[:, b * hc : b * hc + width] = line[:, n * hc : n * hc + width]
        s_total = s_total + line[:, 3 * hc : 3 * hc + SMALL]
    s_lines = jnp.concatenate([s_total, jnp.zeros((w_rows, LANES - SMALL), F32)], axis=1)
    s_lines = tall(s_lines, LANES).T
    at = 0
    for ref in (grouter_ref, gcoef_ref, gvalue_ref, ggains_ref):
        ref[...] = s_lines[at : at + ref.shape[0], :w_rows]
        at += ref.shape[0]
    bag.finish()
    for _, copy in to_pair:
        copy.wait_send()
    for copy in along:
        copy.wait_send()


def backward(sizes, cfg, *operands):
    n_e, n_c, n_d = sizes
    hp, n_ff, n_all, n_loc, slots = cfg
    hc = hp * HEAD_DIM
    rows = operands[1].shape[0]
    length = rows * n_c
    pairs = n_c // 2
    dma = pltpu.SemaphoreType.DMA
    vmem = pl.BlockSpec(memory_space=pltpu.VMEM)
    anywhere = pl.BlockSpec(memory_space=pl.ANY)
    shape = jax.ShapeDtypeStruct
    part = operands[17].shape[1]
    w_rows = D // (n_e * n_c * n_d)
    chunks = up_to(3 * hc + SMALL, LANES) // LANES
    run = up_to(n_d * w_rows, 16)
    turn = up_to(n_c * w_rows, 16)
    few = up_to(w_rows, 16)
    few_wide = up_to(w_rows, 8)
    size = n_d // n_loc
    loads = (size - 1) * n_loc + n_loc - 1
    bags = chunks * (n_e - 1 + n_d - 1) + n_c - 1
    parcels = 2 * pairs - 1 + n_e - 1 + n_d - 1
    n_more = max(1, pairs - 1)
    in_specs = [vmem] * len(operands)
    in_specs[15] = in_specs[16] = in_specs[17] = anywhere
    late = [operands[n] for n in (6, 7, 10, 11, 12, 13, 14)]
    for n in (6, 7, 10, 11, 12, 13, 14):
        in_specs[n] = anywhere
    return pl.pallas_call(
        functools.partial(back_kernel, sizes, cfg),
        out_shape=(
            shape((rows, D), F32),
            shape((rows, D), F32),
            shape((n_all, rows), F32),
            *[shape((w_rows, D), F32)] * 4,
            *[shape((n, w_rows), F32) for n in (n_all, 4, 2, 2)],
            *[shape((n_loc, part // 3, LANES), F32)] * 3,
        ),
        in_specs=in_specs,
        out_specs=(vmem,) * 14,
        scratch_shapes=[
            pltpu.VMEM((n_c, rows, D), BF16),
            pltpu.VMEM((hc, length), BF16),
            pltpu.VMEM((2, length, rows), BF16),
            pltpu.VMEM((hp, length, HEAD_DIM), F32),
            pltpu.VMEM((hp, length, HEAD_DIM), F32),
            pltpu.VMEM((hc, length), F32),
            pltpu.VMEM((length, chunks * LANES), BF16),
            pltpu.VMEM((pairs, rows, D), BF16),
            pltpu.VMEM((n_more, rows, D), BF16),
            pltpu.VMEM((n_more, rows, D), BF16),
            pltpu.VMEM((3, rows, D), BF16),
            pltpu.VMEM((n_d, part, LANES), BF16),
            pltpu.VMEM((size + n_loc - 2, part, LANES), BF16),
            pltpu.VMEM((max(1, size - 1), max(1, n_loc - 1), part, LANES), BF16),
            pltpu.VMEM((max(1, n_loc - 1), part, LANES), BF16),
            pltpu.VMEM((chunks, n_e, D // n_e, LANES), BF16),
            pltpu.VMEM((chunks, n_e - 1, D // n_e, LANES), BF16),
            pltpu.VMEM((chunks, n_d, turn, LANES), BF16),
            pltpu.VMEM((chunks, n_d - 1, turn, LANES), BF16),
            pltpu.VMEM((n_c, chunks, few_wide, LANES), F32),
            pltpu.VMEM((n_c, chunks, few_wide, LANES), F32),
            pltpu.VMEM((n_c, n_e, run, D), BF16),
            pltpu.VMEM((pairs, n_e, run, D), BF16),
            pltpu.VMEM((n_more, n_e, run, D), BF16),
            pltpu.VMEM((n_more, n_e, run, D), BF16),
            pltpu.VMEM((n_e, run, D), BF16),
            pltpu.VMEM((n_e - 1, run, D), BF16),
            pltpu.VMEM((n_d, few, D), BF16),
            pltpu.VMEM((n_d - 1, few, D), BF16),
            dma((5,)),
            dma((n_c - 1,)),
            dma((n_c - 1,)),
            dma((2,)),
            dma((n_c,)),
            dma((n_c,)),
            dma((loads,)),
            dma((loads,)),
            dma((bags,)),
            dma((bags,)),
            dma((parcels,)),
            dma((parcels,)),
            *[pltpu.VMEM(w.shape, w.dtype) for w in late],
            dma((len(late),)),
        ],
        compiler_params=pltpu.CompilerParams(
            collective_id=1, has_side_effects=True, vmem_limit_bytes=VMEM_LIMIT
        ),
        name="backward",
    )(*operands)


def hand_out_kernel(*refs):
    count = (len(refs) - 2) // 3
    sources, results, held = refs[:count], refs[count : 2 * count], refs[2 * count : 3 * count]
    in_sems, out_sems = refs[-2:]
    takes = [pltpu.make_async_copy(sources[n], held[n], in_sems.at[n]) for n in range(count)]
    gives = [pltpu.make_async_copy(held[n], results[n], out_sems.at[n]) for n in range(count)]
    for copy in takes:
        copy.start()
    for take, give in zip(takes, gives):
        take.wait()
        give.start()
    for copy in gives:
        copy.wait()


def hand_out(results):
    anywhere = pl.BlockSpec(memory_space=pl.ANY)
    dma = pltpu.SemaphoreType.DMA((len(results),))
    return pl.pallas_call(
        hand_out_kernel,
        out_shape=tuple(jax.ShapeDtypeStruct(r.shape, r.dtype) for r in results),
        in_specs=[anywhere] * len(results),
        out_specs=(anywhere,) * len(results),
        scratch_shapes=[*[pltpu.VMEM(r.shape, r.dtype) for r in results], dma, dma],
        compiler_params=pltpu.CompilerParams(vmem_limit_bytes=VMEM_LIMIT),
        name="hand_out",
    )(*results)


def body(
    tokens,
    doc_ids,
    routes,
    prev_logits,
    cotangent,
    w_query,
    w_key,
    w_value,
    w_out,
    w_router,
    const_coef,
    const_value,
    norm_gains,
    expert_gate,
    expert_up,
    expert_down,
):
    sizes = n_e, n_c, n_d = tuple(lax.axis_size(axis) for axis in ALL_AXES)
    rows = tokens.shape[1]
    length = doc_ids.shape[1]
    n_loc, _, units = expert_gate.shape
    n_ff = n_loc * n_e
    n_all = w_router.shape[1]
    slots = rows // 4
    hp = -(-HEADS // n_c)
    cfg = (hp, n_ff, n_all, n_loc, slots)
    routes_t = routes[0].T
    upstream = cotangent[0]
    (
        x_all,
        wqkv,
        wo,
        wsm,
        vec,
        a1,
        q_t,
        k_h,
        v_h,
        mixed,
        h,
        a2,
        small,
        grads,
        returned,
        probs,
        *_,
    ) = front(
        sizes,
        cfg,
        w_query,
        w_key,
        w_value,
        w_out,
        w_router.T,
        const_coef.T,
        const_value.T,
        norm_gains.T,
        tokens[0],
        expert_gate,
        expert_up,
        expert_down,
        doc_ids,
        routes_t,
        prev_logits[0].T,
        upstream,
    )
    results = backward(
        sizes,
        cfg,
        returned,
        h,
        a2,
        small,
        upstream,
        routes_t,
        wo,
        wqkv,
        wsm,
        vec,
        mixed,
        a1,
        q_t,
        k_h,
        v_h,
        probs,
        x_all,
        grads.reshape(n_d, 3 * D * units // LANES, LANES),
    )
    block_rows, d_x, d_prev, *square = hand_out(results)
    narrow = square[4:8]
    return (
        block_rows[None],
        d_x[None],
        d_prev.T[None],
        *square[:4],
        *[grad.T for grad in narrow],
        *[grad.reshape(n_loc, D, units) for grad in square[8:]],
    )


def solution(mesh):
    rows = P(("expert", "dp"), "context", None)
    weights = P(ALL_AXES, None)
    units = P("expert", None, ("context", "dp"))
    return jax.shard_map(
        body,
        mesh=mesh,
        in_specs=(rows, P(("expert", "dp"), None), rows, rows, rows)
        + (weights,) * 8
        + (units,) * 3,
        out_specs=(rows,) * 3 + (weights,) * 8 + (units,) * 3,
        check_vma=False,
    )
```

```python
import functools

import jax
import jax.numpy as jnp
from jax import lax
from jax.experimental import pallas as pl
from jax.experimental.pallas import tpu as pltpu
from jax.sharding import PartitionSpec as P

D = 768
HEADS = 12
HEAD_DIM = 64
EPS = 1e-06
SMALL = 64
LANES = 128
VMEM_LIMIT = 63 * 2**20
MESH = pl.DeviceIdType.MESH
F32 = jnp.float32
BF16 = jnp.bfloat16
ALL_AXES = ("expert", "context", "dp")


def dot(left, right, left_dim=1, right_dim=0):
    return lax.dot_general(
        left, right, (((left_dim,), (right_dim,)), ((), ())), preferred_element_type=F32
    )


def position():
    return lax.axis_index("expert"), lax.axis_index("context"), lax.axis_index("dp")


def remote(src, dst, send_sem, recv_sem, device):
    return pltpu.make_async_remote_copy(
        src_ref=src,
        dst_ref=dst,
        send_sem=send_sem,
        recv_sem=recv_sem,
        device_id=device,
        device_id_type=MESH,
    )


def hail(devices):
    barrier = pltpu.get_barrier_semaphore()
    for device in devices:
        pl.semaphore_signal(barrier, inc=1, device_id=device, device_id_type=MESH)


def await_hails(devices):
    pl.semaphore_wait(pltpu.get_barrier_semaphore(), len(devices))


def context_peers(sizes, place):
    e, c, d = place
    pairs = sizes[1] // 2
    outer, inner = c // 2, c % 2
    peers = [(e, outer * 2 + 1 - inner, d)]
    for k in range(1, pairs):
        peers.append((e, lax.rem(outer + k, pairs) * 2 + inner, d))
    return peers


def expert_peers(sizes, place):
    e, c, d = place
    return [(lax.rem(e + j, sizes[0]), c, d) for j in range(1, sizes[0])]


def crossing_only(sizes, n_loc, place):
    _, there, _ = homes(sizes, n_loc, place)
    return [device for j, (_, device) in enumerate(there) if j // n_loc and j % n_loc]


def homes(sizes, n_loc, place):
    n_e, n_c, n_d = sizes
    e, c, d = place
    size = n_d // n_loc
    group, seat = d // size, lax.rem(d, size)
    there, back = [], []
    for j in range(n_e * n_loc):
        je, jg = j // n_loc, j % n_loc
        to_e, to_g = lax.rem(e + je, n_e), lax.rem(group + jg, n_loc)
        from_e, from_g = lax.rem(e - je + n_e, n_e), lax.rem(group - jg + n_loc, n_loc)
        there.append((to_e * n_loc + to_g, (to_e, c, to_g * size + seat)))
        back.append(from_e * n_loc + from_g)
    return e * n_loc + group, there, back


class Courier:
    def __init__(self, send, recv):
        self.send, self.recv = send, recv
        self.copies = []

    def carry(self, src, dst, device):
        n = len(self.copies)
        copy = remote(src, dst, self.send.at[n], self.recv.at[n], device)
        copy.start()
        self.copies.append(copy)
        return copy

    def finish(self):
        for copy in self.copies:
            copy.wait_send()


def up_to(count, step):
    return -(-count // step) * step


class ContextGather:
    def __init__(self, sizes, place, own, slot, send, recv):
        e, c, d = place
        self.pairs = sizes[1] // 2
        self.place, self.own, self.slot = place, own, slot
        self.send, self.recv = send, recv
        self.outer, self.inner = c // 2, c % 2
        self.peers = context_peers(sizes, place)
        self.copies = []
        self.forwards = []

    def start(self):
        for k in [*range(1, self.pairs), 0]:
            copy = remote(
                self.own, self.slot(self.place[1]), self.send(k), self.recv(k), self.peers[k]
            )
            copy.start()
            self.copies.append((k, copy))

    def origin(self, k):
        return lax.rem(self.outer - k + self.pairs, self.pairs) * 2 + self.inner

    def forward(self):
        for k, copy in self.copies:
            if k > 0:
                copy.wait_recv()
                block = self.slot(self.origin(k))
                n = self.pairs - 1 + k
                onward = remote(block, block, self.send(n), self.recv(n), self.peers[0])
                onward.start()
                self.forwards.append(onward)

    def finish(self):
        for k, copy in self.copies:
            if k == 0:
                copy.wait_recv()
            copy.wait_send()
        for copy in self.forwards:
            copy.wait()


class Spread:
    def __init__(self, sizes, place, courier, own, slot):
        self.sizes, self.place, self.courier = sizes, place, courier
        self.slot = slot
        n_e, n_c, n_d = sizes
        e, c, d = place
        self.across_to = expert_peers(sizes, place)
        self.along = [
            courier.carry(own, slot(e, d), (e, c, lax.rem(d + k, n_d))) for k in range(1, n_d)
        ]
        self.across = [courier.carry(own, slot(e, d), device) for device in self.across_to]

    def onward(self):
        e, c, d = self.place
        n_d = self.sizes[2]
        for k in range(1, n_d):
            self.along[k - 1].wait_recv()
            block = self.slot(e, lax.rem(d - k + n_d, n_d))
            for device in self.across_to:
                self.across.append(self.courier.carry(block, block, device))

    def arrive(self):
        for copy in self.across:
            copy.wait_recv()


def spread_count(sizes):
    n_e, n_c, n_d = sizes
    return (n_d - 1) + (n_e - 1) * n_d


def softmax_pair(left, right):
    top = jnp.maximum(left, right)
    left, right = jnp.exp(left - top), jnp.exp(right - top)
    total = left + right
    return left / total, right / total


def tall(array, height):
    if array.shape[0] == height:
        return array
    return jnp.concatenate(
        [array, jnp.zeros((height - array.shape[0], *array.shape[1:]), array.dtype)], axis=0
    )


def route_parts(routes_t, small, n_ff, n_all, slots):
    rows = routes_t.shape[1]
    routes = tall(routes_t.astype(F32), LANES).T
    hot = lax.broadcasted_iota(jnp.int32, (LANES, rows), 0)
    marks = [(hot == routes_t[k : k + 1, :]) & (hot < n_ff) for k in range(2)]
    both = (marks[0] | marks[1]).astype(F32)
    earlier = lax.broadcasted_iota(jnp.int32, (rows, rows), 0) < lax.broadcasted_iota(
        jnp.int32, (rows, rows), 1
    )
    rank = dot(both.astype(BF16), earlier.astype(F32).astype(BF16))
    number = lax.broadcasted_iota(jnp.int32, (slots, rows), 0).astype(F32)
    tables = []
    for k in range(2):
        wanted = jnp.where(marks[k], rank, -1.0)
        tables.append(
            jnp.concatenate(
                [(number == wanted[j : j + 1, :]).astype(F32) for j in range(n_ff)], axis=0
            ).astype(BF16)
        )
    lane = lax.broadcasted_iota(jnp.int32, (rows, LANES), 1)
    picks = [(lane.astype(F32) == routes[:, k : k + 1]).astype(F32) for k in range(2)]
    chosen = [
        jnp.sum(jnp.where(picks[k] > 0, small, 0.0), axis=1, keepdims=True) for k in range(2)
    ]
    w_pair = softmax_pair(chosen[0], chosen[1])
    first = softmax_pair(small[:, n_all : n_all + 1], small[:, n_all + 1 : n_all + 2])
    second = softmax_pair(small[:, n_all + 2 : n_all + 3], small[:, n_all + 3 : n_all + 4])
    return tables, picks, w_pair, first, second


def front_kernel(
    sizes,
    cfg,
    wq_ref,
    wk_ref,
    wv_ref,
    wout_ref,
    router_ref,
    coef_ref,
    value_ref,
    gains_ref,
    xown_ref,
    gate_ref,
    up_ref,
    down_ref,
    drow_ref,
    routest_ref,
    prev_ref,
    g_ref,
    xg_out,
    wqkv_out,
    wo_out,
    wsm_out,
    vec_out,
    a1_out,
    qt_out,
    kh_out,
    vh_out,
    mixed_out,
    h_out,
    a2_out,
    small_out,
    gw_out,
    back_ref,
    p_ref,
    slots_ref,
    res,
    inn,
    osum,
    outr,
    stage,
    blk,
    gate_scr,
    up_scr,
    hid_scr,
    acc_scr,
    ew_ref,
    small_scr,
    row_scr,
    a_ref,
    ow_ref,
    ag,
    og,
    ew_own,
    o_scr,
    vt_scr,
    p_scr,
    sbuf,
    xin,
    p_sem,
    s_o,
    r_o,
    s_x,
    r_x,
    s_g,
    r_g,
    l_g,
    s_c,
    r_c,
    s_ow,
    r_ow,
    s_xg,
    r_xg,
    b_sem,
    s_in,
    r_in,
    s_out,
    r_out,
    s_h,
    r_h,
    xg_ref,
    wqkv_ref,
    wo_ref,
    wsm_ref,
    vec_ref,
    a1_ref,
    qt_ref,
    kh_ref,
    vh_ref,
    mixed_ref,
    h_ref,
    a2_ref,
    small_ref,
    gw_ref,
    o_sem,
):
    n_e, n_c, n_d = sizes
    hp, n_ff, n_all, n_loc, slots = cfg
    hc = hp * HEAD_DIM
    place = e, c, d = position()
    rows = xown_ref.shape[0]
    length = rows * n_c
    c_all = [(e, lax.rem(c + k, n_c), d) for k in range(1, n_c)]
    n_s = n_e * n_loc
    me, there, back = homes(sizes, n_loc, place)
    d_peers = [(e, c, lax.rem(d + k, n_d)) for k in range(1, n_d)]
    neighbours = (
        c_all + d_peers + expert_peers(sizes, place) + crossing_only(sizes, n_loc, place)
    )
    hail(neighbours)
    leaving = []

    def leave(*pairs_of):
        for src, dst in pairs_of:
            copy = pltpu.make_async_copy(src, dst, o_sem.at[len(leaving)])
            copy.start()
            leaving.append(copy)

    w_rows = wq_ref.shape[0]
    small_scr[...] = jnp.zeros_like(small_scr)
    at = 0
    for ref in (router_ref, coef_ref, value_ref, gains_ref):
        small_scr[at : at + ref.shape[0], :w_rows] = ref[...]
        at += ref.shape[0]
    width = row_scr.shape[1]
    w_small = small_scr[...].T[:w_rows, :SMALL]

    def stack(rows_of, tiles, height):
        parts = [rows_of(k * LANES) for k in range(tiles)]
        return tall(jnp.concatenate(parts, axis=0), height).astype(BF16)

    ow_ref[...] = stack(lambda at: wout_ref[:, at : at + LANES], D // LANES, ow_ref.shape[0])
    row_scr[...] = jnp.zeros_like(row_scr)
    row_scr[:w_rows, 3 * hc : 3 * hc + SMALL] = w_small
    for b in range(n_c):
        for n, ref in enumerate((wq_ref, wk_ref, wv_ref)):
            wide = max(0, min(hc, D - b * hc))
            if wide > 0:
                row_scr[:w_rows, n * hc : n * hc + wide] = ref[:, b * hc : b * hc + wide]
            if wide < hc:
                row_scr[:w_rows, n * hc + wide : (n + 1) * hc] = jnp.zeros((w_rows, hc - wide), F32)
        a_ref[b] = stack(
            lambda at: row_scr[:w_rows, at : at + LANES], width // LANES, a_ref.shape[1]
        )
    await_hails(neighbours)
    post = Courier(s_c, r_c)
    turned = [
        post.carry(a_ref.at[lax.rem(c + k, n_c)], ag.at[e, c, d], device)
        for k, device in enumerate(c_all, 1)
    ]
    x_rows = ContextGather(
        sizes,
        place,
        xown_ref,
        lambda k: xg_ref.at[k],
        lambda k: s_xg.at[k],
        lambda k: r_xg.at[k],
    )
    x_rows.start()
    ow_spread = Spread(sizes, place, post, ow_ref, lambda j, k: og.at[j, c, k])
    ag[e, c, d] = a_ref[c]
    og[e, c, d] = ow_ref[...]
    xg_ref[pl.ds(c, 1)] = xown_ref[...][None]
    for n, ref in enumerate((gate_ref, up_ref, down_ref)):
        ew_own[:, n] = ref[...].astype(BF16)
    for copy in turned:
        copy.wait_recv()
    a_spread = Spread(sizes, place, post, ag.at[e, :, d], lambda j, k: ag.at[j, :, k])
    size = n_d // n_loc
    group, seat = d // size, lax.rem(d, size)
    mates = [(e, c, group * size + lax.rem(seat + k, size)) for k in range(1, size)]
    keep_w = pltpu.make_async_copy(ew_own.at[group], ew_ref.at[d], l_g.at[2 * n_s])
    keep_w.start()
    w_far, w_near = {}, {}
    for n in range(3):
        w_near[n] = [post.carry(ew_own.at[group, n], ew_ref.at[d, n], device) for device in mates]
        for k in range(1, n_loc):
            to = lax.rem(group + k, n_loc)
            w_far[n, k] = post.carry(
                ew_own.at[to, n], ew_ref.at[d, n], (e, c, to * size + seat)
            )

    def pass_weights(n):
        for k in range(1, n_loc):
            w_far[n, k].wait_recv()
            block = ew_ref.at[lax.rem(group - k + n_loc, n_loc) * size + seat, n]
            w_near[n].extend([post.carry(block, block, device) for device in mates])

    ow_spread.onward()
    x_rows.forward()
    ow_spread.arrive()
    ow_rows = ContextGather(
        sizes,
        place,
        og.at[:, c],
        lambda k: og.at[:, k],
        lambda k: s_ow.at[k],
        lambda k: r_ow.at[k],
    )
    ow_rows.start()
    a_spread.onward()
    x_rows.finish()
    leave((xg_ref, xg_out))
    a_spread.arrive()

    def unstack(slabs, tiles):
        height = slabs.shape[2]
        slabs = slabs.reshape(n_c * n_d, height, LANES)
        if w_rows % 8 == 0:
            wide = [slabs[n].astype(F32) for n in range(n_c * n_d)]
            return jnp.concatenate(
                [
                    jnp.concatenate([w[k * w_rows : (k + 1) * w_rows] for w in wide], axis=0)
                    for k in range(tiles)
                ],
                axis=1,
            )
        flat = slabs.reshape(n_c * n_d * height, LANES)
        at_row = lax.broadcasted_iota(jnp.int32, (D // n_e, flat.shape[0]), 0)
        at_slab = lax.broadcasted_iota(jnp.int32, (D // n_e, flat.shape[0]), 1)
        first = at_row // w_rows * height + lax.rem(at_row, w_rows)
        return jnp.concatenate(
            [
                dot(jnp.where(at_slab == first + k * w_rows, 1.0, 0.0).astype(BF16), flat)
                for k in range(tiles)
            ],
            axis=1,
        )

    weights = jnp.concatenate([unstack(ag[k], width // LANES) for k in range(n_e)], axis=0)
    wqkv = weights[:, : 3 * hc].astype(BF16)
    wqkv_ref[...] = wqkv
    w_small = jnp.concatenate(
        [weights[:, 3 * hc : 3 * hc + SMALL], jnp.zeros((D, LANES - SMALL), F32)], axis=1
    )
    wsm_ref[...] = w_small.astype(BF16)
    w_lines = w_small.T
    vec_ref[0:2, :] = w_lines[n_all + 6 : n_all + 8, :]
    vec_ref[2:4, :] = w_lines[n_all + 4 : n_all + 6, :]
    vec_ref[4:8, :] = jnp.zeros((4, D), F32)

    gain_one = vec_ref[0:1, :]
    for b in range(n_c):
        x = xg_ref[b].astype(F32)
        inverse = lax.rsqrt(jnp.mean(x * x, axis=-1, keepdims=True) + EPS)
        a1_ref[b * rows : (b + 1) * rows, :] = (x * inverse * gain_one).astype(BF16)
    a1 = a1_ref[...]
    leave((a1_ref, a1_out), (wqkv_ref, wqkv_out), (wsm_ref, wsm_out), (vec_ref, vec_out))
    ow_rows.forward()
    q_t = dot(wqkv[:, :hc], a1, 0, 1).astype(BF16) * jnp.asarray(HEAD_DIM**-0.5, BF16)
    qt_ref[...] = q_t
    kv = dot(a1, wqkv[:, hc:]).astype(BF16)
    for j in range(hp):
        kh_ref[j] = kv[:, j * HEAD_DIM : (j + 1) * HEAD_DIM]
        vh_ref[j] = kv[:, hc + j * HEAD_DIM : hc + (j + 1) * HEAD_DIM]
    vt_scr[...] = dot(wqkv[:, 2 * hc :], a1, 0, 1).astype(BF16)

    leave((qt_ref, qt_out), (kh_ref, kh_out), (vh_ref, vh_out))
    pass_weights(0)
    documents = drow_ref[...].astype(F32)
    document_of = jnp.broadcast_to(documents, (LANES, length)).T[:, :1]
    turn = 0
    p_copies = {}
    for b in reversed(range(n_c)):
        reach = (b + 1) * rows
        key_place = lax.broadcasted_iota(jnp.int32, (reach, rows), 0)
        q_place = lax.broadcasted_iota(jnp.int32, (reach, rows), 1) + b * rows
        allowed = (document_of[:reach] == documents[:, b * rows : reach]) & (key_place <= q_place)
        bias = jnp.where(allowed, 0.0, -1e30)
        for j in range(hp):
            head = slice(j * HEAD_DIM, (j + 1) * HEAD_DIM)
            scores = dot(kh_ref[j, :reach, :], qt_ref[head, b * rows : reach]) + bias
            top = jnp.max(scores, axis=0, keepdims=True)
            exponent = jnp.exp(scores - top)
            total = jnp.sum(exponent, axis=0, keepdims=True)
            rounded = (exponent * (1.0 / total)).astype(BF16)
            slot = turn % 2
            if turn >= 2:
                p_copies[turn - 2].wait()
            p_scr[slot, :reach, :] = rounded
            copy = pltpu.make_async_copy(
                p_scr.at[slot, pl.ds(0, reach)], p_ref.at[j, b, pl.ds(0, reach)], p_sem.at[slot]
            )
            copy.start()
            p_copies[turn] = copy
            turn += 1
            o_scr[b, head, :] = dot(vt_scr[head, :reach], rounded).astype(BF16)

        @pl.when(c != b)
        def _():
            remote(
                o_scr.at[b], mixed_ref.at[c], s_o.at[b], r_o.at[c], (e, b, d)
            ).start()

    pass_weights(1)
    for n in range(max(0, turn - 2), turn):
        p_copies[n].wait()
    ow_rows.finish()
    if n_c * hc > D:
        wo_ref[D:, :] = jnp.zeros((n_c * hc - D, D), BF16)
    for k in range(n_e):
        wo_ref[k * (D // n_e) : (k + 1) * (D // n_e), :] = unstack(og[k], D // LANES).astype(BF16)
    mixed_ref[pl.ds(c, 1)] = o_scr[pl.ds(c, 1)]
    for b in range(n_c):

        @pl.when(c != b)
        def _():
            copy = remote(o_scr.at[b], mixed_ref.at[b], s_o.at[b], r_o.at[b], (e, b, d))
            copy.wait_send()
            copy.wait_recv()

    leave((wo_ref, wo_out), (mixed_ref, mixed_out))
    mixed = mixed_ref[...].reshape(n_c * hc, rows)
    h = xown_ref[...].astype(F32) + dot(mixed, wo_ref[...], 0, 0)
    h_ref[...] = h
    inverse = lax.rsqrt(jnp.mean(h * h, axis=-1, keepdims=True) + EPS)
    a2 = (h * inverse * vec_ref[1:2, :]).astype(BF16)
    a2_ref[...] = a2
    small = dot(a2, wsm_ref[...]) + tall(prev_ref[...], LANES).T
    small_ref[...] = small
    leave((h_ref, h_out), (a2_ref, a2_out), (small_ref, small_out))
    tables, _, w_pair, _, _ = route_parts(routest_ref[...], small, n_ff, n_all, slots)
    crossing = {}
    gathers = {}
    g = g_ref[...]
    for t in range(2):
        if t == 0:
            block = dot(tables[0] + tables[1], a2).astype(BF16)
        else:
            block = dot(tables[0], (w_pair[0] * g).astype(BF16)) + dot(
                tables[1], (w_pair[1] * g).astype(BF16)
            )
            block = block.astype(BF16)
        for k in range(n_s):
            sbuf[t, k] = block[k * slots : (k + 1) * slots, :]
        for j in reversed(range(1, n_s)):
            n = t * n_s + j
            part, device = there[j]
            copy = remote(sbuf.at[t, part], xin.at[t, me], s_x.at[n], r_x.at[n], device)
            copy.start()
            crossing[t, j] = copy

        def gather(j, own, t=t):
            src = back[j]
            base = (t * n_s + j) * (n_c - 1)
            keep = pltpu.make_async_copy(own, slots_ref.at[c, t, src], l_g.at[t * n_s + j])
            keep.start()
            made = ContextGather(
                sizes,
                place,
                own,
                lambda k: slots_ref.at[k, t, src],
                lambda k: s_g.at[base + k],
                lambda k: r_g.at[base + k],
            )
            made.start()
            gathers[t, j] = (made, keep)

        gather(0, sbuf.at[t, me])
        crossing[t, 0] = gather
    for t in range(2):
        for j in range(1, n_s):
            crossing[t, j].wait_recv()
            crossing[t, 0](j, xin.at[t, back[j]])
        if t == 0:
            pass_weights(2)

    def gathered(t):
        for j in range(n_s):
            gathers[t, j][0].forward()
        for j in range(n_s):
            gathers[t, j][0].finish()
            gathers[t, j][1].wait()

    roomy = len(stage.shape) == 2
    take = blk.shape[1]
    blocks = n_c // take
    pairs = n_c // 2
    outer, inner = c // 2, c % 2
    peers = context_peers(sizes, place)

    def load_rows(t, n):
        if roomy:
            return slots_ref[n * take : (n + 1) * take, t].reshape(-1, D)
        copy = pltpu.make_async_copy(slots_ref.at[pl.ds(n * take, take), t], blk.at[t], b_sem.at[0])
        copy.start()
        copy.wait()
        return blk[t].reshape(-1, D)

    def store_rows(t, n, value):
        value = value.astype(BF16).reshape(take, n_s, slots, D)
        if roomy:
            res[n * take : (n + 1) * take, t] = value
        else:
            blk[2] = value
            copy = pltpu.make_async_copy(blk.at[2], res.at[pl.ds(n * take, take), t], b_sem.at[0])
            copy.start()
            copy.wait()

    def load(ref, slot=0):
        if roomy:
            return ref[...].astype(F32)
        copy = pltpu.make_async_copy(ref, stage.at[slot], b_sem.at[0])
        copy.start()
        copy.wait()
        return stage[slot].astype(F32)

    def store(ref, value):
        if roomy:
            ref[...] = value
        else:
            stage[3] = value
            copy = pltpu.make_async_copy(stage.at[3], ref, b_sem.at[0])
            copy.start()
            copy.wait()

    order = [*reversed(range(1, n_s)), 0]
    to_pair, along, home = {}, {}, {}

    def sum_pair(t):
        for j in order:
            src = there[j][0]
            for k in [*range(1, pairs), 0]:
                n = (t * n_s + j) * pairs + k
                far = lax.rem(outer + k, pairs)
                copy = remote(
                    res.at[far * 2 + 1 - inner, t, src],
                    inn.at[far, t, src],
                    s_in.at[n],
                    r_in.at[n],
                    peers[0],
                )
                copy.start()
                to_pair[t, j, k] = copy

    def sum_along(t):
        for j in order:
            src = there[j][0]
            for k in range(1, pairs):
                n = (t * n_s + j) * pairs + k
                far = lax.rem(outer + k, pairs)
                to_pair[t, j, k].wait_recv()
                value = load(res.at[far * 2 + inner, t, src]) + load(inn.at[far, t, src], 1)
                store(osum.at[k - 1, t, src], value.astype(BF16))
                copy = remote(
                    osum.at[k - 1, t, src],
                    outr.at[k - 1, t, src],
                    s_out.at[n],
                    r_out.at[n],
                    peers[k],
                )
                copy.start()
                along[t, j, k] = copy

    def send_home(t):
        for j in order:
            src, device = there[j]
            to_pair[t, j, 0].wait_recv()
            value = load(res.at[c, t, src]) + load(inn.at[outer, t, src], 1)
            for k in range(1, pairs):
                along[t, j, k].wait_recv()
                value = value + load(outr.at[k - 1, t, src], 2)
            if j == 0:
                back_ref[t, me] = value.astype(BF16)
            else:
                xin[t, src] = value.astype(BF16)
                n = t * n_s + j
                copy = remote(xin.at[t, src], back_ref.at[t, me], s_h.at[n], r_h.at[n], device)
                copy.start()
                home[t, j] = copy

    gathered(0)
    keep_w.wait()
    parts, units = ew_ref.shape[0], ew_ref.shape[3]
    def weights_of(n):
        for copy in w_near[n]:
            copy.wait_recv()
        return jnp.concatenate([ew_ref[k, n] for k in range(parts)], axis=1)

    gate, up = weights_of(0), weights_of(1)
    down_of = []

    def hidden_of(n):
        x = load_rows(0, n)
        gate_pre = dot(x, gate)
        up_pre = dot(x, up)
        return gate_pre, up_pre, (gate_pre * jax.nn.sigmoid(gate_pre) * up_pre).astype(BF16)

    for n in range(blocks):
        gate_pre, up_pre, hidden = hidden_of(n)
        if blocks == 1:
            gate_scr[...] = gate_pre
            up_scr[...] = up_pre
            hid_scr[...] = hidden
        if n == 0:
            down_of.append(weights_of(2))
        store_rows(0, n, dot(hidden, down_of[0], 1, 1))
    down = down_of[0]
    sum_pair(0)
    gathered(1)
    for n in range(blocks):
        dy = load_rows(1, n)
        d_hidden = dot(dy, down)
        if n == 0:
            sum_along(0)
        if blocks == 1:
            gate_pre, up_pre, hidden = gate_scr[...], up_scr[...], hid_scr[...]
        else:
            gate_pre, up_pre, hidden = hidden_of(n)
        sig = jax.nn.sigmoid(gate_pre)
        d_gate = (d_hidden * up_pre * sig * (1.0 + gate_pre * (1.0 - sig))).astype(BF16)
        d_up = (d_hidden * gate_pre * sig).astype(BF16)
        store_rows(1, n, dot(d_gate, gate, 1, 1) + dot(d_up, up, 1, 1))
        if n == blocks - 1:
            sum_pair(1)
        x = load_rows(0, n)
        for m, (left, right) in enumerate(((x, d_gate), (x, d_up), (dy, hidden))):
            part = dot(left, right, 0, 0)
            if blocks > 1:
                if n > 0:
                    part = part + acc_scr[m]
                if n < blocks - 1:
                    acc_scr[m] = part
            if n == blocks - 1:
                for k in range(parts):
                    gw_ref[k, m] = part[:, k * units : (k + 1) * units].astype(BF16)
                leave((gw_ref.at[:, m], gw_out.at[:, m]))
            if n == blocks - 1 and m == 0:
                sum_along(1)
            if n == blocks - 1 and m == 1:
                send_home(0)
    send_home(1)
    for copy in home.values():
        copy.wait()
    for copy in [*to_pair.values(), *along.values()]:
        copy.wait_send()
    for t in range(2):
        for j in range(1, n_s):
            crossing[t, j].wait_send()
    post.finish()
    for copy in leaving:
        copy.wait()


def front(sizes, cfg, *operands):
    n_e, n_c, n_d = sizes
    hp, n_ff, n_all, n_loc, slots = cfg
    hc = hp * HEAD_DIM
    rows = operands[8].shape[0]
    length = rows * n_c
    w_rows = operands[0].shape[0]
    width = up_to(3 * hc + SMALL, LANES)
    a_rows = up_to(width // LANES * w_rows, 16)
    o_rows = up_to(D // LANES * w_rows, 16)
    units = operands[9].shape[2]
    size = n_d // n_loc
    posts = (n_c - 1) + 2 * spread_count(sizes) + 3 * (size - 1) + 3 * (n_loc - 1) * size
    n_s = n_e * n_loc
    dma = pltpu.SemaphoreType.DMA
    vmem = pl.BlockSpec(memory_space=pltpu.VMEM)
    anywhere = pl.BlockSpec(memory_space=pl.ANY)
    shape = jax.ShapeDtypeStruct
    gathers = 2 * n_s * (n_c - 1)
    pairs = n_c // 2
    more = max(1, pairs - 1)
    wide = [(n_c, 2), (n_c, 2), (pairs, 2), (more, 2), (more, 2)]
    wide = [(*dims, n_s, slots, D) for dims in wide]
    roomy = n_c * n_s * slots * D <= 2**20
    held = [pltpu.VMEM(dims, BF16) for dims in wide] if roomy else []
    extra = [] if roomy else [shape(dims, BF16) for dims in wide]
    take = n_c if n_c * n_s * slots <= 1024 else max(1, 512 // (n_s * slots))
    kept = (
        shape((n_c, rows, D), BF16),
        shape((D, 3 * hc), BF16),
        shape((n_c * hc, D), BF16),
        shape((D, LANES), BF16),
        shape((8, D), F32),
        shape((length, D), BF16),
        shape((hc, length), BF16),
        shape((hp, length, HEAD_DIM), BF16),
        shape((hp, length, HEAD_DIM), BF16),
        shape((n_c, hc, rows), BF16),
        shape((rows, D), F32),
        shape((rows, D), BF16),
        shape((rows, LANES), F32),
        shape((n_d, 3, D, units), BF16),
    )
    return pl.pallas_call(
        functools.partial(front_kernel, sizes, cfg),
        out_shape=(
            *kept,
            shape((2, n_s, slots, D), BF16),
            shape((hp, n_c, length, rows), BF16),
            *extra,
        ),
        in_specs=[vmem] * len(operands),
        out_specs=(anywhere,) * len(kept) + (vmem,) + (anywhere,) * (1 + len(extra)),
        scratch_shapes=[
            *held,
            pltpu.VMEM((8, LANES) if roomy else (4, slots, D), BF16),
            pltpu.VMEM((3, take, n_s, *((8, LANES) if roomy else (slots, D))), BF16),
            *[
                pltpu.VMEM((n_c * n_s * slots, n_d * units) if take == n_c else (16, LANES), kind)
                for kind in (F32, F32, BF16)
            ],
            pltpu.VMEM((3, D, n_d * units) if take < n_c else (8, LANES), F32),
            pltpu.VMEM((n_d, 3, D, units), BF16),
            pltpu.VMEM((LANES, LANES), F32),
            pltpu.VMEM((up_to(w_rows, 8), width), F32),
            pltpu.VMEM((n_c, a_rows, LANES), BF16),
            pltpu.VMEM((o_rows, LANES), BF16),
            pltpu.VMEM((n_e, n_c, n_d, a_rows, LANES), BF16),
            pltpu.VMEM((n_e, n_c, n_d, o_rows, LANES), BF16),
            pltpu.VMEM((n_loc, 3, D, units), BF16),
            pltpu.VMEM((n_c, hc, rows), BF16),
            pltpu.VMEM((hc, length), BF16),
            pltpu.VMEM((2, length, rows), BF16),
            pltpu.VMEM((2, n_s, slots, D), BF16),
            pltpu.VMEM((2, n_s, slots, D), BF16),
            dma((2,)),
            dma((n_c,)),
            dma((n_c,)),
            dma((2 * n_s,)),
            dma((2 * n_s,)),
            dma((gathers,)),
            dma((gathers,)),
            dma((2 * n_s + 1,)),
            dma((posts,)),
            dma((posts,)),
            *[dma((n_c - 1,))] * 4,
            dma((1,)),
            *[dma((2 * n_s * pairs,))] * 4,
            *[dma((2 * n_s,))] * 2,
            *[pltpu.VMEM(k.shape, k.dtype) for k in kept],
            dma((len(kept) + 2,)),
        ],
        compiler_params=pltpu.CompilerParams(
            collective_id=0, has_side_effects=True, vmem_limit_bytes=VMEM_LIMIT
        ),
        name="front",
    )(*operands)


def back_kernel(
    sizes,
    cfg,
    ret_ref,
    h_ref,
    a2_ref,
    small_ref,
    g_ref,
    routest_ref,
    wo_in,
    wqkv_in,
    wsm_ref,
    vec_ref,
    mixed_in,
    a1_in,
    qt_in,
    kh_in,
    vh_in,
    p_ref,
    xg_ref,
    gw_ref,
    block_ref,
    dx_ref,
    dprev_ref,
    gq_ref,
    gk_ref,
    gv_ref,
    go_ref,
    grouter_ref,
    gcoef_ref,
    gvalue_ref,
    ggains_ref,
    egate_ref,
    eup_ref,
    edown_ref,
    dhg,
    dht_scr,
    p_scr,
    dk_acc,
    dv_acc,
    dqt,
    dqkv,
    da_in,
    da_sum,
    da_out,
    x_scr,
    ew_own,
    ew_in,
    ew_mid,
    ew_out,
    t_send,
    t_recv,
    t_z,
    t_zr,
    t_c,
    t_cr,
    o_own,
    o_in,
    o_sum,
    o_out,
    o_x,
    o_xr,
    o_z,
    o_zr,
    l_sem,
    s_g,
    r_g,
    p_sem,
    s_d,
    r_d,
    s_w,
    r_w,
    s_t,
    r_t,
    s_q,
    r_q,
    wo_ref,
    wqkv_ref,
    mixed_ref,
    a1_ref,
    qt_ref,
    kh_ref,
    vh_ref,
    i_sem,
):
    n_e, n_c, n_d = sizes
    hp, n_ff, n_all, n_loc, slots = cfg
    hc = hp * HEAD_DIM
    place = e, c, d = position()
    pairs = n_c // 2
    outer, inner = c // 2, c % 2
    rows = h_ref.shape[0]
    w_rows = go_ref.shape[0]
    shift = 3 * hc % LANES
    chunks = up_to(3 * hc + SMALL, LANES) // LANES
    d_peers = [(e, c, lax.rem(d + k, n_d)) for k in range(1, n_d)]
    length = rows * n_c
    peers = context_peers(sizes, place)
    e_peers = expert_peers(sizes, place)

    bring = pltpu.make_async_copy(gw_ref, ew_own, l_sem.at[1])
    bring.start()

    def fetch_x(b, slot):
        return pltpu.make_async_copy(xg_ref.at[b], x_scr.at[slot], l_sem.at[2 + slot])

    early = {}
    for name, src, dst in (
        ("mixed", mixed_in, mixed_ref),
        ("wo", wo_in, wo_ref),
        ("kh", kh_in, kh_ref),
        ("vh", vh_in, vh_ref),
        ("qt", qt_in, qt_ref),
        ("a1", a1_in, a1_ref),
        ("wqkv", wqkv_in, wqkv_ref),
    ):
        early[name] = pltpu.make_async_copy(src, dst, i_sem.at[len(early)])
        early[name].start()
    fetch_x(c, 2).start()
    blocks = []
    for k in [*range(1, pairs), 0]:
        there = lax.rem(outer + k, pairs)
        blocks.extend([(k, there, there * 2 + 1 - inner), (None, there, there * 2 + inner)])
    fetch_x(blocks[0][2], 0).start()
    hail(peers + e_peers + d_peers)

    size = n_d // n_loc
    group, seat = d // size, lax.rem(d, size)
    mates = [(e, c, group * size + lax.rem(seat + k, size)) for k in range(1, size)]
    others = [lax.rem(group + k, n_loc) for k in range(1, n_loc)]
    freight = Courier(s_w, r_w)
    e_near = {}
    e_far = []

    def expert_start():
        for k, mate in enumerate(mates):
            for r, other in enumerate(others):
                e_near[k, r] = freight.carry(
                    ew_own.at[other * size + lax.rem(seat + k + 1, size)], ew_mid.at[k, r], mate
                )

    def expert_cross():
        for r, other in enumerate(others):
            target = other * size + seat
            for k in range(size - 1):
                e_near[k, r].wait_recv()

            def one(n, carry):
                at = pl.ds(pl.multiple_of(n * tile, tile), tile)
                total = ew_own[target, at, :].astype(F32)
                for k in range(size - 1):
                    total = total + ew_mid[k, r, at, :].astype(F32)
                ew_out[r, at, :] = total.astype(BF16)
                return carry

            tile = ew_own.shape[1] // 9
            lax.fori_loop(0, 9, one, 0)
            e_far.append(freight.carry(ew_out.at[r], ew_in.at[size - 1 + r], (e, c, target)))
        for k, mate in enumerate(mates):
            e_near[k, -1] = freight.carry(ew_own.at[mate[2]], ew_in.at[k], mate)

    def expert_end():
        for k in range(size - 1):
            e_near[k, -1].wait_recv()
        for copy in e_far:
            copy.wait_recv()
        part = ew_own.shape[1] // 3
        for n, ref in enumerate((egate_ref, eup_ref, edown_ref)):
            at = slice(n * part, (n + 1) * part)
            total = ew_own[d, at, :].astype(F32)
            for k in range(size - 1):
                total = total + ew_in[k, at, :].astype(F32)
            ref[pl.ds(group, 1)] = total[None]
            for r in range(n_loc - 1):
                ref[pl.ds(lax.rem(group - r - 1 + n_loc, n_loc), 1)] = ew_in[
                    size - 1 + r, at, :
                ].astype(F32)[None]
        freight.finish()

    await_hails(peers + e_peers + d_peers)
    bring.wait()
    expert_start()
    h = h_ref[...]
    a2 = a2_ref[...].astype(F32)
    g = g_ref[...]
    small = small_ref[...]
    value_one, value_two = vec_ref[2:3, :], vec_ref[3:4, :]
    tables, picks, w_pair, first, other = route_parts(
        routest_ref[...], small, n_ff, n_all, slots
    )
    copy_on, one_on, two_on = [
        [picks[k][:, n_ff + n : n_ff + n + 1] for k in range(2)] for n in (1, 2, 3)
    ]
    g_a2 = jnp.sum(g * a2, axis=1, keepdims=True)
    g_one = jnp.sum(g * value_one, axis=1, keepdims=True)
    g_two = jnp.sum(g * value_two, axis=1, keepdims=True)
    alpha = [copy_on[k] + one_on[k] * first[0] + two_on[k] * other[0] for k in range(2)]
    a_weight = alpha[0] * w_pair[0] + alpha[1] * w_pair[1]
    one_weight = one_on[0] * w_pair[0] + one_on[1] * w_pair[1]
    two_weight = two_on[0] * w_pair[0] + two_on[1] * w_pair[1]
    returned = [ret_ref[t].reshape(n_ff * slots, D) for t in range(2)]
    block = h
    d_weight = []
    for k in range(2):
        routed = dot(tables[k], returned[0], 0, 0)
        picked = (
            routed
            + alpha[k] * a2
            + (one_on[k] * first[1]) * value_one
            + (two_on[k] * other[1]) * value_two
        )
        block = block + w_pair[k] * picked
        d_weight.append(jnp.sum(g * picked, axis=1, keepdims=True))
    block_ref[...] = block
    center = w_pair[0] * d_weight[0] + w_pair[1] * d_weight[1]
    d_logits = (
        picks[0] * (w_pair[0] * (d_weight[0] - center))
        + picks[1] * (w_pair[1] * (d_weight[1] - center))
    )
    dprev_ref[...] = d_logits.T[:n_all, :]
    lane = lax.broadcasted_iota(jnp.int32, (rows, LANES), 1)
    d_small = d_logits
    for base, pair, weight, g_value in (
        (n_all, first, one_weight, g_one),
        (n_all + 2, other, two_weight, g_two),
    ):
        d_pair = (weight * g_a2, weight * g_value)
        middle = pair[0] * d_pair[0] + pair[1] * d_pair[1]
        for k in range(2):
            d_small = d_small + jnp.where(lane == base + k, pair[k] * (d_pair[k] - middle), 0.0)
    d_small = d_small.astype(BF16)
    d_const_one = jnp.sum((first[1] * one_weight) * g, axis=0, keepdims=True)
    d_const_two = jnp.sum((other[1] * two_weight) * g, axis=0, keepdims=True)
    d_a2 = (
        dot(tables[0] + tables[1], returned[1], 0, 0)
        + a_weight * g
        + dot(d_small, wsm_ref[...], 1, 1)
    )
    gain_two = vec_ref[1:2, :]
    inverse_two = lax.rsqrt(jnp.mean(h * h, axis=-1, keepdims=True) + EPS)
    d_gain_two = jnp.sum(d_a2 * h * inverse_two, axis=0, keepdims=True)
    scaled = gain_two * d_a2
    d_h = (
        g
        + inverse_two * scaled
        - h * inverse_two**3 * jnp.mean(scaled * h, axis=-1, keepdims=True)
    )
    d_hb = d_h.astype(BF16)
    dhg[pl.ds(c, 1)] = d_hb[None]
    gather = ContextGather(
        sizes,
        place,
        dhg.at[c],
        lambda k: dhg.at[k],
        lambda k: s_g.at[k],
        lambda k: r_g.at[k],
    )
    gather.start()
    dx_ref[...] = d_h
    early["mixed"].wait()
    g_o = dot(mixed_ref[...].reshape(n_c * hc, rows), d_hb)
    run = n_d * w_rows
    for b in range(n_c):
        for k in range(n_e):
            o_own[b, k, :run, :] = g_o[(k * n_c + b) * run : (k * n_c + b + 1) * run].astype(BF16)
    parcel = Courier(s_q, r_q)
    o_pair = {}
    for k in [*range(1, pairs), 0]:
        there = lax.rem(outer + k, pairs)
        o_pair[k] = parcel.carry(
            o_own.at[there * 2 + 1 - inner], o_in.at[there], peers[0]
        )
    o_state = {}

    def o_outer():
        o_state["outer"] = []
        for k in range(1, pairs):
            there = lax.rem(outer + k, pairs)
            o_pair[k].wait_recv()
            o_sum[k - 1] = (
                o_own[there * 2 + inner].astype(F32) + o_in[there].astype(F32)
            ).astype(BF16)
            o_state["outer"].append(
                parcel.carry(o_sum.at[k - 1], o_out.at[k - 1], peers[k])
            )

    def o_across():
        o_pair[0].wait_recv()
        total = o_own[c].astype(F32) + o_in[outer].astype(F32)
        for k, copy in enumerate(o_state["outer"]):
            copy.wait_recv()
            total = total + o_out[k].astype(F32)
        o_x[...] = total.astype(BF16)
        o_state["across"] = [
            parcel.carry(o_x.at[lax.rem(e + j, n_e)], o_xr.at[j - 1], e_peers[j - 1])
            for j in range(1, n_e)
        ]

    def o_along():
        total = o_x[e].astype(F32)
        for j, copy in enumerate(o_state["across"]):
            copy.wait_recv()
            total = total + o_xr[j].astype(F32)
        for k in range(n_d):
            o_z[k, :w_rows, :] = total[k * w_rows : (k + 1) * w_rows].astype(BF16)
        o_state["along"] = [
            parcel.carry(o_z.at[lax.rem(d + k, n_d)], o_zr.at[k - 1], d_peers[k - 1])
            for k in range(1, n_d)
        ]

    def o_end():
        total = o_z[d].astype(F32)
        for k, copy in enumerate(o_state["along"]):
            copy.wait_recv()
            total = total + o_zr[k].astype(F32)
        go_ref[...] = total[:w_rows]
        parcel.finish()

    if shift:
        d_small = jnp.concatenate(
            [jnp.zeros((rows, shift), BF16), d_small[:, : LANES - shift]], axis=1
        )
    g_small = dot(a2_ref[...], d_small, 0, 0)
    dk_acc[...] = jnp.zeros_like(dk_acc)
    dv_acc[...] = jnp.zeros_like(dv_acc)
    order = [(b, j) for b in reversed(range(n_c)) for j in range(hp)]

    def fetch(n):
        b, j = order[n]
        reach = pl.ds(0, (b + 1) * rows)
        return pltpu.make_async_copy(p_ref.at[j, b, reach], p_scr.at[n % 2, reach], p_sem.at[n % 2])

    fetch(0).start()
    expert_cross()
    gather.forward()
    gather.finish()
    o_outer()
    for name in ("wo", "kh", "vh", "qt"):
        early[name].wait()
    wo_part = wo_ref[pl.ds(pl.multiple_of(c * hc, hc), hc), :]
    for b in range(n_c):
        dht_scr[:, b * rows : (b + 1) * rows] = dot(wo_part, dhg[b], 1, 1).astype(BF16)
    for n, (b, j) in enumerate(order):
        reach = (b + 1) * rows
        head = slice(j * HEAD_DIM, (j + 1) * HEAD_DIM)
        mine_q = slice(b * rows, reach)
        if n == len(order) // 4:
            o_across()
        if n == len(order) // 2:
            o_along()
        if n + 1 < len(order):
            fetch(n + 1).start()
        fetch(n).wait()
        rounded = p_scr[n % 2, :reach, :]
        prob = rounded.astype(F32)
        d_o = dht_scr[head, mine_q]
        d_prob = dot(vh_ref[j, :reach, :], d_o)
        delta = jnp.sum(prob * d_prob, axis=0, keepdims=True)
        d_scores = (prob * (d_prob - delta)).astype(BF16)
        dqt[head, mine_q] = dot(kh_ref[j, :reach, :], d_scores, 0, 0) * HEAD_DIM**-0.5
        dk_acc[j, :reach, :] += dot(d_scores, qt_ref[head, mine_q], 1, 1)
        dv_acc[j, :reach, :] += dot(rounded, d_o, 1, 1)
    dqkv[:, :hc] = dqt[...].T.astype(BF16)
    for j in range(hp):
        at = j * HEAD_DIM
        dqkv[:, hc + at : hc + at + HEAD_DIM] = dk_acc[j].astype(BF16)
        dqkv[:, 2 * hc + at : 2 * hc + at + HEAD_DIM] = dv_acc[j].astype(BF16)
    dqkv[:, 3 * hc :] = jnp.zeros((length, dqkv.shape[1] - 3 * hc), BF16)
    d_all = dqkv[...]
    bag = Courier(s_t, r_t)
    across = {}
    early["a1"].wait()
    early["wqkv"].wait()
    g_all = dot(a1_ref[...], d_all, 0, 0)
    half = D // n_e

    def send_chunk(k, value):
        for n in range(n_e):
            t_send[k, n] = value[n * half : (n + 1) * half].astype(BF16)
        across[k] = [
            bag.carry(t_send.at[k, lax.rem(e + j, n_e)], t_recv.at[k, j - 1], e_peers[j - 1])
            for j in range(1, n_e)
        ]

    for k in range(chunks - 1):
        send_chunk(k, g_all[:, k * LANES : (k + 1) * LANES])
    wqkv = wqkv_ref[...]
    gain_one = vec_ref[0:1, :]
    d_gain_one = jnp.zeros((1, D), F32)
    to_pair = []
    for n, (k, there, b) in enumerate(blocks):
        if n + 1 < n_c:
            fetch_x(blocks[n + 1][2], (n + 1) % 2).start()
        here = pl.ds(pl.multiple_of(b * rows, rows), rows)
        part = dot(dqkv[here, : 3 * hc], wqkv, 1, 1)
        dhg[pl.ds(b, 1)] = part.astype(BF16)[None]
        if k is not None:
            copy = remote(dhg.at[b], da_in.at[there], s_d.at[k], r_d.at[k], peers[0])
            copy.start()
            to_pair.append((k, copy))
        fetch_x(b, n % 2).wait()
        x = x_scr[n % 2].astype(F32)
        inverse = lax.rsqrt(jnp.mean(x * x, axis=-1, keepdims=True) + EPS)
        d_gain_one = d_gain_one + jnp.sum(part * x * inverse, axis=0, keepdims=True)
    spot = lax.broadcasted_iota(jnp.int32, (LANES, D), 0)
    lines = jnp.zeros((LANES, D), F32)
    for n, row in enumerate((d_const_one, d_const_two, d_gain_one, d_gain_two)):
        lines = lines + jnp.where(spot == shift + n_all + 4 + n, row, 0.0)
    send_chunk(chunks - 1, g_all[:, (chunks - 1) * LANES :] + g_small + lines.T)
    along = []
    for k, copy in to_pair:
        if k == 0:
            continue
        there = lax.rem(outer + k, pairs)
        copy.wait_recv()
        da_sum[k - 1] = (
            dhg[there * 2 + inner].astype(F32) + da_in[there].astype(F32)
        ).astype(BF16)
        onward = remote(
            da_sum.at[k - 1],
            da_out.at[k - 1],
            s_d.at[pairs + k - 1],
            r_d.at[pairs + k - 1],
            peers[k],
        )
        onward.start()
        along.append(onward)
    down = {}
    for k in range(chunks):
        total = t_send[k, e].astype(F32)
        for j, copy in enumerate(across[k]):
            copy.wait_recv()
            total = total + t_recv[k, j].astype(F32)
        for n in range(n_d):
            t_z[k, n, : n_c * w_rows, :] = jnp.concatenate(
                [
                    total[(b * n_d + n) * w_rows : (b * n_d + n + 1) * w_rows]
                    for b in range(n_c)
                ],
                axis=0,
            ).astype(BF16)
        down[k] = [
            bag.carry(t_z.at[k, lax.rem(d + n, n_d)], t_zr.at[k, n - 1], d_peers[n - 1])
            for n in range(1, n_d)
        ]
    o_end()
    to_pair[-1][1].wait_recv()
    d_a1 = dhg[c].astype(F32) + da_in[outer].astype(F32)
    for k, copy in enumerate(along):
        copy.wait_recv()
        d_a1 = d_a1 + da_out[k].astype(F32)
    fetch_x(c, 2).wait()
    x = x_scr[2].astype(F32)
    inverse_one = lax.rsqrt(jnp.mean(x * x, axis=-1, keepdims=True) + EPS)
    scaled = gain_one * d_a1
    dx_ref[...] += inverse_one * scaled - x * inverse_one**3 * jnp.mean(
        scaled * x, axis=-1, keepdims=True
    )
    for k in range(chunks):
        total = t_z[k, d].astype(F32)
        for n, copy in enumerate(down[k]):
            copy.wait_recv()
            total = total + t_zr[k, n].astype(F32)
        for b in range(n_c):
            t_c[b, k, :w_rows, :] = total[b * w_rows : (b + 1) * w_rows]
    t_cr[pl.ds(c, 1)] = t_c[pl.ds(c, 1)]
    turned = [
        bag.carry(t_c.at[lax.rem(c + k, n_c)], t_cr.at[c], (e, lax.rem(c + k, n_c), d))
        for k in range(1, n_c)
    ]
    expert_end()
    for copy in turned:
        copy.wait_recv()
    s_total = jnp.zeros((w_rows, SMALL), F32)
    for b in range(n_c):
        line = jnp.concatenate([t_cr[b, k] for k in range(chunks)], axis=1)[:w_rows]
        for n, ref in enumerate((gq_ref, gk_ref, gv_ref)):
            width = min(hc, D - b * hc)
            if width > 0:
                ref[:, b * hc : b * hc + width] = line[:, n * hc : n * hc + width]
        s_total = s_total + line[:, 3 * hc : 3 * hc + SMALL]
    s_lines = jnp.concatenate([s_total, jnp.zeros((w_rows, LANES - SMALL), F32)], axis=1)
    s_lines = tall(s_lines, LANES).T
    at = 0
    for ref in (grouter_ref, gcoef_ref, gvalue_ref, ggains_ref):
        ref[...] = s_lines[at : at + ref.shape[0], :w_rows]
        at += ref.shape[0]
    bag.finish()
    for _, copy in to_pair:
        copy.wait_send()
    for copy in along:
        copy.wait_send()


def backward(sizes, cfg, *operands):
    n_e, n_c, n_d = sizes
    hp, n_ff, n_all, n_loc, slots = cfg
    hc = hp * HEAD_DIM
    rows = operands[1].shape[0]
    length = rows * n_c
    pairs = n_c // 2
    dma = pltpu.SemaphoreType.DMA
    vmem = pl.BlockSpec(memory_space=pltpu.VMEM)
    anywhere = pl.BlockSpec(memory_space=pl.ANY)
    shape = jax.ShapeDtypeStruct
    part = operands[17].shape[1]
    w_rows = D // (n_e * n_c * n_d)
    chunks = up_to(3 * hc + SMALL, LANES) // LANES
    run = up_to(n_d * w_rows, 16)
    turn = up_to(n_c * w_rows, 16)
    few = up_to(w_rows, 16)
    few_wide = up_to(w_rows, 8)
    size = n_d // n_loc
    loads = (size - 1) * n_loc + n_loc - 1
    bags = chunks * (n_e - 1 + n_d - 1) + n_c - 1
    parcels = 2 * pairs - 1 + n_e - 1 + n_d - 1
    n_more = max(1, pairs - 1)
    in_specs = [vmem] * len(operands)
    in_specs[15] = in_specs[16] = in_specs[17] = anywhere
    late = [operands[n] for n in (6, 7, 10, 11, 12, 13, 14)]
    for n in (6, 7, 10, 11, 12, 13, 14):
        in_specs[n] = anywhere
    return pl.pallas_call(
        functools.partial(back_kernel, sizes, cfg),
        out_shape=(
            shape((rows, D), F32),
            shape((rows, D), F32),
            shape((n_all, rows), F32),
            *[shape((w_rows, D), F32)] * 4,
            *[shape((n, w_rows), F32) for n in (n_all, 4, 2, 2)],
            *[shape((n_loc, part // 3, LANES), F32)] * 3,
        ),
        in_specs=in_specs,
        out_specs=(vmem,) * 14,
        scratch_shapes=[
            pltpu.VMEM((n_c, rows, D), BF16),
            pltpu.VMEM((hc, length), BF16),
            pltpu.VMEM((2, length, rows), BF16),
            pltpu.VMEM((hp, length, HEAD_DIM), F32),
            pltpu.VMEM((hp, length, HEAD_DIM), F32),
            pltpu.VMEM((hc, length), F32),
            pltpu.VMEM((length, chunks * LANES), BF16),
            pltpu.VMEM((pairs, rows, D), BF16),
            pltpu.VMEM((n_more, rows, D), BF16),
            pltpu.VMEM((n_more, rows, D), BF16),
            pltpu.VMEM((3, rows, D), BF16),
            pltpu.VMEM((n_d, part, LANES), BF16),
            pltpu.VMEM((size + n_loc - 2, part, LANES), BF16),
            pltpu.VMEM((max(1, size - 1), max(1, n_loc - 1), part, LANES), BF16),
            pltpu.VMEM((max(1, n_loc - 1), part, LANES), BF16),
            pltpu.VMEM((chunks, n_e, D // n_e, LANES), BF16),
            pltpu.VMEM((chunks, n_e - 1, D // n_e, LANES), BF16),
            pltpu.VMEM((chunks, n_d, turn, LANES), BF16),
            pltpu.VMEM((chunks, n_d - 1, turn, LANES), BF16),
            pltpu.VMEM((n_c, chunks, few_wide, LANES), F32),
            pltpu.VMEM((n_c, chunks, few_wide, LANES), F32),
            pltpu.VMEM((n_c, n_e, run, D), BF16),
            pltpu.VMEM((pairs, n_e, run, D), BF16),
            pltpu.VMEM((n_more, n_e, run, D), BF16),
            pltpu.VMEM((n_more, n_e, run, D), BF16),
            pltpu.VMEM((n_e, run, D), BF16),
            pltpu.VMEM((n_e - 1, run, D), BF16),
            pltpu.VMEM((n_d, few, D), BF16),
            pltpu.VMEM((n_d - 1, few, D), BF16),
            dma((5,)),
            dma((n_c - 1,)),
            dma((n_c - 1,)),
            dma((2,)),
            dma((n_c,)),
            dma((n_c,)),
            dma((loads,)),
            dma((loads,)),
            dma((bags,)),
            dma((bags,)),
            dma((parcels,)),
            dma((parcels,)),
            *[pltpu.VMEM(w.shape, w.dtype) for w in late],
            dma((len(late),)),
        ],
        compiler_params=pltpu.CompilerParams(
            collective_id=1, has_side_effects=True, vmem_limit_bytes=VMEM_LIMIT
        ),
        name="backward",
    )(*operands)


def hand_out_kernel(*refs):
    count = (len(refs) - 2) // 3
    sources, results, held = refs[:count], refs[count : 2 * count], refs[2 * count : 3 * count]
    in_sems, out_sems = refs[-2:]
    takes = [pltpu.make_async_copy(sources[n], held[n], in_sems.at[n]) for n in range(count)]
    gives = [pltpu.make_async_copy(held[n], results[n], out_sems.at[n]) for n in range(count)]
    for copy in takes:
        copy.start()
    for take, give in zip(takes, gives):
        take.wait()
        give.start()
    for copy in gives:
        copy.wait()


def hand_out(results):
    anywhere = pl.BlockSpec(memory_space=pl.ANY)
    dma = pltpu.SemaphoreType.DMA((len(results),))
    return pl.pallas_call(
        hand_out_kernel,
        out_shape=tuple(jax.ShapeDtypeStruct(r.shape, r.dtype) for r in results),
        in_specs=[anywhere] * len(results),
        out_specs=(anywhere,) * len(results),
        scratch_shapes=[*[pltpu.VMEM(r.shape, r.dtype) for r in results], dma, dma],
        compiler_params=pltpu.CompilerParams(vmem_limit_bytes=VMEM_LIMIT),
        name="hand_out",
    )(*results)


def body(
    tokens,
    doc_ids,
    routes,
    prev_logits,
    cotangent,
    w_query,
    w_key,
    w_value,
    w_out,
    w_router,
    const_coef,
    const_value,
    norm_gains,
    expert_gate,
    expert_up,
    expert_down,
):
    sizes = n_e, n_c, n_d = tuple(lax.axis_size(axis) for axis in ALL_AXES)
    rows = tokens.shape[1]
    length = doc_ids.shape[1]
    n_loc, _, units = expert_gate.shape
    n_ff = n_loc * n_e
    n_all = w_router.shape[1]
    slots = rows // 4
    hp = -(-HEADS // n_c)
    cfg = (hp, n_ff, n_all, n_loc, slots)
    routes_t = routes[0].T
    upstream = cotangent[0]
    (
        x_all,
        wqkv,
        wo,
        wsm,
        vec,
        a1,
        q_t,
        k_h,
        v_h,
        mixed,
        h,
        a2,
        small,
        grads,
        returned,
        probs,
        *_,
    ) = front(
        sizes,
        cfg,
        w_query,
        w_key,
        w_value,
        w_out,
        w_router.T,
        const_coef.T,
        const_value.T,
        norm_gains.T,
        tokens[0],
        expert_gate,
        expert_up,
        expert_down,
        doc_ids,
        routes_t,
        prev_logits[0].T,
        upstream,
    )
    results = backward(
        sizes,
        cfg,
        returned,
        h,
        a2,
        small,
        upstream,
        routes_t,
        wo,
        wqkv,
        wsm,
        vec,
        mixed,
        a1,
        q_t,
        k_h,
        v_h,
        probs,
        x_all,
        grads.reshape(n_d, 3 * D * units // LANES, LANES),
    )
    block_rows, d_x, d_prev, *square = hand_out(results)
    narrow = square[4:8]
    return (
        block_rows[None],
        d_x[None],
        d_prev.T[None],
        *square[:4],
        *[grad.T for grad in narrow],
        *[grad.reshape(n_loc, D, units) for grad in square[8:]],
    )


def solution(mesh):
    rows = P(("expert", "dp"), "context", None)
    weights = P(ALL_AXES, None)
    units = P("expert", None, ("context", "dp"))
    return jax.shard_map(
        body,
        mesh=mesh,
        in_specs=(rows, P(("expert", "dp"), None), rows, rows, rows)
        + (weights,) * 8
        + (units,) * 3,
        out_specs=(rows,) * 3 + (weights,) * 8 + (units,) * 3,
        check_vma=False,
    )
```

```python
import functools

import jax
import jax.numpy as jnp
from jax import lax
from jax.experimental import pallas as pl
from jax.experimental.pallas import tpu as pltpu
from jax.sharding import PartitionSpec as P

D = 768
HEADS = 12
HEAD_DIM = 64
EPS = 1e-06
SMALL = 64
LANES = 128
VMEM_LIMIT = 63 * 2**20
MESH = pl.DeviceIdType.MESH
F32 = jnp.float32
BF16 = jnp.bfloat16
ALL_AXES = ("expert", "context", "dp")


def dot(left, right, left_dim=1, right_dim=0):
    return lax.dot_general(
        left, right, (((left_dim,), (right_dim,)), ((), ())), preferred_element_type=F32
    )


def position():
    return lax.axis_index("expert"), lax.axis_index("context"), lax.axis_index("dp")


def remote(src, dst, send_sem, recv_sem, device):
    return pltpu.make_async_remote_copy(
        src_ref=src,
        dst_ref=dst,
        send_sem=send_sem,
        recv_sem=recv_sem,
        device_id=device,
        device_id_type=MESH,
    )


def hail(devices):
    barrier = pltpu.get_barrier_semaphore()
    for device in devices:
        pl.semaphore_signal(barrier, inc=1, device_id=device, device_id_type=MESH)


def await_hails(devices):
    pl.semaphore_wait(pltpu.get_barrier_semaphore(), len(devices))


def context_peers(sizes, place):
    e, c, d = place
    pairs = sizes[1] // 2
    outer, inner = c // 2, c % 2
    peers = [(e, outer * 2 + 1 - inner, d)]
    for k in range(1, pairs):
        peers.append((e, lax.rem(outer + k, pairs) * 2 + inner, d))
    return peers


def expert_peers(sizes, place):
    e, c, d = place
    return [(lax.rem(e + j, sizes[0]), c, d) for j in range(1, sizes[0])]


def crossing_only(sizes, n_loc, place):
    _, there, _ = homes(sizes, n_loc, place)
    return [device for j, (_, device) in enumerate(there) if j // n_loc and j % n_loc]


def homes(sizes, n_loc, place):
    n_e, n_c, n_d = sizes
    e, c, d = place
    size = n_d // n_loc
    group, seat = d // size, lax.rem(d, size)
    there, back = [], []
    for j in range(n_e * n_loc):
        je, jg = j // n_loc, j % n_loc
        to_e, to_g = lax.rem(e + je, n_e), lax.rem(group + jg, n_loc)
        from_e, from_g = lax.rem(e - je + n_e, n_e), lax.rem(group - jg + n_loc, n_loc)
        there.append((to_e * n_loc + to_g, (to_e, c, to_g * size + seat)))
        back.append(from_e * n_loc + from_g)
    return e * n_loc + group, there, back


class Courier:
    def __init__(self, send, recv):
        self.send, self.recv = send, recv
        self.copies = []

    def carry(self, src, dst, device):
        n = len(self.copies)
        copy = remote(src, dst, self.send.at[n], self.recv.at[n], device)
        copy.start()
        self.copies.append(copy)
        return copy

    def finish(self):
        for copy in self.copies:
            copy.wait_send()


def up_to(count, step):
    return -(-count // step) * step


class ContextGather:
    def __init__(self, sizes, place, own, slot, send, recv):
        e, c, d = place
        self.pairs = sizes[1] // 2
        self.place, self.own, self.slot = place, own, slot
        self.send, self.recv = send, recv
        self.outer, self.inner = c // 2, c % 2
        self.peers = context_peers(sizes, place)
        self.copies = []
        self.forwards = []

    def start(self):
        for k in [*range(1, self.pairs), 0]:
            copy = remote(
                self.own, self.slot(self.place[1]), self.send(k), self.recv(k), self.peers[k]
            )
            copy.start()
            self.copies.append((k, copy))

    def origin(self, k):
        return lax.rem(self.outer - k + self.pairs, self.pairs) * 2 + self.inner

    def forward(self):
        for k, copy in self.copies:
            if k > 0:
                copy.wait_recv()
                block = self.slot(self.origin(k))
                n = self.pairs - 1 + k
                onward = remote(block, block, self.send(n), self.recv(n), self.peers[0])
                onward.start()
                self.forwards.append(onward)

    def finish(self):
        for k, copy in self.copies:
            if k == 0:
                copy.wait_recv()
            copy.wait_send()
        for copy in self.forwards:
            copy.wait()


class Spread:
    def __init__(self, sizes, place, courier, own, slot):
        self.sizes, self.place, self.courier = sizes, place, courier
        self.slot = slot
        n_e, n_c, n_d = sizes
        e, c, d = place
        self.across_to = expert_peers(sizes, place)
        self.along = [
            courier.carry(own, slot(e, d), (e, c, lax.rem(d + k, n_d))) for k in range(1, n_d)
        ]
        self.across = [courier.carry(own, slot(e, d), device) for device in self.across_to]

    def onward(self):
        e, c, d = self.place
        n_d = self.sizes[2]
        for k in range(1, n_d):
            self.along[k - 1].wait_recv()
            block = self.slot(e, lax.rem(d - k + n_d, n_d))
            for device in self.across_to:
                self.across.append(self.courier.carry(block, block, device))

    def arrive(self):
        for copy in self.across:
            copy.wait_recv()


def spread_count(sizes):
    n_e, n_c, n_d = sizes
    return (n_d - 1) + (n_e - 1) * n_d


def softmax_pair(left, right):
    top = jnp.maximum(left, right)
    left, right = jnp.exp(left - top), jnp.exp(right - top)
    total = left + right
    return left / total, right / total


def tall(array, height):
    if array.shape[0] == height:
        return array
    return jnp.concatenate(
        [array, jnp.zeros((height - array.shape[0], *array.shape[1:]), array.dtype)], axis=0
    )


def route_parts(routes_t, small, n_ff, n_all, slots):
    rows = routes_t.shape[1]
    routes = tall(routes_t.astype(F32), LANES).T
    hot = lax.broadcasted_iota(jnp.int32, (LANES, rows), 0)
    marks = [(hot == routes_t[k : k + 1, :]) & (hot < n_ff) for k in range(2)]
    both = (marks[0] | marks[1]).astype(F32)
    earlier = lax.broadcasted_iota(jnp.int32, (rows, rows), 0) < lax.broadcasted_iota(
        jnp.int32, (rows, rows), 1
    )
    rank = dot(both.astype(BF16), earlier.astype(F32).astype(BF16))
    number = lax.broadcasted_iota(jnp.int32, (slots, rows), 0).astype(F32)
    tables = []
    for k in range(2):
        wanted = jnp.where(marks[k], rank, -1.0)
        tables.append(
            jnp.concatenate(
                [(number == wanted[j : j + 1, :]).astype(F32) for j in range(n_ff)], axis=0
            ).astype(BF16)
        )
    lane = lax.broadcasted_iota(jnp.int32, (rows, LANES), 1)
    picks = [(lane.astype(F32) == routes[:, k : k + 1]).astype(F32) for k in range(2)]
    chosen = [
        jnp.sum(jnp.where(picks[k] > 0, small, 0.0), axis=1, keepdims=True) for k in range(2)
    ]
    w_pair = softmax_pair(chosen[0], chosen[1])
    first = softmax_pair(small[:, n_all : n_all + 1], small[:, n_all + 1 : n_all + 2])
    second = softmax_pair(small[:, n_all + 2 : n_all + 3], small[:, n_all + 3 : n_all + 4])
    return tables, picks, w_pair, first, second


def front_kernel(
    sizes,
    cfg,
    wq_ref,
    wk_ref,
    wv_ref,
    wout_ref,
    router_ref,
    coef_ref,
    value_ref,
    gains_ref,
    xown_ref,
    gate_ref,
    up_ref,
    down_ref,
    drow_ref,
    routest_ref,
    prev_ref,
    g_ref,
    xg_out,
    wqkv_out,
    wo_out,
    wsm_out,
    vec_out,
    a1_out,
    qt_out,
    kh_out,
    vh_out,
    mixed_out,
    h_out,
    a2_out,
    small_out,
    gw_out,
    back_ref,
    p_ref,
    slots_ref,
    res,
    inn,
    osum,
    outr,
    stage,
    blk,
    gate_scr,
    up_scr,
    hid_scr,
    acc_scr,
    ew_ref,
    small_scr,
    row_scr,
    a_ref,
    ow_ref,
    ag,
    og,
    ew_own,
    o_scr,
    vt_scr,
    p_scr,
    sbuf,
    xin,
    p_sem,
    s_o,
    r_o,
    s_x,
    r_x,
    s_g,
    r_g,
    l_g,
    s_c,
    r_c,
    s_ow,
    r_ow,
    s_xg,
    r_xg,
    b_sem,
    s_in,
    r_in,
    s_out,
    r_out,
    s_h,
    r_h,
    xg_ref,
    wqkv_ref,
    wo_ref,
    wsm_ref,
    vec_ref,
    a1_ref,
    qt_ref,
    kh_ref,
    vh_ref,
    mixed_ref,
    h_ref,
    a2_ref,
    small_ref,
    gw_ref,
    o_sem,
):
    n_e, n_c, n_d = sizes
    hp, n_ff, n_all, n_loc, slots = cfg
    hc = hp * HEAD_DIM
    place = e, c, d = position()
    rows = xown_ref.shape[0]
    length = rows * n_c
    c_all = [(e, lax.rem(c + k, n_c), d) for k in range(1, n_c)]
    n_s = n_e * n_loc
    me, there, back = homes(sizes, n_loc, place)
    d_peers = [(e, c, lax.rem(d + k, n_d)) for k in range(1, n_d)]
    neighbours = (
        c_all + d_peers + expert_peers(sizes, place) + crossing_only(sizes, n_loc, place)
    )
    hail(neighbours)
    leaving = []

    def leave(*pairs_of):
        for src, dst in pairs_of:
            copy = pltpu.make_async_copy(src, dst, o_sem.at[len(leaving)])
            copy.start()
            leaving.append(copy)

    w_rows = wq_ref.shape[0]
    small_scr[...] = jnp.zeros_like(small_scr)
    at = 0
    for ref in (router_ref, coef_ref, value_ref, gains_ref):
        small_scr[at : at + ref.shape[0], :w_rows] = ref[...]
        at += ref.shape[0]
    width = row_scr.shape[1]
    w_small = small_scr[...].T[:w_rows, :SMALL]

    def stack(rows_of, tiles, height):
        parts = [rows_of(k * LANES) for k in range(tiles)]
        return tall(jnp.concatenate(parts, axis=0), height).astype(BF16)

    ow_ref[...] = stack(lambda at: wout_ref[:, at : at + LANES], D // LANES, ow_ref.shape[0])
    row_scr[...] = jnp.zeros_like(row_scr)
    row_scr[:w_rows, 3 * hc : 3 * hc + SMALL] = w_small
    for b in range(n_c):
        for n, ref in enumerate((wq_ref, wk_ref, wv_ref)):
            wide = max(0, min(hc, D - b * hc))
            if wide > 0:
                row_scr[:w_rows, n * hc : n * hc + wide] = ref[:, b * hc : b * hc + wide]
            if wide < hc:
                row_scr[:w_rows, n * hc + wide : (n + 1) * hc] = jnp.zeros((w_rows, hc - wide), F32)
        a_ref[b] = stack(
            lambda at: row_scr[:w_rows, at : at + LANES], width // LANES, a_ref.shape[1]
        )
    await_hails(neighbours)
    post = Courier(s_c, r_c)
    turned = [
        post.carry(a_ref.at[lax.rem(c + k, n_c)], ag.at[e, c, d], device)
        for k, device in enumerate(c_all, 1)
    ]
    x_rows = ContextGather(
        sizes,
        place,
        xown_ref,
        lambda k: xg_ref.at[k],
        lambda k: s_xg.at[k],
        lambda k: r_xg.at[k],
    )
    x_rows.start()
    ow_spread = Spread(sizes, place, post, ow_ref, lambda j, k: og.at[j, c, k])
    ag[e, c, d] = a_ref[c]
    og[e, c, d] = ow_ref[...]
    xg_ref[pl.ds(c, 1)] = xown_ref[...][None]
    for n, ref in enumerate((gate_ref, up_ref, down_ref)):
        ew_own[:, n] = ref[...].astype(BF16)
    for copy in turned:
        copy.wait_recv()
    a_spread = Spread(sizes, place, post, ag.at[e, :, d], lambda j, k: ag.at[j, :, k])
    size = n_d // n_loc
    group, seat = d // size, lax.rem(d, size)
    mates = [(e, c, group * size + lax.rem(seat + k, size)) for k in range(1, size)]
    keep_w = pltpu.make_async_copy(ew_own.at[group], ew_ref.at[d], l_g.at[2 * n_s])
    keep_w.start()
    w_far, w_near = {}, {}
    for n in range(3):
        w_near[n] = [post.carry(ew_own.at[group, n], ew_ref.at[d, n], device) for device in mates]
        for k in range(1, n_loc):
            to = lax.rem(group + k, n_loc)
            w_far[n, k] = post.carry(
                ew_own.at[to, n], ew_ref.at[d, n], (e, c, to * size + seat)
            )

    def pass_weights(n):
        for k in range(1, n_loc):
            w_far[n, k].wait_recv()
            block = ew_ref.at[lax.rem(group - k + n_loc, n_loc) * size + seat, n]
            w_near[n].extend([post.carry(block, block, device) for device in mates])

    ow_spread.onward()
    x_rows.forward()
    ow_spread.arrive()
    ow_rows = ContextGather(
        sizes,
        place,
        og.at[:, c],
        lambda k: og.at[:, k],
        lambda k: s_ow.at[k],
        lambda k: r_ow.at[k],
    )
    ow_rows.start()
    a_spread.onward()
    x_rows.finish()
    leave((xg_ref, xg_out))
    a_spread.arrive()

    def unstack(slabs, tiles):
        height = slabs.shape[2]
        slabs = slabs.reshape(n_c * n_d, height, LANES)
        if w_rows % 8 == 0:
            wide = [slabs[n].astype(F32) for n in range(n_c * n_d)]
            return jnp.concatenate(
                [
                    jnp.concatenate([w[k * w_rows : (k + 1) * w_rows] for w in wide], axis=0)
                    for k in range(tiles)
                ],
                axis=1,
            )
        flat = slabs.reshape(n_c * n_d * height, LANES)
        at_row = lax.broadcasted_iota(jnp.int32, (D // n_e, flat.shape[0]), 0)
        at_slab = lax.broadcasted_iota(jnp.int32, (D // n_e, flat.shape[0]), 1)
        first = at_row // w_rows * height + lax.rem(at_row, w_rows)
        return jnp.concatenate(
            [
                dot(jnp.where(at_slab == first + k * w_rows, 1.0, 0.0).astype(BF16), flat)
                for k in range(tiles)
            ],
            axis=1,
        )

    weights = jnp.concatenate([unstack(ag[k], width // LANES) for k in range(n_e)], axis=0)
    wqkv = weights[:, : 3 * hc].astype(BF16)
    wqkv_ref[...] = wqkv
    w_small = jnp.concatenate(
        [weights[:, 3 * hc : 3 * hc + SMALL], jnp.zeros((D, LANES - SMALL), F32)], axis=1
    )
    wsm_ref[...] = w_small.astype(BF16)
    w_lines = w_small.T
    vec_ref[0:2, :] = w_lines[n_all + 6 : n_all + 8, :]
    vec_ref[2:4, :] = w_lines[n_all + 4 : n_all + 6, :]
    vec_ref[4:8, :] = jnp.zeros((4, D), F32)

    gain_one = vec_ref[0:1, :]
    for b in range(n_c):
        x = xg_ref[b].astype(F32)
        inverse = lax.rsqrt(jnp.mean(x * x, axis=-1, keepdims=True) + EPS)
        a1_ref[b * rows : (b + 1) * rows, :] = (x * inverse * gain_one).astype(BF16)
    a1 = a1_ref[...]
    leave((a1_ref, a1_out), (wqkv_ref, wqkv_out), (wsm_ref, wsm_out), (vec_ref, vec_out))
    ow_rows.forward()
    q_t = dot(wqkv[:, :hc], a1, 0, 1).astype(BF16) * jnp.asarray(HEAD_DIM**-0.5, BF16)
    qt_ref[...] = q_t
    kv = dot(a1, wqkv[:, hc:]).astype(BF16)
    for j in range(hp):
        kh_ref[j] = kv[:, j * HEAD_DIM : (j + 1) * HEAD_DIM]
        vh_ref[j] = kv[:, hc + j * HEAD_DIM : hc + (j + 1) * HEAD_DIM]
    vt_scr[...] = dot(wqkv[:, 2 * hc :], a1, 0, 1).astype(BF16)

    leave((qt_ref, qt_out), (kh_ref, kh_out), (vh_ref, vh_out))
    documents = drow_ref[...].astype(F32)
    document_of = jnp.broadcast_to(documents, (LANES, length)).T[:, :1]
    turn = 0
    p_copies = {}
    for b in reversed(range(n_c)):
        reach = (b + 1) * rows
        key_place = lax.broadcasted_iota(jnp.int32, (reach, rows), 0)
        q_place = lax.broadcasted_iota(jnp.int32, (reach, rows), 1) + b * rows
        allowed = (document_of[:reach] == documents[:, b * rows : reach]) & (key_place <= q_place)
        bias = jnp.where(allowed, 0.0, -1e30)
        for j in range(hp):
            head = slice(j * HEAD_DIM, (j + 1) * HEAD_DIM)
            scores = dot(kh_ref[j, :reach, :], qt_ref[head, b * rows : reach]) + bias
            top = jnp.max(scores, axis=0, keepdims=True)
            exponent = jnp.exp(scores - top)
            total = jnp.sum(exponent, axis=0, keepdims=True)
            rounded = (exponent * (1.0 / total)).astype(BF16)
            slot = turn % 2
            if turn >= 2:
                p_copies[turn - 2].wait()
            p_scr[slot, :reach, :] = rounded
            copy = pltpu.make_async_copy(
                p_scr.at[slot, pl.ds(0, reach)], p_ref.at[j, b, pl.ds(0, reach)], p_sem.at[slot]
            )
            copy.start()
            p_copies[turn] = copy
            turn += 1
            o_scr[b, head, :] = dot(vt_scr[head, :reach], rounded).astype(BF16)
        if b == n_c - 1:
            pass_weights(0)

        @pl.when(c != b)
        def _():
            remote(
                o_scr.at[b], mixed_ref.at[c], s_o.at[b], r_o.at[c], (e, b, d)
            ).start()

    pass_weights(1)
    for n in range(max(0, turn - 2), turn):
        p_copies[n].wait()
    ow_rows.finish()
    if n_c * hc > D:
        wo_ref[D:, :] = jnp.zeros((n_c * hc - D, D), BF16)
    for k in range(n_e):
        wo_ref[k * (D // n_e) : (k + 1) * (D // n_e), :] = unstack(og[k], D // LANES).astype(BF16)
    mixed_ref[pl.ds(c, 1)] = o_scr[pl.ds(c, 1)]
    for b in range(n_c):

        @pl.when(c != b)
        def _():
            copy = remote(o_scr.at[b], mixed_ref.at[b], s_o.at[b], r_o.at[b], (e, b, d))
            copy.wait_send()
            copy.wait_recv()

    leave((wo_ref, wo_out), (mixed_ref, mixed_out))
    mixed = mixed_ref[...].reshape(n_c * hc, rows)
    h = xown_ref[...].astype(F32) + dot(mixed, wo_ref[...], 0, 0)
    h_ref[...] = h
    inverse = lax.rsqrt(jnp.mean(h * h, axis=-1, keepdims=True) + EPS)
    a2 = (h * inverse * vec_ref[1:2, :]).astype(BF16)
    a2_ref[...] = a2
    small = dot(a2, wsm_ref[...]) + tall(prev_ref[...], LANES).T
    small_ref[...] = small
    leave((h_ref, h_out), (a2_ref, a2_out), (small_ref, small_out))
    tables, _, w_pair, _, _ = route_parts(routest_ref[...], small, n_ff, n_all, slots)
    crossing = {}
    gathers = {}
    g = g_ref[...]
    for t in range(2):
        if t == 0:
            block = dot(tables[0] + tables[1], a2).astype(BF16)
        else:
            block = dot(tables[0], (w_pair[0] * g).astype(BF16)) + dot(
                tables[1], (w_pair[1] * g).astype(BF16)
            )
            block = block.astype(BF16)
        for k in range(n_s):
            sbuf[t, k] = block[k * slots : (k + 1) * slots, :]
        for j in reversed(range(1, n_s)):
            n = t * n_s + j
            part, device = there[j]
            copy = remote(sbuf.at[t, part], xin.at[t, me], s_x.at[n], r_x.at[n], device)
            copy.start()
            crossing[t, j] = copy

        def gather(j, own, t=t):
            src = back[j]
            base = (t * n_s + j) * (n_c - 1)
            keep = pltpu.make_async_copy(own, slots_ref.at[c, t, src], l_g.at[t * n_s + j])
            keep.start()
            made = ContextGather(
                sizes,
                place,
                own,
                lambda k: slots_ref.at[k, t, src],
                lambda k: s_g.at[base + k],
                lambda k: r_g.at[base + k],
            )
            made.start()
            gathers[t, j] = (made, keep)

        gather(0, sbuf.at[t, me])
        crossing[t, 0] = gather
    for t in range(2):
        for j in range(1, n_s):
            crossing[t, j].wait_recv()
            crossing[t, 0](j, xin.at[t, back[j]])
        if t == 0:
            pass_weights(2)

    def gathered(t):
        for j in range(n_s):
            gathers[t, j][0].forward()
        for j in range(n_s):
            gathers[t, j][0].finish()
            gathers[t, j][1].wait()

    roomy = len(stage.shape) == 2
    take = blk.shape[1]
    blocks = n_c // take
    pairs = n_c // 2
    outer, inner = c // 2, c % 2
    peers = context_peers(sizes, place)

    def load_rows(t, n):
        if roomy:
            return slots_ref[n * take : (n + 1) * take, t].reshape(-1, D)
        copy = pltpu.make_async_copy(slots_ref.at[pl.ds(n * take, take), t], blk.at[t], b_sem.at[0])
        copy.start()
        copy.wait()
        return blk[t].reshape(-1, D)

    def store_rows(t, n, value):
        value = value.astype(BF16).reshape(take, n_s, slots, D)
        if roomy:
            res[n * take : (n + 1) * take, t] = value
        else:
            blk[2] = value
            copy = pltpu.make_async_copy(blk.at[2], res.at[pl.ds(n * take, take), t], b_sem.at[0])
            copy.start()
            copy.wait()

    def load(ref, slot=0):
        if roomy:
            return ref[...].astype(F32)
        copy = pltpu.make_async_copy(ref, stage.at[slot], b_sem.at[0])
        copy.start()
        copy.wait()
        return stage[slot].astype(F32)

    def store(ref, value):
        if roomy:
            ref[...] = value
        else:
            stage[3] = value
            copy = pltpu.make_async_copy(stage.at[3], ref, b_sem.at[0])
            copy.start()
            copy.wait()

    order = [*reversed(range(1, n_s)), 0]
    to_pair, along, home = {}, {}, {}

    def sum_pair(t):
        for j in order:
            src = there[j][0]
            for k in [*range(1, pairs), 0]:
                n = (t * n_s + j) * pairs + k
                far = lax.rem(outer + k, pairs)
                copy = remote(
                    res.at[far * 2 + 1 - inner, t, src],
                    inn.at[far, t, src],
                    s_in.at[n],
                    r_in.at[n],
                    peers[0],
                )
                copy.start()
                to_pair[t, j, k] = copy

    def sum_along(t):
        for j in order:
            src = there[j][0]
            for k in range(1, pairs):
                n = (t * n_s + j) * pairs + k
                far = lax.rem(outer + k, pairs)
                to_pair[t, j, k].wait_recv()
                value = load(res.at[far * 2 + inner, t, src]) + load(inn.at[far, t, src], 1)
                store(osum.at[k - 1, t, src], value.astype(BF16))
                copy = remote(
                    osum.at[k - 1, t, src],
                    outr.at[k - 1, t, src],
                    s_out.at[n],
                    r_out.at[n],
                    peers[k],
                )
                copy.start()
                along[t, j, k] = copy

    def send_home(t):
        for j in order:
            src, device = there[j]
            to_pair[t, j, 0].wait_recv()
            value = load(res.at[c, t, src]) + load(inn.at[outer, t, src], 1)
            for k in range(1, pairs):
                along[t, j, k].wait_recv()
                value = value + load(outr.at[k - 1, t, src], 2)
            if j == 0:
                back_ref[t, me] = value.astype(BF16)
            else:
                xin[t, src] = value.astype(BF16)
                n = t * n_s + j
                copy = remote(xin.at[t, src], back_ref.at[t, me], s_h.at[n], r_h.at[n], device)
                copy.start()
                home[t, j] = copy

    gathered(0)
    keep_w.wait()
    parts, units = ew_ref.shape[0], ew_ref.shape[3]
    def weights_of(n):
        for copy in w_near[n]:
            copy.wait_recv()
        return jnp.concatenate([ew_ref[k, n] for k in range(parts)], axis=1)

    gate, up = weights_of(0), weights_of(1)
    down_of = []

    def hidden_of(n):
        x = load_rows(0, n)
        gate_pre = dot(x, gate)
        up_pre = dot(x, up)
        return gate_pre, up_pre, (gate_pre * jax.nn.sigmoid(gate_pre) * up_pre).astype(BF16)

    for n in range(blocks):
        gate_pre, up_pre, hidden = hidden_of(n)
        if blocks == 1:
            gate_scr[...] = gate_pre
            up_scr[...] = up_pre
            hid_scr[...] = hidden
        if n == 0:
            down_of.append(weights_of(2))
        store_rows(0, n, dot(hidden, down_of[0], 1, 1))
    down = down_of[0]
    sum_pair(0)
    gathered(1)
    for n in range(blocks):
        dy = load_rows(1, n)
        d_hidden = dot(dy, down)
        if n == 0:
            sum_along(0)
        if blocks == 1:
            gate_pre, up_pre, hidden = gate_scr[...], up_scr[...], hid_scr[...]
        else:
            gate_pre, up_pre, hidden = hidden_of(n)
        sig = jax.nn.sigmoid(gate_pre)
        d_gate = (d_hidden * up_pre * sig * (1.0 + gate_pre * (1.0 - sig))).astype(BF16)
        d_up = (d_hidden * gate_pre * sig).astype(BF16)
        store_rows(1, n, dot(d_gate, gate, 1, 1) + dot(d_up, up, 1, 1))
        if n == blocks - 1:
            sum_pair(1)
        x = load_rows(0, n)
        for m, (left, right) in enumerate(((x, d_gate), (x, d_up), (dy, hidden))):
            part = dot(left, right, 0, 0)
            if blocks > 1:
                if n > 0:
                    part = part + acc_scr[m]
                if n < blocks - 1:
                    acc_scr[m] = part
            if n == blocks - 1:
                for k in range(parts):
                    gw_ref[k, m] = part[:, k * units : (k + 1) * units].astype(BF16)
                leave((gw_ref.at[:, m], gw_out.at[:, m]))
            if n == blocks - 1 and m == 0:
                sum_along(1)
            if n == blocks - 1 and m == 1:
                send_home(0)
    send_home(1)
    for copy in home.values():
        copy.wait()
    for copy in [*to_pair.values(), *along.values()]:
        copy.wait_send()
    for t in range(2):
        for j in range(1, n_s):
            crossing[t, j].wait_send()
    post.finish()
    for copy in leaving:
        copy.wait()


def front(sizes, cfg, *operands):
    n_e, n_c, n_d = sizes
    hp, n_ff, n_all, n_loc, slots = cfg
    hc = hp * HEAD_DIM
    rows = operands[8].shape[0]
    length = rows * n_c
    w_rows = operands[0].shape[0]
    width = up_to(3 * hc + SMALL, LANES)
    a_rows = up_to(width // LANES * w_rows, 16)
    o_rows = up_to(D // LANES * w_rows, 16)
    units = operands[9].shape[2]
    size = n_d // n_loc
    posts = (n_c - 1) + 2 * spread_count(sizes) + 3 * (size - 1) + 3 * (n_loc - 1) * size
    n_s = n_e * n_loc
    dma = pltpu.SemaphoreType.DMA
    vmem = pl.BlockSpec(memory_space=pltpu.VMEM)
    anywhere = pl.BlockSpec(memory_space=pl.ANY)
    shape = jax.ShapeDtypeStruct
    gathers = 2 * n_s * (n_c - 1)
    pairs = n_c // 2
    more = max(1, pairs - 1)
    wide = [(n_c, 2), (n_c, 2), (pairs, 2), (more, 2), (more, 2)]
    wide = [(*dims, n_s, slots, D) for dims in wide]
    roomy = n_c * n_s * slots * D <= 2**20
    held = [pltpu.VMEM(dims, BF16) for dims in wide] if roomy else []
    extra = [] if roomy else [shape(dims, BF16) for dims in wide]
    take = n_c if n_c * n_s * slots <= 1024 else max(1, 512 // (n_s * slots))
    kept = (
        shape((n_c, rows, D), BF16),
        shape((D, 3 * hc), BF16),
        shape((n_c * hc, D), BF16),
        shape((D, LANES), BF16),
        shape((8, D), F32),
        shape((length, D), BF16),
        shape((hc, length), BF16),
        shape((hp, length, HEAD_DIM), BF16),
        shape((hp, length, HEAD_DIM), BF16),
        shape((n_c, hc, rows), BF16),
        shape((rows, D), F32),
        shape((rows, D), BF16),
        shape((rows, LANES), F32),
        shape((n_d, 3, D, units), BF16),
    )
    return pl.pallas_call(
        functools.partial(front_kernel, sizes, cfg),
        out_shape=(
            *kept,
            shape((2, n_s, slots, D), BF16),
            shape((hp, n_c, length, rows), BF16),
            *extra,
        ),
        in_specs=[vmem] * len(operands),
        out_specs=(anywhere,) * len(kept) + (vmem,) + (anywhere,) * (1 + len(extra)),
        scratch_shapes=[
            *held,
            pltpu.VMEM((8, LANES) if roomy else (4, slots, D), BF16),
            pltpu.VMEM((3, take, n_s, *((8, LANES) if roomy else (slots, D))), BF16),
            *[
                pltpu.VMEM((n_c * n_s * slots, n_d * units) if take == n_c else (16, LANES), kind)
                for kind in (F32, F32, BF16)
            ],
            pltpu.VMEM((3, D, n_d * units) if take < n_c else (8, LANES), F32),
            pltpu.VMEM((n_d, 3, D, units), BF16),
            pltpu.VMEM((LANES, LANES), F32),
            pltpu.VMEM((up_to(w_rows, 8), width), F32),
            pltpu.VMEM((n_c, a_rows, LANES), BF16),
            pltpu.VMEM((o_rows, LANES), BF16),
            pltpu.VMEM((n_e, n_c, n_d, a_rows, LANES), BF16),
            pltpu.VMEM((n_e, n_c, n_d, o_rows, LANES), BF16),
            pltpu.VMEM((n_loc, 3, D, units), BF16),
            pltpu.VMEM((n_c, hc, rows), BF16),
            pltpu.VMEM((hc, length), BF16),
            pltpu.VMEM((2, length, rows), BF16),
            pltpu.VMEM((2, n_s, slots, D), BF16),
            pltpu.VMEM((2, n_s, slots, D), BF16),
            dma((2,)),
            dma((n_c,)),
            dma((n_c,)),
            dma((2 * n_s,)),
            dma((2 * n_s,)),
            dma((gathers,)),
            dma((gathers,)),
            dma((2 * n_s + 1,)),
            dma((posts,)),
            dma((posts,)),
            *[dma((n_c - 1,))] * 4,
            dma((1,)),
            *[dma((2 * n_s * pairs,))] * 4,
            *[dma((2 * n_s,))] * 2,
            *[pltpu.VMEM(k.shape, k.dtype) for k in kept],
            dma((len(kept) + 2,)),
        ],
        compiler_params=pltpu.CompilerParams(
            collective_id=0, has_side_effects=True, vmem_limit_bytes=VMEM_LIMIT
        ),
        name="front",
    )(*operands)


def back_kernel(
    sizes,
    cfg,
    ret_ref,
    h_ref,
    a2_ref,
    small_ref,
    g_ref,
    routest_ref,
    wo_in,
    wqkv_in,
    wsm_ref,
    vec_ref,
    mixed_in,
    a1_in,
    qt_in,
    kh_in,
    vh_in,
    p_ref,
    xg_ref,
    gw_ref,
    block_ref,
    dx_ref,
    dprev_ref,
    gq_ref,
    gk_ref,
    gv_ref,
    go_ref,
    grouter_ref,
    gcoef_ref,
    gvalue_ref,
    ggains_ref,
    egate_ref,
    eup_ref,
    edown_ref,
    dhg,
    dht_scr,
    p_scr,
    dk_acc,
    dv_acc,
    dqt,
    dqkv,
    da_in,
    da_sum,
    da_out,
    x_scr,
    ew_own,
    ew_in,
    ew_mid,
    ew_out,
    t_send,
    t_recv,
    t_z,
    t_zr,
    t_c,
    t_cr,
    o_own,
    o_in,
    o_sum,
    o_out,
    o_x,
    o_xr,
    o_z,
    o_zr,
    l_sem,
    s_g,
    r_g,
    p_sem,
    s_d,
    r_d,
    s_w,
    r_w,
    s_t,
    r_t,
    s_q,
    r_q,
    wo_ref,
    wqkv_ref,
    mixed_ref,
    a1_ref,
    qt_ref,
    kh_ref,
    vh_ref,
    i_sem,
):
    n_e, n_c, n_d = sizes
    hp, n_ff, n_all, n_loc, slots = cfg
    hc = hp * HEAD_DIM
    place = e, c, d = position()
    pairs = n_c // 2
    outer, inner = c // 2, c % 2
    rows = h_ref.shape[0]
    w_rows = go_ref.shape[0]
    shift = 3 * hc % LANES
    chunks = up_to(3 * hc + SMALL, LANES) // LANES
    d_peers = [(e, c, lax.rem(d + k, n_d)) for k in range(1, n_d)]
    length = rows * n_c
    peers = context_peers(sizes, place)
    e_peers = expert_peers(sizes, place)

    bring = pltpu.make_async_copy(gw_ref, ew_own, l_sem.at[1])
    bring.start()

    def fetch_x(b, slot):
        return pltpu.make_async_copy(xg_ref.at[b], x_scr.at[slot], l_sem.at[2 + slot])

    early = {}
    for name, src, dst in (
        ("mixed", mixed_in, mixed_ref),
        ("wo", wo_in, wo_ref),
        ("kh", kh_in, kh_ref),
        ("vh", vh_in, vh_ref),
        ("qt", qt_in, qt_ref),
        ("a1", a1_in, a1_ref),
        ("wqkv", wqkv_in, wqkv_ref),
    ):
        early[name] = pltpu.make_async_copy(src, dst, i_sem.at[len(early)])
        early[name].start()
    fetch_x(c, 2).start()
    blocks = []
    for k in [*range(1, pairs), 0]:
        there = lax.rem(outer + k, pairs)
        blocks.extend([(k, there, there * 2 + 1 - inner), (None, there, there * 2 + inner)])
    fetch_x(blocks[0][2], 0).start()
    hail(peers + e_peers + d_peers)

    size = n_d // n_loc
    group, seat = d // size, lax.rem(d, size)
    mates = [(e, c, group * size + lax.rem(seat + k, size)) for k in range(1, size)]
    others = [lax.rem(group + k, n_loc) for k in range(1, n_loc)]
    freight = Courier(s_w, r_w)
    e_near = {}
    e_far = []

    def expert_start():
        for k, mate in enumerate(mates):
            for r, other in enumerate(others):
                e_near[k, r] = freight.carry(
                    ew_own.at[other * size + lax.rem(seat + k + 1, size)], ew_mid.at[k, r], mate
                )

    def expert_cross():
        for r, other in enumerate(others):
            target = other * size + seat
            for k in range(size - 1):
                e_near[k, r].wait_recv()

            def one(n, carry):
                at = pl.ds(pl.multiple_of(n * tile, tile), tile)
                total = ew_own[target, at, :].astype(F32)
                for k in range(size - 1):
                    total = total + ew_mid[k, r, at, :].astype(F32)
                ew_out[r, at, :] = total.astype(BF16)
                return carry

            tile = ew_own.shape[1] // 9
            lax.fori_loop(0, 9, one, 0)
            e_far.append(freight.carry(ew_out.at[r], ew_in.at[size - 1 + r], (e, c, target)))
        for k, mate in enumerate(mates):
            e_near[k, -1] = freight.carry(ew_own.at[mate[2]], ew_in.at[k], mate)

    def expert_end():
        for k in range(size - 1):
            e_near[k, -1].wait_recv()
        for copy in e_far:
            copy.wait_recv()
        part = ew_own.shape[1] // 3
        for n, ref in enumerate((egate_ref, eup_ref, edown_ref)):
            at = slice(n * part, (n + 1) * part)
            total = ew_own[d, at, :].astype(F32)
            for k in range(size - 1):
                total = total + ew_in[k, at, :].astype(F32)
            ref[pl.ds(group, 1)] = total[None]
            for r in range(n_loc - 1):
                ref[pl.ds(lax.rem(group - r - 1 + n_loc, n_loc), 1)] = ew_in[
                    size - 1 + r, at, :
                ].astype(F32)[None]
        freight.finish()

    await_hails(peers + e_peers + d_peers)
    bring.wait()
    expert_start()
    h = h_ref[...]
    a2 = a2_ref[...].astype(F32)
    g = g_ref[...]
    small = small_ref[...]
    value_one, value_two = vec_ref[2:3, :], vec_ref[3:4, :]
    tables, picks, w_pair, first, other = route_parts(
        routest_ref[...], small, n_ff, n_all, slots
    )
    copy_on, one_on, two_on = [
        [picks[k][:, n_ff + n : n_ff + n + 1] for k in range(2)] for n in (1, 2, 3)
    ]
    g_a2 = jnp.sum(g * a2, axis=1, keepdims=True)
    g_one = jnp.sum(g * value_one, axis=1, keepdims=True)
    g_two = jnp.sum(g * value_two, axis=1, keepdims=True)
    alpha = [copy_on[k] + one_on[k] * first[0] + two_on[k] * other[0] for k in range(2)]
    a_weight = alpha[0] * w_pair[0] + alpha[1] * w_pair[1]
    one_weight = one_on[0] * w_pair[0] + one_on[1] * w_pair[1]
    two_weight = two_on[0] * w_pair[0] + two_on[1] * w_pair[1]
    returned = [ret_ref[t].reshape(n_ff * slots, D) for t in range(2)]
    block = h
    d_weight = []
    for k in range(2):
        routed = dot(tables[k], returned[0], 0, 0)
        picked = (
            routed
            + alpha[k] * a2
            + (one_on[k] * first[1]) * value_one
            + (two_on[k] * other[1]) * value_two
        )
        block = block + w_pair[k] * picked
        d_weight.append(jnp.sum(g * picked, axis=1, keepdims=True))
    block_ref[...] = block
    center = w_pair[0] * d_weight[0] + w_pair[1] * d_weight[1]
    d_logits = (
        picks[0] * (w_pair[0] * (d_weight[0] - center))
        + picks[1] * (w_pair[1] * (d_weight[1] - center))
    )
    dprev_ref[...] = d_logits.T[:n_all, :]
    lane = lax.broadcasted_iota(jnp.int32, (rows, LANES), 1)
    d_small = d_logits
    for base, pair, weight, g_value in (
        (n_all, first, one_weight, g_one),
        (n_all + 2, other, two_weight, g_two),
    ):
        d_pair = (weight * g_a2, weight * g_value)
        middle = pair[0] * d_pair[0] + pair[1] * d_pair[1]
        for k in range(2):
            d_small = d_small + jnp.where(lane == base + k, pair[k] * (d_pair[k] - middle), 0.0)
    d_small = d_small.astype(BF16)
    d_const_one = jnp.sum((first[1] * one_weight) * g, axis=0, keepdims=True)
    d_const_two = jnp.sum((other[1] * two_weight) * g, axis=0, keepdims=True)
    d_a2 = (
        dot(tables[0] + tables[1], returned[1], 0, 0)
        + a_weight * g
        + dot(d_small, wsm_ref[...], 1, 1)
    )
    gain_two = vec_ref[1:2, :]
    inverse_two = lax.rsqrt(jnp.mean(h * h, axis=-1, keepdims=True) + EPS)
    d_gain_two = jnp.sum(d_a2 * h * inverse_two, axis=0, keepdims=True)
    scaled = gain_two * d_a2
    d_h = (
        g
        + inverse_two * scaled
        - h * inverse_two**3 * jnp.mean(scaled * h, axis=-1, keepdims=True)
    )
    d_hb = d_h.astype(BF16)
    dhg[pl.ds(c, 1)] = d_hb[None]
    gather = ContextGather(
        sizes,
        place,
        dhg.at[c],
        lambda k: dhg.at[k],
        lambda k: s_g.at[k],
        lambda k: r_g.at[k],
    )
    gather.start()
    dx_ref[...] = d_h
    early["mixed"].wait()
    g_o = dot(mixed_ref[...].reshape(n_c * hc, rows), d_hb)
    run = n_d * w_rows
    for b in range(n_c):
        for k in range(n_e):
            o_own[b, k, :run, :] = g_o[(k * n_c + b) * run : (k * n_c + b + 1) * run].astype(BF16)
    parcel = Courier(s_q, r_q)
    o_pair = {}
    for k in [*range(1, pairs), 0]:
        there = lax.rem(outer + k, pairs)
        o_pair[k] = parcel.carry(
            o_own.at[there * 2 + 1 - inner], o_in.at[there], peers[0]
        )
    o_state = {}

    def o_outer():
        o_state["outer"] = []
        for k in range(1, pairs):
            there = lax.rem(outer + k, pairs)
            o_pair[k].wait_recv()
            o_sum[k - 1] = (
                o_own[there * 2 + inner].astype(F32) + o_in[there].astype(F32)
            ).astype(BF16)
            o_state["outer"].append(
                parcel.carry(o_sum.at[k - 1], o_out.at[k - 1], peers[k])
            )

    def o_across():
        o_pair[0].wait_recv()
        total = o_own[c].astype(F32) + o_in[outer].astype(F32)
        for k, copy in enumerate(o_state["outer"]):
            copy.wait_recv()
            total = total + o_out[k].astype(F32)
        o_x[...] = total.astype(BF16)
        o_state["across"] = [
            parcel.carry(o_x.at[lax.rem(e + j, n_e)], o_xr.at[j - 1], e_peers[j - 1])
            for j in range(1, n_e)
        ]

    def o_along():
        total = o_x[e].astype(F32)
        for j, copy in enumerate(o_state["across"]):
            copy.wait_recv()
            total = total + o_xr[j].astype(F32)
        for k in range(n_d):
            o_z[k, :w_rows, :] = total[k * w_rows : (k + 1) * w_rows].astype(BF16)
        o_state["along"] = [
            parcel.carry(o_z.at[lax.rem(d + k, n_d)], o_zr.at[k - 1], d_peers[k - 1])
            for k in range(1, n_d)
        ]

    def o_end():
        total = o_z[d].astype(F32)
        for k, copy in enumerate(o_state["along"]):
            copy.wait_recv()
            total = total + o_zr[k].astype(F32)
        go_ref[...] = total[:w_rows]
        parcel.finish()

    if shift:
        d_small = jnp.concatenate(
            [jnp.zeros((rows, shift), BF16), d_small[:, : LANES - shift]], axis=1
        )
    g_small = dot(a2_ref[...], d_small, 0, 0)
    dk_acc[...] = jnp.zeros_like(dk_acc)
    dv_acc[...] = jnp.zeros_like(dv_acc)
    order = [(b, j) for b in reversed(range(n_c)) for j in range(hp)]

    def fetch(n):
        b, j = order[n]
        reach = pl.ds(0, (b + 1) * rows)
        return pltpu.make_async_copy(p_ref.at[j, b, reach], p_scr.at[n % 2, reach], p_sem.at[n % 2])

    fetch(0).start()
    expert_cross()
    gather.forward()
    gather.finish()
    o_outer()
    for name in ("wo", "kh", "vh", "qt"):
        early[name].wait()
    wo_part = wo_ref[pl.ds(pl.multiple_of(c * hc, hc), hc), :]
    for b in range(n_c):
        dht_scr[:, b * rows : (b + 1) * rows] = dot(wo_part, dhg[b], 1, 1).astype(BF16)
    for n, (b, j) in enumerate(order):
        reach = (b + 1) * rows
        head = slice(j * HEAD_DIM, (j + 1) * HEAD_DIM)
        mine_q = slice(b * rows, reach)
        if n == len(order) // 4:
            o_across()
        if n == len(order) // 2:
            o_along()
        if n + 1 < len(order):
            fetch(n + 1).start()
        fetch(n).wait()
        rounded = p_scr[n % 2, :reach, :]
        prob = rounded.astype(F32)
        d_o = dht_scr[head, mine_q]
        d_prob = dot(vh_ref[j, :reach, :], d_o)
        delta = jnp.sum(prob * d_prob, axis=0, keepdims=True)
        d_scores = (prob * (d_prob - delta)).astype(BF16)
        dqt[head, mine_q] = dot(kh_ref[j, :reach, :], d_scores, 0, 0) * HEAD_DIM**-0.5
        dk_acc[j, :reach, :] += dot(d_scores, qt_ref[head, mine_q], 1, 1)
        dv_acc[j, :reach, :] += dot(rounded, d_o, 1, 1)
    dqkv[:, :hc] = dqt[...].T.astype(BF16)
    for j in range(hp):
        at = j * HEAD_DIM
        dqkv[:, hc + at : hc + at + HEAD_DIM] = dk_acc[j].astype(BF16)
        dqkv[:, 2 * hc + at : 2 * hc + at + HEAD_DIM] = dv_acc[j].astype(BF16)
    dqkv[:, 3 * hc :] = jnp.zeros((length, dqkv.shape[1] - 3 * hc), BF16)
    d_all = dqkv[...]
    bag = Courier(s_t, r_t)
    across = {}
    early["a1"].wait()
    early["wqkv"].wait()
    g_all = dot(a1_ref[...], d_all, 0, 0)
    half = D // n_e

    def send_chunk(k, value):
        for n in range(n_e):
            t_send[k, n] = value[n * half : (n + 1) * half].astype(BF16)
        across[k] = [
            bag.carry(t_send.at[k, lax.rem(e + j, n_e)], t_recv.at[k, j - 1], e_peers[j - 1])
            for j in range(1, n_e)
        ]

    for k in range(chunks - 1):
        send_chunk(k, g_all[:, k * LANES : (k + 1) * LANES])
    wqkv = wqkv_ref[...]
    gain_one = vec_ref[0:1, :]
    d_gain_one = jnp.zeros((1, D), F32)
    to_pair = []
    for n, (k, there, b) in enumerate(blocks):
        if n + 1 < n_c:
            fetch_x(blocks[n + 1][2], (n + 1) % 2).start()
        here = pl.ds(pl.multiple_of(b * rows, rows), rows)
        part = dot(dqkv[here, : 3 * hc], wqkv, 1, 1)
        dhg[pl.ds(b, 1)] = part.astype(BF16)[None]
        if k is not None:
            copy = remote(dhg.at[b], da_in.at[there], s_d.at[k], r_d.at[k], peers[0])
            copy.start()
            to_pair.append((k, copy))
        fetch_x(b, n % 2).wait()
        x = x_scr[n % 2].astype(F32)
        inverse = lax.rsqrt(jnp.mean(x * x, axis=-1, keepdims=True) + EPS)
        d_gain_one = d_gain_one + jnp.sum(part * x * inverse, axis=0, keepdims=True)
    spot = lax.broadcasted_iota(jnp.int32, (LANES, D), 0)
    lines = jnp.zeros((LANES, D), F32)
    for n, row in enumerate((d_const_one, d_const_two, d_gain_one, d_gain_two)):
        lines = lines + jnp.where(spot == shift + n_all + 4 + n, row, 0.0)
    send_chunk(chunks - 1, g_all[:, (chunks - 1) * LANES :] + g_small + lines.T)
    along = []
    for k, copy in to_pair:
        if k == 0:
            continue
        there = lax.rem(outer + k, pairs)
        copy.wait_recv()
        da_sum[k - 1] = (
            dhg[there * 2 + inner].astype(F32) + da_in[there].astype(F32)
        ).astype(BF16)
        onward = remote(
            da_sum.at[k - 1],
            da_out.at[k - 1],
            s_d.at[pairs + k - 1],
            r_d.at[pairs + k - 1],
            peers[k],
        )
        onward.start()
        along.append(onward)
    down = {}
    for k in range(chunks):
        total = t_send[k, e].astype(F32)
        for j, copy in enumerate(across[k]):
            copy.wait_recv()
            total = total + t_recv[k, j].astype(F32)
        for n in range(n_d):
            t_z[k, n, : n_c * w_rows, :] = jnp.concatenate(
                [
                    total[(b * n_d + n) * w_rows : (b * n_d + n + 1) * w_rows]
                    for b in range(n_c)
                ],
                axis=0,
            ).astype(BF16)
        down[k] = [
            bag.carry(t_z.at[k, lax.rem(d + n, n_d)], t_zr.at[k, n - 1], d_peers[n - 1])
            for n in range(1, n_d)
        ]
    o_end()
    to_pair[-1][1].wait_recv()
    d_a1 = dhg[c].astype(F32) + da_in[outer].astype(F32)
    for k, copy in enumerate(along):
        copy.wait_recv()
        d_a1 = d_a1 + da_out[k].astype(F32)
    fetch_x(c, 2).wait()
    x = x_scr[2].astype(F32)
    inverse_one = lax.rsqrt(jnp.mean(x * x, axis=-1, keepdims=True) + EPS)
    scaled = gain_one * d_a1
    dx_ref[...] += inverse_one * scaled - x * inverse_one**3 * jnp.mean(
        scaled * x, axis=-1, keepdims=True
    )
    for k in range(chunks):
        total = t_z[k, d].astype(F32)
        for n, copy in enumerate(down[k]):
            copy.wait_recv()
            total = total + t_zr[k, n].astype(F32)
        for b in range(n_c):
            t_c[b, k, :w_rows, :] = total[b * w_rows : (b + 1) * w_rows]
    t_cr[pl.ds(c, 1)] = t_c[pl.ds(c, 1)]
    turned = [
        bag.carry(t_c.at[lax.rem(c + k, n_c)], t_cr.at[c], (e, lax.rem(c + k, n_c), d))
        for k in range(1, n_c)
    ]
    expert_end()
    for copy in turned:
        copy.wait_recv()
    s_total = jnp.zeros((w_rows, SMALL), F32)
    for b in range(n_c):
        line = jnp.concatenate([t_cr[b, k] for k in range(chunks)], axis=1)[:w_rows]
        for n, ref in enumerate((gq_ref, gk_ref, gv_ref)):
            width = min(hc, D - b * hc)
            if width > 0:
                ref[:, b * hc : b * hc + width] = line[:, n * hc : n * hc + width]
        s_total = s_total + line[:, 3 * hc : 3 * hc + SMALL]
    s_lines = jnp.concatenate([s_total, jnp.zeros((w_rows, LANES - SMALL), F32)], axis=1)
    s_lines = tall(s_lines, LANES).T
    at = 0
    for ref in (grouter_ref, gcoef_ref, gvalue_ref, ggains_ref):
        ref[...] = s_lines[at : at + ref.shape[0], :w_rows]
        at += ref.shape[0]
    bag.finish()
    for _, copy in to_pair:
        copy.wait_send()
    for copy in along:
        copy.wait_send()


def backward(sizes, cfg, *operands):
    n_e, n_c, n_d = sizes
    hp, n_ff, n_all, n_loc, slots = cfg
    hc = hp * HEAD_DIM
    rows = operands[1].shape[0]
    length = rows * n_c
    pairs = n_c // 2
    dma = pltpu.SemaphoreType.DMA
    vmem = pl.BlockSpec(memory_space=pltpu.VMEM)
    anywhere = pl.BlockSpec(memory_space=pl.ANY)
    shape = jax.ShapeDtypeStruct
    part = operands[17].shape[1]
    w_rows = D // (n_e * n_c * n_d)
    chunks = up_to(3 * hc + SMALL, LANES) // LANES
    run = up_to(n_d * w_rows, 16)
    turn = up_to(n_c * w_rows, 16)
    few = up_to(w_rows, 16)
    few_wide = up_to(w_rows, 8)
    size = n_d // n_loc
    loads = (size - 1) * n_loc + n_loc - 1
    bags = chunks * (n_e - 1 + n_d - 1) + n_c - 1
    parcels = 2 * pairs - 1 + n_e - 1 + n_d - 1
    n_more = max(1, pairs - 1)
    in_specs = [vmem] * len(operands)
    in_specs[15] = in_specs[16] = in_specs[17] = anywhere
    late = [operands[n] for n in (6, 7, 10, 11, 12, 13, 14)]
    for n in (6, 7, 10, 11, 12, 13, 14):
        in_specs[n] = anywhere
    return pl.pallas_call(
        functools.partial(back_kernel, sizes, cfg),
        out_shape=(
            shape((rows, D), F32),
            shape((rows, D), F32),
            shape((n_all, rows), F32),
            *[shape((w_rows, D), F32)] * 4,
            *[shape((n, w_rows), F32) for n in (n_all, 4, 2, 2)],
            *[shape((n_loc, part // 3, LANES), F32)] * 3,
        ),
        in_specs=in_specs,
        out_specs=(vmem,) * 14,
        scratch_shapes=[
            pltpu.VMEM((n_c, rows, D), BF16),
            pltpu.VMEM((hc, length), BF16),
            pltpu.VMEM((2, length, rows), BF16),
            pltpu.VMEM((hp, length, HEAD_DIM), F32),
            pltpu.VMEM((hp, length, HEAD_DIM), F32),
            pltpu.VMEM((hc, length), F32),
            pltpu.VMEM((length, chunks * LANES), BF16),
            pltpu.VMEM((pairs, rows, D), BF16),
            pltpu.VMEM((n_more, rows, D), BF16),
            pltpu.VMEM((n_more, rows, D), BF16),
            pltpu.VMEM((3, rows, D), BF16),
            pltpu.VMEM((n_d, part, LANES), BF16),
            pltpu.VMEM((size + n_loc - 2, part, LANES), BF16),
            pltpu.VMEM((max(1, size - 1), max(1, n_loc - 1), part, LANES), BF16),
            pltpu.VMEM((max(1, n_loc - 1), part, LANES), BF16),
            pltpu.VMEM((chunks, n_e, D // n_e, LANES), BF16),
            pltpu.VMEM((chunks, n_e - 1, D // n_e, LANES), BF16),
            pltpu.VMEM((chunks, n_d, turn, LANES), BF16),
            pltpu.VMEM((chunks, n_d - 1, turn, LANES), BF16),
            pltpu.VMEM((n_c, chunks, few_wide, LANES), F32),
            pltpu.VMEM((n_c, chunks, few_wide, LANES), F32),
            pltpu.VMEM((n_c, n_e, run, D), BF16),
            pltpu.VMEM((pairs, n_e, run, D), BF16),
            pltpu.VMEM((n_more, n_e, run, D), BF16),
            pltpu.VMEM((n_more, n_e, run, D), BF16),
            pltpu.VMEM((n_e, run, D), BF16),
            pltpu.VMEM((n_e - 1, run, D), BF16),
            pltpu.VMEM((n_d, few, D), BF16),
            pltpu.VMEM((n_d - 1, few, D), BF16),
            dma((5,)),
            dma((n_c - 1,)),
            dma((n_c - 1,)),
            dma((2,)),
            dma((n_c,)),
            dma((n_c,)),
            dma((loads,)),
            dma((loads,)),
            dma((bags,)),
            dma((bags,)),
            dma((parcels,)),
            dma((parcels,)),
            *[pltpu.VMEM(w.shape, w.dtype) for w in late],
            dma((len(late),)),
        ],
        compiler_params=pltpu.CompilerParams(
            collective_id=1, has_side_effects=True, vmem_limit_bytes=VMEM_LIMIT
        ),
        name="backward",
    )(*operands)


def hand_out_kernel(*refs):
    count = (len(refs) - 2) // 3
    sources, results, held = refs[:count], refs[count : 2 * count], refs[2 * count : 3 * count]
    in_sems, out_sems = refs[-2:]
    takes = [pltpu.make_async_copy(sources[n], held[n], in_sems.at[n]) for n in range(count)]
    gives = [pltpu.make_async_copy(held[n], results[n], out_sems.at[n]) for n in range(count)]
    for copy in takes:
        copy.start()
    for take, give in zip(takes, gives):
        take.wait()
        give.start()
    for copy in gives:
        copy.wait()


def hand_out(results):
    anywhere = pl.BlockSpec(memory_space=pl.ANY)
    dma = pltpu.SemaphoreType.DMA((len(results),))
    return pl.pallas_call(
        hand_out_kernel,
        out_shape=tuple(jax.ShapeDtypeStruct(r.shape, r.dtype) for r in results),
        in_specs=[anywhere] * len(results),
        out_specs=(anywhere,) * len(results),
        scratch_shapes=[*[pltpu.VMEM(r.shape, r.dtype) for r in results], dma, dma],
        compiler_params=pltpu.CompilerParams(vmem_limit_bytes=VMEM_LIMIT),
        name="hand_out",
    )(*results)


def body(
    tokens,
    doc_ids,
    routes,
    prev_logits,
    cotangent,
    w_query,
    w_key,
    w_value,
    w_out,
    w_router,
    const_coef,
    const_value,
    norm_gains,
    expert_gate,
    expert_up,
    expert_down,
):
    sizes = n_e, n_c, n_d = tuple(lax.axis_size(axis) for axis in ALL_AXES)
    rows = tokens.shape[1]
    length = doc_ids.shape[1]
    n_loc, _, units = expert_gate.shape
    n_ff = n_loc * n_e
    n_all = w_router.shape[1]
    slots = rows // 4
    hp = -(-HEADS // n_c)
    cfg = (hp, n_ff, n_all, n_loc, slots)
    routes_t = routes[0].T
    upstream = cotangent[0]
    (
        x_all,
        wqkv,
        wo,
        wsm,
        vec,
        a1,
        q_t,
        k_h,
        v_h,
        mixed,
        h,
        a2,
        small,
        grads,
        returned,
        probs,
        *_,
    ) = front(
        sizes,
        cfg,
        w_query,
        w_key,
        w_value,
        w_out,
        w_router.T,
        const_coef.T,
        const_value.T,
        norm_gains.T,
        tokens[0],
        expert_gate,
        expert_up,
        expert_down,
        doc_ids,
        routes_t,
        prev_logits[0].T,
        upstream,
    )
    results = backward(
        sizes,
        cfg,
        returned,
        h,
        a2,
        small,
        upstream,
        routes_t,
        wo,
        wqkv,
        wsm,
        vec,
        mixed,
        a1,
        q_t,
        k_h,
        v_h,
        probs,
        x_all,
        grads.reshape(n_d, 3 * D * units // LANES, LANES),
    )
    block_rows, d_x, d_prev, *square = hand_out(results)
    narrow = square[4:8]
    return (
        block_rows[None],
        d_x[None],
        d_prev.T[None],
        *square[:4],
        *[grad.T for grad in narrow],
        *[grad.reshape(n_loc, D, units) for grad in square[8:]],
    )


def solution(mesh):
    rows = P(("expert", "dp"), "context", None)
    weights = P(ALL_AXES, None)
    units = P("expert", None, ("context", "dp"))
    return jax.shard_map(
        body,
        mesh=mesh,
        in_specs=(rows, P(("expert", "dp"), None), rows, rows, rows)
        + (weights,) * 8
        + (units,) * 3,
        out_specs=(rows,) * 3 + (weights,) * 8 + (units,) * 3,
        check_vma=False,
    )
```
